32 devices in a mesh: dp: 4 (over y, x), seq: 8 (over z, core).
Axes of the slice: x: 2, y: 2, z: 4, core: 2. Of those that a mesh axis runs over, the one named last changes fastest.
Arguments:
- char_ids: int32 [4, 4096], P('dp', 'seq'), may hold values from 0 to 255
- seg_starts: int32 [4, 8], P('dp', 'seq'), may hold values from 0 to 1, as said below
- char_table: bfloat16 [256, 1024], replicated, may hold values from -6 to 6
- norm_gain: float32 [1024], replicated, may hold values from 0.5 to 1.5
- qkv_weight: bfloat16 [1024, 3072], replicated, may hold values from -0.1875 to 0.1875
- distance_bias: float32 [256], replicated, may hold values from -3 to 3
- state_query: bfloat16 [512, 1024], replicated, may hold values from -9 to 9
- state_init: bfloat16 [512, 1024], replicated, may hold values from -6 to 6
- state_gain: float32 [1024], replicated, may hold values from 0.5 to 1.5
- state_kv_weight: bfloat16 [1024, 2048], replicated, may hold values from -0.1875 to 0.1875
- gate_logit: float32 [1024], replicated, may hold values from 0 to 6
- out_weight: bfloat16 [1024, 1024], replicated, may hold values from -1.5 to 1.5
- mlp_gain: float32 [1024], replicated, may hold values from 0.5 to 1.5
- up_weight: bfloat16 [1024, 4096], replicated, may hold values from -0.1875 to 0.1875
- down_weight: bfloat16 [4096, 1024], replicated, may hold values from -0.1875 to 0.1875
- cotangent: bfloat16 [4, 4096, 1024], P('dp', 'seq'), may hold values from -6 to 6
Outputs:
- layer_out: bfloat16 [4, 4096, 1024], P('dp', 'seq')
- grad_table: float32 [256, 1024], P('seq')
- grad_norm_gain: float32 [1024], P('seq')
- grad_qkv: float32 [1024, 3072], P('seq')
- grad_distance_bias: float32 [256], P('seq')
- grad_state_query: float32 [512, 1024], P('seq')
- grad_state_init: float32 [512, 1024], P('seq')
- grad_state_gain: float32 [1024], P('seq')
- grad_state_kv: float32 [1024, 2048], P('seq')
- grad_gate: float32 [1024], P('seq')
- grad_out: float32 [1024, 1024], P('seq')
- grad_mlp_gain: float32 [1024], P('seq')
- grad_up: float32 [1024, 4096], P('seq')
- grad_down: float32 [4096, 1024], P('seq')
The draws below stay inside these ranges and needn't reach their ends.
Inputs may be any that keep to these rules, and one draw needn't show every extreme that they name: `seg_starts`: the first window of every row is marked; one of the 4 rows has no other mark.
All inputs are finite; a program needn't handle non-finite values.
Results may differ from the reference program's by a relative error of at most 0.034.
Values may be sent and summed in bfloat16 or wider, within the bound.
No kernel may reach another device: no remote copies, remote signals or barrier semaphores. Data moves between devices by JAX's collectives and lax.ppermute only.
A program may use at most 448 MiB of HBM per device.

```python
import math
import jax
import jax.numpy as jnp
import numpy as np
from jax import lax

D = 1024
HEADS = 8
HEAD_DIM = 128
FF = 4096
VOCAB = 256
STATES = 512
WINDOW = 512
BUCKETS = 32
MAX_DISTANCE = 128
ROWS = 4
WINDOWS = 8
SEQLEN = 4096


def draw_seg_starts(key, part):
    key = jax.random.fold_in(key, 7)
    key_marks, key_whole = jax.random.split(key)
    marks = (jax.random.randint(key_marks, (ROWS, WINDOWS), 0, 8) == 0).astype(jnp.int32)
    whole_row = jax.random.randint(key_whole, (), 0, ROWS)
    keep_marks = (jnp.arange(ROWS, dtype=jnp.int32) != whole_row).astype(jnp.int32)[:, None]
    first_window = (jnp.arange(WINDOWS, dtype=jnp.int32) == 0).astype(jnp.int32)[None, :]
    return jnp.maximum(marks * keep_marks, first_window)


def with_ends(array, stream_key, smallest, top_value):
    longest = array.shape.index(max(array.shape))
    spots = []
    for shift in (0, 1):
        where = [jax.random.randint(jax.random.fold_in(stream_key, axis), (), 0, length) for axis, length in enumerate(array.shape)]
        where[longest] = (where[longest] + shift) % array.shape[longest]
        spots.append(tuple(where))
    return array.at[spots[0]].set(smallest).at[spots[1]].set(top_value)


def block_scale(own_key, dims, cuts, low, largest):
    loudness, own = 1.0, jax.random.fold_in(own_key, 6)
    for dim, shards_of in cuts:
        draws = jnp.exp(jax.random.uniform(jax.random.fold_in(own, dim), (shards_of,), jnp.float32, low / len(cuts), largest / len(cuts)))
        loudness = loudness * jnp.repeat(draws, dims[dim] // shards_of).reshape([-1 if axis == dim else 1 for axis in range(len(dims))])
    return loudness


def bell_draw(own_key, shape, scale, bound, cuts=(), kind=jnp.bfloat16):
    level = block_scale(own_key, shape, cuts, -0.22, 0.18) if cuts else 1.0
    values = jax.random.normal(own_key, shape, jnp.float32) * scale * level
    return jnp.minimum(jnp.maximum(values, -bound), bound).astype(kind)


def setup_inputs(seed: int = 0) -> dict:
    streams_of = jax.random.split(jax.random.key(seed), 17)
    char_ids = with_ends(jax.random.randint(streams_of[0], (ROWS, SEQLEN), 0, VOCAB), jax.random.fold_in(streams_of[0], 1), 0, VOCAB - 1).astype(jnp.int32)
    seg_starts = draw_seg_starts(jax.random.fold_in(streams_of[16], 71), 0)
    char_table = bell_draw(streams_of[2], (VOCAB, D), 1.0, 6.0)
    norm_gain = jnp.clip(1.0 + 0.1 * jax.random.normal(streams_of[3], (D,), jnp.float32), 0.5, 1.5)
    qkv_weight = bell_draw(streams_of[4], (D, 3 * D), D ** -0.5, 0.1875)
    distance_bias = bell_draw(streams_of[5], (HEADS * BUCKETS,), 0.5, 3.0, (), jnp.float32)
    state_query = bell_draw(streams_of[6], (STATES, D), 1.5, 9.0)
    state_init = bell_draw(streams_of[7], (STATES, D), 1.0, 6.0)
    state_gain = jnp.clip(1.0 + 0.1 * jax.random.normal(streams_of[8], (D,), jnp.float32), 0.5, 1.5)
    state_kv_weight = bell_draw(streams_of[9], (D, 2 * D), D ** -0.5, 0.1875)
    gate_logit = jnp.clip(jax.random.uniform(streams_of[10], (D,), jnp.float32, 0.0, 6.0), 0.0, 6.0)
    out_weight = bell_draw(streams_of[11], (D, D), (D // 64) ** -0.5, 1.5)
    mlp_gain = jnp.clip(1.0 + 0.1 * jax.random.normal(streams_of[12], (D,), jnp.float32), 0.5, 1.5)
    up_weight = bell_draw(streams_of[13], (D, FF), D ** -0.5, 0.1875)
    down_weight = bell_draw(streams_of[14], (FF, D), (FF // 4) ** -0.5, 0.1875)
    cotangent = bell_draw(streams_of[15], (ROWS, SEQLEN, D), 1.0, 6.0, ((0, 4), (1, 8)))
    return dict(char_ids=char_ids, seg_starts=seg_starts, char_table=char_table, norm_gain=norm_gain, qkv_weight=qkv_weight, distance_bias=distance_bias, state_query=state_query, state_init=state_init, state_gain=state_gain, state_kv_weight=state_kv_weight, gate_logit=gate_logit, out_weight=out_weight, mlp_gain=mlp_gain, up_weight=up_weight, down_weight=down_weight, cotangent=cotangent)


@jax.custom_vjp
def low(v):
    return lax.optimization_barrier(v.astype(jnp.bfloat16)).astype(jnp.float32)

@jax.custom_vjp
def low_back(v):
    return v

def low_keep(v):
    return (low(v), None)

def low_pass(kept, grad):
    return (grad,)

def back_keep(v):
    return (v, None)

def back_low(kept, grad):
    return (low(grad),)
low.defvjp(low_keep, low_pass)
low_back.defvjp(back_keep, back_low)
epsilon = 1e-05
highest = lax.Precision.HIGHEST

def dense(left, right):
    return jnp.dot(left, right, precision=highest, preferred_element_type=jnp.float32)

def layer_norm(value, gain):
    centre = lax.optimization_barrier(jnp.mean(value, axis=-1, keepdims=True))
    offset = value - centre
    spread = lax.optimization_barrier(jnp.mean(offset * offset, axis=-1, keepdims=True))
    return offset * lax.rsqrt(spread + epsilon) * gain

def bucket_table():
    distance = np.arange(WINDOW)
    exact_count = BUCKETS // 2
    log_ratio = np.log(np.maximum(distance, 1) / exact_count) / math.log(MAX_DISTANCE / exact_count)
    far_bucket = exact_count + np.floor(log_ratio * (BUCKETS - exact_count)).astype(np.int64)
    return np.where(distance < exact_count, distance, np.minimum(far_bucket, BUCKETS - 1))

def distance_bias_matrix(distance_bias):
    table = distance_bias.reshape(HEADS, BUCKETS)[:, bucket_table()]
    query_pos = np.arange(WINDOW)[:, None]
    key_pos = np.arange(2 * WINDOW)[None, :]
    distance = WINDOW + query_pos - key_pos
    token_mask = (distance >= 0) & (distance < WINDOW)
    return (table[:, np.clip(distance, 0, WINDOW - 1)], token_mask)

def layer(char_table, norm_gain, qkv_weight, distance_bias, state_query, state_init, state_gain, state_kv_weight, gate_logit, out_weight, mlp_gain, up_weight, down_weight, onehot, seg_starts):
    score_scale = 1.0 / math.sqrt(HEAD_DIM)
    tokens = dense(onehot, char_table)
    normed = low(layer_norm(tokens, norm_gain))
    qkv = low_back(low(dense(normed, qkv_weight))).reshape(ROWS * WINDOWS, WINDOW, 3, HEADS, HEAD_DIM)
    queries = qkv[:, :, 0]
    own_kv = qkv[:, :, 1:]
    query_state = state_query.reshape(STATES, HEADS, HEAD_DIM)

    def summarise(kv_block):
        scores = jnp.einsum('shd,thd->hst', query_state, kv_block[:, 0], precision=highest) * score_scale
        attention = low(jax.nn.softmax(low_back(scores), axis=-1))
        update = jnp.einsum('hst,thd->shd', attention, kv_block[:, 1], precision=highest)
        return low_back(update.reshape(STATES, D))
    updates = lax.map(jax.checkpoint(summarise), own_kv).reshape(ROWS, WINDOWS, STATES, D)
    forget = jax.nn.sigmoid(gate_logit)

    def chain(carried, item):
        update, flag = item
        state_in = jnp.where(flag[:, None, None] > 0, state_init[None], carried)
        return (forget * state_in + (1.0 - forget) * update, state_in)
    _, states_in = lax.scan(chain, jnp.zeros((ROWS, STATES, D), jnp.float32), (jnp.swapaxes(updates, 0, 1), seg_starts.T))
    states_in = jnp.swapaxes(states_in, 0, 1)
    state_normed = low(layer_norm(states_in, state_gain))
    state_kv = low_back(low(dense(state_normed.reshape(-1, D), state_kv_weight)))
    state_kv = state_kv.reshape(ROWS * WINDOWS, STATES, 2, HEADS, HEAD_DIM)
    prev_kv = jnp.concatenate([jnp.zeros_like(own_kv[:1]), own_kv[:-1]], axis=0)
    token_bias, token_mask = distance_bias_matrix(distance_bias)
    full_bias = jnp.concatenate([token_bias, jnp.zeros((HEADS, WINDOW, STATES), jnp.float32)], axis=2)
    halo_live = (seg_starts == 0).reshape(-1)

    def attend(block):
        query_w, own_w, prev_w, state_w, live_w = block
        context = jnp.concatenate([prev_w, own_w, state_w], axis=0)
        scores = jnp.einsum('qhd,khd->hqk', query_w, context[:, 0], precision=highest) * score_scale + full_bias
        visible = jnp.concatenate([jnp.logical_and(token_mask[:, :WINDOW], live_w), token_mask[:, WINDOW:], jnp.ones((WINDOW, STATES), jnp.bool_)], axis=1)
        scores = low_back(jnp.where(visible[None], scores, -1e+30))
        attention = low(jax.nn.softmax(scores, axis=-1))
        mixed = jnp.einsum('hqk,khd->qhd', attention, context[:, 1], precision=highest)
        return low_back(low(mixed.reshape(WINDOW, D)))
    mixed_heads = lax.map(jax.checkpoint(attend), (queries, own_kv, prev_kv, state_kv, halo_live))
    attention_out = low_back(dense(mixed_heads.reshape(-1, D), out_weight))
    residual = tokens + attention_out
    mlp_in = low(layer_norm(residual, mlp_gain))
    pre_act = low_back(dense(mlp_in, up_weight))
    act_low = low(jax.nn.gelu(pre_act))
    return residual + dense(act_low, down_weight)

def reference(char_ids, seg_starts, char_table, norm_gain, qkv_weight, distance_bias, state_query, state_init, state_gain, state_kv_weight, gate_logit, out_weight, mlp_gain, up_weight, down_weight, cotangent):
    onehot = (char_ids.reshape(-1, 1) == jnp.arange(VOCAB)[None, :]).astype(jnp.float32)
    params = (char_table, norm_gain, qkv_weight, distance_bias, state_query, state_init, state_gain, state_kv_weight, gate_logit, out_weight, mlp_gain, up_weight, down_weight)
    params = tuple((param.astype(jnp.float32) for param in params))

    def forward(*inputs):
        return layer(*inputs, onehot, seg_starts)
    output, pullback = jax.vjp(forward, *params)
    grads = pullback(cotangent.reshape(-1, D).astype(jnp.float32))
    layer_out = output.reshape(ROWS, SEQLEN, D).astype(jnp.bfloat16)
    return (layer_out, grads[0], grads[1], grads[2], grads[3], grads[4], grads[5], grads[6], grads[7], grads[8], grads[9], grads[10], grads[11], grads[12])
```

```python
import functools
import math

import jax
import jax.numpy as jnp
import numpy as np
from jax import lax
from jax.experimental import pallas as pl
from jax.experimental.pallas import tpu as pltpu
from jax.sharding import PartitionSpec as P

D = 1024
HEADS = 8
HEAD_DIM = 128
FF = 4096
VOCAB = 256
STATES = 512
WINDOW = 512
BUCKETS = 32
MAX_DISTANCE = 128
CONTEXT = 2 * WINDOW
TILE = 256
SPLITS = 2

epsilon = 1e-05
hidden = -1e30
log2e = math.log2(math.e)
score_scale = 1.0 / math.sqrt(HEAD_DIM)
f32 = jnp.float32
bf16 = jnp.bfloat16

NN = (((1,), (0,)), ((), ()))
NT = (((1,), (1,)), ((), ()))
TN = (((0,), (0,)), ((), ()))


def dot(a, b, dims=NN):
    return lax.dot_general(a, b, dims, preferred_element_type=f32)


def params(mib=48):
    return pltpu.CompilerParams(
        dimension_semantics=("arbitrary",), vmem_limit_bytes=mib * 1024 * 1024
    )


def cost(flops, moved, exps=0):
    return pl.CostEstimate(
        flops=int(flops), bytes_accessed=int(moved), transcendentals=int(exps)
    )


def norm_parts(value):
    centre = jnp.mean(value, axis=-1, keepdims=True)
    offset = value - centre
    spread = jnp.mean(offset * offset, axis=-1, keepdims=True)
    inv = lax.rsqrt(spread + epsilon)
    return offset * inv, inv


def norm_back(unit, inv, gain, upstream):
    scaled = upstream * gain
    a = jnp.mean(scaled, axis=-1, keepdims=True)
    b = jnp.mean(scaled * unit, axis=-1, keepdims=True)
    return (scaled - a - unit * b) * inv


def bucket_table():
    distance = np.arange(WINDOW)
    exact_count = BUCKETS // 2
    log_ratio = np.log(np.maximum(distance, 1) / exact_count) / math.log(
        MAX_DISTANCE / exact_count
    )
    far_bucket = exact_count + np.floor(log_ratio * (BUCKETS - exact_count)).astype(
        np.int64
    )
    return np.where(
        distance < exact_count, distance, np.minimum(far_bucket, BUCKETS - 1)
    )


def lane_pick():
    pick = np.zeros((BUCKETS, CONTEXT), np.float32)
    table = bucket_table()
    for m in range(1, WINDOW + 1):
        pick[table[WINDOW - m], m] = 1.0
    return pick


def lane_hidden():
    m = np.arange(CONTEXT)
    return np.where((m >= 1) & (m <= WINDOW), 0.0, hidden).astype(np.float32)[None]


def summary_forward_kernel(
    span, sq, kt, vt, lnn, init, fcol, state_out, y_out, lse_out, lg, a_s, y_s
):
    kt_h = kt[...]
    vtr = vt[...].astype(f32).T.astype(bf16)
    lg[...] = dot(kt_h, sq[...], NT) * (score_scale * log2e)
    a_s[...] = init[...].astype(f32).T
    y_s[...] = jnp.zeros_like(y_s)
    f = jnp.concatenate([fcol[...]] * (STATES // 128), axis=1)

    def step(w, _):
        n = lnn[w]
        x = lg[...] + jnp.concatenate([n] * (STATES // 128), axis=1)
        m = jnp.max(x, axis=0, keepdims=True)
        p = jnp.exp2(x - m)
        z = jnp.sum(p, axis=0, keepdims=True)
        u = dot(vtr, p.astype(bf16)) * (1.0 / z)
        lse_out[0, pl.ds(w, 1), :] = m + jnp.log2(z)
        a = a_s[...]
        y_s[...] = a - u + f * y_s[...]
        a_s[...] = u + f * (a - u)
        return 0

    lax.fori_loop(span[0], span[1], step, 0)
    state_out[...] = a_s[...].T
    y_out[...] = y_s[...].T


def summary_forward(span, state_query, qkv_table, lnn, state_init, fcol):
    windows = lnn.shape[0]
    head = lambda k: (lambda h, s: (0, k * HEADS + h))
    return pl.pallas_call(
        summary_forward_kernel,
        grid_spec=pltpu.PrefetchScalarGridSpec(
            num_scalar_prefetch=1,
            grid=(HEADS,),
            in_specs=[
                pl.BlockSpec((STATES, HEAD_DIM), head(0)),
                pl.BlockSpec((VOCAB, HEAD_DIM), head(1)),
                pl.BlockSpec((VOCAB, HEAD_DIM), head(2)),
                pl.BlockSpec((windows, VOCAB, 128), lambda h, s: (0, 0, 0)),
                pl.BlockSpec((STATES, HEAD_DIM), head(0)),
                pl.BlockSpec((HEAD_DIM, 128), lambda h, s: (h, 0)),
            ],
            out_specs=[
                pl.BlockSpec((STATES, HEAD_DIM), head(0)),
                pl.BlockSpec((STATES, HEAD_DIM), head(0)),
                pl.BlockSpec((1, windows, STATES), lambda h, s: (h, 0, 0)),
            ],
            scratch_shapes=[
                pltpu.VMEM((VOCAB, STATES), f32),
                pltpu.VMEM((HEAD_DIM, STATES), f32),
                pltpu.VMEM((HEAD_DIM, STATES), f32),
            ],
        ),
        out_shape=[
            jax.ShapeDtypeStruct((STATES, D), f32),
            jax.ShapeDtypeStruct((STATES, D), f32),
            jax.ShapeDtypeStruct((HEADS, windows, STATES), f32),
        ],
        compiler_params=params(),
        cost_estimate=cost(4e9, 8e6, 8e6),
        name="summary_forward",
    )(span, state_query, qkv_table, qkv_table, lnn, state_init, fcol)


def summary_backward_kernel(
    span,
    sq,
    kt,
    vt,
    lnn,
    lse,
    local,
    fcol,
    gk_in,
    gv_in,
    gk_out,
    gv_out,
    gsq_out,
    ginit_out,
    lg,
    g_s,
    gs_s,
    gv_s,
):
    kt_h = kt[...]
    vt_h = vt[...]
    sq_h = sq[...]
    lg[...] = dot(kt_h, sq_h, NT) * (score_scale * log2e)
    g_s[...] = local[...].T
    gs_s[...] = jnp.zeros_like(gs_s)
    gv_s[...] = gv_in[...]
    f = jnp.concatenate([fcol[...]] * (STATES // 128), axis=1)
    first, here = span[0], span[1]

    def step(t, _):
        w = here - 1 - t
        g = g_s[...]
        fg = f * g
        gu = (g - fg).astype(bf16)
        g_s[...] = fg
        n = lnn[w]
        p = jnp.exp2(
            lg[...]
            + jnp.concatenate([n] * (STATES // 128), axis=1)
            - lse[0, pl.ds(w, 1), :]
        )
        dw = dot(vt_h, gu)
        pd = p * dw
        inner = jnp.sum(pd, axis=0, keepdims=True)
        gs_s[...] += pd - p * inner
        gv_s[...] += dot(p.astype(bf16), gu, NT)
        return 0

    lax.fori_loop(0, here - first, step, 0)
    gs = (gs_s[...] * score_scale).astype(bf16)
    gk_out[...] = (gk_in[...] + dot(gs, sq_h)).astype(bf16)
    gv_out[...] = gv_s[...].astype(bf16)
    gsq_out[...] = dot(gs, kt_h, TN).astype(bf16)
    ginit_out[...] = g_s[...].T.astype(bf16)


def summary_backward(span, state_query, qkv_table, lnn, lse, local, fcol, gk, gv):
    windows = lnn.shape[0]
    head = lambda k: (lambda h, s: (0, k * HEADS + h))
    table = pl.BlockSpec((VOCAB, HEAD_DIM), head(0))
    states = pl.BlockSpec((STATES, HEAD_DIM), head(0))
    return pl.pallas_call(
        summary_backward_kernel,
        grid_spec=pltpu.PrefetchScalarGridSpec(
            num_scalar_prefetch=1,
            grid=(HEADS,),
            in_specs=[
                states,
                pl.BlockSpec((VOCAB, HEAD_DIM), head(1)),
                pl.BlockSpec((VOCAB, HEAD_DIM), head(2)),
                pl.BlockSpec((windows, VOCAB, 128), lambda h, s: (0, 0, 0)),
                pl.BlockSpec((1, windows, STATES), lambda h, s: (h, 0, 0)),
                states,
                pl.BlockSpec((HEAD_DIM, 128), lambda h, s: (h, 0)),
                table,
                table,
            ],
            out_specs=[table, table, states, states],
            scratch_shapes=[
                pltpu.VMEM((VOCAB, STATES), f32),
                pltpu.VMEM((HEAD_DIM, STATES), f32),
                pltpu.VMEM((VOCAB, STATES), f32),
                pltpu.VMEM((VOCAB, HEAD_DIM), f32),
            ],
        ),
        out_shape=[
            jax.ShapeDtypeStruct((VOCAB, D), bf16),
            jax.ShapeDtypeStruct((VOCAB, D), bf16),
            jax.ShapeDtypeStruct((STATES, D), bf16),
            jax.ShapeDtypeStruct((STATES, D), bf16),
        ],
        compiler_params=params(),
        cost_estimate=cost(8e9, 8e6, 8e6),
        name="summary_backward",
    )(span, state_query, qkv_table, qkv_table, lnn, lse, local, fcol, gk, gv)


def bias_tile(row):
    spread = jnp.broadcast_to(row, (TILE, CONTEXT))
    shifted = pltpu.roll(spread, 0, 1, stride=1, stride_axis=0)
    return shifted[:, : 3 * TILE].T


def attention_forward_kernel(
    live, pick, pick_t, qt, kt, vt, sk, sv, bias_row, mixed_out, lse_out, bias
):
    bias[...] = bias_tile(bias_row[0])
    prev_add = jnp.where(live[0] > 0, 0.0, hidden).astype(f32)
    keys = dot(pick[...], kt[...]).astype(bf16)
    values_t = dot(vt[...], pick_t[...], TN).astype(bf16)
    query = dot(pick[WINDOW:, :], qt[...]).astype(bf16)
    state_values_t = sv[...].astype(f32).T.astype(bf16)
    for j in range(WINDOW // TILE):
        q = query[j * TILE : (j + 1) * TILE]
        scores = []
        for rel in range(3):
            kt_i = j + rel
            s = (
                dot(keys[kt_i * TILE : (kt_i + 1) * TILE], q, NT)
                * (score_scale * log2e)
                + bias[rel * TILE : (rel + 1) * TILE]
            )
            if kt_i * TILE < WINDOW:
                s = s + prev_add
            scores.append(s)
        for st in range(STATES // TILE):
            scores.append(
                dot(sk[st * TILE : (st + 1) * TILE, :], q, NT) * (score_scale * log2e)
            )
        peak = functools.reduce(
            jnp.maximum, [jnp.max(s, axis=0, keepdims=True) for s in scores]
        )
        total = jnp.zeros((1, TILE), f32)
        out = jnp.zeros((HEAD_DIM, TILE), f32)
        for i, s in enumerate(scores):
            p = jnp.exp2(s - peak)
            total = total + jnp.sum(p, axis=0, keepdims=True)
            if i < 3:
                v = values_t[:, (j + i) * TILE : (j + i + 1) * TILE]
            else:
                v = state_values_t[:, (i - 3) * TILE : (i - 2) * TILE]
            out = out + dot(v, p.astype(bf16))
        out = out * (1.0 / total)
        mixed_out[j * TILE : (j + 1) * TILE, :] = out.T.astype(bf16)
        lse_out[0, :, j * TILE : (j + 1) * TILE] = peak + jnp.log2(total)


def attention_forward(live, pick, pick_t, qkv_table, sk, sv, bias_rows):
    head = lambda k: (lambda h, s: (0, k * HEADS + h))
    whole = lambda *shape: pl.BlockSpec(shape, lambda h, s: (0,) * len(shape))
    return pl.pallas_call(
        attention_forward_kernel,
        grid_spec=pltpu.PrefetchScalarGridSpec(
            num_scalar_prefetch=1,
            grid=(HEADS,),
            in_specs=[
                whole(CONTEXT, VOCAB),
                whole(VOCAB, CONTEXT),
                pl.BlockSpec((VOCAB, HEAD_DIM), head(0)),
                pl.BlockSpec((VOCAB, HEAD_DIM), head(1)),
                pl.BlockSpec((VOCAB, HEAD_DIM), head(2)),
                pl.BlockSpec((STATES, HEAD_DIM), head(0)),
                pl.BlockSpec((STATES, HEAD_DIM), head(1)),
                pl.BlockSpec((1, 1, CONTEXT), lambda h, s: (h, 0, 0)),
            ],
            out_specs=[
                pl.BlockSpec((WINDOW, HEAD_DIM), head(0)),
                pl.BlockSpec((1, 1, WINDOW), lambda h, s: (h, 0, 0)),
            ],
            scratch_shapes=[pltpu.VMEM((3 * TILE, TILE), f32)],
        ),
        out_shape=[
            jax.ShapeDtypeStruct((WINDOW, D), bf16),
            jax.ShapeDtypeStruct((HEADS, 1, WINDOW), f32),
        ],
        compiler_params=params(),
        cost_estimate=cost(6e9, 8e6, 6e6),
        name="attention_forward",
    )(live, pick, pick_t, qkv_table, qkv_table, qkv_table, sk, sv, bias_rows)


def attention_backward_kernel(
    live,
    pick,
    pick_t,
    qt,
    kt,
    vt,
    sk,
    sv,
    bias_row,
    lse,
    mixed,
    grad,
    gq_out,
    gk_out,
    gv_out,
    gsk_out,
    gsv_out,
    fold_out,
    bias,
    bias_grad,
):
    bias[...] = bias_tile(bias_row[0])
    bias_grad[...] = jnp.zeros_like(bias_grad)
    prev_add = jnp.where(live[0] > 0, 0.0, hidden).astype(f32)
    keys = dot(pick[...], kt[...]).astype(bf16)
    keys_t = dot(kt[...], pick_t[...], TN).astype(bf16)
    values = dot(pick[...], vt[...]).astype(bf16)
    query = dot(pick[WINDOW:, :], qt[...]).astype(bf16)
    state_keys_t = sk[...].astype(f32).T.astype(bf16)
    inner_all = jnp.sum(
        (mixed[...].astype(f32) * grad[...].astype(f32)).T, axis=0, keepdims=True
    )
    blocks = WINDOW // TILE
    gq = [jnp.zeros((HEAD_DIM, TILE), f32) for _ in range(blocks)]
    gk = jnp.zeros((VOCAB, HEAD_DIM), f32)
    gv = jnp.zeros((VOCAB, HEAD_DIM), f32)

    def piece(k, k_t, v, j, add, bias_at):
        rows = slice(j * TILE, (j + 1) * TILE)
        q = query[rows]
        g = grad[rows, :]
        s = dot(k, q, NT) * (score_scale * log2e)
        if bias_at is not None:
            s = s + bias[bias_at * TILE : (bias_at + 1) * TILE]
        shift = lse[0, :, rows]
        if add:
            shift = shift - prev_add
        p = jnp.exp2(s - shift)
        dp = dot(v, g, NT)
        gs = p * (dp - inner_all[:, rows])
        gs16 = gs.astype(bf16)
        gq[j] = gq[j] + dot(k_t, gs16)
        if bias_at is not None:
            bias_grad[bias_at * TILE : (bias_at + 1) * TILE] += gs
        return dot(gs16, q), dot(p.astype(bf16), g)

    for st in range(STATES // TILE):
        at = slice(st * TILE, (st + 1) * TILE)
        parts = [
            piece(sk[at, :], state_keys_t[:, at], sv[at, :], j, False, None)
            for j in range(blocks)
        ]
        gsk_out[at, :] = (sum(p[0] for p in parts) * score_scale).astype(bf16)
        gsv_out[at, :] = sum(p[1] for p in parts).astype(bf16)
    for tile in range(CONTEXT // TILE):
        at = slice(tile * TILE, (tile + 1) * TILE)
        parts = [
            piece(keys[at], keys_t[:, at], values[at], j, tile * TILE < WINDOW, tile - j)
            for j in range(blocks)
            if 0 <= tile - j < 3
        ]
        one = pick_t[:, at]
        gk = gk + dot(one, (sum(p[0] for p in parts) * score_scale).astype(bf16))
        gv = gv + dot(one, sum(p[1] for p in parts).astype(bf16))
    gk_out[...] = gk
    gv_out[...] = gv
    total = jnp.zeros((HEAD_DIM, VOCAB), f32)
    for j in range(blocks):
        rows = slice(WINDOW + j * TILE, WINDOW + (j + 1) * TILE)
        total = total + dot((gq[j] * score_scale).astype(bf16), pick[rows, :])
    gq_out[...] = total.T.astype(bf16)
    rows = jnp.concatenate(
        [bias_grad[...].T, jnp.zeros((TILE, CONTEXT - 3 * TILE), f32)], axis=1
    )
    count = TILE
    while count > 8:
        count //= 2
        rows = rows[:count] + pltpu.roll(rows[count:], CONTEXT - count, 1)
    folded = rows[0:1]
    for r in range(1, 8):
        folded = folded + pltpu.roll(rows, CONTEXT - r, 1)[r : r + 1]
    fold_out[0] = folded


def attention_backward(
    live, pick, pick_t, qkv_table, sk, sv, bias_rows, lse, mixed, grad
):
    head = lambda k: (lambda h, s: (0, k * HEADS + h))
    whole = lambda *shape: pl.BlockSpec(shape, lambda h, s: (0,) * len(shape))
    table = pl.BlockSpec((VOCAB, HEAD_DIM), head(0))
    tokens = pl.BlockSpec((WINDOW, HEAD_DIM), head(0))
    states = pl.BlockSpec((STATES, HEAD_DIM), head(0))
    return pl.pallas_call(
        attention_backward_kernel,
        grid_spec=pltpu.PrefetchScalarGridSpec(
            num_scalar_prefetch=1,
            grid=(HEADS,),
            in_specs=[
                whole(CONTEXT, VOCAB),
                whole(VOCAB, CONTEXT),
                pl.BlockSpec((VOCAB, HEAD_DIM), head(0)),
                pl.BlockSpec((VOCAB, HEAD_DIM), head(1)),
                pl.BlockSpec((VOCAB, HEAD_DIM), head(2)),
                pl.BlockSpec((STATES, HEAD_DIM), head(0)),
                pl.BlockSpec((STATES, HEAD_DIM), head(1)),
                pl.BlockSpec((1, 1, CONTEXT), lambda h, s: (h, 0, 0)),
                pl.BlockSpec((1, 1, WINDOW), lambda h, s: (h, 0, 0)),
                tokens,
                tokens,
            ],
            out_specs=[
                table,
                table,
                table,
                states,
                states,
                pl.BlockSpec((1, 1, CONTEXT), lambda h, s: (h, 0, 0)),
            ],
            scratch_shapes=[
                pltpu.VMEM((3 * TILE, TILE), f32),
                pltpu.VMEM((3 * TILE, TILE), f32),
            ],
        ),
        out_shape=[
            jax.ShapeDtypeStruct((VOCAB, D), bf16),
            jax.ShapeDtypeStruct((VOCAB, D), f32),
            jax.ShapeDtypeStruct((VOCAB, D), f32),
            jax.ShapeDtypeStruct((STATES, D), bf16),
            jax.ShapeDtypeStruct((STATES, D), bf16),
            jax.ShapeDtypeStruct((HEADS, 1, CONTEXT), f32),
        ],
        compiler_params=params(),
        cost_estimate=cost(14e9, 12e6, 6e6),
        name="attention_backward",
    )(
        live,
        pick,
        pick_t,
        qkv_table,
        qkv_table,
        qkv_table,
        sk,
        sv,
        bias_rows,
        lse,
        mixed,
        grad,
    )


def mlp_kernel(x, cot, up, down, out_in, gx_in, gd_out, gu_out, out, gx, xt):
    @pl.when(pl.program_id(0) == 0)
    def _():
        out[...] = out_in[...]
        gx[...] = gx_in[...]
        xt[...] = x[...].astype(f32).T.astype(bf16)

    up_b = up[...]
    down_b = down[...]
    pre = dot(x[...], up_b)
    root = math.sqrt(2.0 / math.pi)
    square = pre * pre
    t = jnp.tanh(root * pre * (1.0 + 0.044715 * square))
    half = 0.5 * (1.0 + t)
    act = (pre * half).astype(bf16)
    slope = half + (0.5 * root) * pre * (1.0 - t * t) * (1.0 + (3 * 0.044715) * square)
    grad_pre = (dot(cot[...], down_b, NT) * slope).astype(bf16)
    out[...] += dot(act, down_b)
    gx[...] += dot(grad_pre, up_b, NT)
    gd_out[...] = dot(act, cot[...], TN).astype(bf16)
    gu_out[...] = dot(xt[...], grad_pre).astype(bf16)


def mlp_part(part, x, cot, up, down, out, gx):
    count = FF // SPLITS // TILE
    whole = pl.BlockSpec((WINDOW, D), lambda s: (0, 0))
    return pl.pallas_call(
        mlp_kernel,
        grid=(count,),
        in_specs=[
            whole,
            whole,
            pl.BlockSpec((D, TILE), lambda s: (0, SPLITS * s + part)),
            pl.BlockSpec((TILE, D), lambda s: (SPLITS * s + part, 0)),
            whole,
            whole,
        ],
        out_specs=[
            pl.BlockSpec((TILE, D), lambda s: (s, 0)),
            pl.BlockSpec((D, TILE), lambda s: (0, s)),
            whole,
            whole,
        ],
        out_shape=[
            jax.ShapeDtypeStruct((count * TILE, D), bf16),
            jax.ShapeDtypeStruct((D, count * TILE), bf16),
            jax.ShapeDtypeStruct((WINDOW, D), f32),
            jax.ShapeDtypeStruct((WINDOW, D), f32),
        ],
        scratch_shapes=[pltpu.VMEM((D, WINDOW), bf16)],
        compiler_params=params(),
        cost_estimate=cost(6 * 2 * WINDOW * D * FF // SPLITS, 40e6 / SPLITS, 1e6),
        name="feed_forward",
    )(x, cot, up, down, out, gx)


def permute(value, axis, to):
    size = lax.axis_size(axis)
    return lax.ppermute(value, axis, [(i, to(i)) for i in range(size)])


def halves(value, which, dim):
    size = value.shape[dim] // 2
    keep = lax.dynamic_slice_in_dim(value, which * size, size, dim)
    send = lax.dynamic_slice_in_dim(value, (1 - which) * size, size, dim)
    return keep, send


def joined(mine, other, which, dim):
    first = jnp.where(which == 0, mine, other)
    second = jnp.where(which == 0, other, mine)
    return jnp.concatenate([first, second], axis=dim)


def fitted():
    return lax.axis_size("seq") == 8 and lax.axis_size("dp") == 4


def total_of(value, order):
    rows = value.shape[1]
    if not fitted():
        flat = value.reshape((-1,) + value.shape[2:])
        own = lax.psum_scatter(flat, "seq", scatter_dimension=0, tiled=True)
        return lax.psum(own, "dp").astype(f32)
    here = lax.axis_index("seq")
    core, depth = here % 2, here // 2
    dp = lax.axis_index("dp")
    places = (dp % 2, dp // 2)
    pairs = value.reshape((4, 2) + value.shape[1:])
    keep = lax.dynamic_index_in_dim(pairs, core, 1, False)
    send = lax.dynamic_index_in_dim(pairs, 1 - core, 1, False)
    value = keep + permute(send, "seq", lambda i: i ^ 1)
    for axis in order:
        keep, send = halves(value, places[axis], 1)
        value = keep + permute(send, "dp", lambda i, axis=axis: i ^ (1 << axis))
    own = lax.dynamic_index_in_dim(value, depth, 0, False).astype(f32)
    for step in (1, 2, 3):
        send = lax.dynamic_index_in_dim(value, (depth + step) % 4, 0, False)
        came = permute(send, "seq", lambda i, step=step: (i + 2 * step) % 8)
        own = own + came.astype(f32)
    own = own.astype(bf16)
    for axis in reversed(order):
        other = permute(own, "dp", lambda i, axis=axis: i ^ (1 << axis))
        own = joined(own, other, places[axis], 0)
    return own.astype(f32)


def gathered(own):
    if not fitted():
        return lax.all_gather(own, "seq", tiled=True)
    here = lax.axis_index("seq")
    core, depth = here % 2, here // 2
    both = joined(own[None], permute(own, "seq", lambda i: i ^ 1)[None], core, 0)
    parts = [both] + [
        permute(both, "seq", lambda i, step=step: (i - 2 * step) % 8)
        for step in (1, 2, 3)
    ]
    ring = jnp.concatenate(parts, axis=0)
    ring = jnp.concatenate([ring, ring], axis=0)
    return lax.dynamic_slice_in_dim(ring, (8 - 2 * depth) % 8, 8, 0).reshape(
        (-1,) + own.shape[1:]
    )


def body(
    char_ids,
    seg_starts,
    char_table,
    norm_gain,
    qkv_weight,
    distance_bias,
    state_query,
    state_init,
    state_gain,
    state_kv_weight,
    gate_logit,
    out_weight,
    mlp_gain,
    up_weight,
    down_weight,
    cotangent,
):
    windows = lax.axis_size("seq")
    here = lax.axis_index("seq")
    shard = lambda n: n // windows

    packed = jnp.concatenate(
        [char_ids.reshape(4, 128), jnp.broadcast_to(seg_starts, (1, 128))], axis=0
    )
    everyone = lax.all_gather(packed, "seq")
    ids_all = everyone[:, :4].reshape(windows, WINDOW)
    flags = everyone[:, 4, 0]
    order = jnp.arange(windows, dtype=jnp.int32)
    first = jnp.max(jnp.where((flags > 0) & (order <= here), order, 0))
    span = jnp.stack([first, here]).astype(jnp.int32)
    live = (1 - seg_starts.reshape(1)).astype(jnp.int32)
    vocab = jnp.arange(VOCAB, dtype=jnp.int32)
    counts = jnp.sum(
        (ids_all[:, :, None] == vocab[None, None, :]).astype(f32), axis=1
    )
    lnn = jnp.where(counts > 0, jnp.log2(jnp.maximum(counts, 1.0)), hidden)
    lnn = jnp.broadcast_to(lnn[:, :, None], (windows, VOCAB, 128))
    before = lax.dynamic_index_in_dim(ids_all, jnp.maximum(here - 1, 0), 0, False)
    context_ids = jnp.concatenate([before, char_ids.reshape(-1)])
    pick = (context_ids[:, None] == vocab[None, :]).astype(bf16)
    pick_t = (vocab[:, None] == context_ids[None, :]).astype(bf16)

    table = char_table.astype(f32)
    table_unit, table_inv = norm_parts(table)
    normed_table = (table_unit * norm_gain).astype(bf16)
    qkv_table = dot(normed_table, qkv_weight).astype(bf16)

    forget = jax.nn.sigmoid(gate_logit)
    fcol = jnp.broadcast_to(forget[:, None], (D, 128))
    states_in, forget_slope, summary_lse = summary_forward(
        span, state_query, qkv_table, lnn, state_init, fcol
    )
    state_unit, state_inv = norm_parts(states_in)
    state_normed = (state_unit * state_gain).astype(bf16)
    state_kv = dot(state_normed, state_kv_weight).astype(bf16)

    bias_rows = (
        jnp.dot(
            distance_bias.reshape(HEADS, BUCKETS),
            jnp.asarray(lane_pick()),
            precision=lax.Precision.HIGHEST,
        )
        * log2e
        + jnp.asarray(lane_hidden())
    ).reshape(HEADS, 1, CONTEXT)
    mixed, lse = attention_forward(
        live, pick, pick_t, qkv_table, state_kv, state_kv, bias_rows
    )
    own_pick = pick[WINDOW:]
    residual = dot(own_pick, char_table) + dot(mixed, out_weight)
    mlp_unit, mlp_inv = norm_parts(residual)
    mlp_in = (mlp_unit * mlp_gain).astype(bf16)
    upstream = cotangent.reshape(WINDOW, D)

    out, gx = residual, jnp.zeros((WINDOW, D), f32)
    grads_down, grads_up = [], []
    for part in range(SPLITS):
        gd, gu, out, gx = mlp_part(part, mlp_in, upstream, up_weight, down_weight, out, gx)
        grads_down.append(gd)
        grads_up.append(gu)
    layer_out = out.astype(bf16).reshape(1, WINDOW, D)

    grad_mlp_gain = jnp.sum(gx * mlp_unit, axis=0)
    grad_residual = upstream.astype(f32) + norm_back(mlp_unit, mlp_inv, mlp_gain, gx)
    grad_attention = grad_residual.astype(bf16)
    grad_out = dot(mixed, grad_attention, TN).astype(bf16)
    grad_mixed = dot(grad_attention, out_weight, NT).astype(bf16)
    rows_sum = dot(own_pick, grad_attention, TN).astype(bf16)

    gq, gk, gv, gsk, gsv, fold = attention_backward(
        live, pick, pick_t, qkv_table, state_kv, state_kv, bias_rows, lse, mixed, grad_mixed
    )
    grad_state_kv = [
        dot(state_normed, gsk, TN).astype(bf16),
        dot(state_normed, gsv, TN).astype(bf16),
    ]
    grad_state_normed = dot(gsk, state_kv_weight[:, :D], NT) + dot(
        gsv, state_kv_weight[:, D:], NT
    )
    grad_state_gain = jnp.sum(grad_state_normed * state_unit, axis=0)
    local = norm_back(state_unit, state_inv, state_gain, grad_state_normed)
    grad_gate = jnp.sum(local * forget_slope, axis=0) * forget * (1.0 - forget)
    grad_distance = lax.dot_general(
        fold.reshape(HEADS, CONTEXT),
        jnp.asarray(lane_pick()),
        NT,
        precision=lax.Precision.HIGHEST,
        preferred_element_type=f32,
    ).reshape(-1)
    gk, gv, gsq, ginit = summary_backward(
        span, state_query, qkv_table, lnn, summary_lse, local, fcol, gk, gv
    )

    own_down, own_up = [], []
    for part in range(SPLITS):
        order = (0, 1) if part % 2 == 0 else (1, 0)
        if fitted():
            gd = grads_down[part].reshape(windows, -1, D)
            gu = grads_up[part].reshape(windows, shard(D), -1)
            own_down.append(total_of(gd, order))
            own_up.append(total_of(gu, order))
    if fitted():
        grad_down = jnp.concatenate(own_down, axis=0)
        grad_up = jnp.stack(
            [part.reshape(shard(D), -1, TILE) for part in own_up], axis=2
        ).reshape(shard(D), FF)
    else:
        full = jnp.stack([g.reshape(-1, TILE, D) for g in grads_down], axis=1)
        grad_down = total_of(full.reshape(windows, -1, D), (0, 1))
        full = jnp.stack([g.reshape(D, -1, TILE) for g in grads_up], axis=2)
        grad_up = total_of(full.reshape(windows, shard(D), FF), (0, 1))
    middle = jnp.concatenate(
        [
            grad_out.reshape(windows, shard(D), D),
            rows_sum.reshape(windows, shard(VOCAB), D),
        ],
        axis=1,
    )
    middle = total_of(middle, (0, 1))
    grad_out = middle[: shard(D)]
    rows_sum = middle[shard(D) :]
    grad_state_kv = jnp.concatenate(
        [g.reshape(windows, shard(D), D) for g in grad_state_kv], axis=1
    )
    grad_state_kv = total_of(grad_state_kv, (1, 0))
    grad_state_kv = jnp.concatenate(
        [grad_state_kv[: shard(D)], grad_state_kv[shard(D) :]], axis=1
    )
    small = jnp.concatenate(
        [
            g.reshape(windows, -1)
            for g in (grad_mlp_gain, grad_state_gain, grad_gate, grad_distance)
        ],
        axis=1,
    ).astype(bf16)
    used = small.shape[1]
    small = jnp.pad(small, ((0, 0), (0, 32 * D - used))).reshape(windows, 32, D)
    last = jnp.concatenate(
        [
            gsq.reshape(windows, shard(STATES), D),
            ginit.reshape(windows, shard(STATES), D),
            gq.reshape(windows, shard(VOCAB), D),
            gk.reshape(windows, shard(VOCAB), D),
            gv.reshape(windows, shard(VOCAB), D),
            small,
        ],
        axis=1,
    )
    last = total_of(last, (0, 1))
    cuts = np.cumsum([shard(STATES), shard(STATES)] + [shard(VOCAB)] * 3)
    grad_state_query, grad_state_init, gq, gk, gv, small = jnp.split(last, cuts, axis=0)
    small = small.reshape(-1)
    span_d = shard(D)
    grad_mlp_gain = small[:span_d]
    grad_state_gain = small[span_d : 2 * span_d]
    grad_gate = small[2 * span_d : 3 * span_d]
    grad_distance = small[3 * span_d : 3 * span_d + shard(HEADS * BUCKETS)]

    grad_rows = jnp.concatenate([gq, gk, gv], axis=1).astype(bf16)
    all_rows = gathered(grad_rows)
    mine = lax.dynamic_slice_in_dim(normed_table, here * span_d, span_d, 1)
    grad_qkv = dot(mine, all_rows, TN)
    weight_rows = lax.dynamic_slice_in_dim(qkv_weight, here * span_d, span_d, 0)
    unit_cols = lax.dynamic_slice_in_dim(table_unit, here * span_d, span_d, 1)
    grad_norm_gain = jnp.sum(dot(all_rows, weight_rows, NT) * unit_cols, axis=0)
    grad_normed = dot(grad_rows, qkv_weight, NT)
    at = here * shard(VOCAB)
    grad_table = rows_sum + norm_back(
        lax.dynamic_slice_in_dim(table_unit, at, shard(VOCAB), 0),
        lax.dynamic_slice_in_dim(table_inv, at, shard(VOCAB), 0),
        norm_gain,
        grad_normed,
    )
    return (
        layer_out,
        grad_table,
        grad_norm_gain,
        grad_qkv,
        grad_distance,
        grad_state_query,
        grad_state_init,
        grad_state_gain,
        grad_state_kv,
        grad_gate,
        grad_out,
        grad_mlp_gain,
        grad_up,
        grad_down,
    )


def solution(mesh):
    placed = (P("dp", "seq"), P("dp", "seq")) + (P(),) * 13 + (P("dp", "seq", None),)
    return jax.shard_map(
        body,
        mesh=mesh,
        in_specs=placed,
        out_specs=(
            P("dp", "seq", None),
            P("seq", None),
            P("seq"),
            P("seq", None),
            P("seq"),
            P("seq", None),
            P("seq", None),
            P("seq"),
            P("seq", None),
            P("seq"),
            P("seq", None),
            P("seq"),
            P("seq", None),
            P("seq", None),
        ),
        check_vma=False,
    )
```

```python
import functools
import math
import types

import jax
import jax.numpy as jnp
import numpy as np
from jax import lax
from jax.experimental import pallas as pl
from jax.experimental.pallas import tpu as pltpu
from jax.sharding import PartitionSpec as P

D = 1024
HEADS = 8
HEAD_DIM = 128
FF = 4096
VOCAB = 256
STATES = 512
WINDOW = 512
BUCKETS = 32
MAX_DISTANCE = 128
CONTEXT = 2 * WINDOW
TILE = 256
SPLITS = 2

epsilon = 1e-05
hidden = -1e30
log2e = math.log2(math.e)
score_scale = 1.0 / math.sqrt(HEAD_DIM)
f32 = jnp.float32
bf16 = jnp.bfloat16

NN = (((1,), (0,)), ((), ()))
NT = (((1,), (1,)), ((), ()))
TN = (((0,), (0,)), ((), ()))


def dot(a, b, dims=NN):
    return lax.dot_general(a, b, dims, preferred_element_type=f32)


def params(mib=26):
    return pltpu.CompilerParams(
        dimension_semantics=("arbitrary",), vmem_limit_bytes=mib * 1024 * 1024
    )


def cost(flops, moved, exps=0):
    return pl.CostEstimate(
        flops=int(flops), bytes_accessed=int(moved), transcendentals=int(exps)
    )


def norm_parts(value):
    centre = jnp.mean(value, axis=-1, keepdims=True)
    offset = value - centre
    spread = jnp.mean(offset * offset, axis=-1, keepdims=True)
    inv = lax.rsqrt(spread + epsilon)
    return offset * inv, inv


def norm_back(unit, inv, gain, upstream):
    scaled = upstream * gain
    a = jnp.mean(scaled, axis=-1, keepdims=True)
    b = jnp.mean(scaled * unit, axis=-1, keepdims=True)
    return (scaled - a - unit * b) * inv


def bucket_table():
    distance = np.arange(WINDOW)
    exact_count = BUCKETS // 2
    log_ratio = np.log(np.maximum(distance, 1) / exact_count) / math.log(
        MAX_DISTANCE / exact_count
    )
    far_bucket = exact_count + np.floor(log_ratio * (BUCKETS - exact_count)).astype(
        np.int64
    )
    return np.where(
        distance < exact_count, distance, np.minimum(far_bucket, BUCKETS - 1)
    )


def lane_pick():
    pick = np.zeros((BUCKETS, CONTEXT), np.float32)
    table = bucket_table()
    for m in range(1, WINDOW + 1):
        pick[table[WINDOW - m], m] = 1.0
    return pick


def lane_hidden():
    m = np.arange(CONTEXT)
    return np.where((m >= 1) & (m <= WINDOW), 0.0, hidden).astype(np.float32)[None]


def summary_forward_kernel(
    span, sq, kt, vt, lnn, init, fcol, state_out, y_out, lse_out, lg, a_s, y_s
):
    kt_h = kt[...]
    vtr = vt[...].astype(f32).T.astype(bf16)
    lg[...] = dot(kt_h, sq[...], NT) * (score_scale * log2e)
    a_s[...] = init[...].astype(f32).T
    y_s[...] = jnp.zeros_like(y_s)
    f = jnp.concatenate([fcol[...]] * (STATES // 128), axis=1)

    def step(w, _):
        n = lnn[w]
        x = lg[...] + jnp.concatenate([n] * (STATES // 128), axis=1)
        m = jnp.max(x, axis=0, keepdims=True)
        p = jnp.exp2(x - m)
        z = jnp.sum(p, axis=0, keepdims=True)
        u = dot(vtr, p.astype(bf16)) * (1.0 / z)
        lse_out[0, pl.ds(w, 1), :] = m + jnp.log2(z)
        a = a_s[...]
        y_s[...] = a - u + f * y_s[...]
        a_s[...] = u + f * (a - u)
        return 0

    lax.fori_loop(span[0], span[1], step, 0)
    state_out[...] = a_s[...].T
    y_out[...] = y_s[...].T


def summary_forward(span, state_query, qkv_table, lnn, state_init, fcol):
    windows = lnn.shape[0]
    head = lambda k: (lambda h, s: (0, k * HEADS + h))
    return pl.pallas_call(
        summary_forward_kernel,
        grid_spec=pltpu.PrefetchScalarGridSpec(
            num_scalar_prefetch=1,
            grid=(HEADS,),
            in_specs=[
                pl.BlockSpec((STATES, HEAD_DIM), head(0)),
                pl.BlockSpec((VOCAB, HEAD_DIM), head(1)),
                pl.BlockSpec((VOCAB, HEAD_DIM), head(2)),
                pl.BlockSpec((windows, VOCAB, 128), lambda h, s: (0, 0, 0)),
                pl.BlockSpec((STATES, HEAD_DIM), head(0)),
                pl.BlockSpec((HEAD_DIM, 128), lambda h, s: (h, 0)),
            ],
            out_specs=[
                pl.BlockSpec((STATES, HEAD_DIM), head(0)),
                pl.BlockSpec((STATES, HEAD_DIM), head(0)),
                pl.BlockSpec((1, windows, STATES), lambda h, s: (h, 0, 0)),
            ],
            scratch_shapes=[
                pltpu.VMEM((VOCAB, STATES), f32),
                pltpu.VMEM((HEAD_DIM, STATES), f32),
                pltpu.VMEM((HEAD_DIM, STATES), f32),
            ],
        ),
        out_shape=[
            jax.ShapeDtypeStruct((STATES, D), f32),
            jax.ShapeDtypeStruct((STATES, D), f32),
            jax.ShapeDtypeStruct((HEADS, windows, STATES), f32),
        ],
        compiler_params=params(),
        cost_estimate=cost(1e3, 1e3),
        name="summary_forward",
    )(span, state_query, qkv_table, qkv_table, lnn, state_init, fcol)


def summary_backward_kernel(
    span,
    sq,
    kt,
    vt,
    lnn,
    lse,
    local,
    fcol,
    *rest,
):
    g_out, gsq_out, ginit_out, lg, g_s, gs_s, gv_s = rest[-7:]
    kt_h = kt[...]
    vt_h = vt[...]
    sq_h = sq[...]
    lg[...] = dot(kt_h, sq_h, NT) * (score_scale * log2e)
    g_s[...] = local[...].T
    gs_s[...] = jnp.zeros_like(gs_s)
    gv_s[...] = jnp.zeros_like(gv_s)
    f = jnp.concatenate([fcol[...]] * (STATES // 128), axis=1)
    first, here = span[0], span[1]

    def step(t, _):
        w = here - 1 - t
        g = g_s[...]
        fg = f * g
        gu = (g - fg).astype(bf16)
        g_s[...] = fg
        n = lnn[w]
        p = jnp.exp2(
            lg[...]
            + jnp.concatenate([n] * (STATES // 128), axis=1)
            - lse[0, pl.ds(w, 1), :]
        )
        dw = dot(vt_h, gu)
        pd = p * dw
        inner = jnp.sum(pd, axis=0, keepdims=True)
        gs_s[...] += pd - p * inner
        gv_s[...] += dot(p.astype(bf16), gu, NT)
        return 0

    lax.fori_loop(0, here - first, step, 0)
    gs = (gs_s[...] * score_scale).astype(bf16)
    g_out[0, :, :128] = jnp.zeros((VOCAB, 128), bf16)
    g_out[0, :, 128:256] = dot(gs, sq_h).astype(bf16)
    g_out[0, :, 256:] = gv_s[...].astype(bf16)
    gsq_out[...] = dot(gs, kt_h, TN).astype(bf16)
    ginit_out[...] = g_s[...].T.astype(bf16)


def summary_backward(span, state_query, qkv_table, lnn, lse, local, fcol, grads=None, deps=()):
    windows = lnn.shape[0]
    head = lambda k: (lambda h, s: (0, k * HEADS + h))
    by_head = pl.BlockSpec((1, VOCAB, 384), lambda h, s: (h, 0, 0))
    states = pl.BlockSpec((STATES, HEAD_DIM), head(0))
    return pl.pallas_call(
        summary_backward_kernel,
        grid_spec=pltpu.PrefetchScalarGridSpec(
            num_scalar_prefetch=1,
            grid=(HEADS,),
            in_specs=[
                states,
                pl.BlockSpec((VOCAB, HEAD_DIM), head(1)),
                pl.BlockSpec((VOCAB, HEAD_DIM), head(2)),
                pl.BlockSpec((windows, VOCAB, 128), lambda h, s: (0, 0, 0)),
                pl.BlockSpec((1, windows, STATES), lambda h, s: (h, 0, 0)),
                states,
                pl.BlockSpec((HEAD_DIM, 128), lambda h, s: (h, 0)),
            ]
            + [pl.BlockSpec(memory_space=pl.ANY)] * len(deps),
            out_specs=[by_head, states, states],
            scratch_shapes=[
                pltpu.VMEM((VOCAB, STATES), f32),
                pltpu.VMEM((HEAD_DIM, STATES), f32),
                pltpu.VMEM((VOCAB, STATES), f32),
                pltpu.VMEM((VOCAB, HEAD_DIM), f32),
            ],
        ),
        out_shape=[
            jax.ShapeDtypeStruct((HEADS, VOCAB, 384), bf16),
            jax.ShapeDtypeStruct((STATES, D), bf16),
            jax.ShapeDtypeStruct((STATES, D), bf16),
        ],
        compiler_params=params(),
        cost_estimate=cost(1e3, 1e3),
        name="summary_backward",
    )(span, state_query, qkv_table, qkv_table, lnn, lse, local, fcol, *deps)


def bias_tile(row):
    spread = jnp.broadcast_to(row, (TILE, CONTEXT))
    shifted = pltpu.roll(spread, 0, 1, stride=1, stride_axis=0)
    return shifted[:, : 3 * TILE].T


def attention_forward_kernel(
    live, pick, pick_t, qt, kt, vt, sk, sv, bias_row, mixed_out, lse_out, bias
):
    bias[...] = bias_tile(bias_row[0])
    prev_add = jnp.where(live[0] > 0, 0.0, hidden).astype(f32)
    keys = dot(pick[...], kt[...]).astype(bf16)
    values_t = dot(vt[...], pick_t[...], TN).astype(bf16)
    query = dot(pick[WINDOW:, :], qt[...]).astype(bf16)
    state_values_t = sv[...].astype(f32).T.astype(bf16)
    for j in range(WINDOW // TILE):
        q = query[j * TILE : (j + 1) * TILE]
        scores = []
        for rel in range(3):
            kt_i = j + rel
            s = (
                dot(keys[kt_i * TILE : (kt_i + 1) * TILE], q, NT)
                * (score_scale * log2e)
                + bias[rel * TILE : (rel + 1) * TILE]
            )
            if kt_i * TILE < WINDOW:
                s = s + prev_add
            scores.append(s)
        for st in range(STATES // TILE):
            scores.append(
                dot(sk[st * TILE : (st + 1) * TILE, :], q, NT) * (score_scale * log2e)
            )
        peak = functools.reduce(
            jnp.maximum, [jnp.max(s, axis=0, keepdims=True) for s in scores]
        )
        total = jnp.zeros((1, TILE), f32)
        out = jnp.zeros((HEAD_DIM, TILE), f32)
        for i, s in enumerate(scores):
            p = jnp.exp2(s - peak)
            total = total + jnp.sum(p, axis=0, keepdims=True)
            if i < 3:
                v = values_t[:, (j + i) * TILE : (j + i + 1) * TILE]
            else:
                v = state_values_t[:, (i - 3) * TILE : (i - 2) * TILE]
            out = out + dot(v, p.astype(bf16))
        out = out * (1.0 / total)
        mixed_out[j * TILE : (j + 1) * TILE, :] = out.T.astype(bf16)
        lse_out[0, :, j * TILE : (j + 1) * TILE] = peak + jnp.log2(total)


def attention_forward(live, pick, pick_t, qkv_table, sk, sv, bias_rows):
    head = lambda k: (lambda h, s: (0, k * HEADS + h))
    whole = lambda *shape: pl.BlockSpec(shape, lambda h, s: (0,) * len(shape))
    return pl.pallas_call(
        attention_forward_kernel,
        grid_spec=pltpu.PrefetchScalarGridSpec(
            num_scalar_prefetch=1,
            grid=(HEADS,),
            in_specs=[
                whole(CONTEXT, VOCAB),
                whole(VOCAB, CONTEXT),
                pl.BlockSpec((VOCAB, HEAD_DIM), head(0)),
                pl.BlockSpec((VOCAB, HEAD_DIM), head(1)),
                pl.BlockSpec((VOCAB, HEAD_DIM), head(2)),
                pl.BlockSpec((STATES, HEAD_DIM), head(0)),
                pl.BlockSpec((STATES, HEAD_DIM), head(1)),
                pl.BlockSpec((1, 1, CONTEXT), lambda h, s: (h, 0, 0)),
            ],
            out_specs=[
                pl.BlockSpec((WINDOW, HEAD_DIM), head(0)),
                pl.BlockSpec((1, 1, WINDOW), lambda h, s: (h, 0, 0)),
            ],
            scratch_shapes=[pltpu.VMEM((3 * TILE, TILE), f32)],
        ),
        out_shape=[
            jax.ShapeDtypeStruct((WINDOW, D), bf16),
            jax.ShapeDtypeStruct((HEADS, 1, WINDOW), f32),
        ],
        compiler_params=params(),
        cost_estimate=cost(1e3, 1e3),
        name="attention_forward",
    )(live, pick, pick_t, qkv_table, qkv_table, qkv_table, sk, sv, bias_rows)


def back_tile(s, dp, shift, inner):
    p = jnp.exp2(s - shift)
    return p, p * (dp - inner)


def state_backward_kernel(pick, qt, sk, sv, lse, mixed, grad, *rest):
    gsk_out, gsv_out, gq_out, inner_out = rest[-4:]
    query = dot(pick[WINDOW:, :], qt[...]).astype(bf16)
    state_keys_t = sk[...].astype(f32).T.astype(bf16)
    inner_all = jnp.sum(
        (mixed[...].astype(f32) * grad[...].astype(f32)).T, axis=0, keepdims=True
    )
    inner_out[0] = inner_all
    blocks = WINDOW // TILE
    gq = [jnp.zeros((HEAD_DIM, TILE), f32) for _ in range(blocks)]
    for st in range(STATES // TILE):
        at = slice(st * TILE, (st + 1) * TILE)
        gk = jnp.zeros((TILE, HEAD_DIM), f32)
        gv = jnp.zeros((TILE, HEAD_DIM), f32)
        for j in range(blocks):
            rows = slice(j * TILE, (j + 1) * TILE)
            p, gs = back_tile(
                dot(sk[at, :], query[rows], NT) * (score_scale * log2e),
                dot(sv[at, :], grad[rows, :], NT),
                lse[0, :, rows],
                inner_all[:, rows],
            )
            gs16 = gs.astype(bf16)
            gq[j] = gq[j] + dot(state_keys_t[:, at], gs16)
            gk = gk + dot(gs16, query[rows])
            gv = gv + dot(p.astype(bf16), grad[rows, :])
        gsk_out[at, :] = (gk * score_scale).astype(bf16)
        gsv_out[at, :] = gv.astype(bf16)
    for j in range(blocks):
        gq_out[0, :, j * TILE : (j + 1) * TILE] = gq[j]


def state_backward(pick, qkv_table, state_kv, lse, mixed, grad, deps=()):
    head = lambda k: (lambda h: (0, k * HEADS + h))
    tokens = pl.BlockSpec((WINDOW, HEAD_DIM), head(0))
    states = pl.BlockSpec((STATES, HEAD_DIM), head(0))
    row = pl.BlockSpec((1, 1, WINDOW), lambda h: (h, 0, 0))
    return pl.pallas_call(
        state_backward_kernel,
        grid=(HEADS,),
        in_specs=[
            pl.BlockSpec((CONTEXT, VOCAB), lambda h: (0, 0)),
            pl.BlockSpec((VOCAB, HEAD_DIM), head(0)),
            pl.BlockSpec((STATES, HEAD_DIM), head(0)),
            pl.BlockSpec((STATES, HEAD_DIM), head(1)),
            row,
            tokens,
            tokens,
        ]
        + [pl.BlockSpec(memory_space=pl.ANY)] * len(deps),
        out_specs=[
            states,
            states,
            pl.BlockSpec((1, HEAD_DIM, WINDOW), lambda h: (h, 0, 0)),
            row,
        ],
        out_shape=[
            jax.ShapeDtypeStruct((STATES, D), bf16),
            jax.ShapeDtypeStruct((STATES, D), bf16),
            jax.ShapeDtypeStruct((HEADS, HEAD_DIM, WINDOW), f32),
            jax.ShapeDtypeStruct((HEADS, 1, WINDOW), f32),
        ],
        compiler_params=params(),
        cost_estimate=cost(1e3, 1e3),
        name="state_backward",
    )(pick, qkv_table, state_kv, state_kv, lse, mixed, grad, *deps)


def token_backward_kernel(
    live, pick, pick_t, qt, kt, vt, bias_row, lse, inner, grad, gq_in, buckets, *rest
):
    g_out, fold_out, bias, bias_grad = rest[-4:]
    bias[...] = bias_tile(bias_row[0])
    bias_grad[...] = jnp.zeros_like(bias_grad)
    prev_add = jnp.where(live[0] > 0, 0.0, hidden).astype(f32)
    both = dot(pick[...], jnp.concatenate([kt[...], vt[...]], axis=1)).astype(bf16)
    keys = both[:, :HEAD_DIM]
    values = both[:, HEAD_DIM:]
    keys_t = dot(kt[...], pick_t[...], TN).astype(bf16)
    query = dot(pick[WINDOW:, :], qt[...]).astype(bf16)
    blocks = WINDOW // TILE
    gq = [gq_in[0, :, j * TILE : (j + 1) * TILE] for j in range(blocks)]
    sums = jnp.zeros((VOCAB, 2 * HEAD_DIM), f32)
    for tile in range(CONTEXT // TILE):
        at = slice(tile * TILE, (tile + 1) * TILE)
        gk = jnp.zeros((TILE, HEAD_DIM), f32)
        gv = jnp.zeros((TILE, HEAD_DIM), f32)
        for j in range(blocks):
            rel = tile - j
            if not 0 <= rel < 3:
                continue
            rows = slice(j * TILE, (j + 1) * TILE)
            rels = slice(rel * TILE, (rel + 1) * TILE)
            shift = lse[0, :, rows]
            if tile * TILE < WINDOW:
                shift = shift - prev_add
            p, gs = back_tile(
                dot(keys[at], query[rows], NT) * (score_scale * log2e) + bias[rels],
                dot(values[at], grad[rows, :], NT),
                shift,
                inner[0, :, rows],
            )
            gs16 = gs.astype(bf16)
            gq[j] = gq[j] + dot(keys_t[:, at], gs16)
            bias_grad[rels] += gs
            gk = gk + dot(gs16, query[rows])
            gv = gv + dot(p.astype(bf16), grad[rows, :])
        pair = jnp.concatenate([gk * score_scale, gv], axis=1).astype(bf16)
        sums = sums + dot(pick_t[:, at], pair)
    g_out[0, :, HEAD_DIM:] = sums
    total = jnp.zeros((HEAD_DIM, VOCAB), f32)
    for j in range(blocks):
        rows = slice(WINDOW + j * TILE, WINDOW + (j + 1) * TILE)
        total = total + dot((gq[j] * score_scale).astype(bf16), pick[rows, :])
    g_out[0, :, :HEAD_DIM] = total.T
    rows = jnp.concatenate(
        [bias_grad[...].T, jnp.zeros((TILE, CONTEXT - 3 * TILE), f32)], axis=1
    )
    count = TILE
    while count > 8:
        count //= 2
        rows = rows[:count] + pltpu.roll(rows[count:], CONTEXT - count, 1)
    folded = rows[0:1]
    for r in range(1, 8):
        folded = folded + pltpu.roll(rows, CONTEXT - r, 1)[r : r + 1]
    pieces = []
    left = folded
    for _ in range(3):
        piece = left.astype(bf16)
        pieces.append(piece)
        left = left - piece.astype(f32)
    pieces = jnp.concatenate(pieces + [jnp.zeros((5, CONTEXT), bf16)], axis=0)
    fold_out[0] = jnp.sum(dot(pieces, buckets[...]), axis=0, keepdims=True)


def token_backward(
    live, pick, pick_t, qkv_table, bias_rows, lse, inner, grad, gq, deps=(), half=None, onto=()
):
    low, count = (0, HEADS) if half is None else (half * HEADS // 2, HEADS // 2)
    deps = (*deps, *onto)
    head = lambda k: (lambda h, s: (0, k * HEADS + low + h))
    by_head = lambda *shape: pl.BlockSpec((1,) + shape, lambda h, s: (low + h, 0, 0))
    flat = lambda *shape: pl.BlockSpec(shape, lambda h, s: (0,) * len(shape))
    return pl.pallas_call(
        token_backward_kernel,
        grid_spec=pltpu.PrefetchScalarGridSpec(
            num_scalar_prefetch=1,
            grid=(count,),
            in_specs=[
                flat(CONTEXT, VOCAB),
                flat(VOCAB, CONTEXT),
                pl.BlockSpec((VOCAB, HEAD_DIM), head(0)),
                pl.BlockSpec((VOCAB, HEAD_DIM), head(1)),
                pl.BlockSpec((VOCAB, HEAD_DIM), head(2)),
                by_head(1, CONTEXT),
                by_head(1, WINDOW),
                by_head(1, WINDOW),
                pl.BlockSpec((WINDOW, HEAD_DIM), head(0)),
                by_head(HEAD_DIM, WINDOW),
                flat(CONTEXT, 128),
            ]
            + [pl.BlockSpec(memory_space=pl.ANY)] * len(deps),
            out_specs=[by_head(VOCAB, 384), by_head(1, 128)],
            scratch_shapes=[
                pltpu.VMEM((3 * TILE, TILE), f32),
                pltpu.VMEM((3 * TILE, TILE), f32),
            ],
        ),
        out_shape=[
            jax.ShapeDtypeStruct((HEADS, VOCAB, 384), f32),
            jax.ShapeDtypeStruct((HEADS, 1, 128), f32),
        ],
        input_output_aliases={12 + len(deps) - 2 + i: i for i in range(len(onto))},
        compiler_params=params(),
        cost_estimate=cost(1e3, 1e3),
        name="token_backward",
    )(
        live,
        pick,
        pick_t,
        qkv_table,
        qkv_table,
        qkv_table,
        bias_rows,
        lse,
        inner,
        grad,
        gq,
        jnp.asarray(np.pad(lane_pick().T, ((0, 0), (0, 96))), bf16),
        *deps,
    )


def mlp_kernel(x, cot, up, down, out_in, gx_in, gd_out, gu_out, out, gx, xt):
    @pl.when(pl.program_id(0) == 0)
    def _():
        out[...] = out_in[...]
        gx[...] = gx_in[...]
        xt[...] = x[...].astype(f32).T.astype(bf16)

    up_b = up[...]
    down_b = down[...]
    pre = dot(x[...], up_b)
    root = math.sqrt(2.0 / math.pi)
    square = pre * pre
    t = jnp.tanh(root * pre * (1.0 + 0.044715 * square))
    half = 0.5 * (1.0 + t)
    act = (pre * half).astype(bf16)
    slope = half + (0.5 * root) * pre * (1.0 - t * t) * (1.0 + (3 * 0.044715) * square)
    grad_pre = (dot(cot[...], down_b, NT) * slope).astype(bf16)
    out[...] += dot(act, down_b)
    gx[...] += dot(grad_pre, up_b, NT)
    gd_out[...] = dot(act, cot[...], TN).astype(bf16)
    gu_out[...] = dot(xt[...], grad_pre).astype(bf16)


def mlp_part(part, x, cot, up, down, out, gx):
    count = FF // SPLITS // TILE
    whole = pl.BlockSpec((WINDOW, D), lambda s: (0, 0))
    return pl.pallas_call(
        mlp_kernel,
        grid=(count,),
        in_specs=[
            whole,
            whole,
            pl.BlockSpec((D, TILE), lambda s: (0, SPLITS * s + part)),
            pl.BlockSpec((TILE, D), lambda s: (SPLITS * s + part, 0)),
            whole,
            whole,
        ],
        out_specs=[
            pl.BlockSpec((TILE, D), lambda s: (s, 0)),
            pl.BlockSpec((D, TILE), lambda s: (0, s)),
            whole,
            whole,
        ],
        out_shape=[
            jax.ShapeDtypeStruct((count * TILE, D), bf16),
            jax.ShapeDtypeStruct((D, count * TILE), bf16),
            jax.ShapeDtypeStruct((WINDOW, D), f32),
            jax.ShapeDtypeStruct((WINDOW, D), f32),
        ],
        scratch_shapes=[pltpu.VMEM((D, WINDOW), bf16)],
        compiler_params=params(),
        cost_estimate=cost(1e3, 1e3),
        name="feed_forward",
    )(x, cot, up, down, out, gx)


def mlp_packed_kernel(
    places, x, cot, up_a, up_b, up_c, up_d, down_a, down_b, down_c, down_d, out_in, gx_in,
    *rest,
):
    send, keep, out, gx, xt, xs, gd_s = rest[-7:]
    core = places[CORE]
    step = pl.program_id(0)

    @pl.when(step == 0)
    def _():
        out[...] = out_in[...]
        gx[...] = gx_in[...]
        xt[...] = x[...].astype(f32).T.astype(bf16)
        for z in range(4):
            for slot, parity in ((0, 1 - core), (1, core)):
                at = pl.multiple_of((2 * z + parity) * 128, 128)
                xs[slot, z * 128 : (z + 1) * 128, :] = xt[pl.ds(at, 128), :]

    up = jnp.concatenate([up_a[...], up_b[...], up_c[...], up_d[...]], axis=1)
    down = jnp.concatenate([down_a[...], down_b[...], down_c[...], down_d[...]], axis=0)
    pre = dot(x[...], up)
    root = math.sqrt(2.0 / math.pi)
    square = pre * pre
    t = jnp.tanh(root * pre * (1.0 + 0.044715 * square))
    half = 0.5 * (1.0 + t)
    act = (pre * half).astype(bf16)
    slope = half + (0.5 * root) * pre * (1.0 - t * t) * (1.0 + (3 * 0.044715) * square)
    grad_pre = (dot(cot[...], down, NT) * slope).astype(bf16)
    out[...] += dot(act, down)
    gx[...] += dot(grad_pre, up, NT)
    gd = dot(act, cot[...], TN).astype(bf16)
    for i in range(2):
        for q in range(2):
            at = (2 * i + q) * 128
            gd_s[q, i] = gd[at : at + 128]
    lanes = pl.ds(pl.multiple_of(step * 512, 512), 512)
    for i in range(2):
        z = 2 * step + i
        send[pl.ds(z, 1), :128, :] = gd_s[pl.ds(1 - core, 1), i]
        keep[pl.ds(z, 1), :128, :] = gd_s[pl.ds(core, 1), i]
    for slot, ref in ((0, send), (1, keep)):
        gu = dot(xs[slot], grad_pre).astype(bf16)
        ref[:, 128:, lanes] = gu.reshape(4, 128, 512)


def mlp_packed(part, places, x, cot, up, down, out, gx, deps=()):
    block = pl.BlockSpec((WINDOW, D), lambda g, s: (0, 0))
    packed = pl.BlockSpec((4, 256, D), lambda g, s: (0, 0, 0))
    at = lambda k: (lambda g: (4 * g + k) * 4 + part)
    return pl.pallas_call(
        mlp_packed_kernel,
        grid_spec=pltpu.PrefetchScalarGridSpec(
            num_scalar_prefetch=1,
            grid=(2,),
            in_specs=[block, block]
            + [
                pl.BlockSpec((D, 128), lambda g, s, k=k: (0, at(k)(g)))
                for k in range(4)
            ]
            + [
                pl.BlockSpec((128, D), lambda g, s, k=k: (at(k)(g), 0))
                for k in range(4)
            ]
            + [block, block]
            + [pl.BlockSpec(memory_space=pl.ANY)] * len(deps),
            out_specs=[packed, packed, block, block],
            scratch_shapes=[
                pltpu.VMEM((D, WINDOW), bf16),
                pltpu.VMEM((2, 512, WINDOW), bf16),
                pltpu.VMEM((2, 2, 128, D), bf16),
            ],
        ),
        out_shape=[
            jax.ShapeDtypeStruct((4, 256, D), bf16),
            jax.ShapeDtypeStruct((4, 256, D), bf16),
            jax.ShapeDtypeStruct((WINDOW, D), f32),
            jax.ShapeDtypeStruct((WINDOW, D), f32),
        ],
        compiler_params=params(32),
        cost_estimate=cost(1e3, 1e3),
        name="feed_forward",
    )(places, x, cot, up, up, up, up, down, down, down, down, out, gx, *deps)


def one_block(array):
    return pl.BlockSpec(array.shape, lambda g: (0,) * array.ndim)


def single(kernel, name, ins, outs, scratch=(), deps=()):
    return pl.pallas_call(
        kernel,
        grid=(1,),
        in_specs=[one_block(a) for a in ins]
        + [pl.BlockSpec(memory_space=pl.ANY)] * len(deps),
        out_specs=[one_block(o) for o in outs],
        out_shape=list(outs),
        scratch_shapes=list(scratch),
        compiler_params=params(),
        cost_estimate=cost(1e3, 1e3),
        name=name,
    )(*ins, *deps)


def like(kind, *shape):
    return jax.ShapeDtypeStruct(shape, kind)


def unit_of(value):
    unit, inv = norm_parts(value)
    return unit, jnp.broadcast_to(inv, (value.shape[0], 128))


def table_kernel(table, gain, weight, unit_out, inv_out, normed_out, qkv_out):
    step = pl.program_id(0)

    @pl.when(step == 0)
    def _():
        unit, inv = unit_of(table[...].astype(f32))
        unit_out[...] = unit
        inv_out[...] = inv
        normed_out[...] = (unit * gain[...]).astype(bf16)

    qkv_out[...] = dot(normed_out[...], weight[...]).astype(bf16)


def table_forward(table, gain, weight):
    flat = lambda *shape: pl.BlockSpec(shape, lambda g: (0, 0))
    return pl.pallas_call(
        table_kernel,
        grid=(6,),
        in_specs=[
            flat(VOCAB, D),
            flat(1, D),
            pl.BlockSpec((D, D // 2), lambda g: (0, g)),
        ],
        out_specs=[
            flat(VOCAB, D),
            flat(VOCAB, 128),
            flat(VOCAB, D),
            pl.BlockSpec((VOCAB, D // 2), lambda g: (0, g)),
        ],
        out_shape=[
            like(f32, VOCAB, D),
            like(f32, VOCAB, 128),
            like(bf16, VOCAB, D),
            like(bf16, VOCAB, 3 * D),
        ],
        compiler_params=params(),
        cost_estimate=cost(1e3, 1e3),
        name="table_forward",
    )(table, gain, weight)


def states_forward_kernel(states, gain, weight, unit_out, inv_out, normed_out, kv_out):
    step = pl.program_id(0)

    @pl.when(step == 0)
    def _():
        unit, inv = unit_of(states[...])
        unit_out[...] = unit
        inv_out[...] = inv
        normed_out[...] = (unit * gain[...]).astype(bf16)

    kv_out[...] = dot(normed_out[...], weight[...]).astype(bf16)


def states_forward(states, gain, weight):
    flat = lambda *shape: pl.BlockSpec(shape, lambda g: (0, 0))
    return pl.pallas_call(
        states_forward_kernel,
        grid=(4,),
        in_specs=[
            flat(STATES, D),
            flat(1, D),
            pl.BlockSpec((D, D // 2), lambda g: (0, g)),
        ],
        out_specs=[
            flat(STATES, D),
            flat(STATES, 128),
            flat(STATES, D),
            pl.BlockSpec((STATES, D // 2), lambda g: (0, g)),
        ],
        out_shape=[
            like(f32, STATES, D),
            like(f32, STATES, 128),
            like(bf16, STATES, D),
            like(bf16, STATES, 2 * D),
        ],
        compiler_params=params(),
        cost_estimate=cost(1e3, 1e3),
        name="states_forward",
    )(states, gain, weight)


def residual_kernel(mixed, out_weight, pick, table, gain, res_out, unit_out, inv_out, in_out):
    res = dot(pick[WINDOW:, :], table[...]) + dot(mixed[...], out_weight[...])
    res_out[...] = res
    unit, inv = unit_of(res)
    unit_out[...] = unit
    inv_out[...] = inv
    in_out[...] = (unit * gain[...]).astype(bf16)


def residual_forward(mixed, out_weight, pick, table, gain):
    return single(
        residual_kernel,
        "residual_forward",
        (mixed, out_weight, pick, table, gain),
        (
            like(f32, WINDOW, D),
            like(f32, WINDOW, D),
            like(f32, WINDOW, 128),
            like(bf16, WINDOW, D),
        ),
    )


def feed_back_kernel(
    gx, unit, inv, gain, upstream, mixed, out_weight, pick, *rest
):
    gain_out, out_out, mixed_out, rows_out = rest[-4:]
    g = gx[...]
    u = unit[...]
    gain_out[...] = jnp.sum(g * u, axis=0, keepdims=True)
    back = norm_back(u, inv[:, :1], gain[...], g)
    grad = (upstream[...].astype(f32) + back).astype(bf16)
    mixed_out[...] = dot(grad, out_weight[...], NT).astype(bf16)
    out_out[...] = dot(mixed[...], grad, TN).astype(bf16)
    rows_out[...] = dot(pick[WINDOW:, :], grad, TN).astype(bf16)


def feed_back(v, gx, deps=()):
    return single(
        feed_back_kernel,
        "feed_back",
        (
            gx,
            v.mlp_unit,
            v.mlp_inv,
            v.mlp_gain,
            v.upstream,
            v.mixed,
            v.out_weight,
            v.pick,
        ),
        (like(f32, 1, D), like(bf16, D, D), like(bf16, WINDOW, D), like(bf16, VOCAB, D)),
        deps=deps,
    )


def states_back_kernel(
    gsk, gsv, weight, normed, unit, inv, gain, slope, forget, *rest
):
    k_out, v_out, gain_out, local_out, gate_out = rest[-5:]
    upstream = dot(gsk[...], weight[:, :D], NT) + dot(gsv[...], weight[:, D:], NT)
    u = unit[...]
    gain_out[...] = jnp.sum(upstream * u, axis=0, keepdims=True)
    local = norm_back(u, inv[:, :1], gain[...], upstream)
    local_out[...] = local
    f = forget[...]
    gate_out[...] = jnp.sum(local * slope[...], axis=0, keepdims=True) * f * (1.0 - f)
    k_out[...] = dot(normed[...], gsk[...], TN).astype(bf16)
    v_out[...] = dot(normed[...], gsv[...], TN).astype(bf16)


def states_back(v, gsk, gsv, deps=()):
    return single(
        states_back_kernel,
        "states_back",
        (
            gsk,
            gsv,
            v.state_kv_weight,
            v.state_normed,
            v.state_unit,
            v.state_inv,
            v.state_gain,
            v.forget_slope,
            v.forget,
        ),
        (
            like(bf16, D, D),
            like(bf16, D, D),
            like(f32, 1, D),
            like(f32, STATES, D),
            like(f32, 1, D),
        ),
        deps=deps,
    )


XI, YI, ZI, CORE, DPI, SEQI = range(6)


def permute(value, axis, to):
    size = lax.axis_size(axis)
    return lax.ppermute(value, axis, [(i, to(i)) for i in range(size)])


def swap_core(value):
    return permute(value, "seq", lambda i: i ^ 1)


def swap_dp(value, step):
    return permute(value, "dp", lambda i: i ^ step)


def ahead(value, step):
    return permute(value, "seq", lambda i: (i + 2 * step) % 8)


def fitted():
    return lax.axis_size("seq") == 8 and lax.axis_size("dp") == 4


def whole(array):
    return pl.BlockSpec(array.shape, lambda g, s: (0,) * array.ndim)


def blend(name, places, outs, deps=(), through=()):
    arrays, in_specs, plan, out_specs = [], [], [], []
    for shape, rows, blocks, segments in outs:
        every = 4 // blocks
        rows_of = []
        for sources in segments:
            names = []
            for array, block_rows, place in sources:
                names.append(len(arrays))
                arrays.append(array)
                in_specs.append(
                    pl.BlockSpec(
                        (1, block_rows, array.shape[2]),
                        lambda g, s, place=place, every=every: (*place(g // every, s), 0),
                    )
                )
            rows_of.append((sources[0][1], names))
        plan.append((every, rows_of))
        out_specs.append(
            pl.BlockSpec((1, rows, shape[2]), lambda g, s, every=every: (g // every, 0, 0))
        )
    count = len(arrays)

    def kernel(s, *refs):
        step = pl.program_id(0)
        out_refs = refs[count + len(deps) + len(through) :]

        def fill(out_ref, rows_of):
            at = 0
            for rows, names in rows_of:
                total = refs[names[0]][0].astype(f32)
                for i in names[1:]:
                    total = total + refs[i][0].astype(f32)
                out_ref[0, at : at + rows, :] = total.astype(out_ref.dtype)
                at += rows

        for out_ref, (every, rows_of) in zip(out_refs, plan):
            if every == 1:
                fill(out_ref, rows_of)
            else:
                pl.when(step % every == 0)(functools.partial(fill, out_ref, rows_of))

    return pl.pallas_call(
        kernel,
        grid_spec=pltpu.PrefetchScalarGridSpec(
            num_scalar_prefetch=1,
            grid=(4,),
            in_specs=in_specs
            + [pl.BlockSpec(memory_space=pl.ANY)] * (len(deps) + len(through)),
            out_specs=out_specs + [pl.BlockSpec(memory_space=pl.ANY)] * len(through),
        ),
        out_shape=[jax.ShapeDtypeStruct(shape, bf16) for shape, _, _, _ in outs]
        + [jax.ShapeDtypeStruct(t.shape, t.dtype) for t in through],
        input_output_aliases={
            1 + count + len(deps) + i: len(outs) + i for i in range(len(through))
        },
        compiler_params=params(),
        cost_estimate=cost(1e3, 1e3),
        name=name,
    )(places, *arrays, *deps, *through)


class Wing:
    def __init__(self, lead, kept, came, base, rows):
        self.lead, self.trail = lead, 1 - lead
        self.kept, self.came, self.base = kept, came, base
        self.half, self.quarter = rows // 2, rows // 4
        self.columns = kept.shape[2]
        self.got = []

    def first(self):
        at = self.base // self.half
        other = lambda g, s: (g, at + 1 - s[self.lead])
        return self.half, [(self.kept, self.half, other), (self.came, self.half, other)]

    def second(self):
        q = self.quarter
        at = self.base // q
        array, start = self.got[0]
        start = start // q
        deep = lambda g, s: (g, at + 2 * s[self.lead] + 1 - s[self.trail])
        flat = lambda g, s: (g, start + 1 - s[self.trail])
        return q, [(self.kept, q, deep), (self.came, q, deep), (array, q, flat)]

    def quarters(self, level):
        q = self.quarter
        at = self.base // q
        (one, start_one), (two, start_two) = self.got
        start_one, start_two = start_one // q, start_two // q
        deep = lambda g, s: (level(g, s), at + 2 * s[self.lead] + s[self.trail])
        flat = lambda g, s: (level(g, s), start_one + s[self.trail])
        last = lambda g, s: (level(g, s), start_two)
        return [(self.kept, q, deep), (self.came, q, deep), (one, q, flat), (two, q, last)]


def wings(kept, came):
    half = kept.shape[1] // 2
    return [Wing(XI, kept, came, 0, half), Wing(YI, kept, came, half, half)]


class Column:
    def __init__(self, parts):
        self.parts = parts
        self.rows = sum(w.quarter for w in parts)
        self.columns = parts[0].columns

    def near(self):
        outs = []
        for own in (False, True):
            level = (
                (lambda g, s: 2 * g + s[ZI] % 2)
                if own
                else (lambda g, s: 2 * g + 1 - s[ZI] % 2)
            )
            segments = [w.quarters(level) for w in self.parts]
            outs.append(((2, self.rows, self.columns), self.rows, 2, segments))
        return outs

    def rest(self, pick, extra=()):
        sources = [
            (array, self.rows, lambda g, s: (pick(s), 0))
            for array in (self.kept, self.from_near)
        ] + [(array, self.rows, lambda g, s: (0, 0)) for array in extra]
        return [((1, self.rows, self.columns), self.rows, 1, [sources])]

    def far(self):
        return self.rest(lambda s: 1 - s[ZI] // 2)

    def close(self):
        return self.rest(lambda s: s[ZI] // 2, [self.from_far])


class Traffic:
    def __init__(self, places):
        self.places = places
        self.pending = []

    def swap(self, send):
        came = swap_core(send)
        self.pending.append(came)
        return came

    def boundary(self, after, first=(), second=(), near=(), far=(), close=(), swap=()):
        outs, sent = [], []
        for axis in (XI, YI):
            groups = {}
            for w in first:
                if w.lead == axis:
                    groups.setdefault(w.columns, []).append((w, w.first()))
            for w in second:
                if w.trail == axis:
                    groups.setdefault(w.columns, []).append((w, w.second()))
            for columns, moves in groups.items():
                moves.sort(key=lambda m: -m[1][0])
                rows = sum(m[1][0] for m in moves)
                outs.append(
                    ((4, rows, columns), rows, 4, [m[1][1] for m in moves])
                )
                sent.append((axis, moves))
        for columns, step in ((near, Column.near), (far, Column.far), (close, Column.close)):
            for c in columns:
                outs += step(c)
        results = blend("boundary", self.places, outs, (*after, *self.pending), swap)
        self.pending = []
        mark = results[0]
        results = list(results)
        for axis, moves in sent:
            came = swap_dp(results.pop(0), 1 << axis)
            self.pending.append(came)
            at = 0
            for w, (rows, _) in moves:
                assert at % w.quarter == 0
                w.got.append((came, at))
                at += rows
        for c in near:
            c.from_near = permute(results.pop(0), "seq", lambda i: i ^ 2)
            c.kept = results.pop(0)
            self.pending.append(c.from_near)
        for c in far:
            c.from_far = permute(results.pop(0), "seq", lambda i: i ^ 4)
            self.pending.append(c.from_far)
        for c in close:
            c.own = results.pop(0)
        self.swapped = [self.swap(send) for send in results]
        return mark

    def spread(self, own, lead=1):
        beside = swap_dp(own, lead)
        other = swap_dp(own, 3 - lead)
        rows = [own, beside, other, swap_dp(beside, 3 - lead)]
        self.pending += rows[1:]
        return rows if lead == 1 else [own, other, beside, rows[3]]


def packed_pair(name, places, pieces, deps=()):
    rows = sum(p.shape[1] for p in pieces)
    columns = pieces[0].shape[2]
    outs = []
    for keep in (False, True):
        place = (
            (lambda g, s: (2 * g + s[CORE], 0))
            if keep
            else (lambda g, s: (2 * g + 1 - s[CORE], 0))
        )
        outs.append(
            ((4, rows, columns), rows, 4, [[(p, p.shape[1], place)] for p in pieces])
        )
    return blend(name, places, outs, deps)


def pack_rows(places, mark, g_tokens, g, rows_sum, *vectors):
    count = 3 + len(vectors)

    def kernel(s, *refs):
        for out_ref, (a, b, r, *rows) in zip(
            refs[2 * count + 1 :], (refs[:count], refs[count : 2 * count])
        ):
            out_ref[0, :VOCAB, :] = (a[0] + b[0].astype(f32)).astype(bf16)
            out_ref[0, VOCAB:, :128] = r[:128, :]
            out_ref[0, VOCAB:, 128:256] = r[128:, :]
            place = lax.broadcasted_iota(jnp.int32, (128, 128), 0)
            small = jnp.zeros((128, 128), f32)
            for i, row in enumerate(rows):
                value = row[...] if len(row.shape) == 2 else row[0]
                small = jnp.where(place == i, value, small)
            out_ref[0, VOCAB:, 256:] = small.astype(bf16)

    specs, arrays = [], []
    for keep in (False, True):
        at = (
            (lambda i, s: 2 * i + s[CORE]) if keep else (lambda i, s: 2 * i + 1 - s[CORE])
        )
        for array in (g_tokens, g, rows_sum, *vectors):
            arrays.append(array)
            if array.ndim == 2:
                specs.append(
                    pl.BlockSpec((array.shape[0], 128), lambda i, s, at=at: (0, at(i, s)))
                )
            else:
                specs.append(
                    pl.BlockSpec(
                        (1,) + array.shape[1:], lambda i, s, at=at: (at(i, s), 0, 0)
                    )
                )
    return pl.pallas_call(
        kernel,
        grid_spec=pltpu.PrefetchScalarGridSpec(
            num_scalar_prefetch=1,
            grid=(4,),
            in_specs=specs + [pl.BlockSpec(memory_space=pl.ANY)],
            out_specs=[pl.BlockSpec((1, 384, 384), lambda i, s: (i, 0, 0))] * 2,
        ),
        out_shape=[like(bf16, 4, 384, 384)] * 2,
        compiler_params=params(),
        cost_estimate=cost(1e3, 1e3),
        name="pack_rows",
    )(places, *arrays, mark)


def slot_of(s, step, lead):
    there = s[DPI] ^ step
    x, y = there % 2, there // 2
    return 2 * x + y if lead == XI else 2 * y + x


def unpack(name, places, quarters, pieces, outs):
    columns = quarters[0].shape[2]
    total = 4 * sum(p[1] for p in pieces)

    def kernel(s, *refs):
        scratch = refs[-1]
        for step in range(4):
            for start, rows, lead, base in pieces:
                at = pl.multiple_of(slot_of(s, step, lead) * rows + base, 16)
                scratch[pl.ds(at, rows), :] = refs[step][0, start : start + rows, :].astype(
                    f32
                )
        for out_ref, (_, moves) in zip(refs[4:-1], outs):
            for row, rows, to, column in moves:
                out_ref[to : to + rows, column : column + columns] = scratch[
                    row : row + rows, :
                ]

    return pl.pallas_call(
        kernel,
        grid_spec=pltpu.PrefetchScalarGridSpec(
            num_scalar_prefetch=1,
            grid=(1,),
            in_specs=[whole(q) for q in quarters],
            out_specs=[
                pl.BlockSpec(shape, lambda g, s: (0, 0)) for shape, _ in outs
            ],
            scratch_shapes=[pltpu.VMEM((total, columns), f32)],
        ),
        out_shape=[jax.ShapeDtypeStruct(shape, f32) for shape, _ in outs],
        compiler_params=params(),
        cost_estimate=cost(1e3, 1e3),
        name=name,
    )(places, *quarters)


def unpack_mlp(places, quarters):
    def kernel(s, *refs):
        down, up, scratch = refs[8:]
        for pair in range(2):
            for step in range(4):
                block = refs[4 * pair + step]
                for part in range(2):
                    for lead in range(2):
                        at = pl.multiple_of(slot_of(s, step, lead) * 32 + 128 * lead, 32)
                        start = part * 64 + lead * 32
                        scratch[2 * pair + part, pl.ds(at, 32), :] = block[
                            0, start : start + 32, :
                        ].astype(f32)
        for part in range(4):
            down[part * 128 : (part + 1) * 128, :] = scratch[part, :128, :]
            for block in range(8):
                at = (4 * block + part) * 128
                up[:, at : at + 128] = scratch[part, 128:, block * 128 : (block + 1) * 128]

    flat = [q for pair in quarters for q in pair]
    return pl.pallas_call(
        kernel,
        grid_spec=pltpu.PrefetchScalarGridSpec(
            num_scalar_prefetch=1,
            grid=(1,),
            in_specs=[whole(q) for q in flat],
            out_specs=[
                pl.BlockSpec((512, D), lambda g, s: (0, 0)),
                pl.BlockSpec((128, FF), lambda g, s: (0, 0)),
            ],
            scratch_shapes=[pltpu.VMEM((4, 256, D), f32)],
        ),
        out_shape=[
            jax.ShapeDtypeStruct((512, D), f32),
            jax.ShapeDtypeStruct((128, FF), f32),
        ],
        compiler_params=params(),
        cost_estimate=cost(1e3, 1e3),
        name="unpack_mlp",
    )(places, *flat)


def ring_rows(places, parts, deps=()):
    def kernel(s, *refs):
        out = refs[-1]
        for k in range(4):
            out[pl.ds(s[ZI] ^ k, 1)] = refs[k][...]

    shape = (4,) + parts[0].shape[1:]
    return pl.pallas_call(
        kernel,
        grid_spec=pltpu.PrefetchScalarGridSpec(
            num_scalar_prefetch=1,
            grid=(1,),
            in_specs=[whole(p) for p in parts]
            + [pl.BlockSpec(memory_space=pl.ANY)] * len(deps),
            out_specs=pl.BlockSpec(shape, lambda g, s: (0, 0, 0)),
        ),
        out_shape=jax.ShapeDtypeStruct(shape, bf16),
        compiler_params=params(),
        cost_estimate=cost(1e3, 1e3),
        name="ring_rows",
    )(places, *parts, *deps)


def stack_rows(places, parts):
    _, rows, columns = parts[0].shape
    rows //= 2

    def kernel(s, *refs):
        out = refs[-1]
        for step in range(4):
            for lead in range(2):
                at = pl.multiple_of(slot_of(s, step, lead) * rows + 4 * rows * lead, 16)
                out[:, pl.ds(at, rows), :] = refs[step][:, lead * rows : (lead + 1) * rows, :]

    shape = (4, 8 * rows, columns)
    return pl.pallas_call(
        kernel,
        grid_spec=pltpu.PrefetchScalarGridSpec(
            num_scalar_prefetch=1,
            grid=(1,),
            in_specs=[whole(p) for p in parts],
            out_specs=pl.BlockSpec(shape, lambda g, s: (0, 0, 0)),
        ),
        out_shape=jax.ShapeDtypeStruct(shape, bf16),
        compiler_params=params(),
        cost_estimate=cost(1e3, 1e3),
        name="stack_rows",
    )(places, *parts)


def last_kernel(
    s, mine, other, norm_cols, unit_cols, weight, weight_rows, unit, inv, gain,
    qkv_out, gain_out, table_out, small_out, by_head,
):
    for z in range(4):
        for q in range(2):
            by_head[2 * z + q] = jnp.where(s[CORE] == q, mine[z], other[z])
    small_out[...] = mine[s[ZI], 256:272, 256:].astype(f32)[:8]
    at = pl.multiple_of(s[SEQI] * 32, 32)
    norm = norm_cols[...]
    cols_grad = jnp.zeros((VOCAB, 128), f32)
    normed_grad = jnp.zeros((32, D), f32)
    for h in range(HEADS):
        for t in range(3):
            lanes = slice(t * 128, (t + 1) * 128)
            to = slice(t * D + h * 128, t * D + (h + 1) * 128)
            g = by_head[h, :VOCAB, lanes]
            qkv_out[:, to] = dot(norm, g, TN)
            cols_grad = cols_grad + dot(g, weight_rows[:, to], NT)
            normed_grad = normed_grad + dot(
                by_head[h, pl.ds(at, 32), lanes], weight[:, to], NT
            )
    gain_out[...] = jnp.sum(cols_grad * unit_cols[...], axis=0, keepdims=True)
    u = unit[...]
    scaled = normed_grad * gain[...]
    a = jnp.mean(scaled, axis=-1, keepdims=True)
    b = jnp.mean(scaled * u, axis=-1, keepdims=True)
    low = pl.multiple_of(VOCAB + (s[SEQI] % 4) * 32, 32)
    rows_sum = [
        jnp.where(
            s[SEQI] < 4,
            by_head[h, pl.ds(low, 32), :128].astype(f32),
            by_head[h, pl.ds(low, 32), 128:256].astype(f32),
        )
        for h in range(HEADS)
    ]
    table_out[...] = (
        jnp.concatenate(rows_sum, axis=1) + (scaled - a - u * b) * inv[:, :1]
    )


def last_products(places, mine, other, normed, unit, weight, inv, gain):
    return pl.pallas_call(
        last_kernel,
        grid_spec=pltpu.PrefetchScalarGridSpec(
            num_scalar_prefetch=1,
            grid=(1,),
            in_specs=[
                whole(mine),
                whole(other),
                pl.BlockSpec((VOCAB, 128), lambda g, s: (0, s[SEQI])),
                pl.BlockSpec((VOCAB, 128), lambda g, s: (0, s[SEQI])),
                whole(weight),
                pl.BlockSpec((128, 3 * D), lambda g, s: (s[SEQI], 0)),
                pl.BlockSpec((32, D), lambda g, s: (s[SEQI], 0)),
                pl.BlockSpec((32, 128), lambda g, s: (s[SEQI], 0)),
                whole(gain),
            ],
            out_specs=[
                pl.BlockSpec((128, 3 * D), lambda g, s: (0, 0)),
                pl.BlockSpec((1, 128), lambda g, s: (0, 0)),
                pl.BlockSpec((32, D), lambda g, s: (0, 0)),
                pl.BlockSpec((8, 128), lambda g, s: (0, 0)),
            ],
            scratch_shapes=[pltpu.VMEM((HEADS, 384, 384), bf16)],
        ),
        out_shape=[
            jax.ShapeDtypeStruct((128, 3 * D), f32),
            jax.ShapeDtypeStruct((1, 128), f32),
            jax.ShapeDtypeStruct((32, D), f32),
            jax.ShapeDtypeStruct((8, 128), f32),
        ],
        compiler_params=params(),
        cost_estimate=cost(1e3, 1e3),
        name="last_products",
    )(places, mine, other, normed, unit, weight, weight, unit, inv, gain)


def total_of(value):
    flat = value.reshape((-1,) + value.shape[2:])
    own = lax.psum_scatter(flat, "seq", scatter_dimension=0, tiled=True)
    return lax.psum(own, "dp").astype(f32)


def body(
    char_ids,
    seg_starts,
    char_table,
    norm_gain,
    qkv_weight,
    distance_bias,
    state_query,
    state_init,
    state_gain,
    state_kv_weight,
    gate_logit,
    out_weight,
    mlp_gain,
    up_weight,
    down_weight,
    cotangent,
):
    windows = lax.axis_size("seq")
    here = lax.axis_index("seq")
    shard = lambda n: n // windows

    packed = jnp.concatenate(
        [char_ids.reshape(4, 128), jnp.broadcast_to(seg_starts, (1, 128))], axis=0
    )
    everyone = lax.all_gather(packed, "seq")
    ids_all = everyone[:, :4].reshape(windows, WINDOW)
    flags = everyone[:, 4, 0]
    order = jnp.arange(windows, dtype=jnp.int32)
    first = jnp.max(jnp.where((flags > 0) & (order <= here), order, 0))
    span = jnp.stack([first, here]).astype(jnp.int32)
    live = (1 - seg_starts.reshape(1)).astype(jnp.int32)
    vocab = jnp.arange(VOCAB, dtype=jnp.int32)
    counts = jnp.sum(
        (ids_all[:, :, None] == vocab[None, None, :]).astype(f32), axis=1
    )
    lnn = jnp.where(counts > 0, jnp.log2(jnp.maximum(counts, 1.0)), hidden)
    lnn = jnp.broadcast_to(lnn[:, :, None], (windows, VOCAB, 128))
    before = lax.dynamic_index_in_dim(ids_all, jnp.maximum(here - 1, 0), 0, False)
    context_ids = jnp.concatenate([before, char_ids.reshape(-1)])
    pick = (context_ids[:, None] == vocab[None, :]).astype(bf16)
    pick_t = (vocab[:, None] == context_ids[None, :]).astype(bf16)

    norm_gain, state_gain, mlp_gain = (
        t.reshape(1, D) for t in (norm_gain, state_gain, mlp_gain)
    )
    table_unit, table_inv, normed_table, qkv_table = table_forward(
        char_table, norm_gain, qkv_weight
    )

    forget = jax.nn.sigmoid(gate_logit)
    fcol = jnp.broadcast_to(forget[:, None], (D, 128))
    states_in, forget_slope, summary_lse = summary_forward(
        span, state_query, qkv_table, lnn, state_init, fcol
    )
    state_unit, state_inv, state_normed, state_kv = states_forward(
        states_in, state_gain, state_kv_weight
    )
    forget = forget.reshape(1, D)

    bias_rows = (
        jnp.dot(
            distance_bias.reshape(HEADS, BUCKETS),
            jnp.asarray(lane_pick()),
            precision=lax.Precision.HIGHEST,
        )
        * log2e
        + jnp.asarray(lane_hidden())
    ).reshape(HEADS, 1, CONTEXT)
    mixed, lse = attention_forward(
        live, pick, pick_t, qkv_table, state_kv, state_kv, bias_rows
    )
    residual, mlp_unit, mlp_inv, mlp_in = residual_forward(
        mixed, out_weight, pick, char_table, mlp_gain
    )
    upstream = cotangent.reshape(WINDOW, D)

    close_up = fitted_tail if fitted() else plain_tail
    return close_up(dict(locals()))


def fitted_tail(values):
    v = types.SimpleNamespace(**values)
    dp = lax.axis_index("dp")
    places = jnp.stack(
        [dp % 2, dp // 2, v.here // 2, v.here % 2, dp, v.here]
    ).astype(jnp.int32)
    weights = (v.upstream, v.up_weight, v.down_weight)

    out, gx = v.residual, jnp.zeros((WINDOW, D), f32)
    traffic = Traffic(places)
    parts, deps = [], ()
    for part in range(4):
        send, keep, out, gx = mlp_packed(
            part, places, v.mlp_in, *weights, out, gx, deps
        )
        if part:
            second = parts[part - 2] if part > 1 else ()
            mark = traffic.boundary((gx,), parts[part - 1], second, swap=[send])
            deps = (mark,)
            came = traffic.swapped[0]
        else:
            came = traffic.swap(send)
        parts.append(wings(keep, came))
    layer_out = out.astype(bf16).reshape(1, WINDOW, D)
    front = Column(parts[0] + parts[1])
    back = Column(parts[2] + parts[3])

    grad_mlp_gain, grad_out, grad_mixed, rows_sum = feed_back(v, gx, (mark,))
    gsk, gsv, gq, inner = state_backward(
        v.pick, v.qkv_table, v.state_kv, v.lse, v.mixed, grad_mixed
    )
    mark = traffic.boundary((gsk,), parts[3], parts[2], near=[front])
    grad_k, grad_v, grad_state_gain, local, grad_gate = states_back(v, gsk, gsv, (mark,))
    send, keep = packed_pair(
        "pack_middle",
        places,
        [t.reshape(8, 128, D) for t in (grad_k, grad_v, grad_out)],
    )
    middle = wings(keep, traffic.swap(send))
    g, gsq, ginit = summary_backward(
        v.span, v.state_query, v.qkv_table, v.lnn, v.summary_lse, local, v.fcol, None,
        (send,),
    )
    mark = traffic.boundary((g,), middle, parts[3], far=[front])
    send, keep = packed_pair(
        "pack_states", places, [gsq.reshape(8, 64, D), ginit.reshape(8, 64, D)], (mark,)
    )
    states = wings(keep, traffic.swap(send))
    tokens_args = (
        v.live, v.pick, v.pick_t, v.qkv_table, v.bias_rows, v.lse, inner, grad_mixed, gq
    )
    onto = token_backward(*tokens_args, (send,), 0)
    mark = traffic.boundary((onto[1],), states, middle, near=[back], close=[front])
    g_tokens, fold = token_backward(*tokens_args, (mark,), 1, onto)
    mark = traffic.boundary((fold,), (), states, far=[back])
    send, keep = pack_rows(
        places, mark, g_tokens, g, rows_sum, grad_mlp_gain, grad_state_gain, grad_gate, fold
    )
    rows = wings(keep, traffic.swap(send))
    side = Column(middle + states)
    last = Column(rows)
    traffic.boundary((), rows, near=[side], close=[back])
    front_rows = traffic.spread(front.own)
    traffic.boundary((), (), rows, far=[side])
    traffic.boundary((), near=[last], close=[side])
    back_rows = traffic.spread(back.own, 2)
    traffic.boundary((), far=[last])
    side_rows = traffic.spread(side.own)
    traffic.boundary((), close=[last])
    beside = permute(last.own, "seq", lambda i: i ^ 2)
    row_ring = [
        last.own,
        beside,
        permute(last.own, "seq", lambda i: i ^ 4),
        permute(beside, "seq", lambda i: i ^ 4),
    ]
    ring = ring_rows(places, row_ring)
    ring_parts = traffic.spread(ring)
    mine = stack_rows(places, ring_parts)
    other = swap_core(mine)
    grad_down, grad_up = unpack_mlp(places, [front_rows, back_rows])
    grad_state_kv, grad_out, grad_state_query, grad_state_init = unpack(
        "unpack_side",
        places,
        side_rows,
        [(0, 48, XI, 0), (48, 48, YI, 192), (96, 16, XI, 384), (112, 16, YI, 448)],
        [
            ((128, 2 * D), [(0, 128, 0, 0), (128, 128, 0, D)]),
            ((128, D), [(256, 128, 0, 0)]),
            ((64, D), [(384, 64, 0, 0)]),
            ((64, D), [(448, 64, 0, 0)]),
        ],
    )
    grad_qkv, grad_norm_gain, grad_table, small = last_products(
        places,
        mine,
        other,
        v.normed_table,
        v.table_unit,
        v.qkv_weight,
        v.table_inv,
        v.norm_gain,
    )
    return (
        layer_out,
        grad_table,
        grad_norm_gain.reshape(-1),
        grad_qkv,
        small[3, :32],
        grad_state_query,
        grad_state_init,
        small[1],
        grad_state_kv,
        small[2],
        grad_out,
        small[0],
        grad_up,
        grad_down,
    )


def plain_tail(values):
    v = types.SimpleNamespace(**values)
    windows, here = v.windows, v.here
    shard = lambda n: n // windows
    out, gx = v.residual, jnp.zeros((WINDOW, D), f32)
    grads_down, grads_up = [], []
    for part in range(SPLITS):
        gd, gu, out, gx = mlp_part(
            part, v.mlp_in, v.upstream, v.up_weight, v.down_weight, out, gx
        )
        grads_down.append(gd)
        grads_up.append(gu)
    layer_out = out.astype(bf16).reshape(1, WINDOW, D)
    grad_mlp_gain, grad_out, grad_mixed, rows_sum = feed_back(v, gx)
    gsk, gsv, gq, inner = state_backward(
        v.pick, v.qkv_table, v.state_kv, v.lse, v.mixed, grad_mixed
    )
    grad_k, grad_v, grad_state_gain, local, grad_gate = states_back(v, gsk, gsv)
    g, gsq, ginit = summary_backward(
        v.span, v.state_query, v.qkv_table, v.lnn, v.summary_lse, local, v.fcol, None
    )
    g_tokens, fold = token_backward(
        v.live, v.pick, v.pick_t, v.qkv_table, v.bias_rows, v.lse, inner, grad_mixed, gq
    )
    g = (g.astype(f32) + g_tokens).astype(bf16)
    sharded = lambda t: total_of(t.reshape(windows, -1, t.shape[-1]))
    full = jnp.stack([t.reshape(-1, TILE, D) for t in grads_down], axis=1)
    grad_down = sharded(full.reshape(FF, D))
    full = jnp.stack([t.reshape(D, -1, TILE) for t in grads_up], axis=2)
    grad_up = sharded(full.reshape(D, FF))
    grad_state_kv = sharded(jnp.concatenate([grad_k, grad_v], axis=1))
    small = jnp.concatenate(
        [
            t.reshape(windows, -1)
            for t in (grad_mlp_gain, grad_state_gain, grad_gate, fold[:, 0, :BUCKETS])
        ],
        axis=1,
    )
    small = total_of(small[:, None, :])[0]
    cut = shard(D)
    all_rows = lax.psum(g, ("dp", "seq"))
    grad_rows = jnp.concatenate(
        [
            all_rows[:, :, t * 128 : (t + 1) * 128].transpose(1, 0, 2).reshape(VOCAB, D)
            for t in range(3)
        ],
        axis=1,
    )
    mine = lax.dynamic_slice_in_dim(v.normed_table, here * cut, cut, 1)
    weight_rows = lax.dynamic_slice_in_dim(v.qkv_weight, here * cut, cut, 0)
    unit_cols = lax.dynamic_slice_in_dim(v.table_unit, here * cut, cut, 1)
    at = here * shard(VOCAB)
    take = lambda t: lax.dynamic_slice_in_dim(t, at, shard(VOCAB), 0)
    grad_table = sharded(rows_sum) + norm_back(
        take(v.table_unit),
        take(v.table_inv)[:, :1],
        v.norm_gain,
        dot(take(grad_rows), v.qkv_weight, NT),
    )
    return (
        layer_out,
        grad_table,
        jnp.sum(dot(grad_rows, weight_rows, NT) * unit_cols, axis=0),
        dot(mine, grad_rows, TN),
        small[3 * cut :],
        sharded(gsq),
        sharded(ginit),
        small[cut : 2 * cut],
        grad_state_kv,
        small[2 * cut : 3 * cut],
        sharded(grad_out),
        small[:cut],
        grad_up,
        grad_down,
    )


def solution(mesh):
    placed = (P("dp", "seq"), P("dp", "seq")) + (P(),) * 13 + (P("dp", "seq", None),)
    return jax.shard_map(
        body,
        mesh=mesh,
        in_specs=placed,
        out_specs=(
            P("dp", "seq", None),
            P("seq", None),
            P("seq"),
            P("seq", None),
            P("seq"),
            P("seq", None),
            P("seq", None),
            P("seq"),
            P("seq", None),
            P("seq"),
            P("seq", None),
            P("seq"),
            P("seq", None),
            P("seq", None),
        ),
        check_vma=False,
    )
```

```python
import functools
import math
import types

import jax
import jax.numpy as jnp
import numpy as np
from jax import lax
from jax.experimental import pallas as pl
from jax.experimental.pallas import tpu as pltpu
from jax.sharding import PartitionSpec as P

D = 1024
HEADS = 8
HEAD_DIM = 128
FF = 4096
VOCAB = 256
STATES = 512
WINDOW = 512
BUCKETS = 32
MAX_DISTANCE = 128
CONTEXT = 2 * WINDOW
TILE = 256
SPLITS = 2

epsilon = 1e-05
hidden = -1e30
log2e = math.log2(math.e)
score_scale = 1.0 / math.sqrt(HEAD_DIM)
f32 = jnp.float32
bf16 = jnp.bfloat16

NN = (((1,), (0,)), ((), ()))
NT = (((1,), (1,)), ((), ()))
TN = (((0,), (0,)), ((), ()))


def dot(a, b, dims=NN):
    return lax.dot_general(a, b, dims, preferred_element_type=f32)


def params(mib=26):
    return pltpu.CompilerParams(
        dimension_semantics=("arbitrary",), vmem_limit_bytes=mib * 1024 * 1024
    )


def cost(flops, moved, exps=0):
    return pl.CostEstimate(
        flops=int(flops), bytes_accessed=int(moved), transcendentals=int(exps)
    )


def norm_parts(value):
    centre = jnp.mean(value, axis=-1, keepdims=True)
    offset = value - centre
    spread = jnp.mean(offset * offset, axis=-1, keepdims=True)
    inv = lax.rsqrt(spread + epsilon)
    return offset * inv, inv


def norm_back(unit, inv, gain, upstream):
    scaled = upstream * gain
    a = jnp.mean(scaled, axis=-1, keepdims=True)
    b = jnp.mean(scaled * unit, axis=-1, keepdims=True)
    return (scaled - a - unit * b) * inv


def bucket_table():
    distance = np.arange(WINDOW)
    exact_count = BUCKETS // 2
    log_ratio = np.log(np.maximum(distance, 1) / exact_count) / math.log(
        MAX_DISTANCE / exact_count
    )
    far_bucket = exact_count + np.floor(log_ratio * (BUCKETS - exact_count)).astype(
        np.int64
    )
    return np.where(
        distance < exact_count, distance, np.minimum(far_bucket, BUCKETS - 1)
    )


def lane_pick():
    pick = np.zeros((BUCKETS, CONTEXT), np.float32)
    table = bucket_table()
    for m in range(1, WINDOW + 1):
        pick[table[WINDOW - m], m] = 1.0
    return pick


def lane_hidden():
    m = np.arange(CONTEXT)
    return np.where((m >= 1) & (m <= WINDOW), 0.0, hidden).astype(np.float32)[None]


smallest_sum = 2.0**-80


def shared_exp(lg, there):
    peak = jnp.max(jnp.where(there > 0, lg, hidden), axis=1, keepdims=True)
    return jnp.exp2(jnp.minimum(lg - peak, 0.0)).astype(bf16)


def window_sides(v, n):
    return jnp.concatenate([v.astype(f32) * n, n], axis=1).astype(bf16)


def own_weights(lg, n_row):
    x = lg + jnp.where(n_row > 0, jnp.log2(jnp.maximum(n_row, 1.0)), hidden)
    p = jnp.exp2(x - jnp.max(x, axis=1, keepdims=True))
    return p / jnp.sum(p, axis=1, keepdims=True)


def characters_there(span, rows):
    return lax.fori_loop(
        span[0], span[1], lambda w, t: t + rows[w], jnp.zeros((1, VOCAB), f32)
    )


TOGETHER = 4


def lanes_of(i):
    return slice(i * HEAD_DIM, (i + 1) * HEAD_DIM)


def summary_forward_kernel(
    span, sq, kt, vt, counts, rows, init, forget, state_out, y_out, low_out, a_s, y_s
):
    heads = range(TOGETHER)
    f = forget[...]
    v = [vt[:, lanes_of(i)] for i in heads]

    def scores(i):
        return dot(sq[:, lanes_of(i)], kt[:, lanes_of(i)], NT) * (score_scale * log2e)

    def begin():
        a_s[...] = init[...].astype(f32)
        y_s[...] = jnp.zeros_like(y_s)

    def move(i, u):
        at = lanes_of(i)
        a = a_s[:, at]
        y_s[:, at] = a - u + f[:, at] * y_s[:, at]
        a_s[:, at] = u + f[:, at] * (a - u)

    begin()
    there = characters_there(span, rows)
    e = [shared_exp(scores(i), there) for i in heads]

    def step(w, low):
        n = counts[w]
        for i in heads:
            both = dot(e[i], window_sides(v[i], n))
            z = both[:, HEAD_DIM:]
            move(i, both[:, :HEAD_DIM] / jnp.maximum(z, smallest_sum))
            low = jnp.minimum(low, jnp.min(z.reshape(STATES // 8, 8, 128), axis=0))
        return low

    low = lax.fori_loop(span[0], span[1], step, jnp.full((8, 128), 1.0, f32))
    low_out[0] = low

    @pl.when(jnp.min(low) < smallest_sum)
    def _():
        begin()
        for i in heads:
            lg = scores(i)

            def slow(w, _):
                move(i, dot(own_weights(lg, rows[w]).astype(bf16), v[i]))
                return 0

            lax.fori_loop(span[0], span[1], slow, 0)

    state_out[...] = a_s[...]
    y_out[...] = y_s[...]


def summary_specs(windows):
    wide = TOGETHER * HEAD_DIM
    head = lambda k: (lambda h, s: (0, k * HEADS // TOGETHER + h))
    return [
        pl.BlockSpec((STATES, wide), head(0)),
        pl.BlockSpec((VOCAB, wide), head(1)),
        pl.BlockSpec((VOCAB, wide), head(2)),
        pl.BlockSpec((windows, VOCAB, 128), lambda h, s: (0, 0, 0)),
        pl.BlockSpec((windows, 1, VOCAB), lambda h, s: (0, 0, 0)),
        pl.BlockSpec((STATES, wide), head(0)),
        pl.BlockSpec((1, wide), head(0)),
    ]


def summary_forward(span, state_query, qkv_table, counts, rows, state_init, forget):
    states = pl.BlockSpec((STATES, TOGETHER * HEAD_DIM), lambda h, s: (0, h))
    return pl.pallas_call(
        summary_forward_kernel,
        grid_spec=pltpu.PrefetchScalarGridSpec(
            num_scalar_prefetch=1,
            grid=(HEADS // TOGETHER,),
            in_specs=summary_specs(counts.shape[0]),
            out_specs=[states, states, pl.BlockSpec((1, 8, 128), lambda h, s: (h, 0, 0))],
            scratch_shapes=[pltpu.VMEM((STATES, TOGETHER * HEAD_DIM), f32)] * 2,
        ),
        out_shape=[
            jax.ShapeDtypeStruct((STATES, D), f32),
            jax.ShapeDtypeStruct((STATES, D), f32),
            jax.ShapeDtypeStruct((HEADS // TOGETHER, 8, 128), f32),
        ],
        compiler_params=params(),
        cost_estimate=cost(1e3, 1e3),
        name="summary_forward",
    )(span, state_query, qkv_table, qkv_table, counts, rows, state_init, forget)


def summary_backward_kernel(span, sq, kt, vt, counts, rows, local, forget, low, *rest):
    g_out, gsq_out, ginit_out, g_s, gs_s, gv_s, gs16, e_s, e_t = rest[-9:]
    heads = range(TOGETHER)
    f = forget[...]
    v = [vt[:, lanes_of(i)] for i in heads]
    g_s[...] = local[...]
    gs_s[...] = jnp.zeros_like(gs_s)
    gv_s[...] = jnp.zeros_like(gv_s)
    first, here = span[0], span[1]
    fast = jnp.min(low[0]) >= smallest_sum

    def scores(i):
        return dot(sq[:, lanes_of(i)], kt[:, lanes_of(i)], NT) * (score_scale * log2e)

    def carried(i):
        at = lanes_of(i)
        g = g_s[:, at]
        fg = f[:, at] * g
        g_s[:, at] = fg
        return g - fg

    @pl.when(fast)
    def _():
        there = characters_there(span, rows)
        for i in heads:
            e = shared_exp(scores(i), there)
            e_s[i] = e
            e_t[i] = e.astype(f32).T.astype(bf16)
        lane = lax.broadcasted_iota(jnp.int32, (STATES, HEAD_DIM), 1)

        def step(t, _):
            w = here - 1 - t
            n = counts[w]
            for i in heads:
                sides = window_sides(v[i], n)
                both = dot(e_s[i], sides)
                part = 1.0 / both[:, HEAD_DIM:]
                gu = (carried(i) * part).astype(bf16)
                inner = gu.astype(f32) * (both[:, :HEAD_DIM] * part)
                inner = inner + pltpu.roll(inner, HEAD_DIM // 2, 1)
                high = inner.astype(bf16)
                tail = jnp.where(
                    lane < HEAD_DIM // 2, high.astype(f32), inner - high.astype(f32)
                )
                gs_s[i] += dot(
                    jnp.concatenate([gu, (-tail).astype(bf16)], axis=1), sides, NT
                )
                gv_s[i] += n * dot(e_t[i], gu)
            return 0

        lax.fori_loop(0, here - first, step, 0)
        for i in heads:
            gs16[i] = (gs_s[i] * e_s[i].astype(f32) * score_scale).astype(bf16)

    @pl.when(jnp.logical_not(fast))
    def _():
        for i in heads:
            lg = scores(i)

            def slow(t, _):
                w = here - 1 - t
                p = own_weights(lg, rows[w])
                gu = carried(i).astype(bf16)
                pd = p * dot(gu, v[i], NT)
                gs_s[i] += pd - p * jnp.sum(pd, axis=1, keepdims=True)
                gv_s[i] += dot(p.astype(bf16), gu, TN)
                return 0

            lax.fori_loop(0, here - first, slow, 0)
            gs16[i] = (gs_s[i] * score_scale).astype(bf16)

    for i in heads:
        gs = gs16[i]
        at = lanes_of(i)
        g_out[i, :, :128] = jnp.zeros((VOCAB, 128), bf16)
        g_out[i, :, 128:256] = dot(gs, sq[:, at], TN).astype(bf16)
        g_out[i, :, 256:] = gv_s[i].astype(bf16)
        gsq_out[:, at] = dot(gs, kt[:, at]).astype(bf16)
    ginit_out[...] = g_s[...].astype(bf16)


def summary_backward(
    span, state_query, qkv_table, counts, rows, local, forget, low, deps=()
):
    states = pl.BlockSpec((STATES, TOGETHER * HEAD_DIM), lambda h, s: (0, h))
    return pl.pallas_call(
        summary_backward_kernel,
        grid_spec=pltpu.PrefetchScalarGridSpec(
            num_scalar_prefetch=1,
            grid=(HEADS // TOGETHER,),
            in_specs=summary_specs(counts.shape[0])
            + [pl.BlockSpec((1, 8, 128), lambda h, s: (h, 0, 0))]
            + [pl.BlockSpec(memory_space=pl.ANY)] * len(deps),
            out_specs=[
                pl.BlockSpec((TOGETHER, VOCAB, 384), lambda h, s: (h, 0, 0)),
                states,
                states,
            ],
            scratch_shapes=[
                pltpu.VMEM((STATES, TOGETHER * HEAD_DIM), f32),
                pltpu.VMEM((TOGETHER, STATES, VOCAB), f32),
                pltpu.VMEM((TOGETHER, VOCAB, HEAD_DIM), f32),
                pltpu.VMEM((TOGETHER, STATES, VOCAB), bf16),
                pltpu.VMEM((TOGETHER, STATES, VOCAB), bf16),
                pltpu.VMEM((TOGETHER, VOCAB, STATES), bf16),
            ],
        ),
        out_shape=[
            jax.ShapeDtypeStruct((HEADS, VOCAB, 384), bf16),
            jax.ShapeDtypeStruct((STATES, D), bf16),
            jax.ShapeDtypeStruct((STATES, D), bf16),
        ],
        compiler_params=params(),
        cost_estimate=cost(1e3, 1e3),
        name="summary_backward",
    )(span, state_query, qkv_table, qkv_table, counts, rows, local, forget, low, *deps)


def bias_tile(row):
    spread = jnp.broadcast_to(row, (TILE, CONTEXT))
    shifted = pltpu.roll(spread, 0, 1, stride=1, stride_axis=0)
    return shifted[:, : 3 * TILE].T


def attention_forward_kernel(
    live, pick, pick_t, qt, kt, vt, sk, sv, bias_row, mixed_out, lse_out, bias
):
    bias[...] = bias_tile(bias_row[0])
    prev_add = jnp.where(live[0] > 0, 0.0, hidden).astype(f32)
    keys = dot(pick[...], kt[...]).astype(bf16)
    values_t = dot(vt[...], pick_t[...], TN).astype(bf16)
    query = dot(pick[WINDOW:, :], qt[...]).astype(bf16)
    state_values_t = sv[...].astype(f32).T.astype(bf16)
    for j in range(WINDOW // TILE):
        q = query[j * TILE : (j + 1) * TILE]
        scores = []
        for rel in range(3):
            kt_i = j + rel
            s = (
                dot(keys[kt_i * TILE : (kt_i + 1) * TILE], q, NT)
                * (score_scale * log2e)
                + bias[rel * TILE : (rel + 1) * TILE]
            )
            if kt_i * TILE < WINDOW:
                s = s + prev_add
            scores.append(s)
        for st in range(STATES // TILE):
            scores.append(
                dot(sk[st * TILE : (st + 1) * TILE, :], q, NT) * (score_scale * log2e)
            )
        peak = functools.reduce(
            jnp.maximum, [jnp.max(s, axis=0, keepdims=True) for s in scores]
        )
        total = jnp.zeros((1, TILE), f32)
        out = jnp.zeros((HEAD_DIM, TILE), f32)
        for i, s in enumerate(scores):
            p = jnp.exp2(s - peak)
            total = total + jnp.sum(p, axis=0, keepdims=True)
            if i < 3:
                v = values_t[:, (j + i) * TILE : (j + i + 1) * TILE]
            else:
                v = state_values_t[:, (i - 3) * TILE : (i - 2) * TILE]
            out = out + dot(v, p.astype(bf16))
        out = out * (1.0 / total)
        mixed_out[j * TILE : (j + 1) * TILE, :] = out.T.astype(bf16)
        lse_out[0, :, j * TILE : (j + 1) * TILE] = peak + jnp.log2(total)


def attention_forward(live, pick, pick_t, qkv_table, sk, sv, bias_rows):
    head = lambda k: (lambda h, s: (0, k * HEADS + h))
    whole = lambda *shape: pl.BlockSpec(shape, lambda h, s: (0,) * len(shape))
    return pl.pallas_call(
        attention_forward_kernel,
        grid_spec=pltpu.PrefetchScalarGridSpec(
            num_scalar_prefetch=1,
            grid=(HEADS,),
            in_specs=[
                whole(CONTEXT, VOCAB),
                whole(VOCAB, CONTEXT),
                pl.BlockSpec((VOCAB, HEAD_DIM), head(0)),
                pl.BlockSpec((VOCAB, HEAD_DIM), head(1)),
                pl.BlockSpec((VOCAB, HEAD_DIM), head(2)),
                pl.BlockSpec((STATES, HEAD_DIM), head(0)),
                pl.BlockSpec((STATES, HEAD_DIM), head(1)),
                pl.BlockSpec((1, 1, CONTEXT), lambda h, s: (h, 0, 0)),
            ],
            out_specs=[
                pl.BlockSpec((WINDOW, HEAD_DIM), head(0)),
                pl.BlockSpec((1, 1, WINDOW), lambda h, s: (h, 0, 0)),
            ],
            scratch_shapes=[pltpu.VMEM((3 * TILE, TILE), f32)],
        ),
        out_shape=[
            jax.ShapeDtypeStruct((WINDOW, D), bf16),
            jax.ShapeDtypeStruct((HEADS, 1, WINDOW), f32),
        ],
        compiler_params=params(),
        cost_estimate=cost(1e3, 1e3),
        name="attention_forward",
    )(live, pick, pick_t, qkv_table, qkv_table, qkv_table, sk, sv, bias_rows)


def back_tile(s, dp, shift, inner):
    p = jnp.exp2(s - shift)
    return p, p * (dp - inner)


def state_backward_kernel(pick, qt, sk, sv, lse, mixed, grad, *rest):
    gsk_out, gsv_out, gq_out, inner_out = rest[-4:]
    query = dot(pick[WINDOW:, :], qt[...]).astype(bf16)
    state_keys_t = sk[...].astype(f32).T.astype(bf16)
    inner_all = jnp.sum(
        (mixed[...].astype(f32) * grad[...].astype(f32)).T, axis=0, keepdims=True
    )
    inner_out[0] = inner_all
    blocks = WINDOW // TILE
    gq = [jnp.zeros((HEAD_DIM, TILE), f32) for _ in range(blocks)]
    for st in range(STATES // TILE):
        at = slice(st * TILE, (st + 1) * TILE)
        gk = jnp.zeros((TILE, HEAD_DIM), f32)
        gv = jnp.zeros((TILE, HEAD_DIM), f32)
        for j in range(blocks):
            rows = slice(j * TILE, (j + 1) * TILE)
            p, gs = back_tile(
                dot(sk[at, :], query[rows], NT) * (score_scale * log2e),
                dot(sv[at, :], grad[rows, :], NT),
                lse[0, :, rows],
                inner_all[:, rows],
            )
            gs16 = gs.astype(bf16)
            gq[j] = gq[j] + dot(state_keys_t[:, at], gs16)
            gk = gk + dot(gs16, query[rows])
            gv = gv + dot(p.astype(bf16), grad[rows, :])
        gsk_out[at, :] = (gk * score_scale).astype(bf16)
        gsv_out[at, :] = gv.astype(bf16)
    for j in range(blocks):
        gq_out[0, :, j * TILE : (j + 1) * TILE] = gq[j]


def state_backward(pick, qkv_table, state_kv, lse, mixed, grad, deps=()):
    head = lambda k: (lambda h: (0, k * HEADS + h))
    tokens = pl.BlockSpec((WINDOW, HEAD_DIM), head(0))
    states = pl.BlockSpec((STATES, HEAD_DIM), head(0))
    row = pl.BlockSpec((1, 1, WINDOW), lambda h: (h, 0, 0))
    return pl.pallas_call(
        state_backward_kernel,
        grid=(HEADS,),
        in_specs=[
            pl.BlockSpec((CONTEXT, VOCAB), lambda h: (0, 0)),
            pl.BlockSpec((VOCAB, HEAD_DIM), head(0)),
            pl.BlockSpec((STATES, HEAD_DIM), head(0)),
            pl.BlockSpec((STATES, HEAD_DIM), head(1)),
            row,
            tokens,
            tokens,
        ]
        + [pl.BlockSpec(memory_space=pl.ANY)] * len(deps),
        out_specs=[
            states,
            states,
            pl.BlockSpec((1, HEAD_DIM, WINDOW), lambda h: (h, 0, 0)),
            row,
        ],
        out_shape=[
            jax.ShapeDtypeStruct((STATES, D), bf16),
            jax.ShapeDtypeStruct((STATES, D), bf16),
            jax.ShapeDtypeStruct((HEADS, HEAD_DIM, WINDOW), f32),
            jax.ShapeDtypeStruct((HEADS, 1, WINDOW), f32),
        ],
        compiler_params=params(),
        cost_estimate=cost(1e3, 1e3),
        name="state_backward",
    )(pick, qkv_table, state_kv, state_kv, lse, mixed, grad, *deps)


def token_backward_kernel(
    live, pick, pick_t, qt, kt, vt, bias_row, lse, inner, grad, gq_in, buckets, *rest
):
    g_out, fold_out, bias, bias_grad = rest[-4:]
    bias[...] = bias_tile(bias_row[0])
    bias_grad[...] = jnp.zeros_like(bias_grad)
    prev_add = jnp.where(live[0] > 0, 0.0, hidden).astype(f32)
    both = dot(pick[...], jnp.concatenate([kt[...], vt[...]], axis=1)).astype(bf16)
    keys = both[:, :HEAD_DIM]
    values = both[:, HEAD_DIM:]
    keys_t = dot(kt[...], pick_t[...], TN).astype(bf16)
    query = dot(pick[WINDOW:, :], qt[...]).astype(bf16)
    blocks = WINDOW // TILE
    gq = [gq_in[0, :, j * TILE : (j + 1) * TILE] for j in range(blocks)]
    sums = jnp.zeros((VOCAB, 2 * HEAD_DIM), f32)
    for tile in range(CONTEXT // TILE):
        at = slice(tile * TILE, (tile + 1) * TILE)
        gk = jnp.zeros((TILE, HEAD_DIM), f32)
        gv = jnp.zeros((TILE, HEAD_DIM), f32)
        for j in range(blocks):
            rel = tile - j
            if not 0 <= rel < 3:
                continue
            rows = slice(j * TILE, (j + 1) * TILE)
            rels = slice(rel * TILE, (rel + 1) * TILE)
            shift = lse[0, :, rows]
            if tile * TILE < WINDOW:
                shift = shift - prev_add
            p, gs = back_tile(
                dot(keys[at], query[rows], NT) * (score_scale * log2e) + bias[rels],
                dot(values[at], grad[rows, :], NT),
                shift,
                inner[0, :, rows],
            )
            gs16 = gs.astype(bf16)
            gq[j] = gq[j] + dot(keys_t[:, at], gs16)
            bias_grad[rels] += gs
            gk = gk + dot(gs16, query[rows])
            gv = gv + dot(p.astype(bf16), grad[rows, :])
        pair = jnp.concatenate([gk * score_scale, gv], axis=1).astype(bf16)
        sums = sums + dot(pick_t[:, at], pair)
    g_out[0, :, HEAD_DIM:] = sums
    total = jnp.zeros((HEAD_DIM, VOCAB), f32)
    for j in range(blocks):
        rows = slice(WINDOW + j * TILE, WINDOW + (j + 1) * TILE)
        total = total + dot((gq[j] * score_scale).astype(bf16), pick[rows, :])
    g_out[0, :, :HEAD_DIM] = total.T
    rows = jnp.concatenate(
        [bias_grad[...].T, jnp.zeros((TILE, CONTEXT - 3 * TILE), f32)], axis=1
    )
    count = TILE
    while count > 8:
        count //= 2
        rows = rows[:count] + pltpu.roll(rows[count:], CONTEXT - count, 1)
    folded = rows[0:1]
    for r in range(1, 8):
        folded = folded + pltpu.roll(rows, CONTEXT - r, 1)[r : r + 1]
    pieces = []
    left = folded
    for _ in range(3):
        piece = left.astype(bf16)
        pieces.append(piece)
        left = left - piece.astype(f32)
    pieces = jnp.concatenate(pieces + [jnp.zeros((5, CONTEXT), bf16)], axis=0)
    fold_out[0] = jnp.sum(dot(pieces, buckets[...]), axis=0, keepdims=True)


def token_backward(
    live, pick, pick_t, qkv_table, bias_rows, lse, inner, grad, gq, deps=(), half=None, onto=()
):
    low, count = (0, HEADS) if half is None else (half * HEADS // 2, HEADS // 2)
    deps = (*deps, *onto)
    head = lambda k: (lambda h, s: (0, k * HEADS + low + h))
    by_head = lambda *shape: pl.BlockSpec((1,) + shape, lambda h, s: (low + h, 0, 0))
    flat = lambda *shape: pl.BlockSpec(shape, lambda h, s: (0,) * len(shape))
    return pl.pallas_call(
        token_backward_kernel,
        grid_spec=pltpu.PrefetchScalarGridSpec(
            num_scalar_prefetch=1,
            grid=(count,),
            in_specs=[
                flat(CONTEXT, VOCAB),
                flat(VOCAB, CONTEXT),
                pl.BlockSpec((VOCAB, HEAD_DIM), head(0)),
                pl.BlockSpec((VOCAB, HEAD_DIM), head(1)),
                pl.BlockSpec((VOCAB, HEAD_DIM), head(2)),
                by_head(1, CONTEXT),
                by_head(1, WINDOW),
                by_head(1, WINDOW),
                pl.BlockSpec((WINDOW, HEAD_DIM), head(0)),
                by_head(HEAD_DIM, WINDOW),
                flat(CONTEXT, 128),
            ]
            + [pl.BlockSpec(memory_space=pl.ANY)] * len(deps),
            out_specs=[by_head(VOCAB, 384), by_head(1, 128)],
            scratch_shapes=[
                pltpu.VMEM((3 * TILE, TILE), f32),
                pltpu.VMEM((3 * TILE, TILE), f32),
            ],
        ),
        out_shape=[
            jax.ShapeDtypeStruct((HEADS, VOCAB, 384), f32),
            jax.ShapeDtypeStruct((HEADS, 1, 128), f32),
        ],
        input_output_aliases={12 + len(deps) - 2 + i: i for i in range(len(onto))},
        compiler_params=params(),
        cost_estimate=cost(1e3, 1e3),
        name="token_backward",
    )(
        live,
        pick,
        pick_t,
        qkv_table,
        qkv_table,
        qkv_table,
        bias_rows,
        lse,
        inner,
        grad,
        gq,
        jnp.asarray(np.pad(lane_pick().T, ((0, 0), (0, 96))), bf16),
        *deps,
    )


def mlp_kernel(x, cot, up, down, out_in, gx_in, gd_out, gu_out, out, gx, xt):
    @pl.when(pl.program_id(0) == 0)
    def _():
        out[...] = out_in[...]
        gx[...] = gx_in[...]
        xt[...] = x[...].astype(f32).T.astype(bf16)

    up_b = up[...]
    down_b = down[...]
    pre = dot(x[...], up_b)
    root = math.sqrt(2.0 / math.pi)
    square = pre * pre
    t = jnp.tanh(root * pre * (1.0 + 0.044715 * square))
    half = 0.5 * (1.0 + t)
    act = (pre * half).astype(bf16)
    slope = half + (0.5 * root) * pre * (1.0 - t * t) * (1.0 + (3 * 0.044715) * square)
    grad_pre = (dot(cot[...], down_b, NT) * slope).astype(bf16)
    out[...] += dot(act, down_b)
    gx[...] += dot(grad_pre, up_b, NT)
    gd_out[...] = dot(act, cot[...], TN).astype(bf16)
    gu_out[...] = dot(xt[...], grad_pre).astype(bf16)


def mlp_part(part, x, cot, up, down, out, gx):
    count = FF // SPLITS // TILE
    whole = pl.BlockSpec((WINDOW, D), lambda s: (0, 0))
    return pl.pallas_call(
        mlp_kernel,
        grid=(count,),
        in_specs=[
            whole,
            whole,
            pl.BlockSpec((D, TILE), lambda s: (0, SPLITS * s + part)),
            pl.BlockSpec((TILE, D), lambda s: (SPLITS * s + part, 0)),
            whole,
            whole,
        ],
        out_specs=[
            pl.BlockSpec((TILE, D), lambda s: (s, 0)),
            pl.BlockSpec((D, TILE), lambda s: (0, s)),
            whole,
            whole,
        ],
        out_shape=[
            jax.ShapeDtypeStruct((count * TILE, D), bf16),
            jax.ShapeDtypeStruct((D, count * TILE), bf16),
            jax.ShapeDtypeStruct((WINDOW, D), f32),
            jax.ShapeDtypeStruct((WINDOW, D), f32),
        ],
        scratch_shapes=[pltpu.VMEM((D, WINDOW), bf16)],
        compiler_params=params(),
        cost_estimate=cost(1e3, 1e3),
        name="feed_forward",
    )(x, cot, up, down, out, gx)


def mlp_packed_kernel(
    places, x, cot, up_a, up_b, up_c, up_d, down_a, down_b, down_c, down_d, out_in, gx_in,
    *rest,
):
    send, keep, out, gx, xt, xs, gd_s = rest[-7:]
    core = places[CORE]
    step = pl.program_id(0)

    @pl.when(step == 0)
    def _():
        out[...] = out_in[...]
        gx[...] = gx_in[...]
        xt[...] = x[...].astype(f32).T.astype(bf16)
        for z in range(4):
            for slot, parity in ((0, 1 - core), (1, core)):
                at = pl.multiple_of((2 * z + parity) * 128, 128)
                xs[slot, z * 128 : (z + 1) * 128, :] = xt[pl.ds(at, 128), :]

    up = jnp.concatenate([up_a[...], up_b[...], up_c[...], up_d[...]], axis=1)
    down = jnp.concatenate([down_a[...], down_b[...], down_c[...], down_d[...]], axis=0)
    pre = dot(x[...], up)
    root = math.sqrt(2.0 / math.pi)
    square = pre * pre
    t = jnp.tanh(root * pre * (1.0 + 0.044715 * square))
    half = 0.5 * (1.0 + t)
    act = (pre * half).astype(bf16)
    slope = half + (0.5 * root) * pre * (1.0 - t * t) * (1.0 + (3 * 0.044715) * square)
    grad_pre = (dot(cot[...], down, NT) * slope).astype(bf16)
    out[...] += dot(act, down)
    gx[...] += dot(grad_pre, up, NT)
    gd = dot(act, cot[...], TN).astype(bf16)
    for i in range(2):
        for q in range(2):
            at = (2 * i + q) * 128
            gd_s[q, i] = gd[at : at + 128]
    lanes = pl.ds(pl.multiple_of(step * 512, 512), 512)
    for i in range(2):
        z = 2 * step + i
        send[pl.ds(z, 1), :128, :] = gd_s[pl.ds(1 - core, 1), i]
        keep[pl.ds(z, 1), :128, :] = gd_s[pl.ds(core, 1), i]
    for slot, ref in ((0, send), (1, keep)):
        gu = dot(xs[slot], grad_pre).astype(bf16)
        ref[:, 128:, lanes] = gu.reshape(4, 128, 512)


def mlp_packed(part, places, x, cot, up, down, out, gx, deps=()):
    block = pl.BlockSpec((WINDOW, D), lambda g, s: (0, 0))
    packed = pl.BlockSpec((4, 256, D), lambda g, s: (0, 0, 0))
    at = lambda k: (lambda g: (4 * g + k) * 4 + part)
    return pl.pallas_call(
        mlp_packed_kernel,
        grid_spec=pltpu.PrefetchScalarGridSpec(
            num_scalar_prefetch=1,
            grid=(2,),
            in_specs=[block, block]
            + [
                pl.BlockSpec((D, 128), lambda g, s, k=k: (0, at(k)(g)))
                for k in range(4)
            ]
            + [
                pl.BlockSpec((128, D), lambda g, s, k=k: (at(k)(g), 0))
                for k in range(4)
            ]
            + [block, block]
            + [pl.BlockSpec(memory_space=pl.ANY)] * len(deps),
            out_specs=[packed, packed, block, block],
            scratch_shapes=[
                pltpu.VMEM((D, WINDOW), bf16),
                pltpu.VMEM((2, 512, WINDOW), bf16),
                pltpu.VMEM((2, 2, 128, D), bf16),
            ],
        ),
        out_shape=[
            jax.ShapeDtypeStruct((4, 256, D), bf16),
            jax.ShapeDtypeStruct((4, 256, D), bf16),
            jax.ShapeDtypeStruct((WINDOW, D), f32),
            jax.ShapeDtypeStruct((WINDOW, D), f32),
        ],
        compiler_params=params(32),
        cost_estimate=cost(1e3, 1e3),
        name="feed_forward",
    )(places, x, cot, up, up, up, up, down, down, down, down, out, gx, *deps)


def one_block(array):
    return pl.BlockSpec(array.shape, lambda g: (0,) * array.ndim)


def single(kernel, name, ins, outs, scratch=(), deps=()):
    return pl.pallas_call(
        kernel,
        grid=(1,),
        in_specs=[one_block(a) for a in ins]
        + [pl.BlockSpec(memory_space=pl.ANY)] * len(deps),
        out_specs=[one_block(o) for o in outs],
        out_shape=list(outs),
        scratch_shapes=list(scratch),
        compiler_params=params(),
        cost_estimate=cost(1e3, 1e3),
        name=name,
    )(*ins, *deps)


def like(kind, *shape):
    return jax.ShapeDtypeStruct(shape, kind)


def unit_of(value):
    unit, inv = norm_parts(value)
    return unit, jnp.broadcast_to(inv, (value.shape[0], 128))


def table_kernel(table, gain, weight, unit_out, inv_out, normed_out, qkv_out):
    step = pl.program_id(0)

    @pl.when(step == 0)
    def _():
        unit, inv = unit_of(table[...].astype(f32))
        unit_out[...] = unit
        inv_out[...] = inv
        normed_out[...] = (unit * gain[...]).astype(bf16)

    qkv_out[...] = dot(normed_out[...], weight[...]).astype(bf16)


def table_forward(table, gain, weight):
    flat = lambda *shape: pl.BlockSpec(shape, lambda g: (0, 0))
    return pl.pallas_call(
        table_kernel,
        grid=(6,),
        in_specs=[
            flat(VOCAB, D),
            flat(1, D),
            pl.BlockSpec((D, D // 2), lambda g: (0, g)),
        ],
        out_specs=[
            flat(VOCAB, D),
            flat(VOCAB, 128),
            flat(VOCAB, D),
            pl.BlockSpec((VOCAB, D // 2), lambda g: (0, g)),
        ],
        out_shape=[
            like(f32, VOCAB, D),
            like(f32, VOCAB, 128),
            like(bf16, VOCAB, D),
            like(bf16, VOCAB, 3 * D),
        ],
        compiler_params=params(),
        cost_estimate=cost(1e3, 1e3),
        name="table_forward",
    )(table, gain, weight)


def states_forward_kernel(states, gain, weight, unit_out, inv_out, normed_out, kv_out):
    step = pl.program_id(0)

    @pl.when(step == 0)
    def _():
        unit, inv = unit_of(states[...])
        unit_out[...] = unit
        inv_out[...] = inv
        normed_out[...] = (unit * gain[...]).astype(bf16)

    kv_out[...] = dot(normed_out[...], weight[...]).astype(bf16)


def states_forward(states, gain, weight):
    flat = lambda *shape: pl.BlockSpec(shape, lambda g: (0, 0))
    return pl.pallas_call(
        states_forward_kernel,
        grid=(4,),
        in_specs=[
            flat(STATES, D),
            flat(1, D),
            pl.BlockSpec((D, D // 2), lambda g: (0, g)),
        ],
        out_specs=[
            flat(STATES, D),
            flat(STATES, 128),
            flat(STATES, D),
            pl.BlockSpec((STATES, D // 2), lambda g: (0, g)),
        ],
        out_shape=[
            like(f32, STATES, D),
            like(f32, STATES, 128),
            like(bf16, STATES, D),
            like(bf16, STATES, 2 * D),
        ],
        compiler_params=params(),
        cost_estimate=cost(1e3, 1e3),
        name="states_forward",
    )(states, gain, weight)


def residual_kernel(mixed, out_weight, pick, table, gain, res_out, unit_out, inv_out, in_out):
    res = dot(pick[WINDOW:, :], table[...]) + dot(mixed[...], out_weight[...])
    res_out[...] = res
    unit, inv = unit_of(res)
    unit_out[...] = unit
    inv_out[...] = inv
    in_out[...] = (unit * gain[...]).astype(bf16)


def residual_forward(mixed, out_weight, pick, table, gain):
    return single(
        residual_kernel,
        "residual_forward",
        (mixed, out_weight, pick, table, gain),
        (
            like(f32, WINDOW, D),
            like(f32, WINDOW, D),
            like(f32, WINDOW, 128),
            like(bf16, WINDOW, D),
        ),
    )


def feed_back_kernel(
    gx, unit, inv, gain, upstream, mixed, out_weight, pick, *rest
):
    gain_out, out_out, mixed_out, rows_out = rest[-4:]
    g = gx[...]
    u = unit[...]
    gain_out[...] = jnp.sum(g * u, axis=0, keepdims=True)
    back = norm_back(u, inv[:, :1], gain[...], g)
    grad = (upstream[...].astype(f32) + back).astype(bf16)
    mixed_out[...] = dot(grad, out_weight[...], NT).astype(bf16)
    out_out[...] = dot(mixed[...], grad, TN).astype(bf16)
    rows_out[...] = dot(pick[WINDOW:, :], grad, TN).astype(bf16)


def feed_back(v, gx, deps=()):
    return single(
        feed_back_kernel,
        "feed_back",
        (
            gx,
            v.mlp_unit,
            v.mlp_inv,
            v.mlp_gain,
            v.upstream,
            v.mixed,
            v.out_weight,
            v.pick,
        ),
        (like(f32, 1, D), like(bf16, D, D), like(bf16, WINDOW, D), like(bf16, VOCAB, D)),
        deps=deps,
    )


def states_back_kernel(
    gsk, gsv, weight, normed, unit, inv, gain, slope, forget, *rest
):
    k_out, v_out, gain_out, local_out, gate_out = rest[-5:]
    upstream = dot(gsk[...], weight[:, :D], NT) + dot(gsv[...], weight[:, D:], NT)
    u = unit[...]
    gain_out[...] = jnp.sum(upstream * u, axis=0, keepdims=True)
    local = norm_back(u, inv[:, :1], gain[...], upstream)
    local_out[...] = local
    f = forget[...]
    gate_out[...] = jnp.sum(local * slope[...], axis=0, keepdims=True) * f * (1.0 - f)
    k_out[...] = dot(normed[...], gsk[...], TN).astype(bf16)
    v_out[...] = dot(normed[...], gsv[...], TN).astype(bf16)


def states_back(v, gsk, gsv, deps=()):
    return single(
        states_back_kernel,
        "states_back",
        (
            gsk,
            gsv,
            v.state_kv_weight,
            v.state_normed,
            v.state_unit,
            v.state_inv,
            v.state_gain,
            v.forget_slope,
            v.forget,
        ),
        (
            like(bf16, D, D),
            like(bf16, D, D),
            like(f32, 1, D),
            like(f32, STATES, D),
            like(f32, 1, D),
        ),
        deps=deps,
    )


XI, YI, ZI, CORE, DPI, SEQI = range(6)


def permute(value, axis, to):
    size = lax.axis_size(axis)
    return lax.ppermute(value, axis, [(i, to(i)) for i in range(size)])


def swap_core(value):
    return permute(value, "seq", lambda i: i ^ 1)


def swap_dp(value, step):
    return permute(value, "dp", lambda i: i ^ step)


def ahead(value, step):
    return permute(value, "seq", lambda i: (i + 2 * step) % 8)


def fitted():
    return lax.axis_size("seq") == 8 and lax.axis_size("dp") == 4


def whole(array):
    return pl.BlockSpec(array.shape, lambda g, s: (0,) * array.ndim)


def blend(name, places, outs, deps=(), through=()):
    arrays, in_specs, plan, out_specs = [], [], [], []
    for shape, rows, blocks, segments in outs:
        every = 4 // blocks
        rows_of = []
        for sources in segments:
            names = []
            for array, block_rows, place in sources:
                names.append(len(arrays))
                arrays.append(array)
                in_specs.append(
                    pl.BlockSpec(
                        (1, block_rows, array.shape[2]),
                        lambda g, s, place=place, every=every: (*place(g // every, s), 0),
                    )
                )
            rows_of.append((sources[0][1], names))
        plan.append((every, rows_of))
        out_specs.append(
            pl.BlockSpec((1, rows, shape[2]), lambda g, s, every=every: (g // every, 0, 0))
        )
    count = len(arrays)

    def kernel(s, *refs):
        step = pl.program_id(0)
        out_refs = refs[count + len(deps) + len(through) :]

        def fill(out_ref, rows_of):
            at = 0
            for rows, names in rows_of:
                total = refs[names[0]][0].astype(f32)
                for i in names[1:]:
                    total = total + refs[i][0].astype(f32)
                out_ref[0, at : at + rows, :] = total.astype(out_ref.dtype)
                at += rows

        for out_ref, (every, rows_of) in zip(out_refs, plan):
            if every == 1:
                fill(out_ref, rows_of)
            else:
                pl.when(step % every == 0)(functools.partial(fill, out_ref, rows_of))

    return pl.pallas_call(
        kernel,
        grid_spec=pltpu.PrefetchScalarGridSpec(
            num_scalar_prefetch=1,
            grid=(4,),
            in_specs=in_specs
            + [pl.BlockSpec(memory_space=pl.ANY)] * (len(deps) + len(through)),
            out_specs=out_specs + [pl.BlockSpec(memory_space=pl.ANY)] * len(through),
        ),
        out_shape=[jax.ShapeDtypeStruct(shape, bf16) for shape, _, _, _ in outs]
        + [jax.ShapeDtypeStruct(t.shape, t.dtype) for t in through],
        input_output_aliases={
            1 + count + len(deps) + i: len(outs) + i for i in range(len(through))
        },
        compiler_params=params(),
        cost_estimate=cost(1e3, 1e3),
        name=name,
    )(places, *arrays, *deps, *through)


class Wing:
    def __init__(self, lead, kept, came, base, rows):
        self.lead, self.trail = lead, 1 - lead
        self.kept, self.came, self.base = kept, came, base
        self.half, self.quarter = rows // 2, rows // 4
        self.columns = kept.shape[2]
        self.got = []

    def first(self):
        at = self.base // self.half
        other = lambda g, s: (g, at + 1 - s[self.lead])
        return self.half, [(self.kept, self.half, other), (self.came, self.half, other)]

    def second(self):
        q = self.quarter
        at = self.base // q
        array, start = self.got[0]
        start = start // q
        deep = lambda g, s: (g, at + 2 * s[self.lead] + 1 - s[self.trail])
        flat = lambda g, s: (g, start + 1 - s[self.trail])
        return q, [(self.kept, q, deep), (self.came, q, deep), (array, q, flat)]

    def quarters(self, level):
        q = self.quarter
        at = self.base // q
        (one, start_one), (two, start_two) = self.got
        start_one, start_two = start_one // q, start_two // q
        deep = lambda g, s: (level(g, s), at + 2 * s[self.lead] + s[self.trail])
        flat = lambda g, s: (level(g, s), start_one + s[self.trail])
        last = lambda g, s: (level(g, s), start_two)
        return [(self.kept, q, deep), (self.came, q, deep), (one, q, flat), (two, q, last)]


def wings(kept, came):
    half = kept.shape[1] // 2
    return [Wing(XI, kept, came, 0, half), Wing(YI, kept, came, half, half)]


class Column:
    def __init__(self, parts):
        self.parts = parts
        self.rows = sum(w.quarter for w in parts)
        self.columns = parts[0].columns

    def near(self):
        outs = []
        for own in (False, True):
            level = (
                (lambda g, s: 2 * g + s[ZI] % 2)
                if own
                else (lambda g, s: 2 * g + 1 - s[ZI] % 2)
            )
            segments = [w.quarters(level) for w in self.parts]
            outs.append(((2, self.rows, self.columns), self.rows, 2, segments))
        return outs

    def rest(self, pick, extra=()):
        sources = [
            (array, self.rows, lambda g, s: (pick(s), 0))
            for array in (self.kept, self.from_near)
        ] + [(array, self.rows, lambda g, s: (0, 0)) for array in extra]
        return [((1, self.rows, self.columns), self.rows, 1, [sources])]

    def far(self):
        return self.rest(lambda s: 1 - s[ZI] // 2)

    def close(self):
        return self.rest(lambda s: s[ZI] // 2, [self.from_far])


class Traffic:
    def __init__(self, places):
        self.places = places
        self.pending = []

    def swap(self, send):
        came = swap_core(send)
        self.pending.append(came)
        return came

    def boundary(self, after, first=(), second=(), near=(), far=(), close=(), swap=()):
        outs, sent = [], []
        for axis in (XI, YI):
            groups = {}
            for w in first:
                if w.lead == axis:
                    groups.setdefault(w.columns, []).append((w, w.first()))
            for w in second:
                if w.trail == axis:
                    groups.setdefault(w.columns, []).append((w, w.second()))
            for columns, moves in groups.items():
                moves.sort(key=lambda m: -m[1][0])
                rows = sum(m[1][0] for m in moves)
                outs.append(
                    ((4, rows, columns), rows, 4, [m[1][1] for m in moves])
                )
                sent.append((axis, moves))
        for columns, step in ((near, Column.near), (far, Column.far), (close, Column.close)):
            for c in columns:
                outs += step(c)
        results = blend("boundary", self.places, outs, (*after, *self.pending), swap)
        self.pending = []
        mark = results[0]
        results = list(results)
        for axis, moves in sent:
            came = swap_dp(results.pop(0), 1 << axis)
            self.pending.append(came)
            at = 0
            for w, (rows, _) in moves:
                assert at % w.quarter == 0
                w.got.append((came, at))
                at += rows
        for c in near:
            c.from_near = permute(results.pop(0), "seq", lambda i: i ^ 2)
            c.kept = results.pop(0)
            self.pending.append(c.from_near)
        for c in far:
            c.from_far = permute(results.pop(0), "seq", lambda i: i ^ 4)
            self.pending.append(c.from_far)
        for c in close:
            c.own = results.pop(0)
        self.swapped = [self.swap(send) for send in results]
        return mark

    def spread(self, own, lead=1):
        beside = swap_dp(own, lead)
        other = swap_dp(own, 3 - lead)
        rows = [own, beside, other, swap_dp(beside, 3 - lead)]
        self.pending += rows[1:]
        return rows if lead == 1 else [own, other, beside, rows[3]]


def packed_pair(name, places, pieces, deps=()):
    rows = sum(p.shape[1] for p in pieces)
    columns = pieces[0].shape[2]
    outs = []
    for keep in (False, True):
        place = (
            (lambda g, s: (2 * g + s[CORE], 0))
            if keep
            else (lambda g, s: (2 * g + 1 - s[CORE], 0))
        )
        outs.append(
            ((4, rows, columns), rows, 4, [[(p, p.shape[1], place)] for p in pieces])
        )
    return blend(name, places, outs, deps)


def pack_rows(places, mark, g_tokens, g, rows_sum, *vectors):
    count = 3 + len(vectors)

    def kernel(s, *refs):
        for out_ref, (a, b, r, *rows) in zip(
            refs[2 * count + 1 :], (refs[:count], refs[count : 2 * count])
        ):
            out_ref[0, :VOCAB, :] = (a[0] + b[0].astype(f32)).astype(bf16)
            out_ref[0, VOCAB:, :128] = r[:128, :]
            out_ref[0, VOCAB:, 128:256] = r[128:, :]
            place = lax.broadcasted_iota(jnp.int32, (128, 128), 0)
            small = jnp.zeros((128, 128), f32)
            for i, row in enumerate(rows):
                value = row[...] if len(row.shape) == 2 else row[0]
                small = jnp.where(place == i, value, small)
            out_ref[0, VOCAB:, 256:] = small.astype(bf16)

    specs, arrays = [], []
    for keep in (False, True):
        at = (
            (lambda i, s: 2 * i + s[CORE]) if keep else (lambda i, s: 2 * i + 1 - s[CORE])
        )
        for array in (g_tokens, g, rows_sum, *vectors):
            arrays.append(array)
            if array.ndim == 2:
                specs.append(
                    pl.BlockSpec((array.shape[0], 128), lambda i, s, at=at: (0, at(i, s)))
                )
            else:
                specs.append(
                    pl.BlockSpec(
                        (1,) + array.shape[1:], lambda i, s, at=at: (at(i, s), 0, 0)
                    )
                )
    return pl.pallas_call(
        kernel,
        grid_spec=pltpu.PrefetchScalarGridSpec(
            num_scalar_prefetch=1,
            grid=(4,),
            in_specs=specs + [pl.BlockSpec(memory_space=pl.ANY)],
            out_specs=[pl.BlockSpec((1, 384, 384), lambda i, s: (i, 0, 0))] * 2,
        ),
        out_shape=[like(bf16, 4, 384, 384)] * 2,
        compiler_params=params(),
        cost_estimate=cost(1e3, 1e3),
        name="pack_rows",
    )(places, *arrays, mark)


def slot_of(s, step, lead):
    there = s[DPI] ^ step
    x, y = there % 2, there // 2
    return 2 * x + y if lead == XI else 2 * y + x


def unpack(name, places, quarters, pieces, outs):
    columns = quarters[0].shape[2]
    total = 4 * sum(p[1] for p in pieces)

    def kernel(s, *refs):
        scratch = refs[-1]
        for step in range(4):
            for start, rows, lead, base in pieces:
                at = pl.multiple_of(slot_of(s, step, lead) * rows + base, 16)
                scratch[pl.ds(at, rows), :] = refs[step][0, start : start + rows, :].astype(
                    f32
                )
        for out_ref, (_, moves) in zip(refs[4:-1], outs):
            for row, rows, to, column in moves:
                out_ref[to : to + rows, column : column + columns] = scratch[
                    row : row + rows, :
                ]

    return pl.pallas_call(
        kernel,
        grid_spec=pltpu.PrefetchScalarGridSpec(
            num_scalar_prefetch=1,
            grid=(1,),
            in_specs=[whole(q) for q in quarters],
            out_specs=[
                pl.BlockSpec(shape, lambda g, s: (0, 0)) for shape, _ in outs
            ],
            scratch_shapes=[pltpu.VMEM((total, columns), f32)],
        ),
        out_shape=[jax.ShapeDtypeStruct(shape, f32) for shape, _ in outs],
        compiler_params=params(),
        cost_estimate=cost(1e3, 1e3),
        name=name,
    )(places, *quarters)


def unpack_mlp(places, quarters):
    def kernel(s, *refs):
        down, up, scratch = refs[8:]
        for pair in range(2):
            for step in range(4):
                block = refs[4 * pair + step]
                for part in range(2):
                    for lead in range(2):
                        at = pl.multiple_of(slot_of(s, step, lead) * 32 + 128 * lead, 32)
                        start = part * 64 + lead * 32
                        scratch[2 * pair + part, pl.ds(at, 32), :] = block[
                            0, start : start + 32, :
                        ].astype(f32)
        for part in range(4):
            down[part * 128 : (part + 1) * 128, :] = scratch[part, :128, :]
            for block in range(8):
                at = (4 * block + part) * 128
                up[:, at : at + 128] = scratch[part, 128:, block * 128 : (block + 1) * 128]

    flat = [q for pair in quarters for q in pair]
    return pl.pallas_call(
        kernel,
        grid_spec=pltpu.PrefetchScalarGridSpec(
            num_scalar_prefetch=1,
            grid=(1,),
            in_specs=[whole(q) for q in flat],
            out_specs=[
                pl.BlockSpec((512, D), lambda g, s: (0, 0)),
                pl.BlockSpec((128, FF), lambda g, s: (0, 0)),
            ],
            scratch_shapes=[pltpu.VMEM((4, 256, D), f32)],
        ),
        out_shape=[
            jax.ShapeDtypeStruct((512, D), f32),
            jax.ShapeDtypeStruct((128, FF), f32),
        ],
        compiler_params=params(),
        cost_estimate=cost(1e3, 1e3),
        name="unpack_mlp",
    )(places, *flat)


def ring_rows(places, parts, deps=()):
    def kernel(s, *refs):
        out = refs[-1]
        for k in range(4):
            out[pl.ds(s[ZI] ^ k, 1)] = refs[k][...]

    shape = (4,) + parts[0].shape[1:]
    return pl.pallas_call(
        kernel,
        grid_spec=pltpu.PrefetchScalarGridSpec(
            num_scalar_prefetch=1,
            grid=(1,),
            in_specs=[whole(p) for p in parts]
            + [pl.BlockSpec(memory_space=pl.ANY)] * len(deps),
            out_specs=pl.BlockSpec(shape, lambda g, s: (0, 0, 0)),
        ),
        out_shape=jax.ShapeDtypeStruct(shape, bf16),
        compiler_params=params(),
        cost_estimate=cost(1e3, 1e3),
        name="ring_rows",
    )(places, *parts, *deps)


def stack_rows(places, parts):
    _, rows, columns = parts[0].shape
    rows //= 2

    def kernel(s, *refs):
        out = refs[-1]
        for step in range(4):
            for lead in range(2):
                at = pl.multiple_of(slot_of(s, step, lead) * rows + 4 * rows * lead, 16)
                out[:, pl.ds(at, rows), :] = refs[step][:, lead * rows : (lead + 1) * rows, :]

    shape = (4, 8 * rows, columns)
    return pl.pallas_call(
        kernel,
        grid_spec=pltpu.PrefetchScalarGridSpec(
            num_scalar_prefetch=1,
            grid=(1,),
            in_specs=[whole(p) for p in parts],
            out_specs=pl.BlockSpec(shape, lambda g, s: (0, 0, 0)),
        ),
        out_shape=jax.ShapeDtypeStruct(shape, bf16),
        compiler_params=params(),
        cost_estimate=cost(1e3, 1e3),
        name="stack_rows",
    )(places, *parts)


def last_kernel(
    s, mine, other, norm_cols, unit_cols, weight, weight_rows, unit, inv, gain,
    qkv_out, gain_out, table_out, small_out, by_head,
):
    for z in range(4):
        for q in range(2):
            by_head[2 * z + q] = jnp.where(s[CORE] == q, mine[z], other[z])
    small_out[...] = mine[s[ZI], 256:272, 256:].astype(f32)[:8]
    at = pl.multiple_of(s[SEQI] * 32, 32)
    norm = norm_cols[...]
    cols_grad = jnp.zeros((VOCAB, 128), f32)
    normed_grad = jnp.zeros((32, D), f32)
    for h in range(HEADS):
        for t in range(3):
            lanes = slice(t * 128, (t + 1) * 128)
            to = slice(t * D + h * 128, t * D + (h + 1) * 128)
            g = by_head[h, :VOCAB, lanes]
            qkv_out[:, to] = dot(norm, g, TN)
            cols_grad = cols_grad + dot(g, weight_rows[:, to], NT)
            normed_grad = normed_grad + dot(
                by_head[h, pl.ds(at, 32), lanes], weight[:, to], NT
            )
    gain_out[...] = jnp.sum(cols_grad * unit_cols[...], axis=0, keepdims=True)
    u = unit[...]
    scaled = normed_grad * gain[...]
    a = jnp.mean(scaled, axis=-1, keepdims=True)
    b = jnp.mean(scaled * u, axis=-1, keepdims=True)
    low = pl.multiple_of(VOCAB + (s[SEQI] % 4) * 32, 32)
    rows_sum = [
        jnp.where(
            s[SEQI] < 4,
            by_head[h, pl.ds(low, 32), :128].astype(f32),
            by_head[h, pl.ds(low, 32), 128:256].astype(f32),
        )
        for h in range(HEADS)
    ]
    table_out[...] = (
        jnp.concatenate(rows_sum, axis=1) + (scaled - a - u * b) * inv[:, :1]
    )


def last_products(places, mine, other, normed, unit, weight, inv, gain):
    return pl.pallas_call(
        last_kernel,
        grid_spec=pltpu.PrefetchScalarGridSpec(
            num_scalar_prefetch=1,
            grid=(1,),
            in_specs=[
                whole(mine),
                whole(other),
                pl.BlockSpec((VOCAB, 128), lambda g, s: (0, s[SEQI])),
                pl.BlockSpec((VOCAB, 128), lambda g, s: (0, s[SEQI])),
                whole(weight),
                pl.BlockSpec((128, 3 * D), lambda g, s: (s[SEQI], 0)),
                pl.BlockSpec((32, D), lambda g, s: (s[SEQI], 0)),
                pl.BlockSpec((32, 128), lambda g, s: (s[SEQI], 0)),
                whole(gain),
            ],
            out_specs=[
                pl.BlockSpec((128, 3 * D), lambda g, s: (0, 0)),
                pl.BlockSpec((1, 128), lambda g, s: (0, 0)),
                pl.BlockSpec((32, D), lambda g, s: (0, 0)),
                pl.BlockSpec((8, 128), lambda g, s: (0, 0)),
            ],
            scratch_shapes=[pltpu.VMEM((HEADS, 384, 384), bf16)],
        ),
        out_shape=[
            jax.ShapeDtypeStruct((128, 3 * D), f32),
            jax.ShapeDtypeStruct((1, 128), f32),
            jax.ShapeDtypeStruct((32, D), f32),
            jax.ShapeDtypeStruct((8, 128), f32),
        ],
        compiler_params=params(),
        cost_estimate=cost(1e3, 1e3),
        name="last_products",
    )(places, mine, other, normed, unit, weight, weight, unit, inv, gain)


def total_of(value):
    flat = value.reshape((-1,) + value.shape[2:])
    own = lax.psum_scatter(flat, "seq", scatter_dimension=0, tiled=True)
    return lax.psum(own, "dp").astype(f32)


def places_of():
    here = lax.axis_index("seq")
    dp = lax.axis_index("dp")
    return jnp.stack([dp % 2, dp // 2, here // 2, here % 2, dp, here]).astype(jnp.int32)


def prepare_kernel(
    places, blocks_a, blocks_b, gate, bias, picks, mask, *rest
):
    span, live, counts, rows, pick, pick_t, forget, bias_out = rest[-8:]
    here = places[SEQI]
    sign = lax.broadcasted_iota(jnp.int32, (VOCAB, 128), 0)
    first = jnp.zeros((1, 128), f32)
    before = jnp.zeros((4, 128), jnp.int32)
    for k in range(8):
        block = blocks_a[k] if k < 4 else blocks_b[k - 4]
        w = here ^ k
        total = jnp.zeros((VOCAB, 128), f32)
        for r in range(4):
            total = total + jnp.where(block[r : r + 1] == sign, 1.0, 0.0)
        count = jnp.broadcast_to(jnp.sum(total, axis=1, keepdims=True), (VOCAB, 128))
        counts[pl.ds(w, 1)] = count[None]
        rows[pl.ds(w, 1)] = count.T[:1][None]
        marked = jnp.where(block[4:5] > 0, w.astype(f32), 0.0)
        first = jnp.maximum(first, jnp.where(w <= here, marked, 0.0))
        before = jnp.where(w == here - 1, block[:4], before)
    span[0] = jnp.max(first).astype(jnp.int32)
    span[1] = here
    live[0] = 1 - jnp.max(blocks_a[0, 4:5].astype(f32)).astype(jnp.int32)
    own = blocks_a[0, :4]
    for r in range(8):
        ids = before[r : r + 1] if r < 4 else own[r - 4 : r - 3]
        one = jnp.where(ids == sign, 1.0, 0.0)
        pick_t[:, r * 128 : (r + 1) * 128] = one.astype(bf16)
        pick[r * 128 : (r + 1) * 128, :] = one.T.astype(bf16)
    forget[...] = 1.0 / (1.0 + jnp.exp(-gate[...]))
    table = lax.dot_general(
        bias[...], picks[...], NN, precision=lax.Precision.HIGHEST, preferred_element_type=f32
    )
    table = table * log2e + mask[...]
    for h in range(HEADS):
        bias_out[h] = table[h : h + 1]


def prepare(places, char_ids, seg_starts, gate_logit, distance_bias, deps=()):
    packed = jnp.concatenate(
        [
            char_ids.reshape(4, 128),
            jnp.broadcast_to(seg_starts, (1, 128)),
            jnp.zeros((3, 128), jnp.int32),
        ],
        axis=0,
    )[None]
    for bit in (1, 2):
        packed = jnp.concatenate(
            [packed, permute(packed, "seq", lambda i, bit=bit: i ^ bit)], axis=0
        )
    beyond = permute(packed, "seq", lambda i: i ^ 4)
    ins = (
        packed,
        beyond,
        gate_logit.reshape(1, D),
        distance_bias.reshape(HEADS, BUCKETS),
        jnp.asarray(lane_pick()),
        jnp.asarray(lane_hidden()),
    )
    outs = (
        like(jnp.int32, 2),
        like(jnp.int32, 1),
        like(f32, 8, VOCAB, 128),
        like(f32, 8, 1, VOCAB),
        like(bf16, CONTEXT, VOCAB),
        like(bf16, VOCAB, CONTEXT),
        like(f32, 1, D),
        like(f32, HEADS, 1, CONTEXT),
    )
    return pl.pallas_call(
        prepare_kernel,
        grid_spec=pltpu.PrefetchScalarGridSpec(
            num_scalar_prefetch=1,
            grid=(1,),
            in_specs=[whole(a) for a in ins]
            + [pl.BlockSpec(memory_space=pl.ANY)] * len(deps),
            out_specs=[pl.BlockSpec(memory_space=pltpu.SMEM)] * 2
            + [whole(o) for o in outs[2:]],
        ),
        out_shape=list(outs),
        compiler_params=params(),
        cost_estimate=cost(1e3, 1e3),
        name="prepare",
    )(places, *ins, *deps)


def plain_prepare(char_ids, seg_starts, gate_logit, distance_bias):
    windows = lax.axis_size("seq")
    here = lax.axis_index("seq")
    packed = jnp.concatenate(
        [char_ids.reshape(4, 128), jnp.broadcast_to(seg_starts, (1, 128))], axis=0
    )
    everyone = lax.all_gather(packed, "seq")
    ids_all = everyone[:, :4].reshape(windows, WINDOW)
    flags = everyone[:, 4, 0]
    order = jnp.arange(windows, dtype=jnp.int32)
    first = jnp.max(jnp.where((flags > 0) & (order <= here), order, 0))
    span = jnp.stack([first, here]).astype(jnp.int32)
    live = (1 - seg_starts.reshape(1)).astype(jnp.int32)
    vocab = jnp.arange(VOCAB, dtype=jnp.int32)
    counts = jnp.sum(
        (ids_all[:, :, None] == vocab[None, None, :]).astype(f32), axis=1
    )
    before = lax.dynamic_index_in_dim(ids_all, jnp.maximum(here - 1, 0), 0, False)
    context_ids = jnp.concatenate([before, char_ids.reshape(-1)])
    bias_rows = jnp.dot(
        distance_bias.reshape(HEADS, BUCKETS),
        jnp.asarray(lane_pick()),
        precision=lax.Precision.HIGHEST,
    ) * log2e + jnp.asarray(lane_hidden())
    return (
        span,
        live,
        jnp.broadcast_to(counts[:, :, None], (windows, VOCAB, 128)),
        counts[:, None, :],
        (context_ids[:, None] == vocab[None, :]).astype(bf16),
        (vocab[:, None] == context_ids[None, :]).astype(bf16),
        jax.nn.sigmoid(gate_logit).reshape(1, D),
        bias_rows.reshape(HEADS, 1, CONTEXT),
    )


def body(
    char_ids,
    seg_starts,
    char_table,
    norm_gain,
    qkv_weight,
    distance_bias,
    state_query,
    state_init,
    state_gain,
    state_kv_weight,
    gate_logit,
    out_weight,
    mlp_gain,
    up_weight,
    down_weight,
    cotangent,
):
    windows = lax.axis_size("seq")
    here = lax.axis_index("seq")
    norm_gain, state_gain, mlp_gain = (
        t.reshape(1, D) for t in (norm_gain, state_gain, mlp_gain)
    )
    table_unit, table_inv, normed_table, qkv_table = table_forward(
        char_table, norm_gain, qkv_weight
    )

    characters = (char_ids, seg_starts, gate_logit, distance_bias)
    if fitted():
        places = places_of()
        prepared = prepare(places, *characters, (qkv_table,))
    else:
        prepared = plain_prepare(*characters)
    span, live, counts, count_rows, pick, pick_t, forget, bias_rows = prepared
    states_in, forget_slope, lowest = summary_forward(
        span, state_query, qkv_table, counts, count_rows, state_init, forget
    )
    state_unit, state_inv, state_normed, state_kv = states_forward(
        states_in, state_gain, state_kv_weight
    )
    mixed, lse = attention_forward(
        live, pick, pick_t, qkv_table, state_kv, state_kv, bias_rows
    )
    residual, mlp_unit, mlp_inv, mlp_in = residual_forward(
        mixed, out_weight, pick, char_table, mlp_gain
    )
    upstream = cotangent.reshape(WINDOW, D)

    close_up = fitted_tail if fitted() else plain_tail
    return close_up(dict(locals()))


def fitted_tail(values):
    v = types.SimpleNamespace(**values)
    places = v.places
    weights = (v.upstream, v.up_weight, v.down_weight)

    out, gx = v.residual, jnp.zeros((WINDOW, D), f32)
    traffic = Traffic(places)
    parts, deps = [], ()
    for part in range(4):
        send, keep, out, gx = mlp_packed(
            part, places, v.mlp_in, *weights, out, gx, deps
        )
        if part:
            second = parts[part - 2] if part > 1 else ()
            mark = traffic.boundary((gx,), parts[part - 1], second, swap=[send])
            deps = (mark,)
            came = traffic.swapped[0]
        else:
            came = traffic.swap(send)
        parts.append(wings(keep, came))
    layer_out = out.astype(bf16).reshape(1, WINDOW, D)
    front = Column(parts[0] + parts[1])
    back = Column(parts[2] + parts[3])

    grad_mlp_gain, grad_out, grad_mixed, rows_sum = feed_back(v, gx, (mark,))
    gsk, gsv, gq, inner = state_backward(
        v.pick, v.qkv_table, v.state_kv, v.lse, v.mixed, grad_mixed
    )
    mark = traffic.boundary((gsk,), parts[3], parts[2], near=[front])
    grad_k, grad_v, grad_state_gain, local, grad_gate = states_back(v, gsk, gsv, (mark,))
    send, keep = packed_pair(
        "pack_middle",
        places,
        [t.reshape(8, 128, D) for t in (grad_k, grad_v, grad_out)],
    )
    middle = wings(keep, traffic.swap(send))
    g, gsq, ginit = summary_backward(
        v.span, v.state_query, v.qkv_table, v.counts, v.count_rows, local, v.forget,
        v.lowest, (send,),
    )
    mark = traffic.boundary((g,), middle, parts[3], far=[front])
    send, keep = packed_pair(
        "pack_states", places, [gsq.reshape(8, 64, D), ginit.reshape(8, 64, D)], (mark,)
    )
    states = wings(keep, traffic.swap(send))
    tokens_args = (
        v.live, v.pick, v.pick_t, v.qkv_table, v.bias_rows, v.lse, inner, grad_mixed, gq
    )
    onto = token_backward(*tokens_args, (send,), 0)
    mark = traffic.boundary((onto[1],), states, middle, near=[back], close=[front])
    g_tokens, fold = token_backward(*tokens_args, (mark,), 1, onto)
    mark = traffic.boundary((fold,), (), states, far=[back])
    front_rows = traffic.spread(front.own)
    send, keep = pack_rows(
        places, mark, g_tokens, g, rows_sum, grad_mlp_gain, grad_state_gain, grad_gate, fold
    )
    rows = wings(keep, traffic.swap(send))
    side = Column(middle + states)
    last = Column(rows)
    traffic.boundary((), rows, near=[side], close=[back])
    traffic.boundary((), (), rows, far=[side])
    back_rows = traffic.spread(back.own, 2)
    traffic.boundary((), near=[last], close=[side])
    traffic.boundary((), far=[last])
    side_rows = traffic.spread(side.own)
    traffic.boundary((), close=[last])
    beside = permute(last.own, "seq", lambda i: i ^ 2)
    row_ring = [
        last.own,
        beside,
        permute(last.own, "seq", lambda i: i ^ 4),
        permute(beside, "seq", lambda i: i ^ 4),
    ]
    ring = ring_rows(places, row_ring)
    ring_parts = traffic.spread(ring)
    mine = stack_rows(places, ring_parts)
    other = swap_core(mine)
    grad_down, grad_up = unpack_mlp(places, [front_rows, back_rows])
    grad_state_kv, grad_out, grad_state_query, grad_state_init = unpack(
        "unpack_side",
        places,
        side_rows,
        [(0, 48, XI, 0), (48, 48, YI, 192), (96, 16, XI, 384), (112, 16, YI, 448)],
        [
            ((128, 2 * D), [(0, 128, 0, 0), (128, 128, 0, D)]),
            ((128, D), [(256, 128, 0, 0)]),
            ((64, D), [(384, 64, 0, 0)]),
            ((64, D), [(448, 64, 0, 0)]),
        ],
    )
    grad_qkv, grad_norm_gain, grad_table, small = last_products(
        places,
        mine,
        other,
        v.normed_table,
        v.table_unit,
        v.qkv_weight,
        v.table_inv,
        v.norm_gain,
    )
    return (
        layer_out,
        grad_table,
        grad_norm_gain.reshape(-1),
        grad_qkv,
        small[3, :32],
        grad_state_query,
        grad_state_init,
        small[1],
        grad_state_kv,
        small[2],
        grad_out,
        small[0],
        grad_up,
        grad_down,
    )


def plain_tail(values):
    v = types.SimpleNamespace(**values)
    windows, here = v.windows, v.here
    shard = lambda n: n // windows
    out, gx = v.residual, jnp.zeros((WINDOW, D), f32)
    grads_down, grads_up = [], []
    for part in range(SPLITS):
        gd, gu, out, gx = mlp_part(
            part, v.mlp_in, v.upstream, v.up_weight, v.down_weight, out, gx
        )
        grads_down.append(gd)
        grads_up.append(gu)
    layer_out = out.astype(bf16).reshape(1, WINDOW, D)
    grad_mlp_gain, grad_out, grad_mixed, rows_sum = feed_back(v, gx)
    gsk, gsv, gq, inner = state_backward(
        v.pick, v.qkv_table, v.state_kv, v.lse, v.mixed, grad_mixed
    )
    grad_k, grad_v, grad_state_gain, local, grad_gate = states_back(v, gsk, gsv)
    g, gsq, ginit = summary_backward(
        v.span, v.state_query, v.qkv_table, v.counts, v.count_rows, local, v.forget,
        v.lowest,
    )
    g_tokens, fold = token_backward(
        v.live, v.pick, v.pick_t, v.qkv_table, v.bias_rows, v.lse, inner, grad_mixed, gq
    )
    g = (g.astype(f32) + g_tokens).astype(bf16)
    sharded = lambda t: total_of(t.reshape(windows, -1, t.shape[-1]))
    full = jnp.stack([t.reshape(-1, TILE, D) for t in grads_down], axis=1)
    grad_down = sharded(full.reshape(FF, D))
    full = jnp.stack([t.reshape(D, -1, TILE) for t in grads_up], axis=2)
    grad_up = sharded(full.reshape(D, FF))
    grad_state_kv = sharded(jnp.concatenate([grad_k, grad_v], axis=1))
    small = jnp.concatenate(
        [
            t.reshape(windows, -1)
            for t in (grad_mlp_gain, grad_state_gain, grad_gate, fold[:, 0, :BUCKETS])
        ],
        axis=1,
    )
    small = total_of(small[:, None, :])[0]
    cut = shard(D)
    all_rows = lax.psum(g, ("dp", "seq"))
    grad_rows = jnp.concatenate(
        [
            all_rows[:, :, t * 128 : (t + 1) * 128].transpose(1, 0, 2).reshape(VOCAB, D)
            for t in range(3)
        ],
        axis=1,
    )
    mine = lax.dynamic_slice_in_dim(v.normed_table, here * cut, cut, 1)
    weight_rows = lax.dynamic_slice_in_dim(v.qkv_weight, here * cut, cut, 0)
    unit_cols = lax.dynamic_slice_in_dim(v.table_unit, here * cut, cut, 1)
    at = here * shard(VOCAB)
    take = lambda t: lax.dynamic_slice_in_dim(t, at, shard(VOCAB), 0)
    grad_table = sharded(rows_sum) + norm_back(
        take(v.table_unit),
        take(v.table_inv)[:, :1],
        v.norm_gain,
        dot(take(grad_rows), v.qkv_weight, NT),
    )
    return (
        layer_out,
        grad_table,
        jnp.sum(dot(grad_rows, weight_rows, NT) * unit_cols, axis=0),
        dot(mine, grad_rows, TN),
        small[3 * cut :],
        sharded(gsq),
        sharded(ginit),
        small[cut : 2 * cut],
        grad_state_kv,
        small[2 * cut : 3 * cut],
        sharded(grad_out),
        small[:cut],
        grad_up,
        grad_down,
    )


def solution(mesh):
    placed = (P("dp", "seq"), P("dp", "seq")) + (P(),) * 13 + (P("dp", "seq", None),)
    return jax.shard_map(
        body,
        mesh=mesh,
        in_specs=placed,
        out_specs=(
            P("dp", "seq", None),
            P("seq", None),
            P("seq"),
            P("seq", None),
            P("seq"),
            P("seq", None),
            P("seq", None),
            P("seq"),
            P("seq", None),
            P("seq"),
            P("seq", None),
            P("seq"),
            P("seq", None),
            P("seq", None),
        ),
        check_vma=False,
    )
```

```python
import functools
import math
import types

import jax
import jax.numpy as jnp
import numpy as np
from jax import lax
from jax.experimental import pallas as pl
from jax.experimental.pallas import tpu as pltpu
from jax.sharding import PartitionSpec as P

D = 1024
HEADS = 8
HEAD_DIM = 128
FF = 4096
VOCAB = 256
STATES = 512
WINDOW = 512
BUCKETS = 32
MAX_DISTANCE = 128
CONTEXT = 2 * WINDOW
TILE = 256
SPLITS = 2

epsilon = 1e-05
hidden = -1e30
log2e = math.log2(math.e)
score_scale = 1.0 / math.sqrt(HEAD_DIM)
f32 = jnp.float32
bf16 = jnp.bfloat16

NN = (((1,), (0,)), ((), ()))
NT = (((1,), (1,)), ((), ()))
TN = (((0,), (0,)), ((), ()))


def dot(a, b, dims=NN):
    return lax.dot_general(a, b, dims, preferred_element_type=f32)


def params(mib=26):
    return pltpu.CompilerParams(
        dimension_semantics=("arbitrary",), vmem_limit_bytes=mib * 1024 * 1024
    )


def cost(flops, moved, exps=0):
    return pl.CostEstimate(
        flops=int(flops), bytes_accessed=int(moved), transcendentals=int(exps)
    )


def norm_parts(value):
    centre = jnp.mean(value, axis=-1, keepdims=True)
    offset = value - centre
    spread = jnp.mean(offset * offset, axis=-1, keepdims=True)
    inv = lax.rsqrt(spread + epsilon)
    return offset * inv, inv


def norm_back(unit, inv, gain, upstream):
    scaled = upstream * gain
    a = jnp.mean(scaled, axis=-1, keepdims=True)
    b = jnp.mean(scaled * unit, axis=-1, keepdims=True)
    return (scaled - a - unit * b) * inv


def bucket_table():
    distance = np.arange(WINDOW)
    exact_count = BUCKETS // 2
    log_ratio = np.log(np.maximum(distance, 1) / exact_count) / math.log(
        MAX_DISTANCE / exact_count
    )
    far_bucket = exact_count + np.floor(log_ratio * (BUCKETS - exact_count)).astype(
        np.int64
    )
    return np.where(
        distance < exact_count, distance, np.minimum(far_bucket, BUCKETS - 1)
    )


def lane_pick():
    pick = np.zeros((BUCKETS, CONTEXT), np.float32)
    table = bucket_table()
    for m in range(1, WINDOW + 1):
        pick[table[WINDOW - m], m] = 1.0
    return pick


def lane_hidden():
    m = np.arange(CONTEXT)
    return np.where((m >= 1) & (m <= WINDOW), 0.0, hidden).astype(np.float32)[None]


smallest_sum = 2.0**-80


def shared_exp(lg, there):
    peak = jnp.max(jnp.where(there > 0, lg, hidden), axis=1, keepdims=True)
    return jnp.exp2(jnp.minimum(lg - peak, 0.0)).astype(bf16)


def window_sides(v, n):
    return jnp.concatenate([v.astype(f32) * n, n], axis=1).astype(bf16)


def own_weights(lg, n_row):
    x = lg + jnp.where(n_row > 0, jnp.log2(jnp.maximum(n_row, 1.0)), hidden)
    p = jnp.exp2(x - jnp.max(x, axis=1, keepdims=True))
    return p / jnp.sum(p, axis=1, keepdims=True)


def characters_there(span, rows):
    return lax.fori_loop(
        span[0], span[1], lambda w, t: t + rows[w], jnp.zeros((1, VOCAB), f32)
    )


TOGETHER = 4


def lanes_of(i):
    return slice(i * HEAD_DIM, (i + 1) * HEAD_DIM)


def summary_forward_kernel(
    span, sq, kt, vt, counts, rows, init, forget, state_out, y_out, low_out, a_s, y_s
):
    heads = range(TOGETHER)
    f = forget[...]
    v = [vt[:, lanes_of(i)] for i in heads]

    def scores(i):
        return dot(sq[:, lanes_of(i)], kt[:, lanes_of(i)], NT) * (score_scale * log2e)

    def begin():
        a_s[...] = init[...].astype(f32)
        y_s[...] = jnp.zeros_like(y_s)

    def move(i, u):
        at = lanes_of(i)
        a = a_s[:, at]
        y_s[:, at] = a - u + f[:, at] * y_s[:, at]
        a_s[:, at] = u + f[:, at] * (a - u)

    begin()
    there = characters_there(span, rows)
    e = [shared_exp(scores(i), there) for i in heads]

    def step(w, low):
        n = counts[w]
        for i in heads:
            both = dot(e[i], window_sides(v[i], n))
            z = both[:, HEAD_DIM:]
            move(i, both[:, :HEAD_DIM] / jnp.maximum(z, smallest_sum))
            low = jnp.minimum(low, jnp.min(z.reshape(STATES // 8, 8, 128), axis=0))
        return low

    low = lax.fori_loop(span[0], span[1], step, jnp.full((8, 128), 1.0, f32))
    low_out[0] = low

    @pl.when(jnp.min(low) < smallest_sum)
    def _():
        begin()
        for i in heads:
            lg = scores(i)

            def slow(w, _):
                move(i, dot(own_weights(lg, rows[w]).astype(bf16), v[i]))
                return 0

            lax.fori_loop(span[0], span[1], slow, 0)

    state_out[...] = a_s[...]
    y_out[...] = y_s[...]


def summary_specs(windows):
    wide = TOGETHER * HEAD_DIM
    head = lambda k: (lambda h, s: (0, k * HEADS // TOGETHER + h))
    return [
        pl.BlockSpec((STATES, wide), head(0)),
        pl.BlockSpec((VOCAB, wide), head(1)),
        pl.BlockSpec((VOCAB, wide), head(2)),
        pl.BlockSpec((windows, VOCAB, 128), lambda h, s: (0, 0, 0)),
        pl.BlockSpec((windows, 1, VOCAB), lambda h, s: (0, 0, 0)),
        pl.BlockSpec((STATES, wide), head(0)),
        pl.BlockSpec((1, wide), head(0)),
    ]


def summary_forward(span, state_query, qkv_table, counts, rows, state_init, forget):
    states = pl.BlockSpec((STATES, TOGETHER * HEAD_DIM), lambda h, s: (0, h))
    return pl.pallas_call(
        summary_forward_kernel,
        grid_spec=pltpu.PrefetchScalarGridSpec(
            num_scalar_prefetch=1,
            grid=(HEADS // TOGETHER,),
            in_specs=summary_specs(counts.shape[0]),
            out_specs=[states, states, pl.BlockSpec((1, 8, 128), lambda h, s: (h, 0, 0))],
            scratch_shapes=[pltpu.VMEM((STATES, TOGETHER * HEAD_DIM), f32)] * 2,
        ),
        out_shape=[
            jax.ShapeDtypeStruct((STATES, D), f32),
            pltpu.HBM((STATES, D), f32),
            jax.ShapeDtypeStruct((HEADS // TOGETHER, 8, 128), f32),
        ],
        compiler_params=params(),
        cost_estimate=cost(1e3, 1e3),
        name="summary_forward",
    )(span, state_query, qkv_table, qkv_table, counts, rows, *stays(state_init), forget)


def summary_backward_kernel(span, sq, kt, vt, counts, rows, local, forget, low, *rest):
    g_out, gsq_out, ginit_out, g_s, gs_s, gv_s, gs16, e_s, e_t = rest[-9:]
    heads = range(TOGETHER)
    f = forget[...]
    v = [vt[:, lanes_of(i)] for i in heads]
    g_s[...] = local[...]
    gs_s[...] = jnp.zeros_like(gs_s)
    gv_s[...] = jnp.zeros_like(gv_s)
    first, here = span[0], span[1]
    fast = jnp.min(low[0]) >= smallest_sum

    def scores(i):
        return dot(sq[:, lanes_of(i)], kt[:, lanes_of(i)], NT) * (score_scale * log2e)

    def carried(i):
        at = lanes_of(i)
        g = g_s[:, at]
        fg = f[:, at] * g
        g_s[:, at] = fg
        return g - fg

    @pl.when(fast)
    def _():
        there = characters_there(span, rows)
        for i in heads:
            e = shared_exp(scores(i), there)
            e_s[i] = e
            e_t[i] = e.astype(f32).T.astype(bf16)
        lane = lax.broadcasted_iota(jnp.int32, (STATES, HEAD_DIM), 1)

        def step(t, _):
            w = here - 1 - t
            n = counts[w]
            for i in heads:
                sides = window_sides(v[i], n)
                both = dot(e_s[i], sides)
                part = 1.0 / both[:, HEAD_DIM:]
                gu = (carried(i) * part).astype(bf16)
                inner = gu.astype(f32) * (both[:, :HEAD_DIM] * part)
                inner = inner + pltpu.roll(inner, HEAD_DIM // 2, 1)
                high = inner.astype(bf16)
                tail = jnp.where(
                    lane < HEAD_DIM // 2, high.astype(f32), inner - high.astype(f32)
                )
                gs_s[i] += dot(
                    jnp.concatenate([gu, (-tail).astype(bf16)], axis=1), sides, NT
                )
                gv_s[i] += n * dot(e_t[i], gu)
            return 0

        lax.fori_loop(0, here - first, step, 0)
        for i in heads:
            gs16[i] = (gs_s[i] * e_s[i].astype(f32) * score_scale).astype(bf16)

    @pl.when(jnp.logical_not(fast))
    def _():
        for i in heads:
            lg = scores(i)

            def slow(t, _):
                w = here - 1 - t
                p = own_weights(lg, rows[w])
                gu = carried(i).astype(bf16)
                pd = p * dot(gu, v[i], NT)
                gs_s[i] += pd - p * jnp.sum(pd, axis=1, keepdims=True)
                gv_s[i] += dot(p.astype(bf16), gu, TN)
                return 0

            lax.fori_loop(0, here - first, slow, 0)
            gs16[i] = (gs_s[i] * score_scale).astype(bf16)

    for i in heads:
        gs = gs16[i]
        at = lanes_of(i)
        g_out[i, :, :128] = jnp.zeros((VOCAB, 128), bf16)
        g_out[i, :, 128:256] = dot(gs, sq[:, at], TN).astype(bf16)
        g_out[i, :, 256:] = gv_s[i].astype(bf16)
        gsq_out[:, at] = dot(gs, kt[:, at]).astype(bf16)
    ginit_out[...] = g_s[...].astype(bf16)


def summary_backward(
    span, state_query, qkv_table, counts, rows, local, forget, low, deps=(), half=None, onto=()
):
    start, steps = (0, HEADS // TOGETHER) if half is None else (half, 1)
    deps = (*deps, *onto)
    wide = TOGETHER * HEAD_DIM
    windows = counts.shape[0]
    head = lambda k: (lambda h, s: (0, k * HEADS // TOGETHER + start + h))
    first = lambda h, s: (start + h, 0, 0)
    states = pl.BlockSpec((STATES, wide), head(0))
    return pl.pallas_call(
        summary_backward_kernel,
        grid_spec=pltpu.PrefetchScalarGridSpec(
            num_scalar_prefetch=1,
            grid=(steps,),
            in_specs=[
                states,
                pl.BlockSpec((VOCAB, wide), head(1)),
                pl.BlockSpec((VOCAB, wide), head(2)),
                pl.BlockSpec((windows, VOCAB, 128), lambda h, s: (0, 0, 0)),
                pl.BlockSpec((windows, 1, VOCAB), lambda h, s: (0, 0, 0)),
                states,
                pl.BlockSpec((1, wide), head(0)),
                pl.BlockSpec((1, 8, 128), first),
            ]
            + [pl.BlockSpec(memory_space=pl.ANY)] * len(deps),
            out_specs=[pl.BlockSpec((TOGETHER, VOCAB, 384), first), states, states],
            scratch_shapes=[
                pltpu.VMEM((STATES, wide), f32),
                pltpu.VMEM((TOGETHER, STATES, VOCAB), f32),
                pltpu.VMEM((TOGETHER, VOCAB, HEAD_DIM), f32),
                pltpu.VMEM((TOGETHER, STATES, VOCAB), bf16),
                pltpu.VMEM((TOGETHER, STATES, VOCAB), bf16),
                pltpu.VMEM((TOGETHER, VOCAB, STATES), bf16),
            ],
        ),
        out_shape=[
            jax.ShapeDtypeStruct((HEADS, VOCAB, 384), bf16),
            jax.ShapeDtypeStruct((STATES, D), bf16),
            jax.ShapeDtypeStruct((STATES, D), bf16),
        ],
        input_output_aliases={9 + len(deps) - 3 + i: i for i in range(len(onto))},
        compiler_params=params(),
        cost_estimate=cost(1e3, 1e3),
        name="summary_backward",
    )(span, state_query, qkv_table, qkv_table, counts, rows, local, forget, low, *deps)


def each_head(kernel, heads, kinds, *refs):
    kinds = "w" * (len(refs) - len(kinds)) + kinds
    for i in range(heads):
        views = {
            "l": lambda r, i=i: r.at[:, lanes_of(i)],
            "b": lambda r, i=i: r.at[i : i + 1],
            "s": lambda r, i=i: r.at[i],
            "w": lambda r: r,
        }
        kernel(*(views[kind](r) for kind, r in zip(kinds, refs)))


def bias_tile(row):
    spread = jnp.broadcast_to(row, (TILE, CONTEXT))
    shifted = pltpu.roll(spread, 0, 1, stride=1, stride_axis=0)
    return shifted[:, : 3 * TILE].T


def attention_forward_kernel(
    live, pick, pick_t, qt, kt, vt, sk, sv, bias_row, mixed_out, lse_out, bias
):
    bias[...] = bias_tile(bias_row[0])
    prev_add = jnp.where(live[0] > 0, 0.0, hidden).astype(f32)
    keys = dot(pick[...], kt[...]).astype(bf16)
    values_t = dot(vt[...], pick_t[...], TN).astype(bf16)
    query = dot(pick[WINDOW:, :], qt[...]).astype(bf16)
    state_values_t = sv[...].astype(f32).T.astype(bf16)
    for j in range(WINDOW // TILE):
        q = query[j * TILE : (j + 1) * TILE]
        scores = []
        for rel in range(3):
            kt_i = j + rel
            s = (
                dot(keys[kt_i * TILE : (kt_i + 1) * TILE], q, NT)
                * (score_scale * log2e)
                + bias[rel * TILE : (rel + 1) * TILE]
            )
            if kt_i * TILE < WINDOW:
                s = s + prev_add
            scores.append(s)
        for st in range(STATES // TILE):
            scores.append(
                dot(sk[st * TILE : (st + 1) * TILE, :], q, NT) * (score_scale * log2e)
            )
        peak = functools.reduce(
            jnp.maximum, [jnp.max(s, axis=0, keepdims=True) for s in scores]
        )
        total = jnp.zeros((1, TILE), f32)
        out = jnp.zeros((HEAD_DIM, TILE), f32)
        for i, s in enumerate(scores):
            p = jnp.exp2(s - peak)
            total = total + jnp.sum(p, axis=0, keepdims=True)
            if i < 3:
                v = values_t[:, (j + i) * TILE : (j + i + 1) * TILE]
            else:
                v = state_values_t[:, (i - 3) * TILE : (i - 2) * TILE]
            out = out + dot(v, p.astype(bf16))
        out = out * (1.0 / total)
        mixed_out[j * TILE : (j + 1) * TILE, :] = out.T.astype(bf16)
        lse_out[0, :, j * TILE : (j + 1) * TILE] = peak + jnp.log2(total)


def attention_forward(live, pick, pick_t, qkv_table, sk, sv, bias_rows):
    heads, wide = 4, 4 * HEAD_DIM
    head = lambda k: (lambda h, s: (0, k * HEADS // heads + h))
    whole = lambda *shape: pl.BlockSpec(shape, lambda h, s: (0,) * len(shape))
    return pl.pallas_call(
        functools.partial(each_head, attention_forward_kernel, heads, "wwwlllllblbs"),
        grid_spec=pltpu.PrefetchScalarGridSpec(
            num_scalar_prefetch=1,
            grid=(HEADS // heads,),
            in_specs=[
                whole(CONTEXT, VOCAB),
                whole(VOCAB, CONTEXT),
                pl.BlockSpec((VOCAB, wide), head(0)),
                pl.BlockSpec((VOCAB, wide), head(1)),
                pl.BlockSpec((VOCAB, wide), head(2)),
                pl.BlockSpec((STATES, wide), head(0)),
                pl.BlockSpec((STATES, wide), head(1)),
                pl.BlockSpec((heads, 1, CONTEXT), lambda h, s: (h, 0, 0)),
            ],
            out_specs=[
                pl.BlockSpec((WINDOW, wide), head(0)),
                pl.BlockSpec((heads, 1, WINDOW), lambda h, s: (h, 0, 0)),
            ],
            scratch_shapes=[pltpu.VMEM((heads, 3 * TILE, TILE), f32)],
        ),
        out_shape=[
            jax.ShapeDtypeStruct((WINDOW, D), bf16),
            jax.ShapeDtypeStruct((HEADS, 1, WINDOW), f32),
        ],
        compiler_params=params(),
        cost_estimate=cost(1e3, 1e3),
        name="attention_forward",
    )(live, pick, pick_t, qkv_table, qkv_table, qkv_table, sk, sv, bias_rows)


def back_tile(s, dp, shift, inner):
    p = jnp.exp2(s - shift)
    return p, p * (dp - inner)


def state_backward_kernel(pick, qt, sk, sv, lse, mixed, grad, *rest):
    gsk_out, gsv_out, gq_out, inner_out = rest[-4:]
    query = dot(pick[WINDOW:, :], qt[...]).astype(bf16)
    state_keys_t = sk[...].astype(f32).T.astype(bf16)
    inner_all = jnp.sum(
        (mixed[...].astype(f32) * grad[...].astype(f32)).T, axis=0, keepdims=True
    )
    inner_out[0] = inner_all
    blocks = WINDOW // TILE
    gq = [jnp.zeros((HEAD_DIM, TILE), f32) for _ in range(blocks)]
    for st in range(STATES // TILE):
        at = slice(st * TILE, (st + 1) * TILE)
        gk = jnp.zeros((TILE, HEAD_DIM), f32)
        gv = jnp.zeros((TILE, HEAD_DIM), f32)
        for j in range(blocks):
            rows = slice(j * TILE, (j + 1) * TILE)
            p, gs = back_tile(
                dot(sk[at, :], query[rows], NT) * (score_scale * log2e),
                dot(sv[at, :], grad[rows, :], NT),
                lse[0, :, rows],
                inner_all[:, rows],
            )
            gs16 = gs.astype(bf16)
            gq[j] = gq[j] + dot(state_keys_t[:, at], gs16)
            gk = gk + dot(gs16, query[rows])
            gv = gv + dot(p.astype(bf16), grad[rows, :])
        gsk_out[at, :] = (gk * score_scale).astype(bf16)
        gsv_out[at, :] = gv.astype(bf16)
    for j in range(blocks):
        gq_out[0, :, j * TILE : (j + 1) * TILE] = gq[j]


def state_backward(pick, qkv_table, state_kv, lse, mixed, grad, deps=()):
    heads, wide = 4, 4 * HEAD_DIM
    head = lambda k: (lambda h: (0, k * HEADS // heads + h))
    tokens = pl.BlockSpec((WINDOW, wide), head(0))
    states = pl.BlockSpec((STATES, wide), head(0))
    row = pl.BlockSpec((heads, 1, WINDOW), lambda h: (h, 0, 0))
    return pl.pallas_call(
        functools.partial(
            each_head, state_backward_kernel, heads, "wlllbll" + "w" * len(deps) + "llbb"
        ),
        grid=(HEADS // heads,),
        in_specs=[
            pl.BlockSpec((CONTEXT, VOCAB), lambda h: (0, 0)),
            pl.BlockSpec((VOCAB, wide), head(0)),
            pl.BlockSpec((STATES, wide), head(0)),
            pl.BlockSpec((STATES, wide), head(1)),
            row,
            tokens,
            tokens,
        ]
        + [pl.BlockSpec(memory_space=pl.ANY)] * len(deps),
        out_specs=[
            states,
            states,
            pl.BlockSpec((heads, HEAD_DIM, WINDOW), lambda h: (h, 0, 0)),
            row,
        ],
        out_shape=[
            pltpu.HBM((STATES, D), bf16),
            pltpu.HBM((STATES, D), bf16),
            jax.ShapeDtypeStruct((HEADS, HEAD_DIM, WINDOW), f32),
            jax.ShapeDtypeStruct((HEADS, 1, WINDOW), f32),
        ],
        compiler_params=params(),
        cost_estimate=cost(1e3, 1e3),
        name="state_backward",
    )(pick, qkv_table, state_kv, state_kv, lse, mixed, grad, *deps)


def token_backward_kernel(
    live, pick, pick_t, qt, kt, vt, bias_row, lse, inner, grad, gq_in, buckets, *rest
):
    g_out, fold_out, bias, bias_grad = rest[-4:]
    bias[...] = bias_tile(bias_row[0])
    bias_grad[...] = jnp.zeros_like(bias_grad)
    prev_add = jnp.where(live[0] > 0, 0.0, hidden).astype(f32)
    both = dot(pick[...], jnp.concatenate([kt[...], vt[...]], axis=1)).astype(bf16)
    keys = both[:, :HEAD_DIM]
    values = both[:, HEAD_DIM:]
    keys_t = dot(kt[...], pick_t[...], TN).astype(bf16)
    query = dot(pick[WINDOW:, :], qt[...]).astype(bf16)
    blocks = WINDOW // TILE
    gq = [gq_in[0, :, j * TILE : (j + 1) * TILE] for j in range(blocks)]
    sums = jnp.zeros((VOCAB, 2 * HEAD_DIM), f32)
    for tile in range(CONTEXT // TILE):
        at = slice(tile * TILE, (tile + 1) * TILE)
        gk = jnp.zeros((TILE, HEAD_DIM), f32)
        gv = jnp.zeros((TILE, HEAD_DIM), f32)
        for j in range(blocks):
            rel = tile - j
            if not 0 <= rel < 3:
                continue
            rows = slice(j * TILE, (j + 1) * TILE)
            rels = slice(rel * TILE, (rel + 1) * TILE)
            shift = lse[0, :, rows]
            if tile * TILE < WINDOW:
                shift = shift - prev_add
            p, gs = back_tile(
                dot(keys[at], query[rows], NT) * (score_scale * log2e) + bias[rels],
                dot(values[at], grad[rows, :], NT),
                shift,
                inner[0, :, rows],
            )
            gs16 = gs.astype(bf16)
            gq[j] = gq[j] + dot(keys_t[:, at], gs16)
            bias_grad[rels] += gs
            gk = gk + dot(gs16, query[rows])
            gv = gv + dot(p.astype(bf16), grad[rows, :])
        pair = jnp.concatenate([gk * score_scale, gv], axis=1).astype(bf16)
        sums = sums + dot(pick_t[:, at], pair)
    g_out[0, :, HEAD_DIM:] = sums
    total = jnp.zeros((HEAD_DIM, VOCAB), f32)
    for j in range(blocks):
        rows = slice(WINDOW + j * TILE, WINDOW + (j + 1) * TILE)
        total = total + dot((gq[j] * score_scale).astype(bf16), pick[rows, :])
    g_out[0, :, :HEAD_DIM] = total.T
    rows = jnp.concatenate(
        [bias_grad[...].T, jnp.zeros((TILE, CONTEXT - 3 * TILE), f32)], axis=1
    )
    count = TILE
    while count > 8:
        count //= 2
        rows = rows[:count] + pltpu.roll(rows[count:], CONTEXT - count, 1)
    folded = rows[0:1]
    for r in range(1, 8):
        folded = folded + pltpu.roll(rows, CONTEXT - r, 1)[r : r + 1]
    pieces = []
    left = folded
    for _ in range(3):
        piece = left.astype(bf16)
        pieces.append(piece)
        left = left - piece.astype(f32)
    pieces = jnp.concatenate(pieces + [jnp.zeros((5, CONTEXT), bf16)], axis=0)
    fold_out[0] = jnp.sum(dot(pieces, buckets[...]), axis=0, keepdims=True)


def token_backward(
    live, pick, pick_t, qkv_table, bias_rows, lse, inner, grad, gq, deps=(), half=None, onto=()
):
    heads, wide = 4, 4 * HEAD_DIM
    count = HEADS // heads if half is None else HEADS // heads // 2
    low = 0 if half is None else half * count
    deps = (*deps, *onto)
    head = lambda k: (lambda h, s: (0, k * HEADS // heads + low + h))
    by_head = lambda *shape: pl.BlockSpec((heads,) + shape, lambda h, s: (low + h, 0, 0))
    flat = lambda *shape: pl.BlockSpec(shape, lambda h, s: (0,) * len(shape))
    return pl.pallas_call(
        functools.partial(
            each_head, token_backward_kernel, heads, "wwwlllbbblbw" + "w" * len(deps) + "bbss"
        ),
        grid_spec=pltpu.PrefetchScalarGridSpec(
            num_scalar_prefetch=1,
            grid=(count,),
            in_specs=[
                flat(CONTEXT, VOCAB),
                flat(VOCAB, CONTEXT),
                pl.BlockSpec((VOCAB, wide), head(0)),
                pl.BlockSpec((VOCAB, wide), head(1)),
                pl.BlockSpec((VOCAB, wide), head(2)),
                by_head(1, CONTEXT),
                by_head(1, WINDOW),
                by_head(1, WINDOW),
                pl.BlockSpec((WINDOW, wide), head(0)),
                by_head(HEAD_DIM, WINDOW),
                flat(CONTEXT, 128),
            ]
            + [pl.BlockSpec(memory_space=pl.ANY)] * len(deps),
            out_specs=[by_head(VOCAB, 384), by_head(1, 128)],
            scratch_shapes=[
                pltpu.VMEM((heads, 3 * TILE, TILE), f32),
                pltpu.VMEM((heads, 3 * TILE, TILE), f32),
            ],
        ),
        out_shape=[
            jax.ShapeDtypeStruct((HEADS, VOCAB, 384), f32),
            jax.ShapeDtypeStruct((HEADS, 1, 128), f32),
        ],
        input_output_aliases={12 + len(deps) - 2 + i: i for i in range(len(onto))},
        compiler_params=params(),
        cost_estimate=cost(1e3, 1e3),
        name="token_backward",
    )(
        live,
        pick,
        pick_t,
        qkv_table,
        qkv_table,
        qkv_table,
        bias_rows,
        lse,
        inner,
        grad,
        gq,
        jnp.asarray(np.pad(lane_pick().T, ((0, 0), (0, 96))), bf16),
        *deps,
    )


def mlp_kernel(x, cot, up, down, out_in, gx_in, gd_out, gu_out, out, gx, xt):
    @pl.when(pl.program_id(0) == 0)
    def _():
        out[...] = out_in[...]
        gx[...] = gx_in[...]
        xt[...] = x[...].astype(f32).T.astype(bf16)

    up_b = up[...]
    down_b = down[...]
    pre = dot(x[...], up_b)
    root = math.sqrt(2.0 / math.pi)
    square = pre * pre
    t = jnp.tanh(root * pre * (1.0 + 0.044715 * square))
    half = 0.5 * (1.0 + t)
    act = (pre * half).astype(bf16)
    slope = half + (0.5 * root) * pre * (1.0 - t * t) * (1.0 + (3 * 0.044715) * square)
    grad_pre = (dot(cot[...], down_b, NT) * slope).astype(bf16)
    out[...] += dot(act, down_b)
    gx[...] += dot(grad_pre, up_b, NT)
    gd_out[...] = dot(act, cot[...], TN).astype(bf16)
    gu_out[...] = dot(xt[...], grad_pre).astype(bf16)


def mlp_part(part, x, cot, up, down, out, gx):
    count = FF // SPLITS // TILE
    whole = pl.BlockSpec((WINDOW, D), lambda s: (0, 0))
    return pl.pallas_call(
        mlp_kernel,
        grid=(count,),
        in_specs=[
            whole,
            whole,
            pl.BlockSpec((D, TILE), lambda s: (0, SPLITS * s + part)),
            pl.BlockSpec((TILE, D), lambda s: (SPLITS * s + part, 0)),
            whole,
            whole,
        ],
        out_specs=[
            pl.BlockSpec((TILE, D), lambda s: (s, 0)),
            pl.BlockSpec((D, TILE), lambda s: (0, s)),
            whole,
            whole,
        ],
        out_shape=[
            jax.ShapeDtypeStruct((count * TILE, D), bf16),
            jax.ShapeDtypeStruct((D, count * TILE), bf16),
            jax.ShapeDtypeStruct((WINDOW, D), f32),
            jax.ShapeDtypeStruct((WINDOW, D), f32),
        ],
        scratch_shapes=[pltpu.VMEM((D, WINDOW), bf16)],
        compiler_params=params(),
        cost_estimate=cost(1e3, 1e3),
        name="feed_forward",
    )(x, cot, up, down, out, gx)


def mlp_packed_kernel(
    places, x, xs, cot, up_a, up_b, up_c, up_d, down_a, down_b, down_c, down_d, out_in, gx_in,
    *rest,
):
    send, keep, out, gx, gd_s = rest[-5:]
    core = places[CORE]
    step = pl.program_id(0)

    @pl.when(step == 0)
    def _():
        out[...] = out_in[...]
        gx[...] = gx_in[...]

    up = jnp.concatenate([up_a[...], up_b[...], up_c[...], up_d[...]], axis=1)
    down = jnp.concatenate([down_a[...], down_b[...], down_c[...], down_d[...]], axis=0)
    pre = dot(x[...], up)
    root = math.sqrt(2.0 / math.pi)
    square = pre * pre
    t = jnp.tanh(root * pre * (1.0 + 0.044715 * square))
    half = 0.5 * (1.0 + t)
    act = (pre * half).astype(bf16)
    slope = half + (0.5 * root) * pre * (1.0 - t * t) * (1.0 + (3 * 0.044715) * square)
    grad_pre = (dot(cot[...], down, NT) * slope).astype(bf16)
    out[...] += dot(act, down)
    gx[...] += dot(grad_pre, up, NT)
    gd = dot(act, cot[...], TN).astype(bf16)
    for i in range(2):
        for q in range(2):
            at = (2 * i + q) * 128
            gd_s[q, i] = gd[at : at + 128]
    lanes = pl.ds(pl.multiple_of(step * 512, 512), 512)
    for i in range(2):
        z = 2 * step + i
        send[pl.ds(z, 1), :128, :] = gd_s[pl.ds(1 - core, 1), i]
        keep[pl.ds(z, 1), :128, :] = gd_s[pl.ds(core, 1), i]
    for slot, ref in ((0, send), (1, keep)):
        gu = dot(xs[slot], grad_pre).astype(bf16)
        ref[:, 128:, lanes] = gu.reshape(4, 128, 512)


def mlp_packed(part, places, x, split, cot, up, down, out, gx, deps=()):
    block = pl.BlockSpec((WINDOW, D), lambda g, s: (0, 0))
    packed = pl.BlockSpec((4, 256, D), lambda g, s: (0, 0, 0))
    at = lambda k: (lambda g: (4 * g + k) * 4 + part)
    return pl.pallas_call(
        mlp_packed_kernel,
        grid_spec=pltpu.PrefetchScalarGridSpec(
            num_scalar_prefetch=1,
            grid=(2,),
            in_specs=[block, pl.BlockSpec((2, WINDOW, WINDOW), lambda g, s: (0, 0, 0)), block]
            + [
                pl.BlockSpec((D, 128), lambda g, s, k=k: (0, at(k)(g)))
                for k in range(4)
            ]
            + [
                pl.BlockSpec((128, D), lambda g, s, k=k: (at(k)(g), 0))
                for k in range(4)
            ]
            + [block, block]
            + [pl.BlockSpec(memory_space=pl.ANY)] * len(deps),
            out_specs=[packed, packed, block, block],
            scratch_shapes=[pltpu.VMEM((2, 2, 128, D), bf16)],
        ),
        out_shape=[
            jax.ShapeDtypeStruct((4, 256, D), bf16),
            jax.ShapeDtypeStruct((4, 256, D), bf16),
            jax.ShapeDtypeStruct((WINDOW, D), f32),
            jax.ShapeDtypeStruct((WINDOW, D), f32),
        ],
        compiler_params=params(32),
        cost_estimate=cost(1e3, 1e3),
        name="feed_forward",
    )(places, x, split, cot, up, up, up, up, down, down, down, down, out, gx, *deps)


def one_block(array):
    return pl.BlockSpec(array.shape, lambda g: (0,) * len(array.shape))


def single(kernel, name, ins, outs, scratch=(), deps=()):
    return pl.pallas_call(
        kernel,
        grid=(1,),
        in_specs=[one_block(a) for a in ins]
        + [pl.BlockSpec(memory_space=pl.ANY)] * len(deps),
        out_specs=[one_block(o) for o in outs],
        out_shape=list(outs),
        scratch_shapes=list(scratch),
        compiler_params=params(),
        cost_estimate=cost(1e3, 1e3),
        name=name,
    )(*ins, *deps)


def like(kind, *shape):
    return jax.ShapeDtypeStruct(shape, kind)


def kept(kind, *shape):
    return pltpu.HBM(shape, kind)


def stays(*arrays):
    return tuple(pltpu.with_memory_space_constraint(a, pltpu.HBM) for a in arrays)


def unit_of(value):
    unit, inv = norm_parts(value)
    return unit, jnp.broadcast_to(inv, (value.shape[0], 128))


def table_kernel(table, gain, weight, unit_out, inv_out, normed_out, qkv_out):
    step = pl.program_id(0)

    @pl.when(step == 0)
    def _():
        unit, inv = unit_of(table[...].astype(f32))
        unit_out[...] = unit
        inv_out[...] = inv
        normed_out[...] = (unit * gain[...]).astype(bf16)

    qkv_out[...] = dot(normed_out[...], weight[...]).astype(bf16)


def table_forward(table, gain, weight):
    flat = lambda *shape: pl.BlockSpec(shape, lambda g: (0, 0))
    return pl.pallas_call(
        table_kernel,
        grid=(6,),
        in_specs=[
            flat(VOCAB, D),
            flat(1, D),
            pl.BlockSpec((D, D // 2), lambda g: (0, g)),
        ],
        out_specs=[
            flat(VOCAB, D),
            flat(VOCAB, 128),
            flat(VOCAB, D),
            pl.BlockSpec((VOCAB, D // 2), lambda g: (0, g)),
        ],
        out_shape=[
            kept(f32, VOCAB, D),
            kept(f32, VOCAB, 128),
            kept(bf16, VOCAB, D),
            like(bf16, VOCAB, 3 * D),
        ],
        compiler_params=params(),
        cost_estimate=cost(1e3, 1e3),
        name="table_forward",
    )(*stays(table), gain, *stays(weight))


def states_forward_kernel(states, gain, weight, unit_out, inv_out, normed_out, kv_out):
    step = pl.program_id(0)

    @pl.when(step == 0)
    def _():
        unit, inv = unit_of(states[...])
        unit_out[...] = unit
        inv_out[...] = inv
        normed_out[...] = (unit * gain[...]).astype(bf16)

    kv_out[...] = dot(normed_out[...], weight[...]).astype(bf16)


def states_forward(states, gain, weight):
    flat = lambda *shape: pl.BlockSpec(shape, lambda g: (0, 0))
    return pl.pallas_call(
        states_forward_kernel,
        grid=(4,),
        in_specs=[
            flat(STATES, D),
            flat(1, D),
            pl.BlockSpec((D, D // 2), lambda g: (0, g)),
        ],
        out_specs=[
            flat(STATES, D),
            flat(STATES, 128),
            flat(STATES, D),
            pl.BlockSpec((STATES, D // 2), lambda g: (0, g)),
        ],
        out_shape=[
            kept(f32, STATES, D),
            kept(f32, STATES, 128),
            kept(bf16, STATES, D),
            like(bf16, STATES, 2 * D),
        ],
        compiler_params=params(),
        cost_estimate=cost(1e3, 1e3),
        name="states_forward",
    )(states, gain, weight)


def residual_kernel(
    places, mixed, out_weight, pick, table, gain, res_out, unit_out, inv_out, in_out, split_out, xt
):
    res = dot(pick[WINDOW:, :], table[...]) + dot(mixed[...], out_weight[...])
    res_out[...] = res
    unit, inv = unit_of(res)
    unit_out[...] = unit
    inv_out[...] = inv
    x = unit * gain[...]
    in_out[...] = x.astype(bf16)
    xt[...] = x.T.astype(bf16)
    core = places[CORE]
    for z in range(4):
        for slot, parity in ((0, 1 - core), (1, core)):
            at = pl.multiple_of((2 * z + parity) * 128, 128)
            split_out[slot, z * 128 : (z + 1) * 128, :] = xt[pl.ds(at, 128), :]


def residual_forward(places, *ins):
    outs = (
        like(f32, WINDOW, D),
        kept(f32, WINDOW, D),
        kept(f32, WINDOW, 128),
        like(bf16, WINDOW, D),
        like(bf16, 2, WINDOW, WINDOW),
    )
    return pl.pallas_call(
        residual_kernel,
        grid_spec=pltpu.PrefetchScalarGridSpec(
            num_scalar_prefetch=1,
            grid=(1,),
            in_specs=[whole(a) for a in ins],
            out_specs=[whole(o) for o in outs],
            scratch_shapes=[pltpu.VMEM((D, WINDOW), bf16)],
        ),
        out_shape=list(outs),
        compiler_params=params(),
        cost_estimate=cost(1e3, 1e3),
        name="residual_forward",
    )(places, *ins)


def feed_back_kernel(
    gx, unit, inv, gain, upstream, mixed, out_weight, pick, *rest
):
    gain_out, out_out, mixed_out, rows_out = rest[-4:]
    g = gx[...]
    u = unit[...]
    gain_out[...] = jnp.sum(g * u, axis=0, keepdims=True)
    back = norm_back(u, inv[:, :1], gain[...], g)
    grad = (upstream[...].astype(f32) + back).astype(bf16)
    mixed_out[...] = dot(grad, out_weight[...], NT).astype(bf16)
    out_out[...] = dot(mixed[...], grad, TN).astype(bf16)
    rows_out[...] = dot(pick[WINDOW:, :], grad, TN).astype(bf16)


def feed_back(v, gx, deps=()):
    return single(
        feed_back_kernel,
        "feed_back",
        (
            gx,
            v.mlp_unit,
            v.mlp_inv,
            v.mlp_gain,
            v.upstream,
            v.mixed,
            v.out_weight,
            v.pick,
        ),
        (like(f32, 1, D), like(bf16, D, D), like(bf16, WINDOW, D), like(bf16, VOCAB, D)),
        deps=deps,
    )


def states_back_kernel(
    gsk, gsv, weight, normed, unit, inv, gain, slope, forget, *rest
):
    k_out, v_out, gain_out, local_out, gate_out = rest[-5:]
    upstream = dot(gsk[...], weight[:, :D], NT) + dot(gsv[...], weight[:, D:], NT)
    u = unit[...]
    gain_out[...] = jnp.sum(upstream * u, axis=0, keepdims=True)
    local = norm_back(u, inv[:, :1], gain[...], upstream)
    local_out[...] = local
    f = forget[...]
    gate_out[...] = jnp.sum(local * slope[...], axis=0, keepdims=True) * f * (1.0 - f)
    k_out[...] = dot(normed[...], gsk[...], TN).astype(bf16)
    v_out[...] = dot(normed[...], gsv[...], TN).astype(bf16)


def states_back(v, gsk, gsv, deps=()):
    return single(
        states_back_kernel,
        "states_back",
        (
            *stays(gsk, gsv, v.state_kv_weight, v.state_normed, v.state_unit, v.state_inv),
            v.state_gain,
            *stays(v.forget_slope),
            v.forget,
        ),
        (
            like(bf16, D, D),
            like(bf16, D, D),
            like(f32, 1, D),
            like(f32, STATES, D),
            like(f32, 1, D),
        ),
        deps=deps,
    )


XI, YI, ZI, CORE, DPI, SEQI = range(6)


def permute(value, axis, to):
    size = lax.axis_size(axis)
    return lax.ppermute(value, axis, [(i, to(i)) for i in range(size)])


def swap_core(value):
    return permute(value, "seq", lambda i: i ^ 1)


def swap_dp(value, step):
    return permute(value, "dp", lambda i: i ^ step)


def ahead(value, step):
    return permute(value, "seq", lambda i: (i + 2 * step) % 8)


def fitted():
    return lax.axis_size("seq") == 8 and lax.axis_size("dp") == 4


def whole(array):
    return pl.BlockSpec(array.shape, lambda g, s: (0,) * len(array.shape))


def blend(name, places, outs, deps=(), through=()):
    arrays, in_specs, plan, out_specs = [], [], [], []
    for shape, rows, blocks, segments in outs:
        every = 4 // blocks
        rows_of = []
        for sources in segments:
            names = []
            for array, block_rows, place in sources:
                names.append(len(arrays))
                arrays.append(array)
                in_specs.append(
                    pl.BlockSpec(
                        (1, block_rows, array.shape[2]),
                        lambda g, s, place=place, every=every: (*place(g // every, s), 0),
                    )
                )
            rows_of.append((sources[0][1], names))
        plan.append((every, rows_of))
        out_specs.append(
            pl.BlockSpec((1, rows, shape[2]), lambda g, s, every=every: (g // every, 0, 0))
        )
    count = len(arrays)

    def kernel(s, *refs):
        step = pl.program_id(0)
        out_refs = refs[count + len(deps) + len(through) :]

        def fill(out_ref, rows_of):
            at = 0
            for rows, names in rows_of:
                total = refs[names[0]][0].astype(f32)
                for i in names[1:]:
                    total = total + refs[i][0].astype(f32)
                out_ref[0, at : at + rows, :] = total.astype(out_ref.dtype)
                at += rows

        for out_ref, (every, rows_of) in zip(out_refs, plan):
            if every == 1:
                fill(out_ref, rows_of)
            else:
                pl.when(step % every == 0)(functools.partial(fill, out_ref, rows_of))

    return pl.pallas_call(
        kernel,
        grid_spec=pltpu.PrefetchScalarGridSpec(
            num_scalar_prefetch=1,
            grid=(4,),
            in_specs=in_specs
            + [pl.BlockSpec(memory_space=pl.ANY)] * (len(deps) + len(through)),
            out_specs=out_specs + [pl.BlockSpec(memory_space=pl.ANY)] * len(through),
        ),
        out_shape=[jax.ShapeDtypeStruct(shape, bf16) for shape, _, _, _ in outs]
        + [jax.ShapeDtypeStruct(t.shape, t.dtype) for t in through],
        input_output_aliases={
            1 + count + len(deps) + i: len(outs) + i for i in range(len(through))
        },
        compiler_params=params(),
        cost_estimate=cost(1e3, 1e3),
        name=name,
    )(places, *arrays, *deps, *through)


class Wing:
    def __init__(self, lead, kept, came, base, rows):
        self.lead, self.trail = lead, 1 - lead
        self.kept, self.came, self.base = kept, came, base
        self.half, self.quarter = rows // 2, rows // 4
        self.columns = kept.shape[2]
        self.got = []

    def first(self):
        at = self.base // self.half
        other = lambda g, s: (g, at + 1 - s[self.lead])
        return self.half, [(self.kept, self.half, other), (self.came, self.half, other)]

    def second(self):
        q = self.quarter
        at = self.base // q
        array, start = self.got[0]
        start = start // q
        deep = lambda g, s: (g, at + 2 * s[self.lead] + 1 - s[self.trail])
        flat = lambda g, s: (g, start + 1 - s[self.trail])
        return q, [(self.kept, q, deep), (self.came, q, deep), (array, q, flat)]

    def quarters(self, level):
        q = self.quarter
        at = self.base // q
        (one, start_one), (two, start_two) = self.got
        start_one, start_two = start_one // q, start_two // q
        deep = lambda g, s: (level(g, s), at + 2 * s[self.lead] + s[self.trail])
        flat = lambda g, s: (level(g, s), start_one + s[self.trail])
        last = lambda g, s: (level(g, s), start_two)
        return [(self.kept, q, deep), (self.came, q, deep), (one, q, flat), (two, q, last)]


def wings(kept, came):
    half = kept.shape[1] // 2
    return [Wing(XI, kept, came, 0, half), Wing(YI, kept, came, half, half)]


class Column:
    def __init__(self, parts):
        self.parts = parts
        self.rows = sum(w.quarter for w in parts)
        self.columns = parts[0].columns

    def near(self):
        outs = []
        for own in (False, True):
            level = (
                (lambda g, s: 2 * g + s[ZI] % 2)
                if own
                else (lambda g, s: 2 * g + 1 - s[ZI] % 2)
            )
            segments = [w.quarters(level) for w in self.parts]
            outs.append(((2, self.rows, self.columns), self.rows, 2, segments))
        return outs

    def rest(self, pick, extra=()):
        sources = [
            (array, self.rows, lambda g, s: (pick(s), 0))
            for array in (self.kept, self.from_near)
        ] + [(array, self.rows, lambda g, s: (0, 0)) for array in extra]
        return [((1, self.rows, self.columns), self.rows, 1, [sources])]

    def far(self):
        return self.rest(lambda s: 1 - s[ZI] // 2)

    def close(self):
        return self.rest(lambda s: s[ZI] // 2, [self.from_far])


class Traffic:
    def __init__(self, places):
        self.places = places
        self.pending = []

    def swap(self, send):
        came = swap_core(send)
        self.pending.append(came)
        return came

    def boundary(self, after, first=(), second=(), near=(), far=(), close=(), swap=(), join=()):
        outs, sent = [], []
        for axis in (XI, YI):
            groups = {}
            for w in first:
                if w.lead == axis:
                    groups.setdefault(w.columns, []).append((w, w.first()))
            for w in second:
                if w.trail == axis:
                    groups.setdefault(w.columns, []).append((w, w.second()))
            for columns, moves in groups.items():
                moves.sort(key=lambda m: -m[1][0])
                rows = sum(m[1][0] for m in moves)
                outs.append(
                    ((4, rows, columns), rows, 4, [m[1][1] for m in moves])
                )
                sent.append((axis, moves))
        for columns, step in ((near, Column.near), (far, Column.far), (close, Column.close)):
            for c in columns:
                outs += step(c)
        if join:
            segments = [c.close()[0][3][0] for c in join]
            total = sum(c.rows for c in join)
            outs.append(((1, total, join[0].columns), total, 1, segments))
        results = blend("boundary", self.places, outs, (*after, *self.pending), swap)
        self.pending = []
        mark = results[0]
        results = list(results)
        for axis, moves in sent:
            came = swap_dp(results.pop(0), 1 << axis)
            self.pending.append(came)
            at = 0
            for w, (rows, _) in moves:
                assert at % w.quarter == 0
                w.got.append((came, at))
                at += rows
        for c in near:
            c.from_near = permute(results.pop(0), "seq", lambda i: i ^ 2)
            c.kept = results.pop(0)
            self.pending.append(c.from_near)
        for c in far:
            c.from_far = permute(results.pop(0), "seq", lambda i: i ^ 4)
            self.pending.append(c.from_far)
        for c in close:
            c.own = results.pop(0)
        if join:
            self.joined = results.pop(0)
        self.swapped = [self.swap(send) for send in results]
        return mark

    def spread(self, own, lead=1):
        beside = swap_dp(own, lead)
        other = swap_dp(own, 3 - lead)
        rows = [own, beside, other, swap_dp(beside, 3 - lead)]
        self.pending += rows[1:]
        return rows if lead == 1 else [own, other, beside, rows[3]]


def packed_pair(name, places, pieces, deps=()):
    rows = sum(p.shape[1] for p in pieces)
    columns = pieces[0].shape[2]
    outs = []
    for keep in (False, True):
        place = (
            (lambda g, s: (2 * g + s[CORE], 0))
            if keep
            else (lambda g, s: (2 * g + 1 - s[CORE], 0))
        )
        outs.append(
            ((4, rows, columns), rows, 4, [[(p, p.shape[1], place)] for p in pieces])
        )
    return blend(name, places, outs, deps)


def pack_rows(places, mark, g_tokens, g, rows_sum, *vectors):
    count = 3 + len(vectors)

    def kernel(s, *refs):
        for out_ref, (a, b, r, *rows) in zip(
            refs[2 * count + 1 :], (refs[:count], refs[count : 2 * count])
        ):
            out_ref[0, :VOCAB, :] = (a[0] + b[0].astype(f32)).astype(bf16)
            out_ref[0, VOCAB:, :128] = r[:128, :]
            out_ref[0, VOCAB:, 128:256] = r[128:, :]
            place = lax.broadcasted_iota(jnp.int32, (128, 128), 0)
            small = jnp.zeros((128, 128), f32)
            for i, row in enumerate(rows):
                value = row[...] if len(row.shape) == 2 else row[0]
                small = jnp.where(place == i, value, small)
            out_ref[0, VOCAB:, 256:] = small.astype(bf16)

    specs, arrays = [], []
    for keep in (False, True):
        at = (
            (lambda i, s: 2 * i + s[CORE]) if keep else (lambda i, s: 2 * i + 1 - s[CORE])
        )
        for array in (g_tokens, g, rows_sum, *vectors):
            arrays.append(array)
            if array.ndim == 2:
                specs.append(
                    pl.BlockSpec((array.shape[0], 128), lambda i, s, at=at: (0, at(i, s)))
                )
            else:
                specs.append(
                    pl.BlockSpec(
                        (1,) + array.shape[1:], lambda i, s, at=at: (at(i, s), 0, 0)
                    )
                )
    return pl.pallas_call(
        kernel,
        grid_spec=pltpu.PrefetchScalarGridSpec(
            num_scalar_prefetch=1,
            grid=(4,),
            in_specs=specs + [pl.BlockSpec(memory_space=pl.ANY)],
            out_specs=[pl.BlockSpec((1, 384, 384), lambda i, s: (i, 0, 0))] * 2,
        ),
        out_shape=[like(bf16, 4, 384, 384)] * 2,
        compiler_params=params(),
        cost_estimate=cost(1e3, 1e3),
        name="pack_rows",
    )(places, *arrays, mark)


def slot_of(s, step, lead):
    there = s[DPI] ^ step
    x, y = there % 2, there // 2
    return 2 * x + y if lead == XI else 2 * y + x


def unpack(name, places, quarters, pieces, outs):
    columns = quarters[0].shape[2]
    total = 4 * sum(p[1] for p in pieces)

    def kernel(s, *refs):
        scratch = refs[-1]
        for step in range(4):
            for start, rows, lead, base in pieces:
                at = pl.multiple_of(slot_of(s, step, lead) * rows + base, 16)
                scratch[pl.ds(at, rows), :] = refs[step][0, start : start + rows, :].astype(
                    f32
                )
        for out_ref, (_, moves) in zip(refs[4:-1], outs):
            if not moves:
                out_ref[...] = jnp.zeros_like(out_ref)
            for row, rows, to, column in moves:
                out_ref[to : to + rows, column : column + columns] = scratch[
                    row : row + rows, :
                ]

    return pl.pallas_call(
        kernel,
        grid_spec=pltpu.PrefetchScalarGridSpec(
            num_scalar_prefetch=1,
            grid=(1,),
            in_specs=[whole(q) for q in quarters],
            out_specs=[
                pl.BlockSpec(shape, lambda g, s: (0, 0)) for shape, _ in outs
            ],
            scratch_shapes=[pltpu.VMEM((total, columns), f32)],
        ),
        out_shape=[jax.ShapeDtypeStruct(shape, f32) for shape, _ in outs],
        compiler_params=params(),
        cost_estimate=cost(1e3, 1e3),
        name=name,
    )(places, *quarters)


def unpack_mlp(places, quarters):
    def kernel(s, *refs):
        down, up, mark, scratch = refs[8:]
        mark[...] = jnp.zeros_like(mark)
        for pair in range(2):
            for step in range(4):
                block = refs[4 * pair + step]
                for part in range(2):
                    for lead in range(2):
                        at = pl.multiple_of(slot_of(s, step, lead) * 32 + 128 * lead, 32)
                        start = part * 64 + lead * 32
                        scratch[2 * pair + part, pl.ds(at, 32), :] = block[
                            0, start : start + 32, :
                        ].astype(f32)
        for part in range(4):
            down[part * 128 : (part + 1) * 128, :] = scratch[part, :128, :]
            for block in range(8):
                at = (4 * block + part) * 128
                up[:, at : at + 128] = scratch[part, 128:, block * 128 : (block + 1) * 128]

    flat = [q for pair in quarters for q in pair]
    return pl.pallas_call(
        kernel,
        grid_spec=pltpu.PrefetchScalarGridSpec(
            num_scalar_prefetch=1,
            grid=(1,),
            in_specs=[whole(q) for q in flat],
            out_specs=[
                pl.BlockSpec((512, D), lambda g, s: (0, 0)),
                pl.BlockSpec((128, FF), lambda g, s: (0, 0)),
                pl.BlockSpec((8, 128), lambda g, s: (0, 0)),
            ],
            scratch_shapes=[pltpu.VMEM((4, 256, D), f32)],
        ),
        out_shape=[
            jax.ShapeDtypeStruct((512, D), f32),
            jax.ShapeDtypeStruct((128, FF), f32),
            jax.ShapeDtypeStruct((8, 128), f32),
        ],
        compiler_params=params(),
        cost_estimate=cost(1e3, 1e3),
        name="unpack_mlp",
    )(places, *flat)


def ring_rows(places, parts, deps=()):
    def kernel(s, *refs):
        out = refs[-1]
        for k in range(4):
            out[pl.ds(s[ZI] ^ k, 1)] = refs[k][...]

    shape = (4,) + parts[0].shape[1:]
    return pl.pallas_call(
        kernel,
        grid_spec=pltpu.PrefetchScalarGridSpec(
            num_scalar_prefetch=1,
            grid=(1,),
            in_specs=[whole(p) for p in parts]
            + [pl.BlockSpec(memory_space=pl.ANY)] * len(deps),
            out_specs=pl.BlockSpec(shape, lambda g, s: (0, 0, 0)),
        ),
        out_shape=jax.ShapeDtypeStruct(shape, bf16),
        compiler_params=params(),
        cost_estimate=cost(1e3, 1e3),
        name="ring_rows",
    )(places, *parts, *deps)


def stack_rows(places, parts, deps=()):
    _, rows, columns = parts[0].shape
    rows //= 2

    def kernel(s, *refs):
        out = refs[-1]
        for step in range(4):
            for lead in range(2):
                at = pl.multiple_of(slot_of(s, step, lead) * rows + 4 * rows * lead, 16)
                out[:, pl.ds(at, rows), :] = refs[step][:, lead * rows : (lead + 1) * rows, :]

    shape = (4, 8 * rows, columns)
    return pl.pallas_call(
        kernel,
        grid_spec=pltpu.PrefetchScalarGridSpec(
            num_scalar_prefetch=1,
            grid=(1,),
            in_specs=[whole(p) for p in parts]
            + [pl.BlockSpec(memory_space=pl.ANY)] * len(deps),
            out_specs=pl.BlockSpec(shape, lambda g, s: (0, 0, 0)),
        ),
        out_shape=jax.ShapeDtypeStruct(shape, bf16),
        compiler_params=params(),
        cost_estimate=cost(1e3, 1e3),
        name="stack_rows",
    )(places, *parts, *deps)


def last_kernel(
    s, mine, other, norm_cols, unit_cols, weight, weight_rows, unit, inv, gain,
    qkv_out, gain_out, table_out, small_out, by_head,
):
    for z in range(4):
        for q in range(2):
            by_head[2 * z + q] = jnp.where(s[CORE] == q, mine[z], other[z])
    small_out[...] = mine[s[ZI], 256:272, 256:].astype(f32)[:8]
    at = pl.multiple_of(s[SEQI] * 32, 32)
    norm = norm_cols[...]
    cols_grad = jnp.zeros((VOCAB, 128), f32)
    normed_grad = jnp.zeros((32, D), f32)
    for h in range(HEADS):
        for t in range(3):
            lanes = slice(t * 128, (t + 1) * 128)
            to = slice(t * D + h * 128, t * D + (h + 1) * 128)
            g = by_head[h, :VOCAB, lanes]
            qkv_out[:, to] = dot(norm, g, TN)
            cols_grad = cols_grad + dot(g, weight_rows[:, to], NT)
            normed_grad = normed_grad + dot(
                by_head[h, pl.ds(at, 32), lanes], weight[:, to], NT
            )
    gain_out[...] = jnp.sum(cols_grad * unit_cols[...], axis=0, keepdims=True)
    u = unit[...]
    scaled = normed_grad * gain[...]
    a = jnp.mean(scaled, axis=-1, keepdims=True)
    b = jnp.mean(scaled * u, axis=-1, keepdims=True)
    low = pl.multiple_of(VOCAB + (s[SEQI] % 4) * 32, 32)
    rows_sum = [
        jnp.where(
            s[SEQI] < 4,
            by_head[h, pl.ds(low, 32), :128].astype(f32),
            by_head[h, pl.ds(low, 32), 128:256].astype(f32),
        )
        for h in range(HEADS)
    ]
    table_out[...] = (
        jnp.concatenate(rows_sum, axis=1) + (scaled - a - u * b) * inv[:, :1]
    )


def last_products(places, mine, other, normed, unit, weight, inv, gain):
    return pl.pallas_call(
        last_kernel,
        grid_spec=pltpu.PrefetchScalarGridSpec(
            num_scalar_prefetch=1,
            grid=(1,),
            in_specs=[
                whole(mine),
                whole(other),
                pl.BlockSpec((VOCAB, 128), lambda g, s: (0, s[SEQI])),
                pl.BlockSpec((VOCAB, 128), lambda g, s: (0, s[SEQI])),
                whole(weight),
                pl.BlockSpec((128, 3 * D), lambda g, s: (s[SEQI], 0)),
                pl.BlockSpec((32, D), lambda g, s: (s[SEQI], 0)),
                pl.BlockSpec((32, 128), lambda g, s: (s[SEQI], 0)),
                whole(gain),
            ],
            out_specs=[
                pl.BlockSpec((128, 3 * D), lambda g, s: (0, 0)),
                pl.BlockSpec((1, 128), lambda g, s: (0, 0)),
                pl.BlockSpec((32, D), lambda g, s: (0, 0)),
                pl.BlockSpec((8, 128), lambda g, s: (0, 0)),
            ],
            scratch_shapes=[pltpu.VMEM((HEADS, 384, 384), bf16)],
        ),
        out_shape=[
            jax.ShapeDtypeStruct((128, 3 * D), f32),
            jax.ShapeDtypeStruct((1, 128), f32),
            jax.ShapeDtypeStruct((32, D), f32),
            jax.ShapeDtypeStruct((8, 128), f32),
        ],
        compiler_params=params(),
        cost_estimate=cost(1e3, 1e3),
        name="last_products",
    )(places, mine, other, normed, unit, weight, weight, unit, inv, gain)


def total_of(value):
    flat = value.reshape((-1,) + value.shape[2:])
    own = lax.psum_scatter(flat, "seq", scatter_dimension=0, tiled=True)
    return lax.psum(own, "dp").astype(f32)


def places_of():
    here = lax.axis_index("seq")
    dp = lax.axis_index("dp")
    return jnp.stack([dp % 2, dp // 2, here // 2, here % 2, dp, here]).astype(jnp.int32)


def prepare_kernel(
    places, blocks_a, blocks_b, gate, bias, picks, mask, *rest
):
    span, live, counts, rows, pick, pick_t, forget, bias_out = rest[-8:]
    here = places[SEQI]
    sign = lax.broadcasted_iota(jnp.int32, (VOCAB, 128), 0)
    first = jnp.zeros((1, 128), f32)
    before = jnp.zeros((4, 128), jnp.int32)
    for k in range(8):
        block = blocks_a[k] if k < 4 else blocks_b[k - 4]
        w = here ^ k
        total = jnp.zeros((VOCAB, 128), f32)
        for r in range(4):
            total = total + jnp.where(block[r : r + 1] == sign, 1.0, 0.0)
        count = jnp.broadcast_to(jnp.sum(total, axis=1, keepdims=True), (VOCAB, 128))
        counts[pl.ds(w, 1)] = count[None]
        rows[pl.ds(w, 1)] = count.T[:1][None]
        marked = jnp.where(block[4:5] > 0, w.astype(f32), 0.0)
        first = jnp.maximum(first, jnp.where(w <= here, marked, 0.0))
        before = jnp.where(w == here - 1, block[:4], before)
    span[0] = jnp.max(first).astype(jnp.int32)
    span[1] = here
    live[0] = 1 - jnp.max(blocks_a[0, 4:5].astype(f32)).astype(jnp.int32)
    own = blocks_a[0, :4]
    for r in range(8):
        ids = before[r : r + 1] if r < 4 else own[r - 4 : r - 3]
        one = jnp.where(ids == sign, 1.0, 0.0)
        pick_t[:, r * 128 : (r + 1) * 128] = one.astype(bf16)
        pick[r * 128 : (r + 1) * 128, :] = one.T.astype(bf16)
    forget[...] = 1.0 / (1.0 + jnp.exp(-gate[...]))
    table = lax.dot_general(
        bias[...], picks[...], NN, precision=lax.Precision.HIGHEST, preferred_element_type=f32
    )
    table = table * log2e + mask[...]
    for h in range(HEADS):
        bias_out[h] = table[h : h + 1]


def prepare(places, char_ids, seg_starts, gate_logit, distance_bias, deps=()):
    packed = jnp.concatenate(
        [
            char_ids.reshape(4, 128),
            jnp.broadcast_to(seg_starts, (1, 128)),
            jnp.zeros((3, 128), jnp.int32),
        ],
        axis=0,
    )[None]
    for bit in (1, 2):
        packed = jnp.concatenate(
            [packed, permute(packed, "seq", lambda i, bit=bit: i ^ bit)], axis=0
        )
    beyond = permute(packed, "seq", lambda i: i ^ 4)
    ins = (
        packed,
        beyond,
        gate_logit.reshape(1, D),
        distance_bias.reshape(HEADS, BUCKETS),
        jnp.asarray(lane_pick()),
        jnp.asarray(lane_hidden()),
    )
    outs = (
        like(jnp.int32, 2),
        like(jnp.int32, 1),
        like(f32, 8, VOCAB, 128),
        like(f32, 8, 1, VOCAB),
        like(bf16, CONTEXT, VOCAB),
        like(bf16, VOCAB, CONTEXT),
        like(f32, 1, D),
        like(f32, HEADS, 1, CONTEXT),
    )
    return pl.pallas_call(
        prepare_kernel,
        grid_spec=pltpu.PrefetchScalarGridSpec(
            num_scalar_prefetch=1,
            grid=(1,),
            in_specs=[whole(a) for a in ins]
            + [pl.BlockSpec(memory_space=pl.ANY)] * len(deps),
            out_specs=[pl.BlockSpec(memory_space=pltpu.SMEM)] * 2
            + [whole(o) for o in outs[2:]],
        ),
        out_shape=list(outs),
        compiler_params=params(),
        cost_estimate=cost(1e3, 1e3),
        name="prepare",
    )(places, *ins, *deps)


def plain_prepare(char_ids, seg_starts, gate_logit, distance_bias):
    windows = lax.axis_size("seq")
    here = lax.axis_index("seq")
    packed = jnp.concatenate(
        [char_ids.reshape(4, 128), jnp.broadcast_to(seg_starts, (1, 128))], axis=0
    )
    everyone = lax.all_gather(packed, "seq")
    ids_all = everyone[:, :4].reshape(windows, WINDOW)
    flags = everyone[:, 4, 0]
    order = jnp.arange(windows, dtype=jnp.int32)
    first = jnp.max(jnp.where((flags > 0) & (order <= here), order, 0))
    span = jnp.stack([first, here]).astype(jnp.int32)
    live = (1 - seg_starts.reshape(1)).astype(jnp.int32)
    vocab = jnp.arange(VOCAB, dtype=jnp.int32)
    counts = jnp.sum(
        (ids_all[:, :, None] == vocab[None, None, :]).astype(f32), axis=1
    )
    before = lax.dynamic_index_in_dim(ids_all, jnp.maximum(here - 1, 0), 0, False)
    context_ids = jnp.concatenate([before, char_ids.reshape(-1)])
    bias_rows = jnp.dot(
        distance_bias.reshape(HEADS, BUCKETS),
        jnp.asarray(lane_pick()),
        precision=lax.Precision.HIGHEST,
    ) * log2e + jnp.asarray(lane_hidden())
    return (
        span,
        live,
        jnp.broadcast_to(counts[:, :, None], (windows, VOCAB, 128)),
        counts[:, None, :],
        (context_ids[:, None] == vocab[None, :]).astype(bf16),
        (vocab[:, None] == context_ids[None, :]).astype(bf16),
        jax.nn.sigmoid(gate_logit).reshape(1, D),
        bias_rows.reshape(HEADS, 1, CONTEXT),
    )


def body(
    char_ids,
    seg_starts,
    char_table,
    norm_gain,
    qkv_weight,
    distance_bias,
    state_query,
    state_init,
    state_gain,
    state_kv_weight,
    gate_logit,
    out_weight,
    mlp_gain,
    up_weight,
    down_weight,
    cotangent,
):
    windows = lax.axis_size("seq")
    here = lax.axis_index("seq")
    norm_gain, state_gain, mlp_gain = (
        t.reshape(1, D) for t in (norm_gain, state_gain, mlp_gain)
    )
    table_unit, table_inv, normed_table, qkv_table = table_forward(
        char_table, norm_gain, qkv_weight
    )

    characters = (char_ids, seg_starts, gate_logit, distance_bias)
    if fitted():
        places = places_of()
        prepared = prepare(places, *characters, (qkv_table,))
    else:
        prepared = plain_prepare(*characters)
    span, live, counts, count_rows, pick, pick_t, forget, bias_rows = prepared
    states_in, forget_slope, lowest = summary_forward(
        span, state_query, qkv_table, counts, count_rows, state_init, forget
    )
    state_unit, state_inv, state_normed, state_kv = states_forward(
        states_in, state_gain, state_kv_weight
    )
    mixed, lse = attention_forward(
        live, pick, pick_t, qkv_table, state_kv, state_kv, bias_rows
    )
    residual, mlp_unit, mlp_inv, mlp_in, mlp_split = residual_forward(
        places if fitted() else jnp.zeros(6, jnp.int32),
        mixed,
        out_weight,
        pick,
        char_table,
        mlp_gain,
    )
    upstream = cotangent.reshape(WINDOW, D)

    close_up = fitted_tail if fitted() else plain_tail
    return close_up(dict(locals()))


def fitted_tail(values):
    v = types.SimpleNamespace(**values)
    places = v.places
    weights = (v.upstream, v.up_weight, v.down_weight)

    out, gx = v.residual, jnp.zeros((WINDOW, D), f32)
    traffic = Traffic(places)
    parts, deps = [], ()
    for part in range(4):
        send, keep, out, gx = mlp_packed(
            part, places, v.mlp_in, v.mlp_split, *weights, out, gx, deps
        )
        if part:
            second = parts[part - 2] if part > 1 else ()
            mark = traffic.boundary((gx,), parts[part - 1], second, swap=[send])
            deps = (mark,)
            came = traffic.swapped[0]
        else:
            came = traffic.swap(send)
        parts.append(wings(keep, came))
    layer_out = out.astype(bf16).reshape(1, WINDOW, D)
    front = Column(parts[0] + parts[1])
    back = Column(parts[2] + parts[3])

    grad_mlp_gain, grad_out, grad_mixed, rows_sum = feed_back(v, gx, (mark,))
    gsk, gsv, gq, inner = state_backward(
        v.pick, v.qkv_table, v.state_kv, v.lse, v.mixed, grad_mixed
    )
    mark = traffic.boundary((inner,), parts[3], parts[2], near=[front])
    grad_k, grad_v, grad_state_gain, local, grad_gate = states_back(v, gsk, gsv, (mark,))
    send, keep = packed_pair(
        "pack_middle",
        places,
        [t.reshape(8, 128, D) for t in (grad_k, grad_v, grad_out)],
    )
    middle = wings(keep, traffic.swap(send))
    summary_args = (
        v.span, v.state_query, v.qkv_table, v.counts, v.count_rows, local, v.forget, v.lowest
    )
    onto = summary_backward(*summary_args, (send,), 0)
    mark = traffic.boundary((onto[0],), middle, parts[3], far=[front])
    g, gsq, ginit = summary_backward(*summary_args, (mark,), 1, onto)
    mark = traffic.boundary((g,), (), middle, near=[back], close=[front])
    send, keep = packed_pair(
        "pack_states", places, [gsq.reshape(8, 64, D), ginit.reshape(8, 64, D)], (mark,)
    )
    states = wings(keep, traffic.swap(send))
    tokens_args = (
        v.live, v.pick, v.pick_t, v.qkv_table, v.bias_rows, v.lse, inner, grad_mixed, gq
    )
    onto = token_backward(*tokens_args, (send,), 0)
    mark = traffic.boundary((onto[1],), states, far=[back])
    front_rows = traffic.spread(front.own)
    g_tokens, fold = token_backward(*tokens_args, (mark,), 1, onto)
    side, rest = Column(middle), Column(states)
    mark = traffic.boundary((fold,), (), states, near=[side], close=[back])
    send, keep = pack_rows(
        places, mark, g_tokens, g, rows_sum, grad_mlp_gain, grad_state_gain, grad_gate, fold
    )
    rows = wings(keep, traffic.swap(send))
    last = Column(rows)
    traffic.boundary((), rows, near=[rest], far=[side])
    traffic.boundary((), (), rows, far=[rest])
    back_rows = traffic.spread(back.own, 2)
    traffic.boundary((), near=[last], join=[side, rest])
    side_own = traffic.joined
    traffic.boundary((), far=[last])
    side_rows = traffic.spread(side_own)
    grad_down, grad_up, mark = unpack_mlp(places, [front_rows, back_rows])
    traffic.boundary((mark,), close=[last])
    beside = permute(last.own, "seq", lambda i: i ^ 2)
    row_ring = [
        last.own,
        beside,
        permute(last.own, "seq", lambda i: i ^ 4),
        permute(beside, "seq", lambda i: i ^ 4),
    ]
    ring = ring_rows(places, row_ring)
    ring_parts = traffic.spread(ring)
    grad_state_kv, grad_out, grad_state_query, grad_state_init, mark = unpack(
        "unpack_side",
        places,
        side_rows,
        [(0, 48, XI, 0), (48, 48, YI, 192), (96, 16, XI, 384), (112, 16, YI, 448)],
        [
            ((128, 2 * D), [(0, 128, 0, 0), (128, 128, 0, D)]),
            ((128, D), [(256, 128, 0, 0)]),
            ((64, D), [(384, 64, 0, 0)]),
            ((64, D), [(448, 64, 0, 0)]),
            ((8, 128), []),
        ],
    )
    mine = stack_rows(places, ring_parts, (mark,))
    other = swap_core(mine)
    grad_qkv, grad_norm_gain, grad_table, small = last_products(
        places,
        mine,
        other,
        v.normed_table,
        v.table_unit,
        v.qkv_weight,
        v.table_inv,
        v.norm_gain,
    )
    return (
        layer_out,
        grad_table,
        grad_norm_gain.reshape(-1),
        grad_qkv,
        small[3, :32],
        grad_state_query,
        grad_state_init,
        small[1],
        grad_state_kv,
        small[2],
        grad_out,
        small[0],
        grad_up,
        grad_down,
    )


def plain_tail(values):
    v = types.SimpleNamespace(**values)
    windows, here = v.windows, v.here
    shard = lambda n: n // windows
    out, gx = v.residual, jnp.zeros((WINDOW, D), f32)
    grads_down, grads_up = [], []
    for part in range(SPLITS):
        gd, gu, out, gx = mlp_part(
            part, v.mlp_in, v.upstream, v.up_weight, v.down_weight, out, gx
        )
        grads_down.append(gd)
        grads_up.append(gu)
    layer_out = out.astype(bf16).reshape(1, WINDOW, D)
    grad_mlp_gain, grad_out, grad_mixed, rows_sum = feed_back(v, gx)
    gsk, gsv, gq, inner = state_backward(
        v.pick, v.qkv_table, v.state_kv, v.lse, v.mixed, grad_mixed
    )
    grad_k, grad_v, grad_state_gain, local, grad_gate = states_back(v, gsk, gsv)
    g, gsq, ginit = summary_backward(
        v.span, v.state_query, v.qkv_table, v.counts, v.count_rows, local, v.forget,
        v.lowest,
    )
    g_tokens, fold = token_backward(
        v.live, v.pick, v.pick_t, v.qkv_table, v.bias_rows, v.lse, inner, grad_mixed, gq
    )
    g = (g.astype(f32) + g_tokens).astype(bf16)
    sharded = lambda t: total_of(t.reshape(windows, -1, t.shape[-1]))
    full = jnp.stack([t.reshape(-1, TILE, D) for t in grads_down], axis=1)
    grad_down = sharded(full.reshape(FF, D))
    full = jnp.stack([t.reshape(D, -1, TILE) for t in grads_up], axis=2)
    grad_up = sharded(full.reshape(D, FF))
    grad_state_kv = sharded(jnp.concatenate([grad_k, grad_v], axis=1))
    small = jnp.concatenate(
        [
            t.reshape(windows, -1)
            for t in (grad_mlp_gain, grad_state_gain, grad_gate, fold[:, 0, :BUCKETS])
        ],
        axis=1,
    )
    small = total_of(small[:, None, :])[0]
    cut = shard(D)
    all_rows = lax.psum(g, ("dp", "seq"))
    grad_rows = jnp.concatenate(
        [
            all_rows[:, :, t * 128 : (t + 1) * 128].transpose(1, 0, 2).reshape(VOCAB, D)
            for t in range(3)
        ],
        axis=1,
    )
    mine = lax.dynamic_slice_in_dim(v.normed_table, here * cut, cut, 1)
    weight_rows = lax.dynamic_slice_in_dim(v.qkv_weight, here * cut, cut, 0)
    unit_cols = lax.dynamic_slice_in_dim(v.table_unit, here * cut, cut, 1)
    at = here * shard(VOCAB)
    take = lambda t: lax.dynamic_slice_in_dim(t, at, shard(VOCAB), 0)
    grad_table = sharded(rows_sum) + norm_back(
        take(v.table_unit),
        take(v.table_inv)[:, :1],
        v.norm_gain,
        dot(take(grad_rows), v.qkv_weight, NT),
    )
    return (
        layer_out,
        grad_table,
        jnp.sum(dot(grad_rows, weight_rows, NT) * unit_cols, axis=0),
        dot(mine, grad_rows, TN),
        small[3 * cut :],
        sharded(gsq),
        sharded(ginit),
        small[cut : 2 * cut],
        grad_state_kv,
        small[2 * cut : 3 * cut],
        sharded(grad_out),
        small[:cut],
        grad_up,
        grad_down,
    )


def solution(mesh):
    placed = (P("dp", "seq"), P("dp", "seq")) + (P(),) * 13 + (P("dp", "seq", None),)
    return jax.shard_map(
        body,
        mesh=mesh,
        in_specs=placed,
        out_specs=(
            P("dp", "seq", None),
            P("seq", None),
            P("seq"),
            P("seq", None),
            P("seq"),
            P("seq", None),
            P("seq", None),
            P("seq"),
            P("seq", None),
            P("seq"),
            P("seq", None),
            P("seq"),
            P("seq", None),
            P("seq", None),
        ),
        check_vma=False,
    )
```

```python
import functools
import math
import types

import jax
import jax.numpy as jnp
import numpy as np
from jax import lax
from jax.experimental import pallas as pl
from jax.experimental.pallas import tpu as pltpu
from jax.sharding import PartitionSpec as P

D = 1024
HEADS = 8
HEAD_DIM = 128
FF = 4096
VOCAB = 256
STATES = 512
WINDOW = 512
BUCKETS = 32
MAX_DISTANCE = 128
CONTEXT = 2 * WINDOW
TILE = 256
SPLITS = 2

epsilon = 1e-05
hidden = -1e30
log2e = math.log2(math.e)
score_scale = 1.0 / math.sqrt(HEAD_DIM)
f32 = jnp.float32
bf16 = jnp.bfloat16

NN = (((1,), (0,)), ((), ()))
NT = (((1,), (1,)), ((), ()))
TN = (((0,), (0,)), ((), ()))


def dot(a, b, dims=NN):
    return lax.dot_general(a, b, dims, preferred_element_type=f32)


def params(mib=18):
    return pltpu.CompilerParams(
        dimension_semantics=("arbitrary",), vmem_limit_bytes=mib * 1024 * 1024
    )


def cost(flops, moved, exps=0):
    return pl.CostEstimate(
        flops=int(flops), bytes_accessed=int(moved), transcendentals=int(exps)
    )


def norm_parts(value):
    centre = jnp.mean(value, axis=-1, keepdims=True)
    offset = value - centre
    spread = jnp.mean(offset * offset, axis=-1, keepdims=True)
    inv = lax.rsqrt(spread + epsilon)
    return offset * inv, inv


def norm_back(unit, inv, gain, upstream):
    scaled = upstream * gain
    a = jnp.mean(scaled, axis=-1, keepdims=True)
    b = jnp.mean(scaled * unit, axis=-1, keepdims=True)
    return (scaled - a - unit * b) * inv


def bucket_table():
    distance = np.arange(WINDOW)
    exact_count = BUCKETS // 2
    log_ratio = np.log(np.maximum(distance, 1) / exact_count) / math.log(
        MAX_DISTANCE / exact_count
    )
    far_bucket = exact_count + np.floor(log_ratio * (BUCKETS - exact_count)).astype(
        np.int64
    )
    return np.where(
        distance < exact_count, distance, np.minimum(far_bucket, BUCKETS - 1)
    )


def lane_pick():
    pick = np.zeros((BUCKETS, CONTEXT), np.float32)
    table = bucket_table()
    for m in range(1, WINDOW + 1):
        pick[table[WINDOW - m], m] = 1.0
    return pick


def lane_hidden():
    m = np.arange(CONTEXT)
    return np.where((m >= 1) & (m <= WINDOW), 0.0, hidden).astype(np.float32)[None]


smallest_sum = 2.0**-80


def shared_exp(lg, there):
    peak = jnp.max(jnp.where(there > 0, lg, hidden), axis=1, keepdims=True)
    return jnp.exp2(jnp.minimum(lg - peak, 0.0)).astype(bf16)


def window_sides(v, n):
    return jnp.concatenate([v.astype(f32) * n, n], axis=1).astype(bf16)


def own_weights(lg, n_row):
    x = lg + jnp.where(n_row > 0, jnp.log2(jnp.maximum(n_row, 1.0)), hidden)
    p = jnp.exp2(x - jnp.max(x, axis=1, keepdims=True))
    return p / jnp.sum(p, axis=1, keepdims=True)


def characters_there(span, rows):
    return lax.fori_loop(
        span[0], span[1], lambda w, t: t + rows[w], jnp.zeros((1, VOCAB), f32)
    )


TOGETHER = 4


def lanes_of(i):
    return slice(i * HEAD_DIM, (i + 1) * HEAD_DIM)


def summary_forward_kernel(
    span, sq, kt, vt, counts, rows, init, forget, state_out, y_out, low_out, a_s, y_s
):
    heads = range(TOGETHER)
    f = forget[...]
    v = [vt[:, lanes_of(i)] for i in heads]

    def scores(i):
        return dot(sq[:, lanes_of(i)], kt[:, lanes_of(i)], NT) * (score_scale * log2e)

    def begin():
        a_s[...] = init[...].astype(f32)
        y_s[...] = jnp.zeros_like(y_s)

    def move(i, u):
        at = lanes_of(i)
        a = a_s[:, at]
        y_s[:, at] = a - u + f[:, at] * y_s[:, at]
        a_s[:, at] = u + f[:, at] * (a - u)

    begin()
    there = characters_there(span, rows)
    e = [shared_exp(scores(i), there) for i in heads]

    def step(w, low):
        n = counts[w]
        for i in heads:
            both = dot(e[i], window_sides(v[i], n))
            z = both[:, HEAD_DIM:]
            move(i, both[:, :HEAD_DIM] / jnp.maximum(z, smallest_sum))
            low = jnp.minimum(low, jnp.min(z.reshape(STATES // 8, 8, 128), axis=0))
        return low

    low = lax.fori_loop(span[0], span[1], step, jnp.full((8, 128), 1.0, f32))
    low_out[0] = low

    @pl.when(jnp.min(low) < smallest_sum)
    def _():
        begin()
        for i in heads:
            lg = scores(i)

            def slow(w, _):
                move(i, dot(own_weights(lg, rows[w]).astype(bf16), v[i]))
                return 0

            lax.fori_loop(span[0], span[1], slow, 0)

    state_out[...] = a_s[...]
    y_out[...] = y_s[...]


def summary_specs(windows):
    wide = TOGETHER * HEAD_DIM
    head = lambda k: (lambda h, s: (0, k * HEADS // TOGETHER + h))
    return [
        pl.BlockSpec((STATES, wide), head(0)),
        pl.BlockSpec((VOCAB, wide), head(1)),
        pl.BlockSpec((VOCAB, wide), head(2)),
        pl.BlockSpec((windows, VOCAB, 128), lambda h, s: (0, 0, 0)),
        pl.BlockSpec((windows, 1, VOCAB), lambda h, s: (0, 0, 0)),
        pl.BlockSpec((STATES, wide), head(0)),
        pl.BlockSpec((1, wide), head(0)),
    ]


def summary_forward(span, state_query, qkv_table, counts, rows, state_init, forget):
    states = pl.BlockSpec((STATES, TOGETHER * HEAD_DIM), lambda h, s: (0, h))
    return pl.pallas_call(
        summary_forward_kernel,
        grid_spec=pltpu.PrefetchScalarGridSpec(
            num_scalar_prefetch=1,
            grid=(HEADS // TOGETHER,),
            in_specs=summary_specs(counts.shape[0]),
            out_specs=[states, states, pl.BlockSpec((1, 8, 128), lambda h, s: (h, 0, 0))],
            scratch_shapes=[pltpu.VMEM((STATES, TOGETHER * HEAD_DIM), f32)] * 2,
        ),
        out_shape=[
            jax.ShapeDtypeStruct((STATES, D), f32),
            pltpu.HBM((STATES, D), f32),
            jax.ShapeDtypeStruct((HEADS // TOGETHER, 8, 128), f32),
        ],
        compiler_params=params(),
        cost_estimate=cost(1e3, 1e3),
        name="summary_forward",
    )(span, state_query, qkv_table, qkv_table, counts, rows, *stays(state_init), forget)


def summary_backward_kernel(span, sq, kt, vt, counts, rows, local, forget, low, *rest):
    g_out, gsq_out, ginit_out, g_s, gs_s, gv_s, gs16, e_s, e_t = rest[-9:]
    heads = range(TOGETHER)
    f = forget[...]
    v = [vt[:, lanes_of(i)] for i in heads]
    g_s[...] = local[...]
    gs_s[...] = jnp.zeros_like(gs_s)
    gv_s[...] = jnp.zeros_like(gv_s)
    first, here = span[0], span[1]
    fast = jnp.min(low[0]) >= smallest_sum

    def scores(i):
        return dot(sq[:, lanes_of(i)], kt[:, lanes_of(i)], NT) * (score_scale * log2e)

    def carried(i):
        at = lanes_of(i)
        g = g_s[:, at]
        fg = f[:, at] * g
        g_s[:, at] = fg
        return g - fg

    @pl.when(fast)
    def _():
        there = characters_there(span, rows)
        for i in heads:
            e = shared_exp(scores(i), there)
            e_s[i] = e
            e_t[i] = e.astype(f32).T.astype(bf16)
        lane = lax.broadcasted_iota(jnp.int32, (STATES, HEAD_DIM), 1)

        def step(t, _):
            w = here - 1 - t
            n = counts[w]
            for i in heads:
                sides = window_sides(v[i], n)
                both = dot(e_s[i], sides)
                part = 1.0 / both[:, HEAD_DIM:]
                gu = (carried(i) * part).astype(bf16)
                inner = gu.astype(f32) * (both[:, :HEAD_DIM] * part)
                inner = inner + pltpu.roll(inner, HEAD_DIM // 2, 1)
                high = inner.astype(bf16)
                tail = jnp.where(
                    lane < HEAD_DIM // 2, high.astype(f32), inner - high.astype(f32)
                )
                gs_s[i] += dot(
                    jnp.concatenate([gu, (-tail).astype(bf16)], axis=1), sides, NT
                )
                gv_s[i] += n * dot(e_t[i], gu)
            return 0

        lax.fori_loop(0, here - first, step, 0)
        for i in heads:
            gs16[i] = (gs_s[i] * e_s[i].astype(f32) * score_scale).astype(bf16)

    @pl.when(jnp.logical_not(fast))
    def _():
        for i in heads:
            lg = scores(i)

            def slow(t, _):
                w = here - 1 - t
                p = own_weights(lg, rows[w])
                gu = carried(i).astype(bf16)
                pd = p * dot(gu, v[i], NT)
                gs_s[i] += pd - p * jnp.sum(pd, axis=1, keepdims=True)
                gv_s[i] += dot(p.astype(bf16), gu, TN)
                return 0

            lax.fori_loop(0, here - first, slow, 0)
            gs16[i] = (gs_s[i] * score_scale).astype(bf16)

    for i in heads:
        gs = gs16[i]
        at = lanes_of(i)
        g_out[i, :, :128] = jnp.zeros((VOCAB, 128), bf16)
        g_out[i, :, 128:256] = dot(gs, sq[:, at], TN).astype(bf16)
        g_out[i, :, 256:] = gv_s[i].astype(bf16)
        gsq_out[:, at] = dot(gs, kt[:, at]).astype(bf16)
    ginit_out[...] = g_s[...].astype(bf16)


def summary_backward(
    span, state_query, qkv_table, counts, rows, local, forget, low, deps=(), half=None, onto=()
):
    start, steps = (0, HEADS // TOGETHER) if half is None else (half, 1)
    deps = (*deps, *onto)
    wide = TOGETHER * HEAD_DIM
    windows = counts.shape[0]
    head = lambda k: (lambda h, s: (0, k * HEADS // TOGETHER + start + h))
    first = lambda h, s: (start + h, 0, 0)
    states = pl.BlockSpec((STATES, wide), head(0))
    return pl.pallas_call(
        summary_backward_kernel,
        grid_spec=pltpu.PrefetchScalarGridSpec(
            num_scalar_prefetch=1,
            grid=(steps,),
            in_specs=[
                states,
                pl.BlockSpec((VOCAB, wide), head(1)),
                pl.BlockSpec((VOCAB, wide), head(2)),
                pl.BlockSpec((windows, VOCAB, 128), lambda h, s: (0, 0, 0)),
                pl.BlockSpec((windows, 1, VOCAB), lambda h, s: (0, 0, 0)),
                states,
                pl.BlockSpec((1, wide), head(0)),
                pl.BlockSpec((1, 8, 128), first),
            ]
            + [pl.BlockSpec(memory_space=pl.ANY)] * len(deps),
            out_specs=[pl.BlockSpec((TOGETHER, VOCAB, 384), first), states, states],
            scratch_shapes=[
                pltpu.VMEM((STATES, wide), f32),
                pltpu.VMEM((TOGETHER, STATES, VOCAB), f32),
                pltpu.VMEM((TOGETHER, VOCAB, HEAD_DIM), f32),
                pltpu.VMEM((TOGETHER, STATES, VOCAB), bf16),
                pltpu.VMEM((TOGETHER, STATES, VOCAB), bf16),
                pltpu.VMEM((TOGETHER, VOCAB, STATES), bf16),
            ],
        ),
        out_shape=[
            jax.ShapeDtypeStruct((HEADS, VOCAB, 384), bf16),
            jax.ShapeDtypeStruct((STATES, D), bf16),
            jax.ShapeDtypeStruct((STATES, D), bf16),
        ],
        input_output_aliases={9 + len(deps) - 3 + i: i for i in range(len(onto))},
        compiler_params=params(),
        cost_estimate=cost(1e3, 1e3),
        name="summary_backward",
    )(span, state_query, qkv_table, qkv_table, counts, rows, local, forget, low, *deps)


def each_head(kernel, heads, kinds, *refs):
    kinds = "w" * (len(refs) - len(kinds)) + kinds
    for i in range(heads):
        views = {
            "l": lambda r, i=i: r.at[:, lanes_of(i)],
            "b": lambda r, i=i: r.at[i : i + 1],
            "s": lambda r, i=i: r.at[i],
            "w": lambda r: r,
        }
        kernel(*(views[kind](r) for kind, r in zip(kinds, refs)))


def bias_tile(row):
    spread = jnp.broadcast_to(row, (TILE, CONTEXT))
    shifted = pltpu.roll(spread, 0, 1, stride=1, stride_axis=0)
    return shifted[:, : 3 * TILE].T


def attention_forward_kernel(
    live, pick, pick_t, qt, kt, vt, sk, sv, bias_row, mixed_out, lse_out, bias
):
    bias[...] = bias_tile(bias_row[0])
    prev_add = jnp.where(live[0] > 0, 0.0, hidden).astype(f32)
    keys = dot(pick[...], kt[...]).astype(bf16)
    values_t = dot(vt[...], pick_t[...], TN).astype(bf16)
    query = dot(pick[WINDOW:, :], qt[...]).astype(bf16)
    state_values_t = sv[...].astype(f32).T.astype(bf16)
    for j in range(WINDOW // TILE):
        q = query[j * TILE : (j + 1) * TILE]
        scores = []
        for rel in range(3):
            kt_i = j + rel
            s = (
                dot(keys[kt_i * TILE : (kt_i + 1) * TILE], q, NT)
                * (score_scale * log2e)
                + bias[rel * TILE : (rel + 1) * TILE]
            )
            if kt_i * TILE < WINDOW:
                s = s + prev_add
            scores.append(s)
        for st in range(STATES // TILE):
            scores.append(
                dot(sk[st * TILE : (st + 1) * TILE, :], q, NT) * (score_scale * log2e)
            )
        peak = functools.reduce(
            jnp.maximum, [jnp.max(s, axis=0, keepdims=True) for s in scores]
        )
        total = jnp.zeros((1, TILE), f32)
        out = jnp.zeros((HEAD_DIM, TILE), f32)
        for i, s in enumerate(scores):
            p = jnp.exp2(s - peak)
            total = total + jnp.sum(p, axis=0, keepdims=True)
            if i < 3:
                v = values_t[:, (j + i) * TILE : (j + i + 1) * TILE]
            else:
                v = state_values_t[:, (i - 3) * TILE : (i - 2) * TILE]
            out = out + dot(v, p.astype(bf16))
        out = out * (1.0 / total)
        mixed_out[j * TILE : (j + 1) * TILE, :] = out.T.astype(bf16)
        lse_out[0, :, j * TILE : (j + 1) * TILE] = peak + jnp.log2(total)


def attention_forward(live, pick, pick_t, qkv_table, sk, sv, bias_rows):
    heads, wide = 4, 4 * HEAD_DIM
    head = lambda k: (lambda h, s: (0, k * HEADS // heads + h))
    whole = lambda *shape: pl.BlockSpec(shape, lambda h, s: (0,) * len(shape))
    return pl.pallas_call(
        functools.partial(each_head, attention_forward_kernel, heads, "wwwlllllblbs"),
        grid_spec=pltpu.PrefetchScalarGridSpec(
            num_scalar_prefetch=1,
            grid=(HEADS // heads,),
            in_specs=[
                whole(CONTEXT, VOCAB),
                whole(VOCAB, CONTEXT),
                pl.BlockSpec((VOCAB, wide), head(0)),
                pl.BlockSpec((VOCAB, wide), head(1)),
                pl.BlockSpec((VOCAB, wide), head(2)),
                pl.BlockSpec((STATES, wide), head(0)),
                pl.BlockSpec((STATES, wide), head(1)),
                pl.BlockSpec((heads, 1, CONTEXT), lambda h, s: (h, 0, 0)),
            ],
            out_specs=[
                pl.BlockSpec((WINDOW, wide), head(0)),
                pl.BlockSpec((heads, 1, WINDOW), lambda h, s: (h, 0, 0)),
            ],
            scratch_shapes=[pltpu.VMEM((heads, 3 * TILE, TILE), f32)],
        ),
        out_shape=[
            jax.ShapeDtypeStruct((WINDOW, D), bf16),
            jax.ShapeDtypeStruct((HEADS, 1, WINDOW), f32),
        ],
        compiler_params=params(),
        cost_estimate=cost(1e3, 1e3),
        name="attention_forward",
    )(live, pick, pick_t, qkv_table, qkv_table, qkv_table, sk, sv, bias_rows)


def back_tile(s, dp, shift, inner):
    p = jnp.exp2(s - shift)
    return p, p * (dp - inner)


def state_backward_kernel(pick, qt, sk, sv, lse, mixed, grad, *rest):
    gsk_out, gsv_out, gq_out, inner_out = rest[-4:]
    query = dot(pick[WINDOW:, :], qt[...]).astype(bf16)
    state_keys_t = sk[...].astype(f32).T.astype(bf16)
    inner_all = jnp.sum(
        (mixed[...].astype(f32) * grad[...].astype(f32)).T, axis=0, keepdims=True
    )
    inner_out[0] = inner_all
    blocks = WINDOW // TILE
    gq = [jnp.zeros((HEAD_DIM, TILE), f32) for _ in range(blocks)]
    for st in range(STATES // TILE):
        at = slice(st * TILE, (st + 1) * TILE)
        gk = jnp.zeros((TILE, HEAD_DIM), f32)
        gv = jnp.zeros((TILE, HEAD_DIM), f32)
        for j in range(blocks):
            rows = slice(j * TILE, (j + 1) * TILE)
            p, gs = back_tile(
                dot(sk[at, :], query[rows], NT) * (score_scale * log2e),
                dot(sv[at, :], grad[rows, :], NT),
                lse[0, :, rows],
                inner_all[:, rows],
            )
            gs16 = gs.astype(bf16)
            gq[j] = gq[j] + dot(state_keys_t[:, at], gs16)
            gk = gk + dot(gs16, query[rows])
            gv = gv + dot(p.astype(bf16), grad[rows, :])
        gsk_out[at, :] = (gk * score_scale).astype(bf16)
        gsv_out[at, :] = gv.astype(bf16)
    for j in range(blocks):
        gq_out[0, :, j * TILE : (j + 1) * TILE] = gq[j]


def state_backward(pick, qkv_table, state_kv, lse, mixed, grad, deps=()):
    heads, wide = 4, 4 * HEAD_DIM
    head = lambda k: (lambda h: (0, k * HEADS // heads + h))
    tokens = pl.BlockSpec((WINDOW, wide), head(0))
    states = pl.BlockSpec((STATES, wide), head(0))
    row = pl.BlockSpec((heads, 1, WINDOW), lambda h: (h, 0, 0))
    return pl.pallas_call(
        functools.partial(
            each_head, state_backward_kernel, heads, "wlllbll" + "w" * len(deps) + "llbb"
        ),
        grid=(HEADS // heads,),
        in_specs=[
            pl.BlockSpec((CONTEXT, VOCAB), lambda h: (0, 0)),
            pl.BlockSpec((VOCAB, wide), head(0)),
            pl.BlockSpec((STATES, wide), head(0)),
            pl.BlockSpec((STATES, wide), head(1)),
            row,
            tokens,
            tokens,
        ]
        + [pl.BlockSpec(memory_space=pl.ANY)] * len(deps),
        out_specs=[
            states,
            states,
            pl.BlockSpec((heads, HEAD_DIM, WINDOW), lambda h: (h, 0, 0)),
            row,
        ],
        out_shape=[
            pltpu.HBM((STATES, D), bf16),
            pltpu.HBM((STATES, D), bf16),
            jax.ShapeDtypeStruct((HEADS, HEAD_DIM, WINDOW), f32),
            jax.ShapeDtypeStruct((HEADS, 1, WINDOW), f32),
        ],
        compiler_params=params(),
        cost_estimate=cost(1e3, 1e3),
        name="state_backward",
    )(pick, qkv_table, state_kv, state_kv, lse, mixed, grad, *deps)


def token_backward_kernel(
    live, pick, pick_t, qt, kt, vt, bias_row, lse, inner, grad, gq_in, buckets, *rest
):
    g_out, fold_out, bias, bias_grad = rest[-4:]
    bias[...] = bias_tile(bias_row[0])
    bias_grad[...] = jnp.zeros_like(bias_grad)
    prev_add = jnp.where(live[0] > 0, 0.0, hidden).astype(f32)
    both = dot(pick[...], jnp.concatenate([kt[...], vt[...]], axis=1)).astype(bf16)
    keys = both[:, :HEAD_DIM]
    values = both[:, HEAD_DIM:]
    keys_t = dot(kt[...], pick_t[...], TN).astype(bf16)
    query = dot(pick[WINDOW:, :], qt[...]).astype(bf16)
    blocks = WINDOW // TILE
    gq = [gq_in[0, :, j * TILE : (j + 1) * TILE] for j in range(blocks)]
    sums = jnp.zeros((VOCAB, 2 * HEAD_DIM), f32)
    for tile in range(CONTEXT // TILE):
        at = slice(tile * TILE, (tile + 1) * TILE)
        gk = jnp.zeros((TILE, HEAD_DIM), f32)
        gv = jnp.zeros((TILE, HEAD_DIM), f32)
        for j in range(blocks):
            rel = tile - j
            if not 0 <= rel < 3:
                continue
            rows = slice(j * TILE, (j + 1) * TILE)
            rels = slice(rel * TILE, (rel + 1) * TILE)
            shift = lse[0, :, rows]
            if tile * TILE < WINDOW:
                shift = shift - prev_add
            p, gs = back_tile(
                dot(keys[at], query[rows], NT) * (score_scale * log2e) + bias[rels],
                dot(values[at], grad[rows, :], NT),
                shift,
                inner[0, :, rows],
            )
            gs16 = gs.astype(bf16)
            gq[j] = gq[j] + dot(keys_t[:, at], gs16)
            bias_grad[rels] += gs
            gk = gk + dot(gs16, query[rows])
            gv = gv + dot(p.astype(bf16), grad[rows, :])
        pair = jnp.concatenate([gk * score_scale, gv], axis=1).astype(bf16)
        sums = sums + dot(pick_t[:, at], pair)
    g_out[0, :, HEAD_DIM:] = sums
    total = jnp.zeros((HEAD_DIM, VOCAB), f32)
    for j in range(blocks):
        rows = slice(WINDOW + j * TILE, WINDOW + (j + 1) * TILE)
        total = total + dot((gq[j] * score_scale).astype(bf16), pick[rows, :])
    g_out[0, :, :HEAD_DIM] = total.T
    rows = jnp.concatenate(
        [bias_grad[...].T, jnp.zeros((TILE, CONTEXT - 3 * TILE), f32)], axis=1
    )
    count = TILE
    while count > 8:
        count //= 2
        rows = rows[:count] + pltpu.roll(rows[count:], CONTEXT - count, 1)
    folded = rows[0:1]
    for r in range(1, 8):
        folded = folded + pltpu.roll(rows, CONTEXT - r, 1)[r : r + 1]
    pieces = []
    left = folded
    for _ in range(3):
        piece = left.astype(bf16)
        pieces.append(piece)
        left = left - piece.astype(f32)
    pieces = jnp.concatenate(pieces + [jnp.zeros((5, CONTEXT), bf16)], axis=0)
    fold_out[0] = jnp.sum(dot(pieces, buckets[...]), axis=0, keepdims=True)


def token_backward(
    live, pick, pick_t, qkv_table, bias_rows, lse, inner, grad, gq, deps=(), half=None, onto=()
):
    heads, wide = 4, 4 * HEAD_DIM
    count = HEADS // heads if half is None else HEADS // heads // 2
    low = 0 if half is None else half * count
    deps = (*deps, *onto)
    head = lambda k: (lambda h, s: (0, k * HEADS // heads + low + h))
    by_head = lambda *shape: pl.BlockSpec((heads,) + shape, lambda h, s: (low + h, 0, 0))
    flat = lambda *shape: pl.BlockSpec(shape, lambda h, s: (0,) * len(shape))
    return pl.pallas_call(
        functools.partial(
            each_head, token_backward_kernel, heads, "wwwlllbbblbw" + "w" * len(deps) + "bbss"
        ),
        grid_spec=pltpu.PrefetchScalarGridSpec(
            num_scalar_prefetch=1,
            grid=(count,),
            in_specs=[
                flat(CONTEXT, VOCAB),
                flat(VOCAB, CONTEXT),
                pl.BlockSpec((VOCAB, wide), head(0)),
                pl.BlockSpec((VOCAB, wide), head(1)),
                pl.BlockSpec((VOCAB, wide), head(2)),
                by_head(1, CONTEXT),
                by_head(1, WINDOW),
                by_head(1, WINDOW),
                pl.BlockSpec((WINDOW, wide), head(0)),
                by_head(HEAD_DIM, WINDOW),
                flat(CONTEXT, 128),
            ]
            + [pl.BlockSpec(memory_space=pl.ANY)] * len(deps),
            out_specs=[by_head(VOCAB, 384), by_head(1, 128)],
            scratch_shapes=[
                pltpu.VMEM((heads, 3 * TILE, TILE), f32),
                pltpu.VMEM((heads, 3 * TILE, TILE), f32),
            ],
        ),
        out_shape=[
            jax.ShapeDtypeStruct((HEADS, VOCAB, 384), f32),
            jax.ShapeDtypeStruct((HEADS, 1, 128), f32),
        ],
        input_output_aliases={12 + len(deps) - 2 + i: i for i in range(len(onto))},
        compiler_params=params(),
        cost_estimate=cost(1e3, 1e3),
        name="token_backward",
    )(
        live,
        pick,
        pick_t,
        qkv_table,
        qkv_table,
        qkv_table,
        bias_rows,
        lse,
        inner,
        grad,
        gq,
        jnp.asarray(np.pad(lane_pick().T, ((0, 0), (0, 96))), bf16),
        *deps,
    )


def mlp_kernel(x, cot, up, down, out_in, gx_in, gd_out, gu_out, out, gx, xt):
    @pl.when(pl.program_id(0) == 0)
    def _():
        out[...] = out_in[...]
        gx[...] = gx_in[...]
        xt[...] = x[...].astype(f32).T.astype(bf16)

    up_b = up[...]
    down_b = down[...]
    pre = dot(x[...], up_b)
    root = math.sqrt(2.0 / math.pi)
    square = pre * pre
    t = jnp.tanh(root * pre * (1.0 + 0.044715 * square))
    half = 0.5 * (1.0 + t)
    act = (pre * half).astype(bf16)
    slope = half + (0.5 * root) * pre * (1.0 - t * t) * (1.0 + (3 * 0.044715) * square)
    grad_pre = (dot(cot[...], down_b, NT) * slope).astype(bf16)
    out[...] += dot(act, down_b)
    gx[...] += dot(grad_pre, up_b, NT)
    gd_out[...] = dot(act, cot[...], TN).astype(bf16)
    gu_out[...] = dot(xt[...], grad_pre).astype(bf16)


def mlp_part(part, x, cot, up, down, out, gx):
    count = FF // SPLITS // TILE
    whole = pl.BlockSpec((WINDOW, D), lambda s: (0, 0))
    return pl.pallas_call(
        mlp_kernel,
        grid=(count,),
        in_specs=[
            whole,
            whole,
            pl.BlockSpec((D, TILE), lambda s: (0, SPLITS * s + part)),
            pl.BlockSpec((TILE, D), lambda s: (SPLITS * s + part, 0)),
            whole,
            whole,
        ],
        out_specs=[
            pl.BlockSpec((TILE, D), lambda s: (s, 0)),
            pl.BlockSpec((D, TILE), lambda s: (0, s)),
            whole,
            whole,
        ],
        out_shape=[
            jax.ShapeDtypeStruct((count * TILE, D), bf16),
            jax.ShapeDtypeStruct((D, count * TILE), bf16),
            jax.ShapeDtypeStruct((WINDOW, D), f32),
            jax.ShapeDtypeStruct((WINDOW, D), f32),
        ],
        scratch_shapes=[pltpu.VMEM((D, WINDOW), bf16)],
        compiler_params=params(),
        cost_estimate=cost(1e3, 1e3),
        name="feed_forward",
    )(x, cot, up, down, out, gx)


def mlp_packed_kernel(
    places, x, xs, cot, up_a, up_b, up_c, up_d, down_a, down_b, down_c, down_d, out_in, gx_in,
    *rest,
):
    send, keep, out, gx, gd_s = rest[-5:]
    core = places[CORE]
    step = pl.program_id(0)

    @pl.when(step == 0)
    def _():
        out[...] = out_in[...]
        gx[...] = gx_in[...]

    up = jnp.concatenate([up_a[...], up_b[...], up_c[...], up_d[...]], axis=1)
    down = jnp.concatenate([down_a[...], down_b[...], down_c[...], down_d[...]], axis=0)
    pre = dot(x[...], up)
    root = math.sqrt(2.0 / math.pi)
    square = pre * pre
    t = jnp.tanh(root * pre * (1.0 + 0.044715 * square))
    half = 0.5 * (1.0 + t)
    act = (pre * half).astype(bf16)
    slope = half + (0.5 * root) * pre * (1.0 - t * t) * (1.0 + (3 * 0.044715) * square)
    grad_pre = (dot(cot[...], down, NT) * slope).astype(bf16)
    out[...] += dot(act, down)
    gx[...] += dot(grad_pre, up, NT)
    gd = dot(act, cot[...], TN).astype(bf16)
    for i in range(2):
        for q in range(2):
            at = (2 * i + q) * 128
            gd_s[q, i] = gd[at : at + 128]
    lanes = pl.ds(pl.multiple_of(step * 512, 512), 512)
    for i in range(2):
        z = 2 * step + i
        send[pl.ds(z, 1), :128, :] = gd_s[pl.ds(1 - core, 1), i]
        keep[pl.ds(z, 1), :128, :] = gd_s[pl.ds(core, 1), i]
    for slot, ref in ((0, send), (1, keep)):
        gu = dot(xs[slot], grad_pre).astype(bf16)
        ref[:, 128:, lanes] = gu.reshape(4, 128, 512)


def mlp_packed(part, places, x, split, cot, up, down, out, gx, deps=()):
    block = pl.BlockSpec((WINDOW, D), lambda g, s: (0, 0))
    packed = pl.BlockSpec((4, 256, D), lambda g, s: (0, 0, 0))
    at = lambda k: (lambda g: (4 * g + k) * 4 + part)
    return pl.pallas_call(
        mlp_packed_kernel,
        grid_spec=pltpu.PrefetchScalarGridSpec(
            num_scalar_prefetch=1,
            grid=(2,),
            in_specs=[block, pl.BlockSpec((2, WINDOW, WINDOW), lambda g, s: (0, 0, 0)), block]
            + [
                pl.BlockSpec((D, 128), lambda g, s, k=k: (0, at(k)(g)))
                for k in range(4)
            ]
            + [
                pl.BlockSpec((128, D), lambda g, s, k=k: (at(k)(g), 0))
                for k in range(4)
            ]
            + [block, block]
            + [pl.BlockSpec(memory_space=pl.ANY)] * len(deps),
            out_specs=[packed, packed, block, block],
            scratch_shapes=[pltpu.VMEM((2, 2, 128, D), bf16)],
        ),
        out_shape=[
            jax.ShapeDtypeStruct((4, 256, D), bf16),
            jax.ShapeDtypeStruct((4, 256, D), bf16),
            jax.ShapeDtypeStruct((WINDOW, D), f32),
            jax.ShapeDtypeStruct((WINDOW, D), f32),
        ],
        compiler_params=params(32),
        cost_estimate=cost(1e3, 1e3),
        name="feed_forward",
    )(places, x, split, cot, up, up, up, up, down, down, down, down, out, gx, *deps)


def one_block(array):
    return pl.BlockSpec(array.shape, lambda g: (0,) * len(array.shape))


def single(kernel, name, ins, outs, scratch=(), deps=()):
    return pl.pallas_call(
        kernel,
        grid=(1,),
        in_specs=[one_block(a) for a in ins]
        + [pl.BlockSpec(memory_space=pl.ANY)] * len(deps),
        out_specs=[one_block(o) for o in outs],
        out_shape=list(outs),
        scratch_shapes=list(scratch),
        compiler_params=params(),
        cost_estimate=cost(1e3, 1e3),
        name=name,
    )(*ins, *deps)


def like(kind, *shape):
    return jax.ShapeDtypeStruct(shape, kind)


def kept(kind, *shape):
    return pltpu.HBM(shape, kind)


def stays(*arrays):
    return tuple(pltpu.with_memory_space_constraint(a, pltpu.HBM) for a in arrays)


def unit_of(value):
    unit, inv = norm_parts(value)
    return unit, jnp.broadcast_to(inv, (value.shape[0], 128))


def table_kernel(table, gain, weight, *rest):
    unit_out, inv_out, normed_out, qkv_out = rest[-4:]

    @pl.when(pl.program_id(0) == 0)
    def _():
        unit, inv = unit_of(table[...].astype(f32))
        unit_out[...] = unit
        inv_out[...] = inv
        normed_out[...] = (unit * gain[...]).astype(bf16)

    qkv_out[...] = dot(normed_out[...], weight[...]).astype(bf16)


def table_more_kernel(normed, weight, *rest):
    rest[-1][...] = dot(normed[...], weight[...]).astype(bf16)


def table_forward(table, gain, weight):
    flat = lambda *shape: pl.BlockSpec(shape, lambda g: (0, 0))
    return pl.pallas_call(
        table_kernel,
        grid=(2,),
        in_specs=[
            flat(VOCAB, D),
            flat(1, D),
            pl.BlockSpec((D, D // 2), lambda g: (0, g)),
        ],
        out_specs=[
            flat(VOCAB, D),
            flat(VOCAB, 128),
            flat(VOCAB, D),
            pl.BlockSpec((VOCAB, D // 2), lambda g: (0, g)),
        ],
        out_shape=[
            kept(f32, VOCAB, D),
            kept(f32, VOCAB, 128),
            like(bf16, VOCAB, D),
            like(bf16, VOCAB, 3 * D),
        ],
        compiler_params=params(),
        cost_estimate=cost(1e3, 1e3),
        name="table_forward",
    )(*stays(table), gain, *stays(weight))


def table_more(third, normed, weight, onto, deps=()):
    return pl.pallas_call(
        table_more_kernel,
        grid=(2,),
        in_specs=[
            pl.BlockSpec((VOCAB, D), lambda g: (0, 0)),
            pl.BlockSpec((D, D // 2), lambda g: (0, 2 * third + g)),
        ]
        + [pl.BlockSpec(memory_space=pl.ANY)] * (1 + len(deps)),
        out_specs=pl.BlockSpec((VOCAB, D // 2), lambda g: (0, 2 * third + g)),
        out_shape=like(bf16, VOCAB, 3 * D),
        input_output_aliases={2: 0},
        compiler_params=params(),
        cost_estimate=cost(1e3, 1e3),
        name="table_more",
    )(normed, *stays(weight), onto, *deps)


def states_forward_kernel(states, gain, weight, unit_out, inv_out, normed_out, kv_out):
    step = pl.program_id(0)

    @pl.when(step == 0)
    def _():
        unit, inv = unit_of(states[...])
        unit_out[...] = unit
        inv_out[...] = inv
        normed_out[...] = (unit * gain[...]).astype(bf16)

    kv_out[...] = dot(normed_out[...], weight[...]).astype(bf16)


def states_forward(states, gain, weight):
    flat = lambda *shape: pl.BlockSpec(shape, lambda g: (0, 0))
    return pl.pallas_call(
        states_forward_kernel,
        grid=(4,),
        in_specs=[
            flat(STATES, D),
            flat(1, D),
            pl.BlockSpec((D, D // 2), lambda g: (0, g)),
        ],
        out_specs=[
            flat(STATES, D),
            flat(STATES, 128),
            flat(STATES, D),
            pl.BlockSpec((STATES, D // 2), lambda g: (0, g)),
        ],
        out_shape=[
            kept(f32, STATES, D),
            kept(f32, STATES, 128),
            kept(bf16, STATES, D),
            like(bf16, STATES, 2 * D),
        ],
        compiler_params=params(),
        cost_estimate=cost(1e3, 1e3),
        name="states_forward",
    )(states, gain, weight)


def residual_kernel(
    places, mixed, out_weight, pick, table, gain, res_out, unit_out, inv_out, in_out, split_out, xt
):
    res = dot(pick[WINDOW:, :], table[...]) + dot(mixed[...], out_weight[...])
    res_out[...] = res
    unit, inv = unit_of(res)
    unit_out[...] = unit
    inv_out[...] = inv
    x = unit * gain[...]
    in_out[...] = x.astype(bf16)
    xt[...] = x.T.astype(bf16)
    core = places[CORE]
    for z in range(4):
        for slot, parity in ((0, 1 - core), (1, core)):
            at = pl.multiple_of((2 * z + parity) * 128, 128)
            split_out[slot, z * 128 : (z + 1) * 128, :] = xt[pl.ds(at, 128), :]


def residual_forward(places, *ins):
    outs = (
        like(f32, WINDOW, D),
        kept(f32, WINDOW, D),
        kept(f32, WINDOW, 128),
        like(bf16, WINDOW, D),
        like(bf16, 2, WINDOW, WINDOW),
    )
    return pl.pallas_call(
        residual_kernel,
        grid_spec=pltpu.PrefetchScalarGridSpec(
            num_scalar_prefetch=1,
            grid=(1,),
            in_specs=[whole(a) for a in ins],
            out_specs=[whole(o) for o in outs],
            scratch_shapes=[pltpu.VMEM((D, WINDOW), bf16)],
        ),
        out_shape=list(outs),
        compiler_params=params(),
        cost_estimate=cost(1e3, 1e3),
        name="residual_forward",
    )(places, *ins)


def feed_back_kernel(
    gx, unit, inv, gain, upstream, mixed, out_weight, pick, *rest
):
    gain_out, out_out, mixed_out, rows_out = rest[-4:]
    g = gx[...]
    u = unit[...]
    gain_out[...] = jnp.sum(g * u, axis=0, keepdims=True)
    back = norm_back(u, inv[:, :1], gain[...], g)
    grad = (upstream[...].astype(f32) + back).astype(bf16)
    mixed_out[...] = dot(grad, out_weight[...], NT).astype(bf16)
    out_out[...] = dot(mixed[...], grad, TN).astype(bf16)
    rows_out[...] = dot(pick[WINDOW:, :], grad, TN).astype(bf16)


def feed_back(v, gx, deps=()):
    return single(
        feed_back_kernel,
        "feed_back",
        (
            gx,
            v.mlp_unit,
            v.mlp_inv,
            v.mlp_gain,
            v.upstream,
            v.mixed,
            v.out_weight,
            v.pick,
        ),
        (like(f32, 1, D), like(bf16, D, D), like(bf16, WINDOW, D), like(bf16, VOCAB, D)),
        deps=deps,
    )


def states_back_kernel(
    gsk, gsv, weight, normed, unit, inv, gain, slope, forget, *rest
):
    k_out, v_out, gain_out, local_out, gate_out = rest[-5:]
    upstream = dot(gsk[...], weight[:, :D], NT) + dot(gsv[...], weight[:, D:], NT)
    u = unit[...]
    gain_out[...] = jnp.sum(upstream * u, axis=0, keepdims=True)
    local = norm_back(u, inv[:, :1], gain[...], upstream)
    local_out[...] = local
    f = forget[...]
    gate_out[...] = jnp.sum(local * slope[...], axis=0, keepdims=True) * f * (1.0 - f)
    k_out[...] = dot(normed[...], gsk[...], TN).astype(bf16)
    v_out[...] = dot(normed[...], gsv[...], TN).astype(bf16)


def states_back(v, gsk, gsv, deps=()):
    return single(
        states_back_kernel,
        "states_back",
        (
            *stays(gsk, gsv, v.state_kv_weight, v.state_normed, v.state_unit, v.state_inv),
            v.state_gain,
            *stays(v.forget_slope),
            v.forget,
        ),
        (
            like(bf16, D, D),
            like(bf16, D, D),
            like(f32, 1, D),
            like(f32, STATES, D),
            like(f32, 1, D),
        ),
        deps=deps,
    )


XI, YI, ZI, CORE, DPI, SEQI = range(6)


def permute(value, axis, to):
    size = lax.axis_size(axis)
    return lax.ppermute(value, axis, [(i, to(i)) for i in range(size)])


def swap_core(value):
    return permute(value, "seq", lambda i: i ^ 1)


def swap_dp(value, step):
    return permute(value, "dp", lambda i: i ^ step)


def ahead(value, step):
    return permute(value, "seq", lambda i: (i + 2 * step) % 8)


def fitted():
    return lax.axis_size("seq") == 8 and lax.axis_size("dp") == 4


def whole(array):
    return pl.BlockSpec(array.shape, lambda g, s: (0,) * len(array.shape))


def blend(name, places, outs, deps=(), through=()):
    arrays, in_specs, plan, out_specs = [], [], [], []
    for shape, rows, blocks, segments in outs:
        every = 4 // blocks
        rows_of = []
        for sources in segments:
            names = []
            for array, block_rows, place in sources:
                names.append(len(arrays))
                arrays.append(array)
                in_specs.append(
                    pl.BlockSpec(
                        (1, block_rows, array.shape[2]),
                        lambda g, s, place=place, every=every: (*place(g // every, s), 0),
                    )
                )
            rows_of.append((sources[0][1], names))
        plan.append((every, rows_of))
        out_specs.append(
            pl.BlockSpec((1, rows, shape[2]), lambda g, s, every=every: (g // every, 0, 0))
        )
    count = len(arrays)

    def kernel(s, *refs):
        step = pl.program_id(0)
        out_refs = refs[count + len(deps) + len(through) :]

        def fill(out_ref, rows_of):
            at = 0
            for rows, names in rows_of:
                total = refs[names[0]][0].astype(f32)
                for i in names[1:]:
                    total = total + refs[i][0].astype(f32)
                out_ref[0, at : at + rows, :] = total.astype(out_ref.dtype)
                at += rows

        for out_ref, (every, rows_of) in zip(out_refs, plan):
            if every == 1:
                fill(out_ref, rows_of)
            else:
                pl.when(step % every == 0)(functools.partial(fill, out_ref, rows_of))

    return pl.pallas_call(
        kernel,
        grid_spec=pltpu.PrefetchScalarGridSpec(
            num_scalar_prefetch=1,
            grid=(4,),
            in_specs=in_specs
            + [pl.BlockSpec(memory_space=pl.ANY)] * (len(deps) + len(through)),
            out_specs=out_specs + [pl.BlockSpec(memory_space=pl.ANY)] * len(through),
        ),
        out_shape=[jax.ShapeDtypeStruct(shape, bf16) for shape, _, _, _ in outs]
        + [jax.ShapeDtypeStruct(t.shape, t.dtype) for t in through],
        input_output_aliases={
            1 + count + len(deps) + i: len(outs) + i for i in range(len(through))
        },
        compiler_params=params(),
        cost_estimate=cost(1e3, 1e3),
        name=name,
    )(places, *arrays, *deps, *through)


class Wing:
    def __init__(self, lead, kept, came, base, rows):
        self.lead, self.trail = lead, 1 - lead
        self.kept, self.came, self.base = kept, came, base
        self.half, self.quarter = rows // 2, rows // 4
        self.columns = kept.shape[2]
        self.got = []

    def first(self):
        at = self.base // self.half
        other = lambda g, s: (g, at + 1 - s[self.lead])
        return self.half, [(self.kept, self.half, other), (self.came, self.half, other)]

    def second(self):
        q = self.quarter
        at = self.base // q
        array, start = self.got[0]
        start = start // q
        deep = lambda g, s: (g, at + 2 * s[self.lead] + 1 - s[self.trail])
        flat = lambda g, s: (g, start + 1 - s[self.trail])
        return q, [(self.kept, q, deep), (self.came, q, deep), (array, q, flat)]

    def quarters(self, level):
        q = self.quarter
        at = self.base // q
        (one, start_one), (two, start_two) = self.got
        start_one, start_two = start_one // q, start_two // q
        deep = lambda g, s: (level(g, s), at + 2 * s[self.lead] + s[self.trail])
        flat = lambda g, s: (level(g, s), start_one + s[self.trail])
        last = lambda g, s: (level(g, s), start_two)
        return [(self.kept, q, deep), (self.came, q, deep), (one, q, flat), (two, q, last)]


def wings(kept, came):
    half = kept.shape[1] // 2
    return [Wing(XI, kept, came, 0, half), Wing(YI, kept, came, half, half)]


class Column:
    def __init__(self, parts):
        self.parts = parts
        self.rows = sum(w.quarter for w in parts)
        self.columns = parts[0].columns

    def near(self):
        outs = []
        for own in (False, True):
            level = (
                (lambda g, s: 2 * g + s[ZI] % 2)
                if own
                else (lambda g, s: 2 * g + 1 - s[ZI] % 2)
            )
            segments = [w.quarters(level) for w in self.parts]
            outs.append(((2, self.rows, self.columns), self.rows, 2, segments))
        return outs

    def rest(self, pick, extra=()):
        sources = [
            (array, self.rows, lambda g, s: (pick(s), 0))
            for array in (self.kept, self.from_near)
        ] + [(array, self.rows, lambda g, s: (0, 0)) for array in extra]
        return [((1, self.rows, self.columns), self.rows, 1, [sources])]

    def doubled(self, step):
        if step == 1:
            sources = [w.quarters(lambda g, s: g) for w in self.parts]
        else:
            sources = [
                [(a, self.rows, lambda g, s: (g, 0)) for a in (self.sum, self.other)]
            ]
        return [((4, self.rows, self.columns), self.rows, 4, sources)]

    def far(self):
        return self.rest(lambda s: 1 - s[ZI] // 2)

    def close(self):
        return self.rest(lambda s: s[ZI] // 2, [self.from_far])


class Traffic:
    def __init__(self, places):
        self.places = places
        self.pending = []

    def swap(self, send):
        came = swap_core(send)
        self.pending.append(came)
        return came

    def boundary(self, after, first=(), second=(), near=(), far=(), close=(), swap=(), join=(), double=None):
        outs, sent = [], []
        for axis in (XI, YI):
            groups = {}
            for w in first:
                if w.lead == axis:
                    groups.setdefault(w.columns, []).append((w, w.first()))
            for w in second:
                if w.trail == axis:
                    groups.setdefault(w.columns, []).append((w, w.second()))
            for columns, moves in groups.items():
                moves.sort(key=lambda m: -m[1][0])
                rows = sum(m[1][0] for m in moves)
                outs.append(
                    ((4, rows, columns), rows, 4, [m[1][1] for m in moves])
                )
                sent.append((axis, moves))
        for columns, step in ((near, Column.near), (far, Column.far), (close, Column.close)):
            for c in columns:
                outs += step(c)
        if double:
            outs += double[0].doubled(double[1])
        if join:
            segments = [c.close()[0][3][0] for c in join]
            total = sum(c.rows for c in join)
            outs.append(((1, total, join[0].columns), total, 1, segments))
        results = blend("boundary", self.places, outs, (*after, *self.pending), swap)
        self.pending = []
        mark = results[0]
        results = list(results)
        for axis, moves in sent:
            came = swap_dp(results.pop(0), 1 << axis)
            self.pending.append(came)
            at = 0
            for w, (rows, _) in moves:
                assert at % w.quarter == 0
                w.got.append((came, at))
                at += rows
        for c in near:
            c.from_near = permute(results.pop(0), "seq", lambda i: i ^ 2)
            c.kept = results.pop(0)
            self.pending.append(c.from_near)
        for c in far:
            c.from_far = permute(results.pop(0), "seq", lambda i: i ^ 4)
            self.pending.append(c.from_far)
        for c in close:
            c.own = results.pop(0)
        if double:
            column, step = double
            column.sum = results.pop(0)
            if step < 3:
                column.other = permute(column.sum, "seq", lambda i: i ^ (2 * step))
                self.pending.append(column.other)
        if join:
            self.joined = results.pop(0)
        self.swapped = [self.swap(send) for send in results]
        return mark

    def spread(self, own, lead=1):
        beside = swap_dp(own, lead)
        other = swap_dp(own, 3 - lead)
        rows = [own, beside, other, swap_dp(beside, 3 - lead)]
        self.pending += rows[1:]
        return rows if lead == 1 else [own, other, beside, rows[3]]


def packed_pair(name, places, pieces, deps=()):
    rows = sum(p.shape[1] for p in pieces)
    columns = pieces[0].shape[2]
    outs = []
    for keep in (False, True):
        place = (
            (lambda g, s: (2 * g + s[CORE], 0))
            if keep
            else (lambda g, s: (2 * g + 1 - s[CORE], 0))
        )
        outs.append(
            ((4, rows, columns), rows, 4, [[(p, p.shape[1], place)] for p in pieces])
        )
    return blend(name, places, outs, deps)


def pack_rows(places, mark, g_tokens, g, rows_sum, *vectors):
    count = 3 + len(vectors)

    def kernel(s, *refs):
        for out_ref, (a, b, r, *rows) in zip(
            refs[2 * count + 1 :], (refs[:count], refs[count : 2 * count])
        ):
            out_ref[0, :VOCAB, :] = (a[0] + b[0].astype(f32)).astype(bf16)
            out_ref[0, VOCAB:, :128] = r[:128, :]
            out_ref[0, VOCAB:, 128:256] = r[128:, :]
            place = lax.broadcasted_iota(jnp.int32, (128, 128), 0)
            small = jnp.zeros((128, 128), f32)
            for i, row in enumerate(rows):
                value = row[...] if len(row.shape) == 2 else row[0]
                small = jnp.where(place == i, value, small)
            out_ref[0, VOCAB:, 256:] = small.astype(bf16)

    specs, arrays = [], []
    for keep in (False, True):
        at = (
            (lambda i, s: 2 * i + s[CORE]) if keep else (lambda i, s: 2 * i + 1 - s[CORE])
        )
        for array in (g_tokens, g, rows_sum, *vectors):
            arrays.append(array)
            if array.ndim == 2:
                specs.append(
                    pl.BlockSpec((array.shape[0], 128), lambda i, s, at=at: (0, at(i, s)))
                )
            else:
                specs.append(
                    pl.BlockSpec(
                        (1,) + array.shape[1:], lambda i, s, at=at: (at(i, s), 0, 0)
                    )
                )
    return pl.pallas_call(
        kernel,
        grid_spec=pltpu.PrefetchScalarGridSpec(
            num_scalar_prefetch=1,
            grid=(4,),
            in_specs=specs + [pl.BlockSpec(memory_space=pl.ANY)],
            out_specs=[pl.BlockSpec((1, 384, 384), lambda i, s: (i, 0, 0))] * 2,
        ),
        out_shape=[like(bf16, 4, 384, 384)] * 2,
        compiler_params=params(),
        cost_estimate=cost(1e3, 1e3),
        name="pack_rows",
    )(places, *arrays, mark)


def slot_of(s, step, lead):
    there = s[DPI] ^ step
    x, y = there % 2, there // 2
    return 2 * x + y if lead == XI else 2 * y + x


def unpack(name, places, quarters, pieces, outs):
    columns = quarters[0].shape[2]
    total = 4 * sum(p[1] for p in pieces)

    def kernel(s, *refs):
        scratch = refs[-1]
        for step in range(4):
            for start, rows, lead, base in pieces:
                at = pl.multiple_of(slot_of(s, step, lead) * rows + base, 16)
                scratch[pl.ds(at, rows), :] = refs[step][0, start : start + rows, :].astype(
                    f32
                )
        for out_ref, (_, moves) in zip(refs[4:-1], outs):
            if not moves:
                out_ref[...] = jnp.zeros_like(out_ref)
            for row, rows, to, column in moves:
                out_ref[to : to + rows, column : column + columns] = scratch[
                    row : row + rows, :
                ]

    return pl.pallas_call(
        kernel,
        grid_spec=pltpu.PrefetchScalarGridSpec(
            num_scalar_prefetch=1,
            grid=(1,),
            in_specs=[whole(q) for q in quarters],
            out_specs=[
                pl.BlockSpec(shape, lambda g, s: (0, 0)) for shape, _ in outs
            ],
            scratch_shapes=[pltpu.VMEM((total, columns), f32)],
        ),
        out_shape=[jax.ShapeDtypeStruct(shape, f32) for shape, _ in outs],
        compiler_params=params(),
        cost_estimate=cost(1e3, 1e3),
        name=name,
    )(places, *quarters)


def unpack_mlp(places, quarters):
    def kernel(s, *refs):
        down, up, mark, scratch = refs[8:]
        mark[...] = jnp.zeros_like(mark)
        for pair in range(2):
            for step in range(4):
                block = refs[4 * pair + step]
                for part in range(2):
                    for lead in range(2):
                        at = pl.multiple_of(slot_of(s, step, lead) * 32 + 128 * lead, 32)
                        start = part * 64 + lead * 32
                        scratch[2 * pair + part, pl.ds(at, 32), :] = block[
                            0, start : start + 32, :
                        ].astype(f32)
        for part in range(4):
            down[part * 128 : (part + 1) * 128, :] = scratch[part, :128, :]
            for block in range(8):
                at = (4 * block + part) * 128
                up[:, at : at + 128] = scratch[part, 128:, block * 128 : (block + 1) * 128]

    flat = [q for pair in quarters for q in pair]
    return pl.pallas_call(
        kernel,
        grid_spec=pltpu.PrefetchScalarGridSpec(
            num_scalar_prefetch=1,
            grid=(1,),
            in_specs=[whole(q) for q in flat],
            out_specs=[
                pl.BlockSpec((512, D), lambda g, s: (0, 0)),
                pl.BlockSpec((128, FF), lambda g, s: (0, 0)),
                pl.BlockSpec((8, 128), lambda g, s: (0, 0)),
            ],
            scratch_shapes=[pltpu.VMEM((4, 256, D), f32)],
        ),
        out_shape=[
            jax.ShapeDtypeStruct((512, D), f32),
            jax.ShapeDtypeStruct((128, FF), f32),
            jax.ShapeDtypeStruct((8, 128), f32),
        ],
        compiler_params=params(),
        cost_estimate=cost(1e3, 1e3),
        name="unpack_mlp",
    )(places, *flat)


def stack_rows(places, parts, deps=()):
    _, rows, columns = parts[0].shape
    rows //= 2

    def kernel(s, *refs):
        out = refs[-1]
        for step in range(4):
            for lead in range(2):
                at = pl.multiple_of(slot_of(s, step, lead) * rows + 4 * rows * lead, 16)
                out[:, pl.ds(at, rows), :] = refs[step][:, lead * rows : (lead + 1) * rows, :]

    shape = (4, 8 * rows, columns)
    return pl.pallas_call(
        kernel,
        grid_spec=pltpu.PrefetchScalarGridSpec(
            num_scalar_prefetch=1,
            grid=(1,),
            in_specs=[whole(p) for p in parts]
            + [pl.BlockSpec(memory_space=pl.ANY)] * len(deps),
            out_specs=pl.BlockSpec(shape, lambda g, s: (0, 0, 0)),
        ),
        out_shape=jax.ShapeDtypeStruct(shape, bf16),
        compiler_params=params(),
        cost_estimate=cost(1e3, 1e3),
        name="stack_rows",
    )(places, *parts, *deps)


def last_kernel(
    s, mine, other, norm_cols, unit_cols, weight, weight_rows, unit, inv, gain,
    qkv_out, gain_out, table_out, small_out, by_head,
):
    for z in range(4):
        for q in range(2):
            by_head[2 * z + q] = jnp.where(s[CORE] == q, mine[z], other[z])
    small_out[...] = mine[s[ZI], 256:272, 256:].astype(f32)[:8]
    at = pl.multiple_of(s[SEQI] * 32, 32)
    norm = norm_cols[...]
    cols_grad = jnp.zeros((VOCAB, 128), f32)
    normed_grad = jnp.zeros((32, D), f32)
    for h in range(HEADS):
        for t in range(3):
            lanes = slice(t * 128, (t + 1) * 128)
            to = slice(t * D + h * 128, t * D + (h + 1) * 128)
            g = by_head[h, :VOCAB, lanes]
            qkv_out[:, to] = dot(norm, g, TN)
            cols_grad = cols_grad + dot(g, weight_rows[:, to], NT)
            normed_grad = normed_grad + dot(
                by_head[h, pl.ds(at, 32), lanes], weight[:, to], NT
            )
    gain_out[...] = jnp.sum(cols_grad * unit_cols[...], axis=0, keepdims=True)
    u = unit[...]
    scaled = normed_grad * gain[...]
    a = jnp.mean(scaled, axis=-1, keepdims=True)
    b = jnp.mean(scaled * u, axis=-1, keepdims=True)
    low = pl.multiple_of(VOCAB + (s[SEQI] % 4) * 32, 32)
    rows_sum = [
        jnp.where(
            s[SEQI] < 4,
            by_head[h, pl.ds(low, 32), :128].astype(f32),
            by_head[h, pl.ds(low, 32), 128:256].astype(f32),
        )
        for h in range(HEADS)
    ]
    table_out[...] = (
        jnp.concatenate(rows_sum, axis=1) + (scaled - a - u * b) * inv[:, :1]
    )


def last_products(places, mine, other, normed, unit, weight, inv, gain):
    return pl.pallas_call(
        last_kernel,
        grid_spec=pltpu.PrefetchScalarGridSpec(
            num_scalar_prefetch=1,
            grid=(1,),
            in_specs=[
                whole(mine),
                whole(other),
                pl.BlockSpec((VOCAB, 128), lambda g, s: (0, s[SEQI])),
                pl.BlockSpec((VOCAB, 128), lambda g, s: (0, s[SEQI])),
                whole(weight),
                pl.BlockSpec((128, 3 * D), lambda g, s: (s[SEQI], 0)),
                pl.BlockSpec((32, D), lambda g, s: (s[SEQI], 0)),
                pl.BlockSpec((32, 128), lambda g, s: (s[SEQI], 0)),
                whole(gain),
            ],
            out_specs=[
                pl.BlockSpec((128, 3 * D), lambda g, s: (0, 0)),
                pl.BlockSpec((1, 128), lambda g, s: (0, 0)),
                pl.BlockSpec((32, D), lambda g, s: (0, 0)),
                pl.BlockSpec((8, 128), lambda g, s: (0, 0)),
            ],
            scratch_shapes=[pltpu.VMEM((HEADS, 384, 384), bf16)],
        ),
        out_shape=[
            jax.ShapeDtypeStruct((128, 3 * D), f32),
            jax.ShapeDtypeStruct((1, 128), f32),
            jax.ShapeDtypeStruct((32, D), f32),
            jax.ShapeDtypeStruct((8, 128), f32),
        ],
        compiler_params=params(),
        cost_estimate=cost(1e3, 1e3),
        name="last_products",
    )(places, mine, other, normed, unit, weight, weight, unit, inv, gain)


def total_of(value):
    flat = value.reshape((-1,) + value.shape[2:])
    own = lax.psum_scatter(flat, "seq", scatter_dimension=0, tiled=True)
    return lax.psum(own, "dp").astype(f32)


def places_of():
    here = lax.axis_index("seq")
    dp = lax.axis_index("dp")
    return jnp.stack([dp % 2, dp // 2, here // 2, here % 2, dp, here]).astype(jnp.int32)


def prepare_kernel(
    places, blocks_a, blocks_b, gate, bias, picks, mask, *rest
):
    span, live, counts, rows, pick, pick_t, forget, bias_out = rest[-8:]
    here = places[SEQI]
    sign = lax.broadcasted_iota(jnp.int32, (VOCAB, 128), 0)
    first = jnp.zeros((1, 128), f32)
    before = jnp.zeros((4, 128), jnp.int32)
    for k in range(8):
        block = blocks_a[k] if k < 4 else blocks_b[k - 4]
        w = here ^ k
        total = jnp.zeros((VOCAB, 128), f32)
        for r in range(4):
            total = total + jnp.where(block[r : r + 1] == sign, 1.0, 0.0)
        count = jnp.broadcast_to(jnp.sum(total, axis=1, keepdims=True), (VOCAB, 128))
        counts[pl.ds(w, 1)] = count[None]
        rows[pl.ds(w, 1)] = count.T[:1][None]
        marked = jnp.where(block[4:5] > 0, w.astype(f32), 0.0)
        first = jnp.maximum(first, jnp.where(w <= here, marked, 0.0))
        before = jnp.where(w == here - 1, block[:4], before)
    span[0] = jnp.max(first).astype(jnp.int32)
    span[1] = here
    live[0] = 1 - jnp.max(blocks_a[0, 4:5].astype(f32)).astype(jnp.int32)
    own = blocks_a[0, :4]
    for r in range(8):
        ids = before[r : r + 1] if r < 4 else own[r - 4 : r - 3]
        one = jnp.where(ids == sign, 1.0, 0.0)
        pick_t[:, r * 128 : (r + 1) * 128] = one.astype(bf16)
        pick[r * 128 : (r + 1) * 128, :] = one.T.astype(bf16)
    forget[...] = 1.0 / (1.0 + jnp.exp(-gate[...]))
    table = lax.dot_general(
        bias[...], picks[...], NN, precision=lax.Precision.HIGHEST, preferred_element_type=f32
    )
    table = table * log2e + mask[...]
    for h in range(HEADS):
        bias_out[h] = table[h : h + 1]


def side_by_side(mine, other, deps):
    def kernel(a, b, *rest):
        rest[-1][: a.shape[0]] = a[...]
        rest[-1][a.shape[0] :] = b[...]

    out = like(mine.dtype, 2 * mine.shape[0], *mine.shape[1:])
    return single(kernel, "side_by_side", (mine, other), (out,), deps=deps)[0]


def prepare(places, char_ids, seg_starts, gate_logit, distance_bias, table_parts):
    packed = jnp.concatenate(
        [
            char_ids.reshape(4, 128),
            jnp.broadcast_to(seg_starts, (1, 128)),
            jnp.zeros((3, 128), jnp.int32),
        ],
        axis=0,
    )[None]
    done = ()
    for bit, part in zip((1, 2), table_parts):
        came = permute(packed, "seq", lambda i, bit=bit: i ^ bit)
        done = part(done)
        packed = side_by_side(packed, came, done)
    beyond = permute(packed, "seq", lambda i: i ^ 4)
    deps = table_parts[2](done)
    ins = (
        packed,
        beyond,
        gate_logit.reshape(1, D),
        distance_bias.reshape(HEADS, BUCKETS),
        jnp.asarray(lane_pick()),
        jnp.asarray(lane_hidden()),
    )
    outs = (
        like(jnp.int32, 2),
        like(jnp.int32, 1),
        like(f32, 8, VOCAB, 128),
        like(f32, 8, 1, VOCAB),
        like(bf16, CONTEXT, VOCAB),
        like(bf16, VOCAB, CONTEXT),
        like(f32, 1, D),
        like(f32, HEADS, 1, CONTEXT),
    )
    prepared = pl.pallas_call(
        prepare_kernel,
        grid_spec=pltpu.PrefetchScalarGridSpec(
            num_scalar_prefetch=1,
            grid=(1,),
            in_specs=[whole(a) for a in ins]
            + [pl.BlockSpec(memory_space=pl.ANY)] * len(deps),
            out_specs=[pl.BlockSpec(memory_space=pltpu.SMEM)] * 2
            + [whole(o) for o in outs[2:]],
        ),
        out_shape=list(outs),
        compiler_params=params(),
        cost_estimate=cost(1e3, 1e3),
        name="prepare",
    )(places, *ins, *deps)
    return (*prepared, deps[0])


def plain_prepare(char_ids, seg_starts, gate_logit, distance_bias):
    windows = lax.axis_size("seq")
    here = lax.axis_index("seq")
    packed = jnp.concatenate(
        [char_ids.reshape(4, 128), jnp.broadcast_to(seg_starts, (1, 128))], axis=0
    )
    everyone = lax.all_gather(packed, "seq")
    ids_all = everyone[:, :4].reshape(windows, WINDOW)
    flags = everyone[:, 4, 0]
    order = jnp.arange(windows, dtype=jnp.int32)
    first = jnp.max(jnp.where((flags > 0) & (order <= here), order, 0))
    span = jnp.stack([first, here]).astype(jnp.int32)
    live = (1 - seg_starts.reshape(1)).astype(jnp.int32)
    vocab = jnp.arange(VOCAB, dtype=jnp.int32)
    counts = jnp.sum(
        (ids_all[:, :, None] == vocab[None, None, :]).astype(f32), axis=1
    )
    before = lax.dynamic_index_in_dim(ids_all, jnp.maximum(here - 1, 0), 0, False)
    context_ids = jnp.concatenate([before, char_ids.reshape(-1)])
    bias_rows = jnp.dot(
        distance_bias.reshape(HEADS, BUCKETS),
        jnp.asarray(lane_pick()),
        precision=lax.Precision.HIGHEST,
    ) * log2e + jnp.asarray(lane_hidden())
    return (
        span,
        live,
        jnp.broadcast_to(counts[:, :, None], (windows, VOCAB, 128)),
        counts[:, None, :],
        (context_ids[:, None] == vocab[None, :]).astype(bf16),
        (vocab[:, None] == context_ids[None, :]).astype(bf16),
        jax.nn.sigmoid(gate_logit).reshape(1, D),
        bias_rows.reshape(HEADS, 1, CONTEXT),
    )


def body(
    char_ids,
    seg_starts,
    char_table,
    norm_gain,
    qkv_weight,
    distance_bias,
    state_query,
    state_init,
    state_gain,
    state_kv_weight,
    gate_logit,
    out_weight,
    mlp_gain,
    up_weight,
    down_weight,
    cotangent,
):
    windows = lax.axis_size("seq")
    here = lax.axis_index("seq")
    norm_gain, state_gain, mlp_gain = (
        t.reshape(1, D) for t in (norm_gain, state_gain, mlp_gain)
    )
    table_unit, table_inv, normed_table, qkv_table = table_forward(
        char_table, norm_gain, qkv_weight
    )
    more = lambda third: lambda done: (
        table_more(third, normed_table, qkv_weight, done[0]),
    )
    table_parts = (lambda done: (qkv_table,), more(1), more(2))

    characters = (char_ids, seg_starts, gate_logit, distance_bias)
    if fitted():
        places = places_of()
        *prepared, qkv_table = prepare(places, *characters, table_parts)
    else:
        prepared = plain_prepare(*characters)
        for part in table_parts:
            (qkv_table,) = part((qkv_table,))
    span, live, counts, count_rows, pick, pick_t, forget, bias_rows = prepared
    states_in, forget_slope, lowest = summary_forward(
        span, state_query, qkv_table, counts, count_rows, state_init, forget
    )
    state_unit, state_inv, state_normed, state_kv = states_forward(
        states_in, state_gain, state_kv_weight
    )
    mixed, lse = attention_forward(
        live, pick, pick_t, qkv_table, state_kv, state_kv, bias_rows
    )
    residual, mlp_unit, mlp_inv, mlp_in, mlp_split = residual_forward(
        places if fitted() else jnp.zeros(6, jnp.int32),
        mixed,
        out_weight,
        pick,
        char_table,
        mlp_gain,
    )
    upstream = cotangent.reshape(WINDOW, D)

    close_up = fitted_tail if fitted() else plain_tail
    return close_up(dict(locals()))


def fitted_tail(values):
    v = types.SimpleNamespace(**values)
    places = v.places
    weights = (v.upstream, v.up_weight, v.down_weight)

    out, gx = v.residual, jnp.zeros((WINDOW, D), f32)
    traffic = Traffic(places)
    parts, deps = [], ()
    for part in range(4):
        send, keep, out, gx = mlp_packed(
            part, places, v.mlp_in, v.mlp_split, *weights, out, gx, deps
        )
        if part:
            second = parts[part - 2] if part > 1 else ()
            mark = traffic.boundary((gx,), parts[part - 1], second, swap=[send])
            deps = (mark,)
            came = traffic.swapped[0]
        else:
            came = traffic.swap(send)
        parts.append(wings(keep, came))
    layer_out = out.astype(bf16).reshape(1, WINDOW, D)
    front = Column(parts[0] + parts[1])
    back = Column(parts[2] + parts[3])

    grad_mlp_gain, grad_out, grad_mixed, rows_sum = feed_back(v, gx, (mark,))
    gsk, gsv, gq, inner = state_backward(
        v.pick, v.qkv_table, v.state_kv, v.lse, v.mixed, grad_mixed
    )
    mark = traffic.boundary((inner,), parts[3], parts[2], near=[front])
    grad_k, grad_v, grad_state_gain, local, grad_gate = states_back(v, gsk, gsv, (mark,))
    send, keep = packed_pair(
        "pack_middle",
        places,
        [t.reshape(8, 128, D) for t in (grad_k, grad_v, grad_out)],
    )
    middle = wings(keep, traffic.swap(send))
    summary_args = (
        v.span, v.state_query, v.qkv_table, v.counts, v.count_rows, local, v.forget, v.lowest
    )
    onto = summary_backward(*summary_args, (send,), 0)
    mark = traffic.boundary((onto[0],), middle, parts[3], far=[front])
    g, gsq, ginit = summary_backward(*summary_args, (mark,), 1, onto)
    send, keep = packed_pair(
        "pack_states", places, [gsq.reshape(8, 64, D), ginit.reshape(8, 64, D)]
    )
    mark = traffic.boundary((), (), middle, near=[back], close=[front], swap=[send])
    states = wings(keep, traffic.swapped[0])
    tokens_args = (
        v.live, v.pick, v.pick_t, v.qkv_table, v.bias_rows, v.lse, inner, grad_mixed, gq
    )
    onto = token_backward(*tokens_args, (mark,), 0)
    mark = traffic.boundary((onto[1],), states, far=[back])
    front_rows = traffic.spread(front.own)
    g_tokens, fold = token_backward(*tokens_args, (mark,), 1, onto)
    side, rest = Column(middle), Column(states)
    send, keep = pack_rows(
        places, fold, g_tokens, g, rows_sum, grad_mlp_gain, grad_state_gain, grad_gate, fold
    )
    traffic.boundary((), (), states, near=[side], close=[back], swap=[send])
    rows = wings(keep, traffic.swapped[0])
    last = Column(rows)
    traffic.boundary((), rows, near=[rest], far=[side])
    traffic.boundary((), (), rows, far=[rest])
    back_rows = traffic.spread(back.own, 2)
    traffic.boundary((), double=(last, 1), join=[side, rest])
    side_own = traffic.joined
    traffic.boundary((), double=(last, 2))
    side_rows = traffic.spread(side_own)
    grad_down, grad_up, mark = unpack_mlp(places, [front_rows, back_rows])
    traffic.boundary((mark,), double=(last, 3))
    ring_parts = traffic.spread(last.sum)
    grad_state_kv, grad_out, grad_state_query, grad_state_init, mark = unpack(
        "unpack_side",
        places,
        side_rows,
        [(0, 48, XI, 0), (48, 48, YI, 192), (96, 16, XI, 384), (112, 16, YI, 448)],
        [
            ((128, 2 * D), [(0, 128, 0, 0), (128, 128, 0, D)]),
            ((128, D), [(256, 128, 0, 0)]),
            ((64, D), [(384, 64, 0, 0)]),
            ((64, D), [(448, 64, 0, 0)]),
            ((8, 128), []),
        ],
    )
    mine = stack_rows(places, ring_parts, (mark,))
    other = swap_core(mine)
    grad_qkv, grad_norm_gain, grad_table, small = last_products(
        places,
        mine,
        other,
        v.normed_table,
        v.table_unit,
        v.qkv_weight,
        v.table_inv,
        v.norm_gain,
    )
    return (
        layer_out,
        grad_table,
        grad_norm_gain.reshape(-1),
        grad_qkv,
        small[3, :32],
        grad_state_query,
        grad_state_init,
        small[1],
        grad_state_kv,
        small[2],
        grad_out,
        small[0],
        grad_up,
        grad_down,
    )


def plain_tail(values):
    v = types.SimpleNamespace(**values)
    windows, here = v.windows, v.here
    shard = lambda n: n // windows
    out, gx = v.residual, jnp.zeros((WINDOW, D), f32)
    grads_down, grads_up = [], []
    for part in range(SPLITS):
        gd, gu, out, gx = mlp_part(
            part, v.mlp_in, v.upstream, v.up_weight, v.down_weight, out, gx
        )
        grads_down.append(gd)
        grads_up.append(gu)
    layer_out = out.astype(bf16).reshape(1, WINDOW, D)
    grad_mlp_gain, grad_out, grad_mixed, rows_sum = feed_back(v, gx)
    gsk, gsv, gq, inner = state_backward(
        v.pick, v.qkv_table, v.state_kv, v.lse, v.mixed, grad_mixed
    )
    grad_k, grad_v, grad_state_gain, local, grad_gate = states_back(v, gsk, gsv)
    g, gsq, ginit = summary_backward(
        v.span, v.state_query, v.qkv_table, v.counts, v.count_rows, local, v.forget,
        v.lowest,
    )
    g_tokens, fold = token_backward(
        v.live, v.pick, v.pick_t, v.qkv_table, v.bias_rows, v.lse, inner, grad_mixed, gq
    )
    g = (g.astype(f32) + g_tokens).astype(bf16)
    sharded = lambda t: total_of(t.reshape(windows, -1, t.shape[-1]))
    full = jnp.stack([t.reshape(-1, TILE, D) for t in grads_down], axis=1)
    grad_down = sharded(full.reshape(FF, D))
    full = jnp.stack([t.reshape(D, -1, TILE) for t in grads_up], axis=2)
    grad_up = sharded(full.reshape(D, FF))
    grad_state_kv = sharded(jnp.concatenate([grad_k, grad_v], axis=1))
    small = jnp.concatenate(
        [
            t.reshape(windows, -1)
            for t in (grad_mlp_gain, grad_state_gain, grad_gate, fold[:, 0, :BUCKETS])
        ],
        axis=1,
    )
    small = total_of(small[:, None, :])[0]
    cut = shard(D)
    all_rows = lax.psum(g, ("dp", "seq"))
    grad_rows = jnp.concatenate(
        [
            all_rows[:, :, t * 128 : (t + 1) * 128].transpose(1, 0, 2).reshape(VOCAB, D)
            for t in range(3)
        ],
        axis=1,
    )
    mine = lax.dynamic_slice_in_dim(v.normed_table, here * cut, cut, 1)
    weight_rows = lax.dynamic_slice_in_dim(v.qkv_weight, here * cut, cut, 0)
    unit_cols = lax.dynamic_slice_in_dim(v.table_unit, here * cut, cut, 1)
    at = here * shard(VOCAB)
    take = lambda t: lax.dynamic_slice_in_dim(t, at, shard(VOCAB), 0)
    grad_table = sharded(rows_sum) + norm_back(
        take(v.table_unit),
        take(v.table_inv)[:, :1],
        v.norm_gain,
        dot(take(grad_rows), v.qkv_weight, NT),
    )
    return (
        layer_out,
        grad_table,
        jnp.sum(dot(grad_rows, weight_rows, NT) * unit_cols, axis=0),
        dot(mine, grad_rows, TN),
        small[3 * cut :],
        sharded(gsq),
        sharded(ginit),
        small[cut : 2 * cut],
        grad_state_kv,
        small[2 * cut : 3 * cut],
        sharded(grad_out),
        small[:cut],
        grad_up,
        grad_down,
    )


def solution(mesh):
    placed = (P("dp", "seq"), P("dp", "seq")) + (P(),) * 13 + (P("dp", "seq", None),)
    return jax.shard_map(
        body,
        mesh=mesh,
        in_specs=placed,
        out_specs=(
            P("dp", "seq", None),
            P("seq", None),
            P("seq"),
            P("seq", None),
            P("seq"),
            P("seq", None),
            P("seq", None),
            P("seq"),
            P("seq", None),
            P("seq"),
            P("seq", None),
            P("seq"),
            P("seq", None),
            P("seq", None),
        ),
        check_vma=False,
    )
```

```python
import functools
import math
import types

import jax
import jax.numpy as jnp
import numpy as np
from jax import lax
from jax.experimental import pallas as pl
from jax.experimental.pallas import tpu as pltpu
from jax.sharding import PartitionSpec as P

D = 1024
HEADS = 8
HEAD_DIM = 128
FF = 4096
VOCAB = 256
STATES = 512
WINDOW = 512
BUCKETS = 32
MAX_DISTANCE = 128
CONTEXT = 2 * WINDOW
TILE = 256
SPLITS = 2

epsilon = 1e-05
hidden = -1e30
log2e = math.log2(math.e)
score_scale = 1.0 / math.sqrt(HEAD_DIM)
f32 = jnp.float32
bf16 = jnp.bfloat16

NN = (((1,), (0,)), ((), ()))
NT = (((1,), (1,)), ((), ()))
TN = (((0,), (0,)), ((), ()))


def dot(a, b, dims=NN):
    return lax.dot_general(a, b, dims, preferred_element_type=f32)


def params(mib=18):
    return pltpu.CompilerParams(
        dimension_semantics=("arbitrary",), vmem_limit_bytes=mib * 1024 * 1024
    )


def cost(flops, moved, exps=0):
    return pl.CostEstimate(
        flops=int(flops), bytes_accessed=int(moved), transcendentals=int(exps)
    )


def norm_parts(value):
    centre = jnp.mean(value, axis=-1, keepdims=True)
    offset = value - centre
    spread = jnp.mean(offset * offset, axis=-1, keepdims=True)
    inv = lax.rsqrt(spread + epsilon)
    return offset * inv, inv


def norm_back(unit, inv, gain, upstream):
    scaled = upstream * gain
    a = jnp.mean(scaled, axis=-1, keepdims=True)
    b = jnp.mean(scaled * unit, axis=-1, keepdims=True)
    return (scaled - a - unit * b) * inv


def bucket_table():
    distance = np.arange(WINDOW)
    exact_count = BUCKETS // 2
    log_ratio = np.log(np.maximum(distance, 1) / exact_count) / math.log(
        MAX_DISTANCE / exact_count
    )
    far_bucket = exact_count + np.floor(log_ratio * (BUCKETS - exact_count)).astype(
        np.int64
    )
    return np.where(
        distance < exact_count, distance, np.minimum(far_bucket, BUCKETS - 1)
    )


def lane_pick():
    pick = np.zeros((BUCKETS, CONTEXT), np.float32)
    table = bucket_table()
    for m in range(1, WINDOW + 1):
        pick[table[WINDOW - m], m] = 1.0
    return pick


def lane_hidden():
    m = np.arange(CONTEXT)
    return np.where((m >= 1) & (m <= WINDOW), 0.0, hidden).astype(np.float32)[None]


smallest_sum = 2.0**-80


def shared_exp(lg, there):
    peak = jnp.max(jnp.where(there > 0, lg, hidden), axis=1, keepdims=True)
    return jnp.exp2(jnp.minimum(lg - peak, 0.0)).astype(bf16)


def window_sides(v, n):
    return jnp.concatenate([v.astype(f32) * n, n], axis=1).astype(bf16)


def own_weights(lg, n_row):
    x = lg + jnp.where(n_row > 0, jnp.log2(jnp.maximum(n_row, 1.0)), hidden)
    p = jnp.exp2(x - jnp.max(x, axis=1, keepdims=True))
    return p / jnp.sum(p, axis=1, keepdims=True)


def characters_there(span, rows):
    return lax.fori_loop(
        span[0], span[1], lambda w, t: t + rows[w], jnp.zeros((1, VOCAB), f32)
    )


TOGETHER = 4


def lanes_of(i):
    return slice(i * HEAD_DIM, (i + 1) * HEAD_DIM)


def summary_forward_kernel(
    span, sq, kt, vt, counts, rows, init, forget, state_out, y_out, low_out, a_s, y_s
):
    heads = range(TOGETHER)
    f = forget[...]
    v = [vt[:, lanes_of(i)] for i in heads]

    def scores(i):
        return dot(sq[:, lanes_of(i)], kt[:, lanes_of(i)], NT) * (score_scale * log2e)

    def begin():
        a_s[...] = init[...].astype(f32)
        y_s[...] = jnp.zeros_like(y_s)

    def move(i, u):
        at = lanes_of(i)
        a = a_s[:, at]
        y_s[:, at] = a - u + f[:, at] * y_s[:, at]
        a_s[:, at] = u + f[:, at] * (a - u)

    begin()
    there = characters_there(span, rows)
    e = [shared_exp(scores(i), there) for i in heads]

    def step(w, low):
        n = counts[w]
        for i in heads:
            both = dot(e[i], window_sides(v[i], n))
            z = both[:, HEAD_DIM:]
            move(i, both[:, :HEAD_DIM] / jnp.maximum(z, smallest_sum))
            low = jnp.minimum(low, jnp.min(z.reshape(STATES // 8, 8, 128), axis=0))
        return low

    low = lax.fori_loop(span[0], span[1], step, jnp.full((8, 128), 1.0, f32))
    low_out[0] = low

    @pl.when(jnp.min(low) < smallest_sum)
    def _():
        begin()
        for i in heads:
            lg = scores(i)

            def slow(w, _):
                move(i, dot(own_weights(lg, rows[w]).astype(bf16), v[i]))
                return 0

            lax.fori_loop(span[0], span[1], slow, 0)

    state_out[...] = a_s[...]
    y_out[...] = y_s[...]


def summary_specs(windows):
    wide = TOGETHER * HEAD_DIM
    head = lambda k: (lambda h, s: (0, k * HEADS // TOGETHER + h))
    return [
        pl.BlockSpec((STATES, wide), head(0)),
        pl.BlockSpec((VOCAB, wide), head(1)),
        pl.BlockSpec((VOCAB, wide), head(2)),
        pl.BlockSpec((windows, VOCAB, 128), lambda h, s: (0, 0, 0)),
        pl.BlockSpec((windows, 1, VOCAB), lambda h, s: (0, 0, 0)),
        pl.BlockSpec((STATES, wide), head(0)),
        pl.BlockSpec((1, wide), head(0)),
    ]


def summary_forward(span, state_query, qkv_table, counts, rows, state_init, forget):
    states = pl.BlockSpec((STATES, TOGETHER * HEAD_DIM), lambda h, s: (0, h))
    return pl.pallas_call(
        summary_forward_kernel,
        grid_spec=pltpu.PrefetchScalarGridSpec(
            num_scalar_prefetch=1,
            grid=(HEADS // TOGETHER,),
            in_specs=summary_specs(counts.shape[0]),
            out_specs=[states, states, pl.BlockSpec((1, 8, 128), lambda h, s: (h, 0, 0))],
            scratch_shapes=[pltpu.VMEM((STATES, TOGETHER * HEAD_DIM), f32)] * 2,
        ),
        out_shape=[
            jax.ShapeDtypeStruct((STATES, D), f32),
            pltpu.HBM((STATES, D), f32),
            jax.ShapeDtypeStruct((HEADS // TOGETHER, 8, 128), f32),
        ],
        compiler_params=params(),
        cost_estimate=cost(1e3, 1e3),
        name="summary_forward",
    )(span, state_query, qkv_table, qkv_table, counts, rows, *stays(state_init), forget)


def summary_backward_kernel(span, sq, kt, vt, counts, rows, local, forget, low, *rest):
    g_out, gsq_out, ginit_out, g_s, gs_s, gv_s, gs16, e_s, e_t = rest[-9:]
    heads = range(TOGETHER)
    f = forget[...]
    v = [vt[:, lanes_of(i)] for i in heads]
    g_s[...] = local[...]
    gs_s[...] = jnp.zeros_like(gs_s)
    gv_s[...] = jnp.zeros_like(gv_s)
    first, here = span[0], span[1]
    fast = jnp.min(low[0]) >= smallest_sum

    def scores(i):
        return dot(sq[:, lanes_of(i)], kt[:, lanes_of(i)], NT) * (score_scale * log2e)

    def carried(i):
        at = lanes_of(i)
        g = g_s[:, at]
        fg = f[:, at] * g
        g_s[:, at] = fg
        return g - fg

    @pl.when(fast)
    def _():
        there = characters_there(span, rows)
        for i in heads:
            e = shared_exp(scores(i), there)
            e_s[i] = e
            e_t[i] = e.astype(f32).T.astype(bf16)
        lane = lax.broadcasted_iota(jnp.int32, (STATES, HEAD_DIM), 1)

        def step(t, _):
            w = here - 1 - t
            n = counts[w]
            for i in heads:
                sides = window_sides(v[i], n)
                both = dot(e_s[i], sides)
                part = 1.0 / both[:, HEAD_DIM:]
                gu = (carried(i) * part).astype(bf16)
                inner = gu.astype(f32) * (both[:, :HEAD_DIM] * part)
                inner = inner + pltpu.roll(inner, HEAD_DIM // 2, 1)
                high = inner.astype(bf16)
                tail = jnp.where(
                    lane < HEAD_DIM // 2, high.astype(f32), inner - high.astype(f32)
                )
                gs_s[i] += dot(
                    jnp.concatenate([gu, (-tail).astype(bf16)], axis=1), sides, NT
                )
                gv_s[i] += n * dot(e_t[i], gu)
            return 0

        lax.fori_loop(0, here - first, step, 0)
        for i in heads:
            gs16[i] = (gs_s[i] * e_s[i].astype(f32) * score_scale).astype(bf16)

    @pl.when(jnp.logical_not(fast))
    def _():
        for i in heads:
            lg = scores(i)

            def slow(t, _):
                w = here - 1 - t
                p = own_weights(lg, rows[w])
                gu = carried(i).astype(bf16)
                pd = p * dot(gu, v[i], NT)
                gs_s[i] += pd - p * jnp.sum(pd, axis=1, keepdims=True)
                gv_s[i] += dot(p.astype(bf16), gu, TN)
                return 0

            lax.fori_loop(0, here - first, slow, 0)
            gs16[i] = (gs_s[i] * score_scale).astype(bf16)

    for i in heads:
        gs = gs16[i]
        at = lanes_of(i)
        g_out[i, :, :128] = jnp.zeros((VOCAB, 128), bf16)
        g_out[i, :, 128:256] = dot(gs, sq[:, at], TN).astype(bf16)
        g_out[i, :, 256:] = gv_s[i].astype(bf16)
        gsq_out[:, at] = dot(gs, kt[:, at]).astype(bf16)
    ginit_out[...] = g_s[...].astype(bf16)


def summary_backward(
    span, state_query, qkv_table, counts, rows, local, forget, low, deps=(), half=None, onto=()
):
    start, steps = (0, HEADS // TOGETHER) if half is None else (half, 1)
    deps = (*deps, *onto)
    wide = TOGETHER * HEAD_DIM
    windows = counts.shape[0]
    head = lambda k: (lambda h, s: (0, k * HEADS // TOGETHER + start + h))
    first = lambda h, s: (start + h, 0, 0)
    states = pl.BlockSpec((STATES, wide), head(0))
    return pl.pallas_call(
        summary_backward_kernel,
        grid_spec=pltpu.PrefetchScalarGridSpec(
            num_scalar_prefetch=1,
            grid=(steps,),
            in_specs=[
                states,
                pl.BlockSpec((VOCAB, wide), head(1)),
                pl.BlockSpec((VOCAB, wide), head(2)),
                pl.BlockSpec((windows, VOCAB, 128), lambda h, s: (0, 0, 0)),
                pl.BlockSpec((windows, 1, VOCAB), lambda h, s: (0, 0, 0)),
                states,
                pl.BlockSpec((1, wide), head(0)),
                pl.BlockSpec((1, 8, 128), first),
            ]
            + [pl.BlockSpec(memory_space=pl.ANY)] * len(deps),
            out_specs=[pl.BlockSpec((TOGETHER, VOCAB, 384), first), states, states],
            scratch_shapes=[
                pltpu.VMEM((STATES, wide), f32),
                pltpu.VMEM((TOGETHER, STATES, VOCAB), f32),
                pltpu.VMEM((TOGETHER, VOCAB, HEAD_DIM), f32),
                pltpu.VMEM((TOGETHER, STATES, VOCAB), bf16),
                pltpu.VMEM((TOGETHER, STATES, VOCAB), bf16),
                pltpu.VMEM((TOGETHER, VOCAB, STATES), bf16),
            ],
        ),
        out_shape=[
            jax.ShapeDtypeStruct((HEADS, VOCAB, 384), bf16),
            jax.ShapeDtypeStruct((STATES, D), bf16),
            jax.ShapeDtypeStruct((STATES, D), bf16),
        ],
        input_output_aliases={9 + len(deps) - 3 + i: i for i in range(len(onto))},
        compiler_params=params(),
        cost_estimate=cost(1e3, 1e3),
        name="summary_backward",
    )(span, state_query, qkv_table, qkv_table, counts, rows, local, forget, low, *deps)


def each_head(kernel, heads, kinds, *refs):
    kinds = "w" * (len(refs) - len(kinds)) + kinds
    for i in range(heads):
        views = {
            "l": lambda r, i=i: r.at[:, lanes_of(i)],
            "b": lambda r, i=i: r.at[i : i + 1],
            "s": lambda r, i=i: r.at[i],
            "w": lambda r: r,
        }
        kernel(*(views[kind](r) for kind, r in zip(kinds, refs)))


def bias_tile(row):
    spread = jnp.broadcast_to(row, (TILE, CONTEXT))
    shifted = pltpu.roll(spread, 0, 1, stride=1, stride_axis=0)
    return shifted[:, : 3 * TILE].T


def attention_forward_kernel(
    live, pick, pick_t, qt, kt, vt, sk, sv, bias_row, mixed_out, lse_out, bias
):
    bias[...] = bias_tile(bias_row[0])
    prev_add = jnp.where(live[0] > 0, 0.0, hidden).astype(f32)
    keys = dot(pick[...], kt[...]).astype(bf16)
    values_t = dot(vt[...], pick_t[...], TN).astype(bf16)
    query = dot(pick[WINDOW:, :], qt[...]).astype(bf16)
    state_values_t = sv[...].astype(f32).T.astype(bf16)
    for j in range(WINDOW // TILE):
        q = query[j * TILE : (j + 1) * TILE]
        scores = []
        for rel in range(3):
            kt_i = j + rel
            s = (
                dot(keys[kt_i * TILE : (kt_i + 1) * TILE], q, NT)
                * (score_scale * log2e)
                + bias[rel * TILE : (rel + 1) * TILE]
            )
            if kt_i * TILE < WINDOW:
                s = s + prev_add
            scores.append(s)
        for st in range(STATES // TILE):
            scores.append(
                dot(sk[st * TILE : (st + 1) * TILE, :], q, NT) * (score_scale * log2e)
            )
        peak = functools.reduce(
            jnp.maximum, [jnp.max(s, axis=0, keepdims=True) for s in scores]
        )
        total = jnp.zeros((1, TILE), f32)
        out = jnp.zeros((HEAD_DIM, TILE), f32)
        for i, s in enumerate(scores):
            p = jnp.exp2(s - peak)
            total = total + jnp.sum(p, axis=0, keepdims=True)
            if i < 3:
                v = values_t[:, (j + i) * TILE : (j + i + 1) * TILE]
            else:
                v = state_values_t[:, (i - 3) * TILE : (i - 2) * TILE]
            out = out + dot(v, p.astype(bf16))
        out = out * (1.0 / total)
        mixed_out[j * TILE : (j + 1) * TILE, :] = out.T.astype(bf16)
        lse_out[0, :, j * TILE : (j + 1) * TILE] = peak + jnp.log2(total)


def attention_forward(live, pick, pick_t, qkv_table, sk, sv, bias_rows):
    heads, wide = 4, 4 * HEAD_DIM
    head = lambda k: (lambda h, s: (0, k * HEADS // heads + h))
    whole = lambda *shape: pl.BlockSpec(shape, lambda h, s: (0,) * len(shape))
    return pl.pallas_call(
        functools.partial(each_head, attention_forward_kernel, heads, "wwwlllllblbs"),
        grid_spec=pltpu.PrefetchScalarGridSpec(
            num_scalar_prefetch=1,
            grid=(HEADS // heads,),
            in_specs=[
                whole(CONTEXT, VOCAB),
                whole(VOCAB, CONTEXT),
                pl.BlockSpec((VOCAB, wide), head(0)),
                pl.BlockSpec((VOCAB, wide), head(1)),
                pl.BlockSpec((VOCAB, wide), head(2)),
                pl.BlockSpec((STATES, wide), head(0)),
                pl.BlockSpec((STATES, wide), head(1)),
                pl.BlockSpec((heads, 1, CONTEXT), lambda h, s: (h, 0, 0)),
            ],
            out_specs=[
                pl.BlockSpec((WINDOW, wide), head(0)),
                pl.BlockSpec((heads, 1, WINDOW), lambda h, s: (h, 0, 0)),
            ],
            scratch_shapes=[pltpu.VMEM((heads, 3 * TILE, TILE), f32)],
        ),
        out_shape=[
            jax.ShapeDtypeStruct((WINDOW, D), bf16),
            jax.ShapeDtypeStruct((HEADS, 1, WINDOW), f32),
        ],
        compiler_params=params(),
        cost_estimate=cost(1e3, 1e3),
        name="attention_forward",
    )(live, pick, pick_t, qkv_table, qkv_table, qkv_table, sk, sv, bias_rows)


def back_tile(s, dp, shift, inner):
    p = jnp.exp2(s - shift)
    return p, p * (dp - inner)


def state_backward_kernel(pick, qt, sk, sv, lse, mixed, grad, *rest):
    gsk_out, gsv_out, gq_out, inner_out = rest[-4:]
    query = dot(pick[WINDOW:, :], qt[...]).astype(bf16)
    state_keys_t = sk[...].astype(f32).T.astype(bf16)
    inner_all = jnp.sum(
        (mixed[...].astype(f32) * grad[...].astype(f32)).T, axis=0, keepdims=True
    )
    inner_out[0] = inner_all
    blocks = WINDOW // TILE
    gq = [jnp.zeros((HEAD_DIM, TILE), f32) for _ in range(blocks)]
    for st in range(STATES // TILE):
        at = slice(st * TILE, (st + 1) * TILE)
        gk = jnp.zeros((TILE, HEAD_DIM), f32)
        gv = jnp.zeros((TILE, HEAD_DIM), f32)
        for j in range(blocks):
            rows = slice(j * TILE, (j + 1) * TILE)
            p, gs = back_tile(
                dot(sk[at, :], query[rows], NT) * (score_scale * log2e),
                dot(sv[at, :], grad[rows, :], NT),
                lse[0, :, rows],
                inner_all[:, rows],
            )
            gs16 = gs.astype(bf16)
            gq[j] = gq[j] + dot(state_keys_t[:, at], gs16)
            gk = gk + dot(gs16, query[rows])
            gv = gv + dot(p.astype(bf16), grad[rows, :])
        gsk_out[at, :] = (gk * score_scale).astype(bf16)
        gsv_out[at, :] = gv.astype(bf16)
    for j in range(blocks):
        gq_out[0, :, j * TILE : (j + 1) * TILE] = gq[j]


def state_backward(pick, qkv_table, state_kv, lse, mixed, grad, deps=()):
    heads, wide = 4, 4 * HEAD_DIM
    head = lambda k: (lambda h: (0, k * HEADS // heads + h))
    tokens = pl.BlockSpec((WINDOW, wide), head(0))
    states = pl.BlockSpec((STATES, wide), head(0))
    row = pl.BlockSpec((heads, 1, WINDOW), lambda h: (h, 0, 0))
    return pl.pallas_call(
        functools.partial(
            each_head, state_backward_kernel, heads, "wlllbll" + "w" * len(deps) + "llbb"
        ),
        grid=(HEADS // heads,),
        in_specs=[
            pl.BlockSpec((CONTEXT, VOCAB), lambda h: (0, 0)),
            pl.BlockSpec((VOCAB, wide), head(0)),
            pl.BlockSpec((STATES, wide), head(0)),
            pl.BlockSpec((STATES, wide), head(1)),
            row,
            tokens,
            tokens,
        ]
        + [pl.BlockSpec(memory_space=pl.ANY)] * len(deps),
        out_specs=[
            states,
            states,
            pl.BlockSpec((heads, HEAD_DIM, WINDOW), lambda h: (h, 0, 0)),
            row,
        ],
        out_shape=[
            pltpu.HBM((STATES, D), bf16),
            pltpu.HBM((STATES, D), bf16),
            jax.ShapeDtypeStruct((HEADS, HEAD_DIM, WINDOW), f32),
            jax.ShapeDtypeStruct((HEADS, 1, WINDOW), f32),
        ],
        compiler_params=params(),
        cost_estimate=cost(1e3, 1e3),
        name="state_backward",
    )(pick, qkv_table, state_kv, state_kv, lse, mixed, grad, *deps)


def token_backward_kernel(
    live, pick, pick_t, qt, kt, vt, bias_row, lse, inner, grad, gq_in, buckets, *rest
):
    g_out, fold_out, bias, bias_grad = rest[-4:]
    bias[...] = bias_tile(bias_row[0])
    bias_grad[...] = jnp.zeros_like(bias_grad)
    prev_add = jnp.where(live[0] > 0, 0.0, hidden).astype(f32)
    both = dot(pick[...], jnp.concatenate([kt[...], vt[...]], axis=1)).astype(bf16)
    keys = both[:, :HEAD_DIM]
    values = both[:, HEAD_DIM:]
    keys_t = dot(kt[...], pick_t[...], TN).astype(bf16)
    query = dot(pick[WINDOW:, :], qt[...]).astype(bf16)
    blocks = WINDOW // TILE
    gq = [gq_in[0, :, j * TILE : (j + 1) * TILE] for j in range(blocks)]
    sums = jnp.zeros((VOCAB, 2 * HEAD_DIM), f32)
    for tile in range(CONTEXT // TILE):
        at = slice(tile * TILE, (tile + 1) * TILE)
        gk = jnp.zeros((TILE, HEAD_DIM), f32)
        gv = jnp.zeros((TILE, HEAD_DIM), f32)
        for j in range(blocks):
            rel = tile - j
            if not 0 <= rel < 3:
                continue
            rows = slice(j * TILE, (j + 1) * TILE)
            rels = slice(rel * TILE, (rel + 1) * TILE)
            shift = lse[0, :, rows]
            if tile * TILE < WINDOW:
                shift = shift - prev_add
            p, gs = back_tile(
                dot(keys[at], query[rows], NT) * (score_scale * log2e) + bias[rels],
                dot(values[at], grad[rows, :], NT),
                shift,
                inner[0, :, rows],
            )
            gs16 = gs.astype(bf16)
            gq[j] = gq[j] + dot(keys_t[:, at], gs16)
            bias_grad[rels] += gs
            gk = gk + dot(gs16, query[rows])
            gv = gv + dot(p.astype(bf16), grad[rows, :])
        pair = jnp.concatenate([gk * score_scale, gv], axis=1).astype(bf16)
        sums = sums + dot(pick_t[:, at], pair)
    g_out[0, :, HEAD_DIM:] = sums
    total = jnp.zeros((HEAD_DIM, VOCAB), f32)
    for j in range(blocks):
        rows = slice(WINDOW + j * TILE, WINDOW + (j + 1) * TILE)
        total = total + dot((gq[j] * score_scale).astype(bf16), pick[rows, :])
    g_out[0, :, :HEAD_DIM] = total.T
    rows = jnp.concatenate(
        [bias_grad[...].T, jnp.zeros((TILE, CONTEXT - 3 * TILE), f32)], axis=1
    )
    count = TILE
    while count > 8:
        count //= 2
        rows = rows[:count] + pltpu.roll(rows[count:], CONTEXT - count, 1)
    folded = rows[0:1]
    for r in range(1, 8):
        folded = folded + pltpu.roll(rows, CONTEXT - r, 1)[r : r + 1]
    pieces = []
    left = folded
    for _ in range(3):
        piece = left.astype(bf16)
        pieces.append(piece)
        left = left - piece.astype(f32)
    pieces = jnp.concatenate(pieces + [jnp.zeros((5, CONTEXT), bf16)], axis=0)
    fold_out[0] = jnp.sum(dot(pieces, buckets[...]), axis=0, keepdims=True)


def token_backward(
    live, pick, pick_t, qkv_table, bias_rows, lse, inner, grad, gq, deps=(), half=None, onto=()
):
    heads, wide = 4, 4 * HEAD_DIM
    count = HEADS // heads if half is None else HEADS // heads // 2
    low = 0 if half is None else half * count
    deps = (*deps, *onto)
    head = lambda k: (lambda h, s: (0, k * HEADS // heads + low + h))
    by_head = lambda *shape: pl.BlockSpec((heads,) + shape, lambda h, s: (low + h, 0, 0))
    flat = lambda *shape: pl.BlockSpec(shape, lambda h, s: (0,) * len(shape))
    return pl.pallas_call(
        functools.partial(
            each_head, token_backward_kernel, heads, "wwwlllbbblbw" + "w" * len(deps) + "bbss"
        ),
        grid_spec=pltpu.PrefetchScalarGridSpec(
            num_scalar_prefetch=1,
            grid=(count,),
            in_specs=[
                flat(CONTEXT, VOCAB),
                flat(VOCAB, CONTEXT),
                pl.BlockSpec((VOCAB, wide), head(0)),
                pl.BlockSpec((VOCAB, wide), head(1)),
                pl.BlockSpec((VOCAB, wide), head(2)),
                by_head(1, CONTEXT),
                by_head(1, WINDOW),
                by_head(1, WINDOW),
                pl.BlockSpec((WINDOW, wide), head(0)),
                by_head(HEAD_DIM, WINDOW),
                flat(CONTEXT, 128),
            ]
            + [pl.BlockSpec(memory_space=pl.ANY)] * len(deps),
            out_specs=[by_head(VOCAB, 384), by_head(1, 128)],
            scratch_shapes=[
                pltpu.VMEM((heads, 3 * TILE, TILE), f32),
                pltpu.VMEM((heads, 3 * TILE, TILE), f32),
            ],
        ),
        out_shape=[
            jax.ShapeDtypeStruct((HEADS, VOCAB, 384), f32),
            jax.ShapeDtypeStruct((HEADS, 1, 128), f32),
        ],
        input_output_aliases={12 + len(deps) - 2 + i: i for i in range(len(onto))},
        compiler_params=params(),
        cost_estimate=cost(1e3, 1e3),
        name="token_backward",
    )(
        live,
        pick,
        pick_t,
        qkv_table,
        qkv_table,
        qkv_table,
        bias_rows,
        lse,
        inner,
        grad,
        gq,
        jnp.asarray(np.pad(lane_pick().T, ((0, 0), (0, 96))), bf16),
        *deps,
    )


def mlp_kernel(x, cot, up, down, out_in, gx_in, gd_out, gu_out, out, gx, xt):
    @pl.when(pl.program_id(0) == 0)
    def _():
        out[...] = out_in[...]
        gx[...] = gx_in[...]
        xt[...] = x[...].astype(f32).T.astype(bf16)

    up_b = up[...]
    down_b = down[...]
    pre = dot(x[...], up_b)
    root = math.sqrt(2.0 / math.pi)
    square = pre * pre
    t = jnp.tanh(root * pre * (1.0 + 0.044715 * square))
    half = 0.5 * (1.0 + t)
    act = (pre * half).astype(bf16)
    slope = half + (0.5 * root) * pre * (1.0 - t * t) * (1.0 + (3 * 0.044715) * square)
    grad_pre = (dot(cot[...], down_b, NT) * slope).astype(bf16)
    out[...] += dot(act, down_b)
    gx[...] += dot(grad_pre, up_b, NT)
    gd_out[...] = dot(act, cot[...], TN).astype(bf16)
    gu_out[...] = dot(xt[...], grad_pre).astype(bf16)


def mlp_part(part, x, cot, up, down, out, gx):
    count = FF // SPLITS // TILE
    whole = pl.BlockSpec((WINDOW, D), lambda s: (0, 0))
    return pl.pallas_call(
        mlp_kernel,
        grid=(count,),
        in_specs=[
            whole,
            whole,
            pl.BlockSpec((D, TILE), lambda s: (0, SPLITS * s + part)),
            pl.BlockSpec((TILE, D), lambda s: (SPLITS * s + part, 0)),
            whole,
            whole,
        ],
        out_specs=[
            pl.BlockSpec((TILE, D), lambda s: (s, 0)),
            pl.BlockSpec((D, TILE), lambda s: (0, s)),
            whole,
            whole,
        ],
        out_shape=[
            jax.ShapeDtypeStruct((count * TILE, D), bf16),
            jax.ShapeDtypeStruct((D, count * TILE), bf16),
            jax.ShapeDtypeStruct((WINDOW, D), f32),
            jax.ShapeDtypeStruct((WINDOW, D), f32),
        ],
        scratch_shapes=[pltpu.VMEM((D, WINDOW), bf16)],
        compiler_params=params(),
        cost_estimate=cost(1e3, 1e3),
        name="feed_forward",
    )(x, cot, up, down, out, gx)


def mlp_packed_kernel(
    places, x, xs, cot, up_a, up_b, up_c, up_d, down_a, down_b, down_c, down_d, out_in, gx_in,
    *rest,
):
    send, keep, out, gx, gd_s = rest[-5:]
    core = places[CORE]
    step = pl.program_id(0)

    @pl.when(step == 0)
    def _():
        out[...] = out_in[...]
        gx[...] = gx_in[...]

    up = jnp.concatenate([up_a[...], up_b[...], up_c[...], up_d[...]], axis=1)
    down = jnp.concatenate([down_a[...], down_b[...], down_c[...], down_d[...]], axis=0)
    pre = dot(x[...], up)
    root = math.sqrt(2.0 / math.pi)
    square = pre * pre
    t = jnp.tanh(root * pre * (1.0 + 0.044715 * square))
    half = 0.5 * (1.0 + t)
    act = (pre * half).astype(bf16)
    slope = half + (0.5 * root) * pre * (1.0 - t * t) * (1.0 + (3 * 0.044715) * square)
    grad_pre = (dot(cot[...], down, NT) * slope).astype(bf16)
    out[...] += dot(act, down)
    gx[...] += dot(grad_pre, up, NT)
    gd = dot(act, cot[...], TN).astype(bf16)
    for i in range(2):
        for q in range(2):
            at = (2 * i + q) * 128
            gd_s[q, i] = gd[at : at + 128]
    lanes = pl.ds(pl.multiple_of(step * 512, 512), 512)
    for i in range(2):
        z = 2 * step + i
        send[pl.ds(z, 1), :128, :] = gd_s[pl.ds(1 - core, 1), i]
        keep[pl.ds(z, 1), :128, :] = gd_s[pl.ds(core, 1), i]
    for slot, ref in ((0, send), (1, keep)):
        gu = dot(xs[slot], grad_pre).astype(bf16)
        ref[:, 128:, lanes] = gu.reshape(4, 128, 512)


def mlp_packed(part, places, x, split, cot, up, down, out, gx, deps=()):
    block = pl.BlockSpec((WINDOW, D), lambda g, s: (0, 0))
    packed = pl.BlockSpec((4, 256, D), lambda g, s: (0, 0, 0))
    at = lambda k: (lambda g: (4 * g + k) * 4 + part)
    return pl.pallas_call(
        mlp_packed_kernel,
        grid_spec=pltpu.PrefetchScalarGridSpec(
            num_scalar_prefetch=1,
            grid=(2,),
            in_specs=[block, pl.BlockSpec((2, WINDOW, WINDOW), lambda g, s: (0, 0, 0)), block]
            + [
                pl.BlockSpec((D, 128), lambda g, s, k=k: (0, at(k)(g)))
                for k in range(4)
            ]
            + [
                pl.BlockSpec((128, D), lambda g, s, k=k: (at(k)(g), 0))
                for k in range(4)
            ]
            + [block, block]
            + [pl.BlockSpec(memory_space=pl.ANY)] * len(deps),
            out_specs=[packed, packed, block, block],
            scratch_shapes=[pltpu.VMEM((2, 2, 128, D), bf16)],
        ),
        out_shape=[
            jax.ShapeDtypeStruct((4, 256, D), bf16),
            jax.ShapeDtypeStruct((4, 256, D), bf16),
            jax.ShapeDtypeStruct((WINDOW, D), f32),
            jax.ShapeDtypeStruct((WINDOW, D), f32),
        ],
        compiler_params=params(32),
        cost_estimate=cost(1e3, 1e3),
        name="feed_forward",
    )(places, x, split, cot, up, up, up, up, down, down, down, down, out, gx, *deps)


def one_block(array):
    return pl.BlockSpec(array.shape, lambda g: (0,) * len(array.shape))


def single(kernel, name, ins, outs, scratch=(), deps=()):
    return pl.pallas_call(
        kernel,
        grid=(1,),
        in_specs=[one_block(a) for a in ins]
        + [pl.BlockSpec(memory_space=pl.ANY)] * len(deps),
        out_specs=[one_block(o) for o in outs],
        out_shape=list(outs),
        scratch_shapes=list(scratch),
        compiler_params=params(),
        cost_estimate=cost(1e3, 1e3),
        name=name,
    )(*ins, *deps)


def like(kind, *shape):
    return jax.ShapeDtypeStruct(shape, kind)


def kept(kind, *shape):
    return pltpu.HBM(shape, kind)


def stays(*arrays):
    return tuple(pltpu.with_memory_space_constraint(a, pltpu.HBM) for a in arrays)


def unit_of(value):
    unit, inv = norm_parts(value)
    return unit, jnp.broadcast_to(inv, (value.shape[0], 128))


def table_kernel(table, gain, weight, *rest):
    unit_out, inv_out, normed_out, qkv_out = rest[-4:]

    @pl.when(pl.program_id(0) == 0)
    def _():
        unit, inv = unit_of(table[...].astype(f32))
        unit_out[...] = unit
        inv_out[...] = inv
        normed_out[...] = (unit * gain[...]).astype(bf16)

    qkv_out[...] = dot(normed_out[...], weight[...]).astype(bf16)


def table_more_kernel(normed, weight, *rest):
    rest[-1][...] = dot(normed[...], weight[...]).astype(bf16)


def table_forward(table, gain, weight):
    flat = lambda *shape: pl.BlockSpec(shape, lambda g: (0, 0))
    return pl.pallas_call(
        table_kernel,
        grid=(2,),
        in_specs=[
            flat(VOCAB, D),
            flat(1, D),
            pl.BlockSpec((D, D // 2), lambda g: (0, g)),
        ],
        out_specs=[
            flat(VOCAB, D),
            flat(VOCAB, 128),
            flat(VOCAB, D),
            pl.BlockSpec((VOCAB, D // 2), lambda g: (0, g)),
        ],
        out_shape=[
            kept(f32, VOCAB, D),
            kept(f32, VOCAB, 128),
            like(bf16, VOCAB, D),
            like(bf16, VOCAB, 3 * D),
        ],
        compiler_params=params(),
        cost_estimate=cost(1e3, 1e3),
        name="table_forward",
    )(*stays(table), gain, *stays(weight))


def table_more(third, normed, weight, onto, deps=()):
    return pl.pallas_call(
        table_more_kernel,
        grid=(2,),
        in_specs=[
            pl.BlockSpec((VOCAB, D), lambda g: (0, 0)),
            pl.BlockSpec((D, D // 2), lambda g: (0, 2 * third + g)),
        ]
        + [pl.BlockSpec(memory_space=pl.ANY)] * (1 + len(deps)),
        out_specs=pl.BlockSpec((VOCAB, D // 2), lambda g: (0, 2 * third + g)),
        out_shape=like(bf16, VOCAB, 3 * D),
        input_output_aliases={2: 0},
        compiler_params=params(),
        cost_estimate=cost(1e3, 1e3),
        name="table_more",
    )(normed, *stays(weight), onto, *deps)


def states_forward_kernel(states, gain, weight, unit_out, inv_out, normed_out, kv_out):
    step = pl.program_id(0)

    @pl.when(step == 0)
    def _():
        unit, inv = unit_of(states[...])
        unit_out[...] = unit
        inv_out[...] = inv
        normed_out[...] = (unit * gain[...]).astype(bf16)

    kv_out[...] = dot(normed_out[...], weight[...]).astype(bf16)


def states_forward(states, gain, weight):
    flat = lambda *shape: pl.BlockSpec(shape, lambda g: (0, 0))
    return pl.pallas_call(
        states_forward_kernel,
        grid=(4,),
        in_specs=[
            flat(STATES, D),
            flat(1, D),
            pl.BlockSpec((D, D // 2), lambda g: (0, g)),
        ],
        out_specs=[
            flat(STATES, D),
            flat(STATES, 128),
            flat(STATES, D),
            pl.BlockSpec((STATES, D // 2), lambda g: (0, g)),
        ],
        out_shape=[
            kept(f32, STATES, D),
            kept(f32, STATES, 128),
            kept(bf16, STATES, D),
            like(bf16, STATES, 2 * D),
        ],
        compiler_params=params(),
        cost_estimate=cost(1e3, 1e3),
        name="states_forward",
    )(states, gain, weight)


def residual_kernel(
    places, mixed, out_weight, pick, table, gain, res_out, unit_out, inv_out, in_out, split_out, xt
):
    res = dot(pick[WINDOW:, :], table[...]) + dot(mixed[...], out_weight[...])
    res_out[...] = res
    unit, inv = unit_of(res)
    unit_out[...] = unit
    inv_out[...] = inv
    x = unit * gain[...]
    in_out[...] = x.astype(bf16)
    xt[...] = x.T.astype(bf16)
    core = places[CORE]
    for z in range(4):
        for slot, parity in ((0, 1 - core), (1, core)):
            at = pl.multiple_of((2 * z + parity) * 128, 128)
            split_out[slot, z * 128 : (z + 1) * 128, :] = xt[pl.ds(at, 128), :]


def residual_forward(places, *ins):
    outs = (
        like(f32, WINDOW, D),
        kept(f32, WINDOW, D),
        kept(f32, WINDOW, 128),
        like(bf16, WINDOW, D),
        like(bf16, 2, WINDOW, WINDOW),
    )
    return pl.pallas_call(
        residual_kernel,
        grid_spec=pltpu.PrefetchScalarGridSpec(
            num_scalar_prefetch=1,
            grid=(1,),
            in_specs=[whole(a) for a in ins],
            out_specs=[whole(o) for o in outs],
            scratch_shapes=[pltpu.VMEM((D, WINDOW), bf16)],
        ),
        out_shape=list(outs),
        compiler_params=params(),
        cost_estimate=cost(1e3, 1e3),
        name="residual_forward",
    )(places, *ins)


def feed_back_kernel(
    gx, unit, inv, gain, upstream, mixed, out_weight, pick, *rest
):
    gain_out, out_out, mixed_out, rows_out = rest[-4:]
    g = gx[...]
    u = unit[...]
    gain_out[...] = jnp.sum(g * u, axis=0, keepdims=True)
    back = norm_back(u, inv[:, :1], gain[...], g)
    grad = (upstream[...].astype(f32) + back).astype(bf16)
    mixed_out[...] = dot(grad, out_weight[...], NT).astype(bf16)
    out_out[...] = dot(mixed[...], grad, TN).astype(bf16)
    rows_out[...] = dot(pick[WINDOW:, :], grad, TN).astype(bf16)


def feed_back(v, gx, deps=()):
    return single(
        feed_back_kernel,
        "feed_back",
        (
            gx,
            v.mlp_unit,
            v.mlp_inv,
            v.mlp_gain,
            v.upstream,
            v.mixed,
            v.out_weight,
            v.pick,
        ),
        (like(f32, 1, D), like(bf16, D, D), like(bf16, WINDOW, D), like(bf16, VOCAB, D)),
        deps=deps,
    )


def states_back_kernel(
    gsk, gsv, weight, normed, unit, inv, gain, slope, forget, *rest
):
    k_out, v_out, gain_out, local_out, gate_out = rest[-5:]
    upstream = dot(gsk[...], weight[:, :D], NT) + dot(gsv[...], weight[:, D:], NT)
    u = unit[...]
    gain_out[...] = jnp.sum(upstream * u, axis=0, keepdims=True)
    local = norm_back(u, inv[:, :1], gain[...], upstream)
    local_out[...] = local
    f = forget[...]
    gate_out[...] = jnp.sum(local * slope[...], axis=0, keepdims=True) * f * (1.0 - f)
    k_out[...] = dot(normed[...], gsk[...], TN).astype(bf16)
    v_out[...] = dot(normed[...], gsv[...], TN).astype(bf16)


def states_back(v, gsk, gsv, deps=()):
    return single(
        states_back_kernel,
        "states_back",
        (
            *stays(gsk, gsv),
            v.state_kv_weight,
            *stays(v.state_normed, v.state_unit, v.state_inv),
            v.state_gain,
            *stays(v.forget_slope),
            v.forget,
        ),
        (
            like(bf16, D, D),
            like(bf16, D, D),
            like(f32, 1, D),
            like(f32, STATES, D),
            like(f32, 1, D),
        ),
        deps=deps,
    )


XI, YI, ZI, CORE, DPI, SEQI = range(6)


def permute(value, axis, to):
    size = lax.axis_size(axis)
    return lax.ppermute(value, axis, [(i, to(i)) for i in range(size)])


def swap_core(value):
    return permute(value, "seq", lambda i: i ^ 1)


def swap_dp(value, step):
    return permute(value, "dp", lambda i: i ^ step)


def ahead(value, step):
    return permute(value, "seq", lambda i: (i + 2 * step) % 8)


def fitted():
    return lax.axis_size("seq") == 8 and lax.axis_size("dp") == 4


def whole(array):
    return pl.BlockSpec(array.shape, lambda g, s: (0,) * len(array.shape))


def blend(name, places, outs, deps=(), through=()):
    arrays, in_specs, plan, out_specs = [], [], [], []
    for shape, rows, blocks, segments in outs:
        every = 4 // blocks
        rows_of = []
        for sources in segments:
            names = []
            for array, block_rows, place in sources:
                names.append(len(arrays))
                arrays.append(array)
                in_specs.append(
                    pl.BlockSpec(
                        (1, block_rows, array.shape[2]),
                        lambda g, s, place=place, every=every: (*place(g // every, s), 0),
                    )
                )
            rows_of.append((sources[0][1], names))
        plan.append((every, rows_of))
        out_specs.append(
            pl.BlockSpec((1, rows, shape[2]), lambda g, s, every=every: (g // every, 0, 0))
        )
    count = len(arrays)

    def kernel(s, *refs):
        step = pl.program_id(0)
        out_refs = refs[count + len(deps) + len(through) :]

        def fill(out_ref, rows_of):
            at = 0
            for rows, names in rows_of:
                total = refs[names[0]][0].astype(f32)
                for i in names[1:]:
                    total = total + refs[i][0].astype(f32)
                out_ref[0, at : at + rows, :] = total.astype(out_ref.dtype)
                at += rows

        for out_ref, (every, rows_of) in zip(out_refs, plan):
            if every == 1:
                fill(out_ref, rows_of)
            else:
                pl.when(step % every == 0)(functools.partial(fill, out_ref, rows_of))

    return pl.pallas_call(
        kernel,
        grid_spec=pltpu.PrefetchScalarGridSpec(
            num_scalar_prefetch=1,
            grid=(4,),
            in_specs=in_specs
            + [pl.BlockSpec(memory_space=pl.ANY)] * (len(deps) + len(through)),
            out_specs=out_specs + [pl.BlockSpec(memory_space=pl.ANY)] * len(through),
        ),
        out_shape=[jax.ShapeDtypeStruct(shape, bf16) for shape, _, _, _ in outs]
        + [jax.ShapeDtypeStruct(t.shape, t.dtype) for t in through],
        input_output_aliases={
            1 + count + len(deps) + i: len(outs) + i for i in range(len(through))
        },
        compiler_params=params(),
        cost_estimate=cost(1e3, 1e3),
        name=name,
    )(places, *arrays, *deps, *through)


class Wing:
    def __init__(self, lead, kept, came, base, rows):
        self.lead, self.trail = lead, 1 - lead
        self.kept, self.came, self.base = kept, came, base
        self.half, self.quarter = rows // 2, rows // 4
        self.columns = kept.shape[2]
        self.got = []

    def first(self):
        at = self.base // self.half
        other = lambda g, s: (g, at + 1 - s[self.lead])
        return self.half, [(self.kept, self.half, other), (self.came, self.half, other)]

    def second(self):
        q = self.quarter
        at = self.base // q
        array, start = self.got[0]
        start = start // q
        deep = lambda g, s: (g, at + 2 * s[self.lead] + 1 - s[self.trail])
        flat = lambda g, s: (g, start + 1 - s[self.trail])
        return q, [(self.kept, q, deep), (self.came, q, deep), (array, q, flat)]

    def quarters(self, level):
        q = self.quarter
        at = self.base // q
        (one, start_one), (two, start_two) = self.got
        start_one, start_two = start_one // q, start_two // q
        deep = lambda g, s: (level(g, s), at + 2 * s[self.lead] + s[self.trail])
        flat = lambda g, s: (level(g, s), start_one + s[self.trail])
        last = lambda g, s: (level(g, s), start_two)
        return [(self.kept, q, deep), (self.came, q, deep), (one, q, flat), (two, q, last)]


def wings(kept, came):
    half = kept.shape[1] // 2
    return [Wing(XI, kept, came, 0, half), Wing(YI, kept, came, half, half)]


class Column:
    def __init__(self, parts):
        self.parts = parts
        self.rows = sum(w.quarter for w in parts)
        self.columns = parts[0].columns

    def near(self):
        outs = []
        for own in (False, True):
            level = (
                (lambda g, s: 2 * g + s[ZI] % 2)
                if own
                else (lambda g, s: 2 * g + 1 - s[ZI] % 2)
            )
            segments = [w.quarters(level) for w in self.parts]
            outs.append(((2, self.rows, self.columns), self.rows, 2, segments))
        return outs

    def rest(self, pick, extra=()):
        sources = [
            (array, self.rows, lambda g, s: (pick(s), 0))
            for array in (self.kept, self.from_near)
        ] + [(array, self.rows, lambda g, s: (0, 0)) for array in extra]
        return [((1, self.rows, self.columns), self.rows, 1, [sources])]

    def doubled(self, step):
        if step == 1:
            sources = [w.quarters(lambda g, s: g) for w in self.parts]
        else:
            sources = [
                [(a, self.rows, lambda g, s: (g, 0)) for a in (self.sum, self.other)]
            ]
        return [((4, self.rows, self.columns), self.rows, 4, sources)]

    def far(self):
        return self.rest(lambda s: 1 - s[ZI] // 2)

    def close(self):
        return self.rest(lambda s: s[ZI] // 2, [self.from_far])


class Traffic:
    def __init__(self, places):
        self.places = places
        self.pending = []

    def swap(self, send):
        came = swap_core(send)
        self.pending.append(came)
        return came

    def boundary(self, after, first=(), second=(), near=(), far=(), close=(), swap=(), join=(), double=None):
        outs, sent = [], []
        for axis in (XI, YI):
            groups = {}
            for w in first:
                if w.lead == axis:
                    groups.setdefault(w.columns, []).append((w, w.first()))
            for w in second:
                if w.trail == axis:
                    groups.setdefault(w.columns, []).append((w, w.second()))
            for columns, moves in groups.items():
                moves.sort(key=lambda m: -m[1][0])
                rows = sum(m[1][0] for m in moves)
                outs.append(
                    ((4, rows, columns), rows, 4, [m[1][1] for m in moves])
                )
                sent.append((axis, moves))
        for columns, step in ((near, Column.near), (far, Column.far), (close, Column.close)):
            for c in columns:
                outs += step(c)
        if double:
            outs += double[0].doubled(double[1])
        if join:
            segments = [c.close()[0][3][0] for c in join]
            total = sum(c.rows for c in join)
            outs.append(((1, total, join[0].columns), total, 1, segments))
        results = blend("boundary", self.places, outs, (*after, *self.pending), swap)
        self.pending = []
        mark = results[0]
        results = list(results)
        for axis, moves in sent:
            came = swap_dp(results.pop(0), 1 << axis)
            self.pending.append(came)
            at = 0
            for w, (rows, _) in moves:
                assert at % w.quarter == 0
                w.got.append((came, at))
                at += rows
        for c in near:
            c.from_near = permute(results.pop(0), "seq", lambda i: i ^ 2)
            c.kept = results.pop(0)
            self.pending.append(c.from_near)
        for c in far:
            c.from_far = permute(results.pop(0), "seq", lambda i: i ^ 4)
            self.pending.append(c.from_far)
        for c in close:
            c.own = results.pop(0)
        if double:
            column, step = double
            column.sum = results.pop(0)
            if step < 3:
                column.other = permute(column.sum, "seq", lambda i: i ^ (2 * step))
                self.pending.append(column.other)
        if join:
            self.joined = results.pop(0)
        self.swapped = [self.swap(send) for send in results]
        return mark

    def spread(self, own, lead=1):
        beside = swap_dp(own, lead)
        other = swap_dp(own, 3 - lead)
        rows = [own, beside, other, swap_dp(beside, 3 - lead)]
        self.pending += rows[1:]
        return rows if lead == 1 else [own, other, beside, rows[3]]


def packed_pair(name, places, pieces, deps=()):
    rows = sum(p.shape[1] for p in pieces)
    columns = pieces[0].shape[2]
    outs = []
    for keep in (False, True):
        place = (
            (lambda g, s: (2 * g + s[CORE], 0))
            if keep
            else (lambda g, s: (2 * g + 1 - s[CORE], 0))
        )
        outs.append(
            ((4, rows, columns), rows, 4, [[(p, p.shape[1], place)] for p in pieces])
        )
    return blend(name, places, outs, deps)


def pack_rows(places, mark, g_tokens, g, rows_sum, *vectors):
    count = 3 + len(vectors)

    def kernel(s, *refs):
        for out_ref, (a, b, r, *rows) in zip(
            refs[2 * count + 1 :], (refs[:count], refs[count : 2 * count])
        ):
            out_ref[0, :VOCAB, :] = (a[0] + b[0].astype(f32)).astype(bf16)
            out_ref[0, VOCAB:, :128] = r[:128, :]
            out_ref[0, VOCAB:, 128:256] = r[128:, :]
            place = lax.broadcasted_iota(jnp.int32, (128, 128), 0)
            small = jnp.zeros((128, 128), f32)
            for i, row in enumerate(rows):
                value = row[...] if len(row.shape) == 2 else row[0]
                small = jnp.where(place == i, value, small)
            out_ref[0, VOCAB:, 256:] = small.astype(bf16)

    specs, arrays = [], []
    for keep in (False, True):
        at = (
            (lambda i, s: 2 * i + s[CORE]) if keep else (lambda i, s: 2 * i + 1 - s[CORE])
        )
        for array in (g_tokens, g, rows_sum, *vectors):
            arrays.append(array)
            if array.ndim == 2:
                specs.append(
                    pl.BlockSpec((array.shape[0], 128), lambda i, s, at=at: (0, at(i, s)))
                )
            else:
                specs.append(
                    pl.BlockSpec(
                        (1,) + array.shape[1:], lambda i, s, at=at: (at(i, s), 0, 0)
                    )
                )
    return pl.pallas_call(
        kernel,
        grid_spec=pltpu.PrefetchScalarGridSpec(
            num_scalar_prefetch=1,
            grid=(4,),
            in_specs=specs + [pl.BlockSpec(memory_space=pl.ANY)],
            out_specs=[pl.BlockSpec((1, 384, 384), lambda i, s: (i, 0, 0))] * 2,
        ),
        out_shape=[like(bf16, 4, 384, 384)] * 2,
        compiler_params=params(),
        cost_estimate=cost(1e3, 1e3),
        name="pack_rows",
    )(places, *arrays, mark)


def slot_of(s, step, lead):
    there = s[DPI] ^ step
    x, y = there % 2, there // 2
    return 2 * x + y if lead == XI else 2 * y + x


def unpack(name, places, quarters, pieces, outs):
    columns = quarters[0].shape[2]
    total = 4 * sum(p[1] for p in pieces)

    def kernel(s, *refs):
        scratch = refs[-1]
        for step in range(4):
            for start, rows, lead, base in pieces:
                at = pl.multiple_of(slot_of(s, step, lead) * rows + base, 16)
                scratch[pl.ds(at, rows), :] = refs[step][0, start : start + rows, :].astype(
                    f32
                )
        for out_ref, (_, moves) in zip(refs[4:-1], outs):
            if not moves:
                out_ref[...] = jnp.zeros_like(out_ref)
            for row, rows, to, column in moves:
                out_ref[to : to + rows, column : column + columns] = scratch[
                    row : row + rows, :
                ]

    return pl.pallas_call(
        kernel,
        grid_spec=pltpu.PrefetchScalarGridSpec(
            num_scalar_prefetch=1,
            grid=(1,),
            in_specs=[whole(q) for q in quarters],
            out_specs=[
                pl.BlockSpec(shape, lambda g, s: (0, 0)) for shape, _ in outs
            ],
            scratch_shapes=[pltpu.VMEM((total, columns), f32)],
        ),
        out_shape=[jax.ShapeDtypeStruct(shape, f32) for shape, _ in outs],
        compiler_params=params(),
        cost_estimate=cost(1e3, 1e3),
        name=name,
    )(places, *quarters)


def unpack_mlp(places, quarters):
    def kernel(s, *refs):
        down, up, mark, scratch = refs[8:]
        mark[...] = jnp.zeros_like(mark)
        for pair in range(2):
            for step in range(4):
                block = refs[4 * pair + step]
                for part in range(2):
                    for lead in range(2):
                        at = pl.multiple_of(slot_of(s, step, lead) * 32 + 128 * lead, 32)
                        start = part * 64 + lead * 32
                        scratch[2 * pair + part, pl.ds(at, 32), :] = block[
                            0, start : start + 32, :
                        ].astype(f32)
        for part in range(4):
            down[part * 128 : (part + 1) * 128, :] = scratch[part, :128, :]
            for block in range(8):
                at = (4 * block + part) * 128
                up[:, at : at + 128] = scratch[part, 128:, block * 128 : (block + 1) * 128]

    flat = [q for pair in quarters for q in pair]
    return pl.pallas_call(
        kernel,
        grid_spec=pltpu.PrefetchScalarGridSpec(
            num_scalar_prefetch=1,
            grid=(1,),
            in_specs=[whole(q) for q in flat],
            out_specs=[
                pl.BlockSpec((512, D), lambda g, s: (0, 0)),
                pl.BlockSpec((128, FF), lambda g, s: (0, 0)),
                pl.BlockSpec((8, 128), lambda g, s: (0, 0)),
            ],
            scratch_shapes=[pltpu.VMEM((4, 256, D), f32)],
        ),
        out_shape=[
            jax.ShapeDtypeStruct((512, D), f32),
            jax.ShapeDtypeStruct((128, FF), f32),
            jax.ShapeDtypeStruct((8, 128), f32),
        ],
        compiler_params=params(),
        cost_estimate=cost(1e3, 1e3),
        name="unpack_mlp",
    )(places, *flat)


def stack_rows(places, parts, deps=()):
    _, rows, columns = parts[0].shape
    rows //= 2

    def kernel(s, *refs):
        out = refs[-1]
        for step in range(4):
            for lead in range(2):
                at = pl.multiple_of(slot_of(s, step, lead) * rows + 4 * rows * lead, 16)
                out[:, pl.ds(at, rows), :] = refs[step][:, lead * rows : (lead + 1) * rows, :]

    shape = (4, 8 * rows, columns)
    return pl.pallas_call(
        kernel,
        grid_spec=pltpu.PrefetchScalarGridSpec(
            num_scalar_prefetch=1,
            grid=(1,),
            in_specs=[whole(p) for p in parts]
            + [pl.BlockSpec(memory_space=pl.ANY)] * len(deps),
            out_specs=pl.BlockSpec(shape, lambda g, s: (0, 0, 0)),
        ),
        out_shape=jax.ShapeDtypeStruct(shape, bf16),
        compiler_params=params(),
        cost_estimate=cost(1e3, 1e3),
        name="stack_rows",
    )(places, *parts, *deps)


def last_kernel(
    s, mine, other, norm_cols, unit_cols, weight, weight_rows, unit, inv, gain,
    qkv_out, gain_out, table_out, small_out, by_head,
):
    for z in range(4):
        for q in range(2):
            by_head[2 * z + q] = jnp.where(s[CORE] == q, mine[z], other[z])
    small_out[...] = mine[s[ZI], 256:272, 256:].astype(f32)[:8]
    at = pl.multiple_of(s[SEQI] * 32, 32)
    norm = norm_cols[...]
    cols_grad = jnp.zeros((VOCAB, 128), f32)
    normed_grad = jnp.zeros((32, D), f32)
    for h in range(HEADS):
        for t in range(3):
            lanes = slice(t * 128, (t + 1) * 128)
            to = slice(t * D + h * 128, t * D + (h + 1) * 128)
            g = by_head[h, :VOCAB, lanes]
            qkv_out[:, to] = dot(norm, g, TN)
            cols_grad = cols_grad + dot(g, weight_rows[:, to], NT)
            normed_grad = normed_grad + dot(
                by_head[h, pl.ds(at, 32), lanes], weight[:, to], NT
            )
    gain_out[...] = jnp.sum(cols_grad * unit_cols[...], axis=0, keepdims=True)
    u = unit[...]
    scaled = normed_grad * gain[...]
    a = jnp.mean(scaled, axis=-1, keepdims=True)
    b = jnp.mean(scaled * u, axis=-1, keepdims=True)
    low = pl.multiple_of(VOCAB + (s[SEQI] % 4) * 32, 32)
    rows_sum = [
        jnp.where(
            s[SEQI] < 4,
            by_head[h, pl.ds(low, 32), :128].astype(f32),
            by_head[h, pl.ds(low, 32), 128:256].astype(f32),
        )
        for h in range(HEADS)
    ]
    table_out[...] = (
        jnp.concatenate(rows_sum, axis=1) + (scaled - a - u * b) * inv[:, :1]
    )


def last_products(places, mine, other, normed, unit, weight, inv, gain):
    return pl.pallas_call(
        last_kernel,
        grid_spec=pltpu.PrefetchScalarGridSpec(
            num_scalar_prefetch=1,
            grid=(1,),
            in_specs=[
                whole(mine),
                whole(other),
                pl.BlockSpec((VOCAB, 128), lambda g, s: (0, s[SEQI])),
                pl.BlockSpec((VOCAB, 128), lambda g, s: (0, s[SEQI])),
                whole(weight),
                pl.BlockSpec((128, 3 * D), lambda g, s: (s[SEQI], 0)),
                pl.BlockSpec((32, D), lambda g, s: (s[SEQI], 0)),
                pl.BlockSpec((32, 128), lambda g, s: (s[SEQI], 0)),
                whole(gain),
            ],
            out_specs=[
                pl.BlockSpec((128, 3 * D), lambda g, s: (0, 0)),
                pl.BlockSpec((1, 128), lambda g, s: (0, 0)),
                pl.BlockSpec((32, D), lambda g, s: (0, 0)),
                pl.BlockSpec((8, 128), lambda g, s: (0, 0)),
            ],
            scratch_shapes=[pltpu.VMEM((HEADS, 384, 384), bf16)],
        ),
        out_shape=[
            jax.ShapeDtypeStruct((128, 3 * D), f32),
            jax.ShapeDtypeStruct((1, 128), f32),
            jax.ShapeDtypeStruct((32, D), f32),
            jax.ShapeDtypeStruct((8, 128), f32),
        ],
        compiler_params=params(),
        cost_estimate=cost(1e3, 1e3),
        name="last_products",
    )(places, mine, other, normed, unit, weight, weight, unit, inv, gain)


def total_of(value):
    flat = value.reshape((-1,) + value.shape[2:])
    own = lax.psum_scatter(flat, "seq", scatter_dimension=0, tiled=True)
    return lax.psum(own, "dp").astype(f32)


def places_of():
    here = lax.axis_index("seq")
    dp = lax.axis_index("dp")
    return jnp.stack([dp % 2, dp // 2, here // 2, here % 2, dp, here]).astype(jnp.int32)


def prepare_kernel(
    places, blocks_a, blocks_b, gate, bias, picks, mask, *rest
):
    span, live, counts, rows, pick, pick_t, forget, bias_out = rest[-8:]
    here = places[SEQI]
    sign = lax.broadcasted_iota(jnp.int32, (VOCAB, 128), 0)
    first = jnp.zeros((1, 128), f32)
    before = jnp.zeros((4, 128), jnp.int32)
    for k in range(8):
        block = blocks_a[k] if k < 4 else blocks_b[k - 4]
        w = here ^ k
        total = jnp.zeros((VOCAB, 128), f32)
        for r in range(4):
            total = total + jnp.where(block[r : r + 1] == sign, 1.0, 0.0)
        count = jnp.broadcast_to(jnp.sum(total, axis=1, keepdims=True), (VOCAB, 128))
        counts[pl.ds(w, 1)] = count[None]
        rows[pl.ds(w, 1)] = count.T[:1][None]
        marked = jnp.where(block[4:5] > 0, w.astype(f32), 0.0)
        first = jnp.maximum(first, jnp.where(w <= here, marked, 0.0))
        before = jnp.where(w == here - 1, block[:4], before)
    span[0] = jnp.max(first).astype(jnp.int32)
    span[1] = here
    live[0] = 1 - jnp.max(blocks_a[0, 4:5].astype(f32)).astype(jnp.int32)
    own = blocks_a[0, :4]
    for r in range(8):
        ids = before[r : r + 1] if r < 4 else own[r - 4 : r - 3]
        one = jnp.where(ids == sign, 1.0, 0.0)
        pick_t[:, r * 128 : (r + 1) * 128] = one.astype(bf16)
        pick[r * 128 : (r + 1) * 128, :] = one.T.astype(bf16)
    forget[...] = 1.0 / (1.0 + jnp.exp(-gate[...]))
    table = lax.dot_general(
        bias[...], picks[...], NN, precision=lax.Precision.HIGHEST, preferred_element_type=f32
    )
    table = table * log2e + mask[...]
    for h in range(HEADS):
        bias_out[h] = table[h : h + 1]


def side_by_side(mine, other, deps):
    def kernel(a, b, *rest):
        rest[-1][: a.shape[0]] = a[...]
        rest[-1][a.shape[0] :] = b[...]

    out = like(mine.dtype, 2 * mine.shape[0], *mine.shape[1:])
    return single(kernel, "side_by_side", (mine, other), (out,), deps=deps)[0]


def prepare(places, char_ids, seg_starts, gate_logit, distance_bias, table_parts):
    packed = jnp.concatenate(
        [
            char_ids.reshape(4, 128),
            jnp.broadcast_to(seg_starts, (1, 128)),
            jnp.zeros((3, 128), jnp.int32),
        ],
        axis=0,
    )[None]
    done = ()
    for bit, part in zip((1, 2), table_parts):
        came = permute(packed, "seq", lambda i, bit=bit: i ^ bit)
        done = part(done)
        packed = side_by_side(packed, came, done)
    beyond = permute(packed, "seq", lambda i: i ^ 4)
    deps = table_parts[2](done)
    ins = (
        packed,
        beyond,
        gate_logit.reshape(1, D),
        distance_bias.reshape(HEADS, BUCKETS),
        jnp.asarray(lane_pick()),
        jnp.asarray(lane_hidden()),
    )
    outs = (
        like(jnp.int32, 2),
        like(jnp.int32, 1),
        like(f32, 8, VOCAB, 128),
        like(f32, 8, 1, VOCAB),
        like(bf16, CONTEXT, VOCAB),
        like(bf16, VOCAB, CONTEXT),
        like(f32, 1, D),
        like(f32, HEADS, 1, CONTEXT),
    )
    prepared = pl.pallas_call(
        prepare_kernel,
        grid_spec=pltpu.PrefetchScalarGridSpec(
            num_scalar_prefetch=1,
            grid=(1,),
            in_specs=[whole(a) for a in ins]
            + [pl.BlockSpec(memory_space=pl.ANY)] * len(deps),
            out_specs=[pl.BlockSpec(memory_space=pltpu.SMEM)] * 2
            + [whole(o) for o in outs[2:]],
        ),
        out_shape=list(outs),
        compiler_params=params(),
        cost_estimate=cost(1e3, 1e3),
        name="prepare",
    )(places, *ins, *deps)
    return (*prepared, deps[0])


def plain_prepare(char_ids, seg_starts, gate_logit, distance_bias):
    windows = lax.axis_size("seq")
    here = lax.axis_index("seq")
    packed = jnp.concatenate(
        [char_ids.reshape(4, 128), jnp.broadcast_to(seg_starts, (1, 128))], axis=0
    )
    everyone = lax.all_gather(packed, "seq")
    ids_all = everyone[:, :4].reshape(windows, WINDOW)
    flags = everyone[:, 4, 0]
    order = jnp.arange(windows, dtype=jnp.int32)
    first = jnp.max(jnp.where((flags > 0) & (order <= here), order, 0))
    span = jnp.stack([first, here]).astype(jnp.int32)
    live = (1 - seg_starts.reshape(1)).astype(jnp.int32)
    vocab = jnp.arange(VOCAB, dtype=jnp.int32)
    counts = jnp.sum(
        (ids_all[:, :, None] == vocab[None, None, :]).astype(f32), axis=1
    )
    before = lax.dynamic_index_in_dim(ids_all, jnp.maximum(here - 1, 0), 0, False)
    context_ids = jnp.concatenate([before, char_ids.reshape(-1)])
    bias_rows = jnp.dot(
        distance_bias.reshape(HEADS, BUCKETS),
        jnp.asarray(lane_pick()),
        precision=lax.Precision.HIGHEST,
    ) * log2e + jnp.asarray(lane_hidden())
    return (
        span,
        live,
        jnp.broadcast_to(counts[:, :, None], (windows, VOCAB, 128)),
        counts[:, None, :],
        (context_ids[:, None] == vocab[None, :]).astype(bf16),
        (vocab[:, None] == context_ids[None, :]).astype(bf16),
        jax.nn.sigmoid(gate_logit).reshape(1, D),
        bias_rows.reshape(HEADS, 1, CONTEXT),
    )


def body(
    char_ids,
    seg_starts,
    char_table,
    norm_gain,
    qkv_weight,
    distance_bias,
    state_query,
    state_init,
    state_gain,
    state_kv_weight,
    gate_logit,
    out_weight,
    mlp_gain,
    up_weight,
    down_weight,
    cotangent,
):
    windows = lax.axis_size("seq")
    here = lax.axis_index("seq")
    norm_gain, state_gain, mlp_gain = (
        t.reshape(1, D) for t in (norm_gain, state_gain, mlp_gain)
    )
    table_unit, table_inv, normed_table, qkv_table = table_forward(
        char_table, norm_gain, qkv_weight
    )
    more = lambda third: lambda done: (
        table_more(third, normed_table, qkv_weight, done[0]),
    )
    table_parts = (lambda done: (qkv_table,), more(1), more(2))

    characters = (char_ids, seg_starts, gate_logit, distance_bias)
    if fitted():
        places = places_of()
        *prepared, qkv_table = prepare(places, *characters, table_parts)
    else:
        prepared = plain_prepare(*characters)
        for part in table_parts:
            (qkv_table,) = part((qkv_table,))
    span, live, counts, count_rows, pick, pick_t, forget, bias_rows = prepared
    states_in, forget_slope, lowest = summary_forward(
        span, state_query, qkv_table, counts, count_rows, state_init, forget
    )
    state_unit, state_inv, state_normed, state_kv = states_forward(
        states_in, state_gain, state_kv_weight
    )
    mixed, lse = attention_forward(
        live, pick, pick_t, qkv_table, state_kv, state_kv, bias_rows
    )
    residual, mlp_unit, mlp_inv, mlp_in, mlp_split = residual_forward(
        places if fitted() else jnp.zeros(6, jnp.int32),
        mixed,
        out_weight,
        pick,
        char_table,
        mlp_gain,
    )
    upstream = cotangent.reshape(WINDOW, D)

    close_up = fitted_tail if fitted() else plain_tail
    return close_up(dict(locals()))


def fitted_tail(values):
    v = types.SimpleNamespace(**values)
    places = v.places
    weights = (v.upstream, v.up_weight, v.down_weight)

    out, gx = v.residual, jnp.zeros((WINDOW, D), f32)
    traffic = Traffic(places)
    parts, deps = [], ()
    for part in range(4):
        send, keep, out, gx = mlp_packed(
            part, places, v.mlp_in, v.mlp_split, *weights, out, gx, deps
        )
        if part:
            second = parts[part - 2] if part > 1 else ()
            mark = traffic.boundary((gx,), parts[part - 1], second, swap=[send])
            deps = (mark,)
            came = traffic.swapped[0]
        else:
            came = traffic.swap(send)
        parts.append(wings(keep, came))
    layer_out = out.astype(bf16).reshape(1, WINDOW, D)
    front = Column(parts[0] + parts[1])
    back = Column(parts[2] + parts[3])

    grad_mlp_gain, grad_out, grad_mixed, rows_sum = feed_back(v, gx, (mark,))
    gsk, gsv, gq, inner = state_backward(
        v.pick, v.qkv_table, v.state_kv, v.lse, v.mixed, grad_mixed
    )
    mark = traffic.boundary((inner,), parts[3], parts[2], near=[front])
    grad_k, grad_v, grad_state_gain, local, grad_gate = states_back(v, gsk, gsv, (mark,))
    send, keep = packed_pair(
        "pack_middle",
        places,
        [t.reshape(8, 128, D) for t in (grad_k, grad_v, grad_out)],
    )
    middle = wings(keep, traffic.swap(send))
    summary_args = (
        v.span, v.state_query, v.qkv_table, v.counts, v.count_rows, local, v.forget, v.lowest
    )
    onto = summary_backward(*summary_args, (send,), 0)
    mark = traffic.boundary((onto[0],), middle, parts[3], far=[front])
    g, gsq, ginit = summary_backward(*summary_args, (mark,), 1, onto)
    send, keep = packed_pair(
        "pack_states", places, [gsq.reshape(8, 64, D), ginit.reshape(8, 64, D)]
    )
    mark = traffic.boundary((), (), middle, near=[back], close=[front], swap=[send])
    states = wings(keep, traffic.swapped[0])
    tokens_args = (
        v.live, v.pick, v.pick_t, v.qkv_table, v.bias_rows, v.lse, inner, grad_mixed, gq
    )
    onto = token_backward(*tokens_args, (mark,), 0)
    mark = traffic.boundary((onto[1],), states, far=[back])
    front_rows = traffic.spread(front.own)
    g_tokens, fold = token_backward(*tokens_args, (mark,), 1, onto)
    side, rest = Column(middle), Column(states)
    send, keep = pack_rows(
        places, fold, g_tokens, g, rows_sum, grad_mlp_gain, grad_state_gain, grad_gate, fold
    )
    traffic.boundary((), (), states, near=[side], close=[back], swap=[send])
    rows = wings(keep, traffic.swapped[0])
    last = Column(rows)
    traffic.boundary((), rows, near=[rest], far=[side])
    traffic.boundary((), (), rows, far=[rest])
    back_rows = traffic.spread(back.own, 2)
    traffic.boundary((), double=(last, 1), join=[side, rest])
    side_own = traffic.joined
    traffic.boundary((), double=(last, 2))
    side_rows = traffic.spread(side_own)
    grad_down, grad_up, mark = unpack_mlp(places, [front_rows, back_rows])
    traffic.boundary((mark,), double=(last, 3))
    ring_parts = traffic.spread(last.sum)
    grad_state_kv, grad_out, grad_state_query, grad_state_init, mark = unpack(
        "unpack_side",
        places,
        side_rows,
        [(0, 48, XI, 0), (48, 48, YI, 192), (96, 16, XI, 384), (112, 16, YI, 448)],
        [
            ((128, 2 * D), [(0, 128, 0, 0), (128, 128, 0, D)]),
            ((128, D), [(256, 128, 0, 0)]),
            ((64, D), [(384, 64, 0, 0)]),
            ((64, D), [(448, 64, 0, 0)]),
            ((8, 128), []),
        ],
    )
    mine = stack_rows(places, ring_parts, (mark,))
    other = swap_core(mine)
    grad_qkv, grad_norm_gain, grad_table, small = last_products(
        places,
        mine,
        other,
        v.normed_table,
        v.table_unit,
        v.qkv_weight,
        v.table_inv,
        v.norm_gain,
    )
    return (
        layer_out,
        grad_table,
        grad_norm_gain.reshape(-1),
        grad_qkv,
        small[3, :32],
        grad_state_query,
        grad_state_init,
        small[1],
        grad_state_kv,
        small[2],
        grad_out,
        small[0],
        grad_up,
        grad_down,
    )


def plain_tail(values):
    v = types.SimpleNamespace(**values)
    windows, here = v.windows, v.here
    shard = lambda n: n // windows
    out, gx = v.residual, jnp.zeros((WINDOW, D), f32)
    grads_down, grads_up = [], []
    for part in range(SPLITS):
        gd, gu, out, gx = mlp_part(
            part, v.mlp_in, v.upstream, v.up_weight, v.down_weight, out, gx
        )
        grads_down.append(gd)
        grads_up.append(gu)
    layer_out = out.astype(bf16).reshape(1, WINDOW, D)
    grad_mlp_gain, grad_out, grad_mixed, rows_sum = feed_back(v, gx)
    gsk, gsv, gq, inner = state_backward(
        v.pick, v.qkv_table, v.state_kv, v.lse, v.mixed, grad_mixed
    )
    grad_k, grad_v, grad_state_gain, local, grad_gate = states_back(v, gsk, gsv)
    g, gsq, ginit = summary_backward(
        v.span, v.state_query, v.qkv_table, v.counts, v.count_rows, local, v.forget,
        v.lowest,
    )
    g_tokens, fold = token_backward(
        v.live, v.pick, v.pick_t, v.qkv_table, v.bias_rows, v.lse, inner, grad_mixed, gq
    )
    g = (g.astype(f32) + g_tokens).astype(bf16)
    sharded = lambda t: total_of(t.reshape(windows, -1, t.shape[-1]))
    full = jnp.stack([t.reshape(-1, TILE, D) for t in grads_down], axis=1)
    grad_down = sharded(full.reshape(FF, D))
    full = jnp.stack([t.reshape(D, -1, TILE) for t in grads_up], axis=2)
    grad_up = sharded(full.reshape(D, FF))
    grad_state_kv = sharded(jnp.concatenate([grad_k, grad_v], axis=1))
    small = jnp.concatenate(
        [
            t.reshape(windows, -1)
            for t in (grad_mlp_gain, grad_state_gain, grad_gate, fold[:, 0, :BUCKETS])
        ],
        axis=1,
    )
    small = total_of(small[:, None, :])[0]
    cut = shard(D)
    all_rows = lax.psum(g, ("dp", "seq"))
    grad_rows = jnp.concatenate(
        [
            all_rows[:, :, t * 128 : (t + 1) * 128].transpose(1, 0, 2).reshape(VOCAB, D)
            for t in range(3)
        ],
        axis=1,
    )
    mine = lax.dynamic_slice_in_dim(v.normed_table, here * cut, cut, 1)
    weight_rows = lax.dynamic_slice_in_dim(v.qkv_weight, here * cut, cut, 0)
    unit_cols = lax.dynamic_slice_in_dim(v.table_unit, here * cut, cut, 1)
    at = here * shard(VOCAB)
    take = lambda t: lax.dynamic_slice_in_dim(t, at, shard(VOCAB), 0)
    grad_table = sharded(rows_sum) + norm_back(
        take(v.table_unit),
        take(v.table_inv)[:, :1],
        v.norm_gain,
        dot(take(grad_rows), v.qkv_weight, NT),
    )
    return (
        layer_out,
        grad_table,
        jnp.sum(dot(grad_rows, weight_rows, NT) * unit_cols, axis=0),
        dot(mine, grad_rows, TN),
        small[3 * cut :],
        sharded(gsq),
        sharded(ginit),
        small[cut : 2 * cut],
        grad_state_kv,
        small[2 * cut : 3 * cut],
        sharded(grad_out),
        small[:cut],
        grad_up,
        grad_down,
    )


def solution(mesh):
    placed = (P("dp", "seq"), P("dp", "seq")) + (P(),) * 13 + (P("dp", "seq", None),)
    return jax.shard_map(
        body,
        mesh=mesh,
        in_specs=placed,
        out_specs=(
            P("dp", "seq", None),
            P("seq", None),
            P("seq"),
            P("seq", None),
            P("seq"),
            P("seq", None),
            P("seq", None),
            P("seq"),
            P("seq", None),
            P("seq"),
            P("seq", None),
            P("seq"),
            P("seq", None),
            P("seq", None),
        ),
        check_vma=False,
    )
```
